32 devices in a mesh: groups: 2 (over y), panel: 4 (over z), rhs: 2 (over x), coef: 2 (over core).
Axes of the slice: x: 2, y: 2, z: 4, core: 2. Of those that a mesh axis runs over, the one named last changes fastest.
Arguments:
- couplings: bfloat16 [4, 9, 2, 1024, 2, 2, 512], P('panel', None, 'coef', None, None, 'rhs'), may hold values from -1 to 66, as said below
- observations: bfloat16 [1024, 4, 2, 1024], P(('groups', 'rhs'), 'panel', 'coef'), parts along dimension 0, may hold values from -1 to 1
- replicate_mask: int32 [1024, 128], P(('groups', 'rhs')), parts along dimension 0, may hold values 0 or 1
Outputs:
- solution: float32 [8, 2, 1024, 128], P(('groups', 'panel'), 'coef', 'rhs'), parts along dimension 0
- residual: float32 [8, 2, 1024, 128], P(('groups', 'panel'), 'coef', 'rhs'), parts along dimension 0
The draws below stay inside these ranges and needn't reach their ends.
There are 2 independent parts, one for each index of `groups`. The reference program is written for one: setup_inputs(seed, part) draws one part's arguments, and reference() takes and returns one part's arrays. A program takes and returns all parts, laid end to end along the dimension named above; an argument that names none is the same for every part. Nothing has to cross between parts.
Inputs may be any that keep to these rules, and one draw needn't show every extreme that they name: `couplings`: K[p, m] equals the transpose of K[(p + m - 4) mod 4, 8 - m], and the operator A is positive definite.
All inputs are finite; a program needn't handle non-finite values. No bound on the sum of `replicate_mask` on one device may be relied on, other than what follows from the above.
Results may differ from the reference program's by a relative error of at most 0.0075.
The reference program's roundings to bfloat16 on the way (of `signs` and `rounded`) count: a program that leaves them out, or rounds other values in their place, can miss the bound.
Values may be sent and summed in bfloat16 or wider, within the bound.
No kernel may reach another device: no remote copies, remote signals or barrier semaphores. Data moves between devices by JAX's collectives and lax.ppermute only.
A program may use at most 128 MiB of HBM per device.

```python
import jax
import jax.numpy as jnp
from jax import lax

COEFS = 2048
RIGHTS = 128
REACH = 4
ITERS = 3
LINKS = 9
PANELS = 4
OBSERV = 512
HALVES = 2
STRIPS = 2
HALF = 1024
SLAB = 512


def draw_couplings(key, part):
    key = jax.random.fold_in(key, 11)
    key_off = jax.random.fold_in(key, 1)
    key_diag = jax.random.fold_in(key, 2)
    key_gain = jax.random.fold_in(key, 3)
    key_link = jax.random.fold_in(key, 4)
    forward = jax.random.truncated_normal(key_off, -3.0, 3.0, (PANELS, REACH, COEFS, COEFS), jnp.float32)
    inner = jax.random.truncated_normal(key_diag, -3.0, 3.0, (PANELS, COEFS, COEFS), jnp.float32)
    low_log, high_log = (jnp.log(0.4), jnp.log(40.0))
    link_gain = jnp.exp(jax.random.uniform(key_link, (PANELS, REACH, COEFS), jnp.float32, jnp.log(0.5), jnp.log(2.0)))
    noise_scale = 0.4
    places = jnp.arange(COEFS)
    forward = forward * (noise_scale / COEFS ** 0.5)
    forward = forward.at[:, :, places, places].add(link_gain)
    inner = inner * (noise_scale / (2.0 * COEFS) ** 0.5)
    levels = jnp.exp(jax.random.uniform(key_gain, (PANELS, COEFS), jnp.float32, low_log, high_log))
    linked = jnp.zeros((PANELS, COEFS), jnp.float32)
    for offset in range(1, REACH + 1):
        linked = linked + link_gain[:, offset - 1] + jnp.roll(link_gain[:, offset - 1], offset, axis=0)
    diagonal_block = inner + jnp.swapaxes(inner, 1, 2)
    diagonal_block = diagonal_block.at[:, places, places].add(levels + linked + 10.0 * noise_scale)
    backward = []
    for offset in range(REACH, 0, -1):
        moved = jnp.roll(forward[:, offset - 1], offset, axis=0)
        backward.append(jnp.swapaxes(moved, 1, 2))
    ahead = [forward[:, offset - 1] for offset in range(1, REACH + 1)]
    stacked = jnp.stack(backward + [diagonal_block] + ahead, axis=1)
    return stacked.reshape(PANELS, LINKS, HALVES, HALF, HALVES, STRIPS, SLAB).astype(jnp.bfloat16)


def draw_observations(key, part):
    key = jax.random.fold_in(key, 23)
    key_common = jax.random.fold_in(key, 1)
    key_single = jax.random.fold_in(key, 2)
    common = jax.random.truncated_normal(key_common, -3.0, 3.0, (OBSERV, 1, HALVES, HALF), jnp.float32)
    single = jax.random.truncated_normal(key_single, -3.0, 3.0, (OBSERV, PANELS, HALVES, HALF), jnp.float32)
    shared_weight, single_weight = (0.7071, 0.7071)
    values = (shared_weight * common + single_weight * single) / OBSERV ** 0.5
    return values.astype(jnp.bfloat16)


def plant(entries, own_key, least, top_value):
    index_at = [jax.random.randint(jax.random.fold_in(own_key, axis), (), 0, length) for axis, length in enumerate(entries.shape)]
    widest = entries.shape.index(max(entries.shape))
    beside = index_at[:widest] + [(index_at[widest] + 1) % entries.shape[widest]] + index_at[widest + 1:]
    return entries.at[tuple(index_at)].set(least).at[tuple(beside)].set(top_value)


def setup_inputs(seed: int = 0, part: int = 0) -> dict:
    streams_of = jax.random.split(jax.random.key(seed), 4)
    part_splits = jax.random.split(jax.random.fold_in(streams_of[3], part), 4)
    couplings = draw_couplings(jax.random.fold_in(streams_of[3], 71), part)
    observations = draw_observations(jax.random.fold_in(jax.random.fold_in(streams_of[3], part), 71), part)
    replicate_mask = plant((jax.random.randint(part_splits[2], (OBSERV, RIGHTS), 0, 2) < 1).astype(jnp.int32), jax.random.fold_in(part_splits[2], 1), 0, 1)
    return dict(couplings=couplings, observations=observations, replicate_mask=replicate_mask)


def solve_spd(matrix, rhs_matrix):
    factor = jnp.linalg.cholesky(matrix)
    return jax.scipy.linalg.cho_solve((factor, True), rhs_matrix)

def gram_of(left, right):
    return jnp.dot(left.T.astype(jnp.float32), right.astype(jnp.float32), precision=lax.Precision.HIGHEST, preferred_element_type=jnp.float32)

def times_small(field, small):
    return jnp.dot(field.astype(jnp.float32), small.astype(jnp.float32), precision=lax.Precision.HIGHEST, preferred_element_type=jnp.float32)

def reference(couplings, observations, replicate_mask):
    blocks = couplings.reshape(PANELS, LINKS, COEFS, COEFS)
    obs_matrix = observations.reshape(OBSERV, PANELS * COEFS)
    signs = (2 * replicate_mask - 1).astype(jnp.bfloat16)
    right_side = jnp.dot(obs_matrix.T.astype(jnp.float32), signs.astype(jnp.float32), preferred_element_type=jnp.float32)

    def operate(field):
        rounded = field.astype(jnp.bfloat16).reshape(PANELS, COEFS, RIGHTS)
        total = jnp.zeros((PANELS, COEFS, RIGHTS), jnp.float32)
        for link in range(LINKS):
            offset = link - REACH
            partner = jnp.roll(rounded, -offset, axis=0)
            total = total + jnp.einsum('pij,pjr->pir', blocks[:, link].astype(jnp.float32), partner.astype(jnp.float32), precision=lax.Precision.HIGHEST)
        return total.reshape(PANELS * COEFS, RIGHTS)
    solution = jnp.zeros_like(right_side)
    residual = right_side
    direction = right_side
    gram = gram_of(residual, residual)
    for step in range(ITERS):
        image = operate(direction)
        raw = gram_of(direction, image)
        curvature = 0.5 * (raw + raw.T)
        alpha = solve_spd(curvature, gram)
        solution = solution + times_small(direction, alpha)
        residual = residual - times_small(image, alpha)
        if step + 1 < ITERS:
            following = gram_of(residual, residual)
            beta = solve_spd(gram, following)
            direction = residual + times_small(direction, beta)
            gram = following
    shape_out = (PANELS, HALVES, HALF, RIGHTS)
    return (solution.reshape(shape_out), residual.reshape(shape_out))
```

```python
import functools

import jax
import jax.numpy as jnp
from jax import lax
from jax.experimental import pallas as pl
from jax.experimental.pallas import tpu as pltpu
from jax.sharding import PartitionSpec as P

ITERS = 3
LANES = 128
SUB = 8
VMEM_LIMIT = 48 * 2**20
F32 = jnp.float32
BF16 = jnp.bfloat16
VMEM = pl.BlockSpec(memory_space=pltpu.VMEM)


def mm(a, b, dims=(1, 0)):
    return lax.dot_general(
        a,
        b,
        (((dims[0],), (dims[1],)), ((), ())),
        precision=lax.Precision.HIGHEST,
        preferred_element_type=F32,
    )


def call(body, out_shape, *args, flops=0, moved=0, specs=None, scratch=()):
    return pl.pallas_call(
        body,
        out_shape=out_shape,
        in_specs=specs or [VMEM] * len(args),
        out_specs=jax.tree.map(lambda _: VMEM, out_shape),
        scratch_shapes=list(scratch),
        cost_estimate=pl.CostEstimate(flops=flops, bytes_accessed=moved, transcendentals=0),
        compiler_params=pltpu.CompilerParams(vmem_limit_bytes=VMEM_LIMIT),
    )(*args)


def shape(rows, cols=LANES, dtype=F32):
    return jax.ShapeDtypeStruct((rows, cols), dtype)


def permute(value, axis, pairs):
    return lax.ppermute(value, axis, pairs)


def shifted(value, axis, by):
    n = lax.axis_size(axis)
    return permute(value, axis, [((i + by) % n, i) for i in range(n)])


def mate(i, s, n):
    return i ^ s if n & (n - 1) == 0 else (s - i) % n


def swapped(value, axis, s, n):
    return permute(value, axis, [(mate(i, s, n), i) for i in range(n)])


def plane_index():
    return lax.axis_index("rhs") * lax.axis_size("coef") + lax.axis_index("coef")


def plane_size():
    return lax.axis_size("rhs") * lax.axis_size("coef")


def sum_over_panels(value):
    n = lax.axis_size("panel")
    if n == 4:
        one, two, three = (shifted(value, "panel", s) for s in (1, 2, 3))
        return (value + two) + (one + three)
    return lax.psum(value, "panel")


def reduce_pieces(pieces):
    n = plane_size()
    axes = ("rhs", "coef")
    total = pieces[0]
    for s in range(1, n):
        total = total + swapped(pieces[s], axes, s, n)
    total = sum_over_panels(total)
    return [total] + [swapped(total, axes, s, n) for s in range(1, n)]


def right_side_parts(obs, mask, n, strip):
    def body(obs_ref, mask_ref, *outs):
        signs = (2 * mask_ref[...] - 1).astype(BF16)
        me = lax.axis_index("rhs")
        for s in range(n):
            place = pl.multiple_of(mate(me, s, n) * strip, strip)
            outs[s][...] = lax.dot_general(
                obs_ref[:, pl.ds(place, strip)],
                signs,
                (((0,), (0,)), ((), ())),
                preferred_element_type=F32,
            )

    return call(body, [shape(strip)] * n, obs, mask, flops=2 * obs.size * LANES, moved=2 * obs.size)


def sum_and_round(parts):
    strip = parts[0].shape[0]

    def body(*refs):
        *ins, out, low = refs
        total = ins[0][...]
        for ref in ins[1:]:
            total = total + ref[...]
        out[...] = total
        low[...] = total.astype(BF16)

    return call(body, [shape(strip), shape(strip, dtype=BF16)], *parts, moved=2**20)


def link_products(blocks, links, pieces, acc, n, last):
    rows, strip = blocks.shape[1], blocks.shape[3]
    tiles = strip // LANES
    wide = min(2, tiles)
    count = len(links)

    def body(*refs):
        k_ref, own_ref, other_ref = refs[:3]
        acc_ref = refs[3] if acc is not None else None
        outs = refs[3 + (acc is not None) : -5]
        own_out = outs
        buf, weights, even_acc, odd_acc, sems = refs[-5:]
        copies = []
        for i, link in enumerate(links):
            for t in range(tiles):
                copy = pltpu.make_async_copy(
                    k_ref.at[link, :, :, pl.ds(t * LANES, LANES)], buf.at[i, t], sems.at[i, t]
                )
                copy.start()
                copies.append(copy)
        half = lax.axis_index("coef")
        weights[:, pl.ds(pl.multiple_of(half * LANES, LANES), LANES)] = own_ref[...]
        weights[:, pl.ds(pl.multiple_of((1 - half) * LANES, LANES), LANES)] = other_ref[...]
        for i in range(count):
            for t in range(0, tiles, wide):
                for u in range(wide):
                    copies[i * tiles + t + u].wait()
                left = jnp.concatenate(
                    [buf.at[i, t + u].reshape(2 * rows, LANES)[...] for u in range(wide)], axis=1
                )
                product = jnp.dot(
                    left,
                    weights[t * LANES : (t + wide) * LANES, :],
                    preferred_element_type=F32,
                )
                if i == 0 and t == 0:
                    even_acc[...] = product[:, :LANES]
                    odd_acc[...] = product[:, LANES:]
                else:
                    even_acc[...] += product[:, :LANES]
                    odd_acc[...] += product[:, LANES:]
        me = lax.axis_index("rhs")
        size = rows // len(own_out)
        for s in range(len(own_out)):
            start = mate(me, s, n) * size if last else 0
            even = even_acc[pl.ds(2 * start, size, stride=2), :]
            odd = odd_acc[pl.ds(2 * start + 1, size, stride=2), :]
            total = even + odd
            if acc_ref is not None:
                total = total + acc_ref[pl.ds(start, size), :]
            own_out[s][...] = total

    args = [blocks, *pieces] + ([acc] if acc is not None else [])
    out = [shape(rows // n)] * n if last else [shape(rows)]
    result = call(
        body,
        out,
        *args,
        flops=4 * count * rows * 2 * strip * LANES,
        moved=count * rows * 2 * strip * 2,
        specs=[pl.BlockSpec(memory_space=pl.ANY)] + [VMEM] * (len(args) - 1),
        scratch=[
            pltpu.VMEM((count, tiles, rows, 2, LANES), BF16),
            pltpu.VMEM((strip, 2 * LANES), BF16),
            pltpu.VMEM((2 * rows, LANES), F32),
            pltpu.VMEM((2 * rows, LANES), F32),
            pltpu.SemaphoreType.DMA((count, tiles)),
        ],
    )
    return result if last else result[0]


def operate(blocks, low):
    links = blocks.shape[0]
    reach = (links - 1) // 2
    panels = lax.axis_size("panel")
    n = lax.axis_size("rhs")
    groups = {}
    for link in range(links):
        groups.setdefault((link - reach) % panels, []).append(link)
    order = sorted(groups, key=lambda o: min(o, panels - o))
    arrived = {o: low if o == 0 else shifted(low, "panel", o) for o in order}
    acc = None
    for place, o in enumerate(order):
        pair = [arrived[o], swapped(arrived[o], "coef", 1, 2)]
        acc = link_products(blocks, groups[o], pair, acc, n, place == len(order) - 1)
    return acc


def grams_of(image_parts, residual, direction, first, final):
    strip = residual.shape[0]
    count = 3 if not final else 1
    n = plane_size()
    rows = count * LANES // n
    parts = len(image_parts)

    def body(*refs):
        ins = refs[:parts]
        r_ref, d_ref = refs[parts : parts + 2]
        image_out = refs[parts + 2]
        outs = refs[parts + 3 : -1]
        small = refs[-1]
        image = ins[0][...]
        for ref in ins[1:]:
            image = image + ref[...]
        image_out[...] = image
        r = r_ref[...]
        if final:
            small[...] = mm(d_ref[...], image, (0, 0))
        elif first:
            small[:LANES] = mm(r, image, (0, 0))
            small[LANES : 2 * LANES] = mm(r, r, (0, 0))
            small[2 * LANES :] = mm(image, image, (0, 0))
        else:
            small[:LANES] = mm(d_ref[...], image, (0, 0))
            small[LANES : 2 * LANES] = mm(r, image, (0, 0))
            small[2 * LANES :] = mm(image, image, (0, 0))
        me = plane_index()
        for s in range(n):
            outs[s][...] = small[pl.ds(pl.multiple_of(mate(me, s, n) * rows, SUB), rows), :]

    out = [shape(strip)] + [shape(rows)] * n
    image, *pieces = call(
        body,
        out,
        *image_parts,
        residual,
        direction,
        flops=12 * count * strip * LANES * LANES,
        moved=2**20,
        scratch=[pltpu.VMEM((count * LANES, LANES), F32)],
    )
    return image, pieces


def eliminated(matrix, sides):
    n = matrix.shape[0]
    strips = n // SUB
    place = lax.broadcasted_iota(jnp.int32, (SUB, LANES), 0)
    a = [matrix[SUB * k : SUB * (k + 1)] for k in range(strips)]
    b = [sides[SUB * k : SUB * (k + 1)] for k in range(strips)]
    for j in range(strips):
        columns = [
            jnp.broadcast_to(a[j][:, SUB * j + i : SUB * j + i + 1], (SUB, LANES))
            for i in range(SUB)
        ]
        left, right = a[j], b[j]
        for i in range(SUB):
            here = place == i
            inverse = 1.0 / columns[i][i : i + 1]

            def step(value):
                row = value[i : i + 1] * inverse
                return jnp.where(here, row, value - columns[i] * row)

            left, right = step(left), step(right)
            columns = columns[: i + 1] + [step(c) for c in columns[i + 1 :]]
        a[j], b[j] = left, right
        for k in range(strips):
            if k == j:
                continue
            row_a, row_b = a[k], b[k]
            for i in range(SUB):
                factor = jnp.broadcast_to(
                    a[k][:, SUB * j + i : SUB * j + i + 1], (SUB, LANES)
                )
                row_a = row_a - factor * left[i : i + 1]
                row_b = row_b - factor * right[i : i + 1]
            a[k], b[k] = row_a, row_b
    return jnp.concatenate(b, axis=0)


def advance(pieces, gram, solution, residual, direction, image, first, final):
    strip = residual.shape[0]
    n = len(pieces)
    rows = pieces[0].shape[0]
    fields = [residual, image] + ([] if first else [direction, solution, gram])

    def body(*refs):
        ins = refs[:n]
        rest = refs[n : n + len(fields)]
        outs = refs[n + len(fields) : -1]
        small = refs[-1]
        me = plane_index()
        for s in range(n):
            small[pl.ds(pl.multiple_of(mate(me, s, n) * rows, SUB), rows), :] = ins[s][...]
        r, image_value = rest[0][...], rest[1][...]
        raw = small[:LANES]
        if first:
            d = r
            cross = raw
            g = small[LANES : 2 * LANES]
        else:
            d = rest[2][...]
            g = rest[4][...]
        curvature = 0.5 * (raw + raw.T)
        alpha = eliminated(curvature, g)
        change = mm(d, alpha)
        outs[0][...] = change if first else rest[3][...] + change
        new_r = r - mm(image_value, alpha)
        outs[1][...] = new_r
        if final:
            return
        if not first:
            cross = small[LANES : 2 * LANES]
        square = small[2 * LANES :]
        eye = (
            lax.broadcasted_iota(jnp.int32, (LANES, LANES), 0)
            == lax.broadcasted_iota(jnp.int32, (LANES, LANES), 1)
        ).astype(F32)
        inverse = eliminated(g, eye)
        shared = mm(cross, alpha)
        following = g - (shared + shared.T) + mm(alpha, mm(square, alpha), (0, 0))
        beta = mm(inverse, following)
        new_d = new_r + mm(d, beta)
        outs[2][...] = new_d
        outs[3][...] = new_d.astype(BF16)
        outs[4][...] = following

    out = [shape(strip), shape(strip)]
    if not final:
        out += [shape(strip), shape(strip, dtype=BF16), shape(LANES)]
    return call(
        body,
        out,
        *pieces,
        *fields,
        flops=2**30,
        moved=2**20,
        scratch=[pltpu.VMEM((n * rows, LANES), F32)],
    )


def shards(couplings, observations, replicate_mask):
    links, rows = couplings.shape[1], couplings.shape[3]
    strip = couplings.shape[6]
    blocks = couplings.reshape(links, rows, couplings.shape[4], strip)
    n = lax.axis_size("rhs")
    obs_matrix = observations.reshape(observations.shape[0], rows)
    parts = right_side_parts(obs_matrix, replicate_mask, n, strip)
    own = [parts[0]] + [swapped(parts[s], "rhs", s, n) for s in range(1, n)]
    residual, low = sum_and_round(own)
    direction = residual
    solution = gram = None
    for step in range(ITERS):
        first, final = step == 0, step + 1 == ITERS
        parts = operate(blocks, low)
        image_parts = [parts[0]] + [swapped(parts[s], "rhs", s, n) for s in range(1, n)]
        image, pieces = grams_of(image_parts, residual, direction, first, final)
        pieces = reduce_pieces(pieces)
        results = advance(
            pieces, gram, solution, residual, direction, image, first, final
        )
        if final:
            solution, residual = results
        else:
            solution, residual, direction, low, gram = results
    shape_out = (1, 1, strip, LANES)
    return (solution.reshape(shape_out), residual.reshape(shape_out))


def solution(mesh):
    placed = (
        P("panel", None, "coef", None, None, "rhs", None),
        P(("groups", "rhs"), "panel", "coef", None),
        P(("groups", "rhs"), None),
    )
    return jax.shard_map(
        shards,
        mesh=mesh,
        in_specs=placed,
        out_specs=(
            P(("groups", "panel"), "coef", "rhs", None),
            P(("groups", "panel"), "coef", "rhs", None),
        ),
        check_vma=False,
    )
```

```python
import jax
import jax.numpy as jnp
from jax import lax
from jax.experimental import pallas as pl
from jax.experimental.pallas import tpu as pltpu
from jax.sharding import PartitionSpec as P

ITERS = 3
LANES = 128
SUB = 8
VMEM_LIMIT = 14 * 2**20
F32 = jnp.float32
BF16 = jnp.bfloat16
VMEM = pl.BlockSpec(memory_space=pltpu.VMEM)
ANY = pl.BlockSpec(memory_space=pl.ANY)
HBM = pl.BlockSpec(memory_space=pltpu.HBM)


def mm(a, b, dims=(1, 0)):
    return lax.dot_general(
        a,
        b,
        (((dims[0],), (dims[1],)), ((), ())),
        precision=lax.Precision.HIGHEST,
        preferred_element_type=F32,
    )


def call(body, outs, *args, flops=0, moved=0, scratch=(), after=(), any_args=0, any_outs=False):
    inputs, outputs, waits = len(args), len(outs), len(after)

    def ordered(*refs):
        token = refs[inputs + waits + outputs]
        token[...] = jnp.zeros_like(token)
        body(
            *refs[:inputs],
            *refs[inputs + waits : inputs + waits + outputs],
            *refs[inputs + waits + outputs + 1 :],
        )

    return pl.pallas_call(
        ordered,
        out_shape=list(outs) + [shape(SUB)],
        in_specs=[HBM] * any_args + [VMEM] * (inputs - any_args) + [ANY] * waits,
        out_specs=[ANY if any_outs else VMEM] * outputs + [VMEM],
        scratch_shapes=list(scratch),
        cost_estimate=pl.CostEstimate(flops=flops, bytes_accessed=moved, transcendentals=0),
        compiler_params=pltpu.CompilerParams(vmem_limit_bytes=VMEM_LIMIT),
    )(*args, *after)


def shape(rows, cols=LANES, dtype=F32):
    return jax.ShapeDtypeStruct((rows, cols), dtype)


def permute(value, axis, pairs):
    return lax.ppermute(value, axis, pairs)


def shifted(value, axis, by):
    n = lax.axis_size(axis)
    return permute(value, axis, [((i + by) % n, i) for i in range(n)])


def mate(i, s, n):
    return i ^ s if n & (n - 1) == 0 else (s - i) % n


def swapped(value, axis, s, n):
    return permute(value, axis, [(mate(i, s, n), i) for i in range(n)])


def plane_index():
    return lax.axis_index("rhs") * lax.axis_size("coef") + lax.axis_index("coef")


def plane_size():
    return lax.axis_size("rhs") * lax.axis_size("coef")


def collected(value, axes):
    copies = jnp.broadcast_to(value, (lax.axis_size(axes), *value.shape))
    return lax.all_to_all(copies, axes, 0, 0, tiled=True)


def reduce_chunks(chunks):
    axes = ("rhs", "coef")
    total = jnp.sum(lax.all_to_all(chunks, axes, 0, 0, tiled=True), axis=0)
    total = jnp.sum(collected(total, "panel"), axis=0)
    return collected(total, axes)


def right_side_parts(obs, mask, n, strip):
    def body(obs_ref, mask_ref, *outs):
        signs = (2 * mask_ref[...] - 1).astype(BF16)
        me = lax.axis_index("rhs")
        for s in range(n):
            place = pl.multiple_of(mate(me, s, n) * strip, strip)
            outs[s][...] = lax.dot_general(
                obs_ref[:, pl.ds(place, strip)],
                signs,
                (((0,), (0,)), ((), ())),
                preferred_element_type=F32,
            )

    *parts, token = call(
        body, [shape(strip)] * n, obs, mask, flops=2 * obs.size * LANES, moved=2 * obs.size
    )
    return parts, token


def sum_and_round(parts, token):
    strip = parts[0].shape[0]

    def body(*refs):
        *ins, out, low = refs
        total = ins[0][...]
        for ref in ins[1:]:
            total = total + ref[...]
        out[...] = total
        low[...] = total.astype(BF16)

    return call(
        body, [shape(strip), shape(strip, dtype=BF16)], *parts, moved=2**20, after=[token]
    )


def retiled(blocks, links, token):
    rows, strip = blocks.shape[1], blocks.shape[3]
    tiles = strip // LANES
    count = len(links)

    def body(k_ref, out, sems):
        copies = []
        for i, link in enumerate(links):
            for t in range(tiles):
                copy = pltpu.make_async_copy(
                    k_ref.at[link, :, :, pl.ds(t * LANES, LANES)], out.at[i, t], sems.at[i, t]
                )
                copy.start()
                copies.append(copy)
        for copy in copies:
            copy.wait()

    packed, token = call(
        body,
        [pltpu.VMEM((count, tiles, rows, 2, LANES), BF16)],
        blocks,
        moved=count * rows * 2 * strip * 4,
        scratch=[pltpu.SemaphoreType.DMA((count, tiles))],
        after=[token],
        any_args=1,
        any_outs=True,
    )
    return packed.reshape(count, tiles, 2 * rows, LANES), token


def link_products(packed, pieces, acc, n, last, after=()):
    count, tiles, rows, _ = packed.shape
    rows //= 2
    strip = tiles * LANES
    block = min(512, 2 * rows)

    def body(*refs):
        k_ref, own_ref, other_ref = refs[:3]
        acc_ref = refs[3] if acc is not None else None
        outs = refs[3 + (acc is not None) : -3]
        weights, even_acc, odd_acc = refs[-3:]
        half = lax.axis_index("coef")
        weights[:, pl.ds(pl.multiple_of(half * LANES, LANES), LANES)] = own_ref[...]
        weights[:, pl.ds(pl.multiple_of((1 - half) * LANES, LANES), LANES)] = other_ref[...]
        for start in range(0, 2 * rows, block):
            here = slice(start, start + block)
            left = jnp.concatenate(
                [k_ref[i, t, here, :] for i in range(count) for t in range(tiles)], axis=1
            )
            right = jnp.concatenate([weights[...]] * count, axis=0)
            product = jnp.dot(left, right, preferred_element_type=F32)
            even_acc[here, :] = product[:, :LANES]
            odd_acc[here, :] = product[:, LANES:]
        me = lax.axis_index("rhs")
        size = rows // len(outs)
        for s in range(len(outs)):
            start = mate(me, s, n) * size if last else 0
            even = even_acc[pl.ds(2 * start, size, stride=2), :]
            odd = odd_acc[pl.ds(2 * start + 1, size, stride=2), :]
            total = even + odd
            if acc_ref is not None:
                total = total + acc_ref[pl.ds(start, size), :]
            outs[s][...] = total

    args = [packed, *pieces] + ([acc] if acc is not None else [])
    *result, token = call(
        body,
        [shape(rows // n)] * n if last else [shape(rows)],
        *args,
        flops=4 * count * rows * 2 * strip * LANES,
        moved=count * rows * 2 * strip * 2,
        scratch=[
            pltpu.VMEM((strip, 2 * LANES), BF16),
            pltpu.VMEM((2 * rows, LANES), F32),
            pltpu.VMEM((2 * rows, LANES), F32),
        ],
        after=after,
    )
    return (result if last else result[0]), token


def link_groups(links):
    reach = (links - 1) // 2
    panels = lax.axis_size("panel")
    groups = {}
    for link in range(links):
        groups.setdefault((link - reach) % panels, []).append(link)
    return {o: groups[o] for o in sorted(groups, key=lambda o: min(o, panels - o))}


def operate(packed, low, between):
    n = lax.axis_size("rhs")
    order = list(packed)
    arrived = {o: low if o == 0 else shifted(low, "panel", o) for o in order}
    acc, after = None, ()
    for place, o in enumerate(order):
        pair = [arrived[o], swapped(arrived[o], "coef", 1, 2)]
        acc, token = link_products(
            packed[o], pair, acc, n, place == len(order) - 1, after
        )
        after = ()
        if place == 0:
            after = (token, between(token))
            for late in order[1:]:
                arrived[late], _ = lax.optimization_barrier((arrived[late], after))
    return acc


def grams_of(image_parts, residual, direction, first, final):
    strip = residual.shape[0]
    count = 3 if not final else 1
    n = plane_size()
    rows = count * LANES // n
    parts = len(image_parts)

    def body(*refs):
        ins = refs[:parts]
        r_ref, d_ref, image_out, out = refs[parts:]
        image = ins[0][...]
        for ref in ins[1:]:
            image = image + ref[...]
        image_out[...] = image
        r = r_ref[...]
        if final:
            small = [mm(d_ref[...], image, (0, 0))]
        elif first:
            small = [mm(r, image, (0, 0)), mm(r, r, (0, 0)), mm(image, image, (0, 0))]
        else:
            small = [mm(d_ref[...], image, (0, 0)), mm(r, image, (0, 0)), mm(image, image, (0, 0))]
        small = jnp.concatenate(small, axis=0)
        for c in range(n):
            out[c] = small[c * rows : (c + 1) * rows]

    image, chunks, _ = call(
        body,
        [shape(strip), jax.ShapeDtypeStruct((n, rows, LANES), F32)],
        *image_parts,
        residual,
        direction,
        flops=12 * count * strip * LANES * LANES,
        moved=2**20,
    )
    return image, chunks


def eliminated(matrix, sides):
    n = matrix.shape[0]
    strips = n // SUB
    place = lax.broadcasted_iota(jnp.int32, (SUB, LANES), 0)
    a = [matrix[SUB * k : SUB * (k + 1)] for k in range(strips)]
    b = [sides[SUB * k : SUB * (k + 1)] for k in range(strips)]
    for j in range(strips):
        columns = [
            jnp.broadcast_to(a[j][:, SUB * j + i : SUB * j + i + 1], (SUB, LANES))
            for i in range(SUB)
        ]
        left, right = a[j], b[j]
        for i in range(SUB):
            here = place == i
            inverse = 1.0 / columns[i][i : i + 1]

            def step(value):
                row = value[i : i + 1] * inverse
                return jnp.where(here, row, value - columns[i] * row)

            left, right = step(left), step(right)
            columns = columns[: i + 1] + [step(c) for c in columns[i + 1 :]]
        a[j], b[j] = left, right
        for k in range(strips):
            if k == j:
                continue
            row_a, row_b = a[k], b[k]
            for i in range(SUB):
                factor = jnp.broadcast_to(
                    a[k][:, SUB * j + i : SUB * j + i + 1], (SUB, LANES)
                )
                row_a = row_a - factor * left[i : i + 1]
                row_b = row_b - factor * right[i : i + 1]
            a[k], b[k] = row_a, row_b
    return jnp.concatenate(b, axis=0)


def identity():
    return (
        lax.broadcasted_iota(jnp.int32, (LANES, LANES), 0)
        == lax.broadcasted_iota(jnp.int32, (LANES, LANES), 1)
    ).astype(F32)


def inverse_of(gram, token):
    def body(g_ref, out):
        out[...] = eliminated(g_ref[...], identity())

    return call(body, [shape(LANES)], gram, flops=2**30, moved=2**20, after=[token])


def advance(chunks, gram, inverse, solution, residual, direction, image, first, final):
    strip = residual.shape[0]
    fields = [residual, image]
    if not first:
        fields += [direction, solution, gram]
    if not first and not final:
        fields += [inverse]
    small = chunks.reshape(-1, LANES)

    def body(small, *refs):
        rest, outs = refs[: len(fields)], refs[len(fields) :]
        r, image_value = rest[0][...], rest[1][...]
        raw = small[:LANES, :]
        if first:
            d = r
            cross = raw
            g = small[LANES : 2 * LANES, :]
        else:
            d = rest[2][...]
            g = rest[4][...]
        curvature = 0.5 * (raw + raw.T)
        alpha = eliminated(curvature, g)
        change = mm(d, alpha)
        outs[0][...] = change if first else rest[3][...] + change
        new_r = r - mm(image_value, alpha)
        outs[1][...] = new_r
        if final:
            return
        if first:
            inverse_value = eliminated(g, identity())
        else:
            cross = small[LANES : 2 * LANES, :]
            inverse_value = rest[5][...]
        square = small[2 * LANES :, :]
        shared = mm(cross, alpha)
        following = g - (shared + shared.T) + mm(alpha, mm(square, alpha), (0, 0))
        beta = mm(inverse_value, following)
        new_d = new_r + mm(d, beta)
        outs[2][...] = new_d
        outs[3][...] = new_d.astype(BF16)
        outs[4][...] = following

    out = [shape(strip), shape(strip)]
    if not final:
        out += [shape(strip), shape(strip, dtype=BF16), shape(LANES)]
    return call(body, out, small, *fields, flops=2**30, moved=2**20)


def shards(couplings, observations, replicate_mask):
    links, rows = couplings.shape[1], couplings.shape[3]
    strip = couplings.shape[6]
    blocks = couplings.reshape(links, rows, couplings.shape[4], strip)
    blocks = pltpu.with_memory_space_constraint(blocks, pltpu.HBM)
    n = lax.axis_size("rhs")
    obs_matrix = observations.reshape(observations.shape[0], rows)
    parts, token = right_side_parts(obs_matrix, replicate_mask, n, strip)
    own = [parts[0]] + [swapped(parts[s], "rhs", s, n) for s in range(1, n)]
    groups = link_groups(links)
    packed = {}
    ahead = list(groups)[:2]
    for o in ahead:
        packed[o], token = retiled(blocks, groups[o], token)
    residual, low, token = sum_and_round(own, token)
    for o in list(groups)[2:]:
        packed[o], token = retiled(blocks, groups[o], token)
    retile_token = token
    direction = residual
    solution = gram = inverse = None
    for step in range(ITERS):
        first, final = step == 0, step + 1 == ITERS
        found = []

        def between(token):
            if first:
                return retile_token
            if final:
                return token
            value, token = inverse_of(gram, token)
            found.append(value)
            return token

        parts = operate({o: packed[o] for o in groups}, low, between)
        image_parts = [parts[0]] + [swapped(parts[s], "rhs", s, n) for s in range(1, n)]
        image, chunks = grams_of(image_parts, residual, direction, first, final)
        chunks = reduce_chunks(chunks)
        inverse = found[0] if found else None
        results = advance(
            chunks, gram, inverse, solution, residual, direction, image, first, final
        )
        if final:
            solution, residual, _ = results
        else:
            solution, residual, direction, low, gram, _ = results
    shape_out = (1, 1, strip, LANES)
    return (solution.reshape(shape_out), residual.reshape(shape_out))


def solution(mesh):
    placed = (
        P("panel", None, "coef", None, None, "rhs", None),
        P(("groups", "rhs"), "panel", "coef", None),
        P(("groups", "rhs"), None),
    )
    return jax.shard_map(
        shards,
        mesh=mesh,
        in_specs=placed,
        out_specs=(
            P(("groups", "panel"), "coef", "rhs", None),
            P(("groups", "panel"), "coef", "rhs", None),
        ),
        check_vma=False,
    )
```

```python
import jax
import jax.numpy as jnp
from jax import lax
from jax.experimental import pallas as pl
from jax.experimental.pallas import tpu as pltpu
from jax.sharding import PartitionSpec as P

ITERS = 3
LANES = 128
SUB = 8
VMEM_LIMIT = 14 * 2**20
F32 = jnp.float32
BF16 = jnp.bfloat16
VMEM = pl.BlockSpec(memory_space=pltpu.VMEM)
ANY = pl.BlockSpec(memory_space=pl.ANY)
HBM = pl.BlockSpec(memory_space=pltpu.HBM)


def mm(a, b, dims=(1, 0)):
    return lax.dot_general(
        a,
        b,
        (((dims[0],), (dims[1],)), ((), ())),
        precision=lax.Precision.HIGHEST,
        preferred_element_type=F32,
    )


def call(body, outs, *args, flops=0, moved=0, scratch=(), after=(), any_args=0, any_outs=False):
    inputs, outputs, waits = len(args), len(outs), len(after)

    def ordered(*refs):
        token = refs[inputs + waits + outputs]
        token[...] = jnp.zeros_like(token)
        body(
            *refs[:inputs],
            *refs[inputs + waits : inputs + waits + outputs],
            *refs[inputs + waits + outputs + 1 :],
        )

    return pl.pallas_call(
        ordered,
        out_shape=list(outs) + [shape(SUB)],
        in_specs=[HBM] * any_args + [VMEM] * (inputs - any_args) + [ANY] * waits,
        out_specs=[ANY if any_outs else VMEM] * outputs + [VMEM],
        scratch_shapes=list(scratch),
        cost_estimate=pl.CostEstimate(flops=flops, bytes_accessed=moved, transcendentals=0),
        compiler_params=pltpu.CompilerParams(vmem_limit_bytes=VMEM_LIMIT),
    )(*args, *after)


def shape(rows, cols=LANES, dtype=F32):
    return jax.ShapeDtypeStruct((rows, cols), dtype)


def permute(value, axis, pairs):
    return lax.ppermute(value, axis, pairs)


def shifted(value, axis, by):
    n = lax.axis_size(axis)
    return permute(value, axis, [((i + by) % n, i) for i in range(n)])


def mate(i, s, n):
    return i ^ s if n & (n - 1) == 0 else (s - i) % n


def swapped(value, axis, s, n):
    return permute(value, axis, [(mate(i, s, n), i) for i in range(n)])


def plane_index():
    return lax.axis_index("rhs") * lax.axis_size("coef") + lax.axis_index("coef")


def plane_size():
    return lax.axis_size("rhs") * lax.axis_size("coef")


def sum_over_panels(value):
    n = lax.axis_size("panel")
    if n != 4:
        return lax.psum(value, "panel")
    one, two, three = (shifted(value, "panel", s) for s in (1, 2, 3))
    return (value + two) + (one + three)


def reduce_pieces(pieces):
    n = plane_size()
    axes = ("rhs", "coef")
    total = pieces[0]
    for s in range(1, n):
        total = total + swapped(pieces[s], axes, s, n)
    total = sum_over_panels(total)
    return [total] + [swapped(total, axes, s, n) for s in range(1, n)]


def right_side_parts(obs, mask, n, strip):
    def body(obs_ref, mask_ref, *outs):
        signs = (2 * mask_ref[...] - 1).astype(BF16)
        me = lax.axis_index("rhs")
        for s in range(n):
            place = pl.multiple_of(mate(me, s, n) * strip, strip)
            outs[s][...] = lax.dot_general(
                obs_ref[:, pl.ds(place, strip)],
                signs,
                (((0,), (0,)), ((), ())),
                preferred_element_type=F32,
            )

    *parts, token = call(
        body, [shape(strip)] * n, obs, mask, flops=2 * obs.size * LANES, moved=2 * obs.size
    )
    return parts, token


def sum_and_round(parts, token):
    strip = parts[0].shape[0]

    def body(*refs):
        *ins, out, low = refs
        total = ins[0][...]
        for ref in ins[1:]:
            total = total + ref[...]
        out[...] = total
        low[...] = total.astype(BF16)

    return call(
        body, [shape(strip), shape(strip, dtype=BF16)], *parts, moved=2**20, after=[token]
    )


def retiled(blocks, links, token):
    rows, strip = blocks.shape[1], blocks.shape[3]
    tiles = strip // LANES
    count = len(links)

    def body(k_ref, out, sems):
        copies = []
        for i, link in enumerate(links):
            for t in range(tiles):
                copy = pltpu.make_async_copy(
                    k_ref.at[link, :, :, pl.ds(t * LANES, LANES)], out.at[i, t], sems.at[i, t]
                )
                copy.start()
                copies.append(copy)
        for copy in copies:
            copy.wait()

    packed, token = call(
        body,
        [pltpu.VMEM((count, tiles, rows, 2, LANES), BF16)],
        blocks,
        moved=count * rows * 2 * strip * 4,
        scratch=[pltpu.SemaphoreType.DMA((count, tiles))],
        after=[token],
        any_args=1,
        any_outs=True,
    )
    return packed, token


def link_products(packed, pieces, acc, n, last, after=()):
    count, tiles, rows = packed.shape[:3]
    packed = packed.reshape(count, tiles, 2 * rows, LANES)
    packed = pltpu.with_memory_space_constraint(packed, pltpu.VMEM)
    strip = tiles * LANES
    block = min(512, 2 * rows)

    def body(*refs):
        k_ref, own_ref, other_ref = refs[:3]
        acc_ref = refs[3] if acc is not None else None
        outs = refs[3 + (acc is not None) : -3]
        weights, even_acc, odd_acc = refs[-3:]
        half = lax.axis_index("coef")
        weights[:, pl.ds(pl.multiple_of(half * LANES, LANES), LANES)] = own_ref[...]
        weights[:, pl.ds(pl.multiple_of((1 - half) * LANES, LANES), LANES)] = other_ref[...]
        for start in range(0, 2 * rows, block):
            here = slice(start, start + block)
            left = jnp.concatenate(
                [k_ref[i, t, here, :] for i in range(count) for t in range(tiles)], axis=1
            )
            right = jnp.concatenate([weights[...]] * count, axis=0)
            product = jnp.dot(left, right, preferred_element_type=F32)
            even_acc[here, :] = product[:, :LANES]
            odd_acc[here, :] = product[:, LANES:]
        me = lax.axis_index("rhs")
        size = rows // len(outs)
        for s in range(len(outs)):
            start = mate(me, s, n) * size if last else 0
            even = even_acc[pl.ds(2 * start, size, stride=2), :]
            odd = odd_acc[pl.ds(2 * start + 1, size, stride=2), :]
            total = even + odd
            if acc_ref is not None:
                total = total + acc_ref[pl.ds(start, size), :]
            outs[s][...] = total

    args = [packed, *pieces] + ([acc] if acc is not None else [])
    *result, token = call(
        body,
        [shape(rows // n)] * n if last else [shape(rows)],
        *args,
        flops=4 * count * rows * 2 * strip * LANES,
        moved=count * rows * 2 * strip * 2,
        scratch=[
            pltpu.VMEM((strip, 2 * LANES), BF16),
            pltpu.VMEM((2 * rows, LANES), F32),
            pltpu.VMEM((2 * rows, LANES), F32),
        ],
        after=after,
    )
    return (result if last else result[0]), token


def link_groups(links):
    reach = (links - 1) // 2
    panels = lax.axis_size("panel")
    groups = {}
    for link in range(links):
        groups.setdefault((link - reach) % panels, []).append(link)
    return {o: groups[o] for o in sorted(groups, key=lambda o: min(o, panels - o))}


def operate(packed, low, between):
    n = lax.axis_size("rhs")
    order = list(packed)
    arrived = {o: low if o == 0 else shifted(low, "panel", o) for o in order}
    acc, after = None, ()
    for place, o in enumerate(order):
        pair = [arrived[o], swapped(arrived[o], "coef", 1, 2)]
        acc, token = link_products(
            packed[o], pair, acc, n, place == len(order) - 1, after
        )
        after = ()
        if place == 0:
            after = (token, between(token))
            for late in order[1:]:
                arrived[late], _ = lax.optimization_barrier((arrived[late], after))
    return acc


def spread(values, outs):
    *outs, stacked = outs
    n = len(outs)
    rows = stacked.shape[0] // n
    for i, value in enumerate(values):
        stacked[i * LANES : (i + 1) * LANES] = value
    me = plane_index()
    for s in range(n):
        outs[s][...] = stacked[pl.ds(pl.multiple_of(mate(me, s, n) * rows, SUB), rows), :]


def joined(pieces, stacked):
    n = len(pieces)
    rows = pieces[0].shape[0]
    me = plane_index()
    for s in range(n):
        stacked[pl.ds(pl.multiple_of(mate(me, s, n) * rows, SUB), rows), :] = pieces[s][...]


def linear_grams(parts, directions, before, beta, first, final):
    strip = parts[0].shape[0]
    n = len(parts)
    count = 1 if final else 2
    plane = plane_size()
    rows = count * LANES // plane
    extra = [] if first or final else [*before, beta]

    def body(*refs):
        images, ds = refs[:n], refs[n : 2 * n]
        rest = refs[2 * n : 2 * n + len(extra)]
        outs = refs[2 * n + len(extra) :]
        curve = cross = None
        for s in range(n):
            image, d = images[s][...], ds[s][...]
            term = mm(d, image, (0, 0))
            curve = term if s == 0 else curve + term
            if extra:
                r = d - mm(rest[s][...], rest[n][...])
                term = mm(r, image, (0, 0))
                cross = term if s == 0 else cross + term
        if first:
            r = ds[0][...]
            cross = mm(r, r, (0, 0))
        spread([curve] if final else [curve, cross], outs)

    *pieces, _ = call(
        body,
        [shape(rows)] * plane,
        *parts,
        *directions,
        *extra,
        flops=12 * count * n * strip * LANES * LANES,
        moved=2**20,
        scratch=[pltpu.VMEM((count * LANES, LANES), F32)],
    )
    return pieces


def square_gram(image_parts):
    strip = image_parts[0].shape[0]
    parts = len(image_parts)
    plane = plane_size()

    def body(*refs):
        ins, image_out, outs = refs[:parts], refs[parts], refs[parts + 1 :]
        image = ins[0][...]
        for ref in ins[1:]:
            image = image + ref[...]
        image_out[...] = image
        spread([mm(image, image, (0, 0))], outs)

    image, *pieces, _ = call(
        body,
        [shape(strip)] + [shape(LANES // plane)] * plane,
        *image_parts,
        flops=12 * strip * LANES * LANES,
        moved=2**20,
        scratch=[pltpu.VMEM((LANES, LANES), F32)],
    )
    return image, pieces


def eliminated(matrix, sides):
    n = matrix.shape[0]
    strips = n // SUB
    place = lax.broadcasted_iota(jnp.int32, (SUB, LANES), 0)
    a = [matrix[SUB * k : SUB * (k + 1)] for k in range(strips)]
    b = [sides[SUB * k : SUB * (k + 1)] for k in range(strips)]
    for j in range(strips):
        columns = [
            jnp.broadcast_to(a[j][:, SUB * j + i : SUB * j + i + 1], (SUB, LANES))
            for i in range(SUB)
        ]
        left, right = a[j], b[j]
        for i in range(SUB):
            here = place == i
            inverse = 1.0 / columns[i][i : i + 1]

            def step(value):
                row = value[i : i + 1] * inverse
                return jnp.where(here, row, value - columns[i] * row)

            left, right = step(left), step(right)
            columns = columns[: i + 1] + [step(c) for c in columns[i + 1 :]]
        a[j], b[j] = left, right
        for k in range(strips):
            if k == j:
                continue
            row_a, row_b = a[k], b[k]
            for i in range(SUB):
                factor = jnp.broadcast_to(
                    a[k][:, SUB * j + i : SUB * j + i + 1], (SUB, LANES)
                )
                row_a = row_a - factor * left[i : i + 1]
                row_b = row_b - factor * right[i : i + 1]
            a[k], b[k] = row_a, row_b
    return jnp.concatenate(b, axis=0)


def identity():
    return (
        lax.broadcasted_iota(jnp.int32, (LANES, LANES), 0)
        == lax.broadcasted_iota(jnp.int32, (LANES, LANES), 1)
    ).astype(F32)


def inverse_of(gram, token):
    def body(g_ref, out):
        out[...] = eliminated(g_ref[...], identity())

    return call(body, [shape(LANES)], gram, flops=2**30, moved=2**20, after=[token])


def advance(pieces, gram, solution, residual, direction, image, first, final):
    strip = residual.shape[0]
    n = len(pieces)
    images = image if final else [image]
    fields = [residual, direction, *images] + ([] if first else [solution, gram])
    many = len(images)

    def body(*refs):
        ins, refs = refs[:n], refs[n:]
        rest, outs = refs[: len(fields)], refs[len(fields) : -1]
        small = refs[-1]
        joined(ins, small)
        raw = small[:LANES]
        g = small[LANES:] if first else rest[-1][...]
        curvature = 0.5 * (raw + raw.T)
        alpha = eliminated(curvature, g)
        d = rest[1][...]
        image_value = rest[2][...]
        for ref in rest[3 : 2 + many]:
            image_value = image_value + ref[...]
        change = mm(d, alpha)
        outs[0][...] = change if first else rest[-2][...] + change
        outs[1][...] = rest[0][...] - mm(image_value, alpha)
        if final:
            return
        shared = mm(raw if first else small[LANES:], alpha)
        outs[2][...] = alpha
        outs[3][...] = g - (shared + shared.T)
        if first:
            outs[4][...] = g

    out = [shape(strip), shape(strip)]
    if not final:
        out += [shape(LANES)] * (3 if first else 2)
    return call(
        body,
        out,
        *pieces,
        *fields,
        flops=2**30,
        moved=2**20,
        scratch=[pltpu.VMEM((n * pieces[0].shape[0], LANES), F32)],
    )


def turn(pieces, alpha, partial, inverse, residual, direction):
    strip = residual.shape[0]
    n = len(pieces)

    def body(*refs):
        ins, refs = refs[:n], refs[n:]
        alpha, partial, inverse, r, d, new_d, low, beta_out, gram_out, small = refs
        joined(ins, small)
        a = alpha[...]
        following = partial[...] + mm(a, mm(small[...], a), (0, 0))
        beta = mm(inverse[...], following)
        value = r[...] + mm(d[...], beta)
        low[...] = value.astype(BF16)
        new_d[...] = value
        beta_out[...] = beta
        gram_out[...] = following

    return call(
        body,
        [shape(strip), shape(strip, dtype=BF16), shape(LANES), shape(LANES)],
        *pieces,
        alpha,
        partial,
        inverse,
        residual,
        direction,
        flops=2**28,
        moved=2**20,
        scratch=[pltpu.VMEM((n * pieces[0].shape[0], LANES), F32)],
    )


def shards(couplings, observations, replicate_mask):
    links, rows = couplings.shape[1], couplings.shape[3]
    strip = couplings.shape[6]
    blocks = couplings.reshape(links, rows, couplings.shape[4], strip)
    blocks = pltpu.with_memory_space_constraint(blocks, pltpu.HBM)
    n = lax.axis_size("rhs")
    obs_matrix = observations.reshape(observations.shape[0], rows)
    parts, token = right_side_parts(obs_matrix, replicate_mask, n, strip)
    own = [parts[0]] + [swapped(parts[s], "rhs", s, n) for s in range(1, n)]
    groups = link_groups(links)
    packed = {}
    ahead = list(groups)[:2]
    for o in ahead:
        packed[o], token = retiled(blocks, groups[o], token)
    residual, low, token = sum_and_round(own, token)
    for o in list(groups)[2:]:
        packed[o], token = retiled(blocks, groups[o], token)
    retile_token = token
    direction = residual
    solution = gram = beta = before = None
    for step in range(ITERS):
        first, final = step == 0, step + 1 == ITERS
        found = []

        def between(token):
            if first:
                return retile_token
            if final:
                return token
            value, token = inverse_of(gram, token)
            found.append(value)
            return token

        parts = operate(packed, low, between)
        directions = [direction] + [swapped(direction, "rhs", s, n) for s in range(1, n)]
        image_parts = [parts[0]] + [swapped(parts[s], "rhs", s, n) for s in range(1, n)]
        pieces = reduce_pieces(
            linear_grams(parts, directions, before, beta, first, final)
        )
        if final:
            solution, residual, _ = advance(
                pieces, gram, solution, residual, direction, image_parts, first, final
            )
            break
        image, square = square_gram(image_parts)
        square = reduce_pieces(square)
        solution, residual, alpha, partial, *rest = advance(
            pieces, gram, solution, residual, direction, image, first, final
        )
        if first:
            gram, token = rest
            found = [inverse_of(gram, token)[0]]
        before = directions
        direction, low, beta, gram, _ = turn(
            square, alpha, partial, found[0], residual, direction
        )
    shape_out = (1, 1, strip, LANES)
    return (solution.reshape(shape_out), residual.reshape(shape_out))


def solution(mesh):
    placed = (
        P("panel", None, "coef", None, None, "rhs", None),
        P(("groups", "rhs"), "panel", "coef", None),
        P(("groups", "rhs"), None),
    )
    return jax.shard_map(
        shards,
        mesh=mesh,
        in_specs=placed,
        out_specs=(
            P(("groups", "panel"), "coef", "rhs", None),
            P(("groups", "panel"), "coef", "rhs", None),
        ),
        check_vma=False,
    )
```

```python
import jax
import jax.numpy as jnp
from jax import lax
from jax.experimental import pallas as pl
from jax.experimental.pallas import tpu as pltpu
from jax.sharding import PartitionSpec as P

ITERS = 3
LANES = 128
SUB = 8
VMEM_LIMIT = 14 * 2**20
F32 = jnp.float32
BF16 = jnp.bfloat16
VMEM = pl.BlockSpec(memory_space=pltpu.VMEM)
ANY = pl.BlockSpec(memory_space=pl.ANY)
HBM = pl.BlockSpec(memory_space=pltpu.HBM)


def mm(a, b, dims=(1, 0)):
    return lax.dot_general(
        a,
        b,
        (((dims[0],), (dims[1],)), ((), ())),
        precision=lax.Precision.HIGHEST,
        preferred_element_type=F32,
    )


def call(body, outs, *args, flops=0, moved=0, scratch=(), after=(), any_args=0, any_outs=False):
    inputs, outputs, waits = len(args), len(outs), len(after)

    def ordered(*refs):
        token = refs[inputs + waits + outputs]
        token[...] = jnp.zeros_like(token)
        body(
            *refs[:inputs],
            *refs[inputs + waits : inputs + waits + outputs],
            *refs[inputs + waits + outputs + 1 :],
        )

    return pl.pallas_call(
        ordered,
        out_shape=list(outs) + [shape(SUB)],
        in_specs=[HBM] * any_args + [VMEM] * (inputs - any_args) + [ANY] * waits,
        out_specs=[ANY if any_outs else VMEM] * outputs + [VMEM],
        scratch_shapes=list(scratch),
        cost_estimate=pl.CostEstimate(flops=flops, bytes_accessed=moved, transcendentals=0),
        compiler_params=pltpu.CompilerParams(vmem_limit_bytes=VMEM_LIMIT),
    )(*args, *after)


def shape(rows, cols=LANES, dtype=F32):
    return jax.ShapeDtypeStruct((rows, cols), dtype)


def permute(value, axis, pairs):
    return lax.ppermute(value, axis, pairs)


def shifted(value, axis, by):
    n = lax.axis_size(axis)
    return permute(value, axis, [((i + by) % n, i) for i in range(n)])


def mate(i, s, n):
    return i ^ s if n & (n - 1) == 0 else (s - i) % n


def swapped(value, axis, s, n):
    return permute(value, axis, [(mate(i, s, n), i) for i in range(n)])


def sum_over(value, axis):
    n = lax.axis_size(axis)
    if n == 2:
        return value + swapped(value, axis, 1, 2)
    if n == 4:
        one, two, three = (shifted(value, axis, s) for s in (1, 2, 3))
        return (value + two) + (one + three)
    return lax.psum(value, axis)


def reduce_whole(value):
    for axis in ("coef", "rhs", "panel"):
        value = sum_over(value, axis)
    return [value]


def reduce_halves(mine, mates):
    value = mine + swapped(mates, "coef", 1, 2)
    for axis in ("rhs", "panel"):
        value = sum_over(value, axis)
    return [value, swapped(value, "coef", 1, 2)]


def right_side_parts(obs, mask, n, strip):
    def body(obs_ref, mask_ref, *outs):
        signs = (2 * mask_ref[...] - 1).astype(BF16)
        me = lax.axis_index("rhs")
        for s in range(n):
            place = pl.multiple_of(mate(me, s, n) * strip, strip)
            outs[s][...] = lax.dot_general(
                obs_ref[:, pl.ds(place, strip)],
                signs,
                (((0,), (0,)), ((), ())),
                preferred_element_type=F32,
            )

    *parts, token = call(
        body, [shape(strip)] * n, obs, mask, flops=2 * obs.size * LANES, moved=2 * obs.size
    )
    return parts, token


def sum_and_round(parts, token):
    strip = parts[0].shape[0]

    def body(*refs):
        *ins, out, low = refs
        total = ins[0][...]
        for ref in ins[1:]:
            total = total + ref[...]
        out[...] = total
        low[...] = total.astype(BF16)

    return call(
        body, [shape(strip), shape(strip, dtype=BF16)], *parts, moved=2**20, after=[token]
    )


def retiled(blocks, links, token):
    rows, strip = blocks.shape[1], blocks.shape[3]
    tiles = strip // LANES
    count = len(links)

    def body(k_ref, out, sems):
        copies = []
        for i, link in enumerate(links):
            for t in range(tiles):
                copy = pltpu.make_async_copy(
                    k_ref.at[link, :, :, pl.ds(t * LANES, LANES)], out.at[i, t], sems.at[i, t]
                )
                copy.start()
                copies.append(copy)
        for copy in copies:
            copy.wait()

    packed, token = call(
        body,
        [pltpu.VMEM((count, tiles, rows, 2, LANES), BF16)],
        blocks,
        moved=count * rows * 2 * strip * 4,
        scratch=[pltpu.SemaphoreType.DMA((count, tiles))],
        after=[token],
        any_args=1,
        any_outs=True,
    )
    return packed, token


def link_products(packed, pieces, acc, n, last, after=()):
    count, tiles, rows = packed.shape[:3]
    packed = packed.reshape(count, tiles, 2 * rows, LANES)
    packed = pltpu.with_memory_space_constraint(packed, pltpu.VMEM)
    strip = tiles * LANES
    block = min(512, 2 * rows)

    def body(*refs):
        k_ref, own_ref, other_ref = refs[:3]
        acc_ref = refs[3] if acc is not None else None
        outs = refs[3 + (acc is not None) : -3]
        weights, even_acc, odd_acc = refs[-3:]
        half = lax.axis_index("coef")
        weights[:, pl.ds(pl.multiple_of(half * LANES, LANES), LANES)] = own_ref[...]
        weights[:, pl.ds(pl.multiple_of((1 - half) * LANES, LANES), LANES)] = other_ref[...]
        for start in range(0, 2 * rows, block):
            here = slice(start, start + block)
            left = jnp.concatenate(
                [k_ref[i, t, here, :] for i in range(count) for t in range(tiles)], axis=1
            )
            right = jnp.concatenate([weights[...]] * count, axis=0)
            product = jnp.dot(left, right, preferred_element_type=F32)
            even_acc[here, :] = product[:, :LANES]
            odd_acc[here, :] = product[:, LANES:]
        me = lax.axis_index("rhs")
        size = rows // len(outs)
        for s in range(len(outs)):
            start = mate(me, s, n) * size if last else 0
            even = even_acc[pl.ds(2 * start, size, stride=2), :]
            odd = odd_acc[pl.ds(2 * start + 1, size, stride=2), :]
            total = even + odd
            if acc_ref is not None:
                total = total + acc_ref[pl.ds(start, size), :]
            outs[s][...] = total

    args = [packed, *pieces] + ([acc] if acc is not None else [])
    *result, token = call(
        body,
        [shape(rows // n)] * n if last else [shape(rows)],
        *args,
        flops=4 * count * rows * 2 * strip * LANES,
        moved=count * rows * 2 * strip * 2,
        scratch=[
            pltpu.VMEM((strip, 2 * LANES), BF16),
            pltpu.VMEM((2 * rows, LANES), F32),
            pltpu.VMEM((2 * rows, LANES), F32),
        ],
        after=after,
    )
    return (result if last else result[0]), token


def link_groups(links):
    reach = (links - 1) // 2
    panels = lax.axis_size("panel")
    groups = {}
    for link in range(links):
        groups.setdefault((link - reach) % panels, []).append(link)
    return {o: groups[o] for o in sorted(groups, key=lambda o: min(o, panels - o))}


def operate(packed, low, between):
    n = lax.axis_size("rhs")
    order = list(packed)
    arrived = {o: low if o == 0 else shifted(low, "panel", o) for o in order}
    acc, after = None, ()
    for place, o in enumerate(order):
        pair = [arrived[o], swapped(arrived[o], "coef", 1, 2)]
        acc, token = link_products(
            packed[o], pair, acc, n, place == len(order) - 1, after
        )
        after = ()
        if place == 0:
            after = (token, between(token))
            for late in order[1:]:
                arrived[late], _ = lax.optimization_barrier((arrived[late], after))
    return acc


PACKED = LANES // 2 + SUB


def corner():
    row = lax.broadcasted_iota(jnp.int32, (LANES // 2, LANES), 0)
    lane = lax.broadcasted_iota(jnp.int32, (LANES // 2, LANES), 1)
    return row, lane, lane < LANES // 2


def packed_symmetric(matrix):
    half = LANES // 2
    row, lane, left = corner()
    top = matrix[:half]
    last = pltpu.roll(matrix[half:], half, 1)
    body = jnp.where(left & (lane > row), last, top)
    diagonal = jnp.sum(jnp.where(lane == row, last, 0.0), axis=0, keepdims=True)
    return jnp.concatenate([body, jnp.broadcast_to(diagonal, (SUB, LANES))], axis=0)


def unpacked_symmetric(rows):
    half = LANES // 2
    row, lane, left = corner()
    body, diagonal = rows[:half], rows[half : half + 1]
    top = jnp.where(left & (lane >= row), 0.0, body)
    last = jnp.where(left & (lane > row), body, 0.0)
    sides = jnp.concatenate([top, pltpu.roll(last, half, 1)], axis=0)
    top = jnp.where(lane == row, body, 0.0)
    last = jnp.where(lane == row, jnp.broadcast_to(diagonal, body.shape), 0.0)
    return sides + sides.T + jnp.concatenate([top, pltpu.roll(last, half, 1)], axis=0)


def symmetric(raw):
    return 0.5 * (raw + raw.T)


def linear_grams(parts, directions, before, beta, first, final):
    strip = parts[0].shape[0]
    n = len(parts)
    extra = [] if first or final else [*before, beta]
    rows = PACKED if final else (PACKED if first else (PACKED + SUB + LANES) // 2)

    def body(*refs):
        images, ds = refs[:n], refs[n : 2 * n]
        rest = refs[2 * n : 2 * n + len(extra)]
        outs = refs[2 * n + len(extra) :]
        curve = cross = None
        for s in range(n):
            image, d = images[s][...], ds[s][...]
            term = mm(d, image, (0, 0))
            curve = term if s == 0 else curve + term
            if extra:
                r = d - mm(rest[s][...], rest[n][...])
                term = mm(r, image, (0, 0))
                cross = term if s == 0 else cross + term
        curve = packed_symmetric(symmetric(curve))
        if final:
            outs[0][...] = curve
            return
        mine, mates, stacked = outs
        stacked[:PACKED] = curve
        if first:
            r = ds[0][...]
            stacked[PACKED:] = packed_symmetric(mm(r, r, (0, 0)))
        else:
            stacked[PACKED : PACKED + SUB] = jnp.zeros((SUB, LANES), F32)
            stacked[PACKED + SUB :] = cross
        half = lax.axis_index("coef")
        mine[...] = stacked[pl.ds(pl.multiple_of(half * rows, SUB), rows), :]
        mates[...] = stacked[pl.ds(pl.multiple_of((1 - half) * rows, SUB), rows), :]

    *pieces, _ = call(
        body,
        [shape(rows)] * (1 if final else 2),
        *parts,
        *directions,
        *extra,
        flops=24 * n * strip * LANES * LANES,
        moved=2**20,
        scratch=[] if final else [pltpu.VMEM((2 * rows, LANES), F32)],
    )
    return pieces


def square_gram(image_parts):
    strip = image_parts[0].shape[0]
    parts = len(image_parts)

    def body(*refs):
        ins, image_out, out = refs[:parts], refs[parts], refs[parts + 1]
        image = ins[0][...]
        for ref in ins[1:]:
            image = image + ref[...]
        image_out[...] = image
        out[...] = packed_symmetric(mm(image, image, (0, 0)))

    image, square, _ = call(
        body,
        [shape(strip), shape(PACKED)],
        *image_parts,
        flops=12 * strip * LANES * LANES,
        moved=2**20,
    )
    return image, square


def eliminated(*systems):
    n = systems[0][0].shape[0]
    strips = n // SUB
    place = lax.broadcasted_iota(jnp.int32, (SUB, LANES), 0)

    def cut(value):
        return [value[SUB * k : SUB * (k + 1)] for k in range(strips)]

    def lanes_of(value, lane):
        return jnp.broadcast_to(value[:, lane : lane + 1], (SUB, LANES))

    held = [(cut(matrix), cut(sides)) for matrix, sides in systems]

    def update(k, j):
        for a, b in held:
            row_a, row_b = a[k], b[k]
            for i in range(SUB):
                factor = lanes_of(a[k], SUB * j + i)
                row_a = row_a - factor * a[j][i : i + 1]
                row_b = row_b - factor * b[j][i : i + 1]
            a[k], b[k] = row_a, row_b

    for j in range(strips):
        if j:
            update(j, j - 1)
        waiting = [k for k in range(strips) if j and k not in (j, j - 1)]
        now = [
            [a[j], b[j], *(lanes_of(a[j], SUB * j + i) for i in range(SUB))] for a, b in held
        ]
        for i in range(SUB):
            here = place == i
            for index, values in enumerate(now):
                column = values[2 + i]
                inverse = 1.0 / column[i : i + 1]

                def step(value):
                    row = value[i : i + 1] * inverse
                    return jnp.where(here, row, value - column * row)

                now[index] = [
                    step(value) if place_of < 2 or place_of > 2 + i else value
                    for place_of, value in enumerate(values)
                ]
            for k in waiting[2 * i : 2 * i + 2]:
                update(k, j - 1)
        for (a, b), values in zip(held, now):
            a[j], b[j] = values[:2]
    for k in range(strips - 1):
        update(k, strips - 1)
    return [jnp.concatenate(b, axis=0) for _, b in held]


def identity():
    return (
        lax.broadcasted_iota(jnp.int32, (LANES, LANES), 0)
        == lax.broadcasted_iota(jnp.int32, (LANES, LANES), 1)
    ).astype(F32)


def between_iterations(gram, solution, direction, alpha, token):
    strip = direction.shape[0]
    fields = [direction, alpha] + ([] if solution is None else [solution])

    def body(g, d, a, *refs):
        inverse, out = refs[-2:]
        inverse[...] = eliminated((g[...], identity()))[0]
        change = mm(d[...], a[...])
        out[...] = change if solution is None else refs[0][...] + change

    return call(
        body,
        [shape(LANES), shape(strip)],
        gram,
        *fields,
        flops=2**30,
        moved=2**20,
        after=[token],
    )


def advance(pieces, gram, residual, direction, solution, image, first, final):
    strip = residual.shape[0]
    n = len(pieces)
    rows = pieces[0].shape[0]
    fields = [residual, *image, *([] if first else [gram])]
    fields += [direction, solution] if final else []
    many = len(image)

    def body(*refs):
        ins, refs = refs[:n], refs[n:]
        rest, outs = refs[: len(fields)], refs[len(fields) :]
        if final:
            raw = ins[0]
        else:
            *outs, raw = outs
            half = lax.axis_index("coef")
            raw[pl.ds(pl.multiple_of(half * rows, SUB), rows), :] = ins[0][...]
            raw[pl.ds(pl.multiple_of((1 - half) * rows, SUB), rows), :] = ins[1][...]
        curvature = unpacked_symmetric(raw[:PACKED, :])
        if first:
            g = unpacked_symmetric(raw[PACKED:, :])
            alpha, inverse = eliminated((curvature, g), (g, identity()))
        else:
            g = rest[1 + many][...]
            (alpha,) = eliminated((curvature, g))
        image_value = rest[1][...]
        for ref in rest[2 : 1 + many]:
            image_value = image_value + ref[...]
        outs[0][...] = rest[0][...] - mm(image_value, alpha)
        if final:
            outs[1][...] = rest[-1][...] + mm(rest[-2][...], alpha)
            return
        shared = mm(curvature if first else raw[PACKED + SUB :, :], alpha)
        outs[1][...] = alpha
        outs[2][...] = g - (shared + shared.T)
        if first:
            outs[3][...] = inverse

    out = [shape(strip), shape(strip)] if final else [shape(strip)] + [shape(LANES)] * (2 + first)
    return call(
        body,
        out,
        *pieces,
        *fields,
        flops=2**30,
        moved=2**20,
        scratch=[] if final else [pltpu.VMEM((2 * rows, LANES), F32)],
    )[:-1]


def turn(square, alpha, partial, inverse, residual, direction):
    strip = residual.shape[0]

    def body(square, alpha, partial, inverse, r, d, new_d, low, beta_out, gram_out):
        a = alpha[...]
        following = partial[...] + mm(a, mm(unpacked_symmetric(square[...]), a), (0, 0))
        beta = mm(inverse[...], following)
        value = r[...] + mm(d[...], beta)
        low[...] = value.astype(BF16)
        new_d[...] = value
        beta_out[...] = beta
        gram_out[...] = following

    return call(
        body,
        [shape(strip), shape(strip, dtype=BF16), shape(LANES), shape(LANES)],
        square,
        alpha,
        partial,
        inverse,
        residual,
        direction,
        flops=2**28,
        moved=2**20,
    )[:-1]


def shards(couplings, observations, replicate_mask):
    links, rows = couplings.shape[1], couplings.shape[3]
    strip = couplings.shape[6]
    blocks = couplings.reshape(links, rows, couplings.shape[4], strip)
    blocks = pltpu.with_memory_space_constraint(blocks, pltpu.HBM)
    n = lax.axis_size("rhs")
    obs_matrix = observations.reshape(observations.shape[0], rows)
    parts, token = right_side_parts(obs_matrix, replicate_mask, n, strip)
    own = [parts[0]] + [swapped(parts[s], "rhs", s, n) for s in range(1, n)]
    groups = link_groups(links)
    packed = {}
    ahead = list(groups)[:2]
    for o in ahead:
        packed[o], token = retiled(blocks, groups[o], token)
    residual, low, token = sum_and_round(own, token)
    for o in list(groups)[2:]:
        packed[o], token = retiled(blocks, groups[o], token)
    retile_token = token
    direction = residual
    solution = gram = beta = before = alpha = inverse = None
    for step in range(ITERS):
        first, final = step == 0, step + 1 == ITERS
        state = [inverse, solution]

        def between(token):
            if first:
                return retile_token
            *state[:], token = between_iterations(gram, solution, before[0], alpha, token)
            return token

        parts = operate(packed, low, between)
        inverse, solution = state
        directions = [direction] + [swapped(direction, "rhs", s, n) for s in range(1, n)]
        image_parts = [parts[0]] + [swapped(parts[s], "rhs", s, n) for s in range(1, n)]
        linear = linear_grams(parts, directions, before, beta, first, final)
        if final:
            residual, solution = advance(
                reduce_whole(*linear), gram, residual, direction, solution, image_parts, first, final
            )
            break
        image, square = square_gram(image_parts)
        linear = reduce_halves(*linear)
        (square,) = reduce_whole(square)
        residual, alpha, partial, *rest = advance(
            linear, gram, residual, direction, solution, [image], first, final
        )
        if first:
            (inverse,) = rest
        before = directions
        direction, low, beta, gram = turn(
            square, alpha, partial, inverse, residual, direction
        )
    shape_out = (1, 1, strip, LANES)
    return (solution.reshape(shape_out), residual.reshape(shape_out))


def solution(mesh):
    placed = (
        P("panel", None, "coef", None, None, "rhs", None),
        P(("groups", "rhs"), "panel", "coef", None),
        P(("groups", "rhs"), None),
    )
    return jax.shard_map(
        shards,
        mesh=mesh,
        in_specs=placed,
        out_specs=(
            P(("groups", "panel"), "coef", "rhs", None),
            P(("groups", "panel"), "coef", "rhs", None),
        ),
        check_vma=False,
    )
```

```python
import functools

import jax
import jax.numpy as jnp
from jax import lax
from jax.experimental import pallas as pl
from jax.experimental.pallas import tpu as pltpu
from jax.sharding import PartitionSpec as P

ITERS = 3
LANES = 128
SUB = 8
VMEM_LIMIT = 14 * 2**20
F32 = jnp.float32
BF16 = jnp.bfloat16
VMEM = pl.BlockSpec(memory_space=pltpu.VMEM)
ANY = pl.BlockSpec(memory_space=pl.ANY)
HBM = pl.BlockSpec(memory_space=pltpu.HBM)


def mm(a, b, dims=(1, 0)):
    return lax.dot_general(
        a,
        b,
        (((dims[0],), (dims[1],)), ((), ())),
        precision=lax.Precision.HIGHEST,
        preferred_element_type=F32,
    )


def call(body, outs, *args, flops=0, moved=0, scratch=(), after=(), any_args=0, any_outs=False):
    inputs, outputs, waits = len(args), len(outs), len(after)

    def ordered(*refs):
        token = refs[inputs + waits + outputs]
        token[...] = jnp.zeros_like(token)
        body(
            *refs[:inputs],
            *refs[inputs + waits : inputs + waits + outputs],
            *refs[inputs + waits + outputs + 1 :],
        )

    return pl.pallas_call(
        ordered,
        out_shape=list(outs) + [shape(SUB)],
        in_specs=[HBM] * any_args + [VMEM] * (inputs - any_args) + [ANY] * waits,
        out_specs=[ANY if any_outs else VMEM] * outputs + [VMEM],
        scratch_shapes=list(scratch),
        cost_estimate=pl.CostEstimate(flops=flops, bytes_accessed=moved, transcendentals=0),
        compiler_params=pltpu.CompilerParams(vmem_limit_bytes=VMEM_LIMIT),
    )(*args, *after)


def shape(rows, cols=LANES, dtype=F32):
    return jax.ShapeDtypeStruct((rows, cols), dtype)


def permute(value, axis, pairs):
    return lax.ppermute(value, axis, pairs)


def shifted(value, axis, by):
    n = lax.axis_size(axis)
    return permute(value, axis, [((i + by) % n, i) for i in range(n)])


def mate(i, s, n):
    return i ^ s if n & (n - 1) == 0 else (s - i) % n


def swapped(value, axis, s, n):
    return permute(value, axis, [(mate(i, s, n), i) for i in range(n)])


def sum_near(value):
    axes = ("panel", "rhs")
    count = lax.axis_size(axes)
    one, two, three = (swapped(value, axes, s, count) for s in (1, 2, 3))
    return (value + one) + (two + three)


def sum_far(value, meanwhile=None):
    axes = ("panel", "rhs")
    other = swapped(value, axes, 4, lax.axis_size(axes))
    if meanwhile is not None:
        other, _ = lax.optimization_barrier((other, meanwhile))
    return value + other


def sum_chips(value, stages):
    if lax.axis_size("panel") != 4 or lax.axis_size("rhs") != 2:
        return lax.psum(value, ("panel", "rhs"))
    for stage in stages:
        value = stage(value)
    return value


def reduce_whole(value):
    value = value + swapped(value, "coef", 1, 2)
    return [sum_chips(value, (sum_near, sum_far))]


def reduce_halves(mine, mates, meanwhile):
    value = mine + swapped(mates, "coef", 1, 2)
    value = sum_chips(value, (functools.partial(sum_far, meanwhile=meanwhile), sum_near))
    return [value, swapped(value, "coef", 1, 2)]


def right_side_parts(obs, mask, n, strip):
    def body(obs_hbm, mask_hbm, *refs):
        *outs, obs_ref, mask_ref, sems = refs
        copies = [
            pltpu.make_async_copy(mask_hbm, mask_ref, sems.at[0]),
            pltpu.make_async_copy(obs_hbm, obs_ref, sems.at[1]),
        ]
        for copy in copies:
            copy.start()
        for copy in copies:
            copy.wait()
        signs = (2 * mask_ref[...] - 1).astype(BF16)
        me = lax.axis_index("rhs")
        for s in range(n):
            place = pl.multiple_of(mate(me, s, n) * strip, strip)
            outs[s][...] = lax.dot_general(
                obs_ref[:, pl.ds(place, strip)],
                signs,
                (((0,), (0,)), ((), ())),
                preferred_element_type=F32,
            )

    *parts, token = call(
        body,
        [shape(strip)] * n,
        pltpu.with_memory_space_constraint(obs, pltpu.HBM),
        pltpu.with_memory_space_constraint(mask, pltpu.HBM),
        flops=2 * obs.size * LANES,
        moved=2 * obs.size,
        scratch=[
            pltpu.VMEM(obs.shape, BF16),
            pltpu.VMEM(mask.shape, mask.dtype),
            pltpu.SemaphoreType.DMA((2,)),
        ],
        any_args=2,
    )
    return parts, token


def sum_and_round(parts, token):
    strip = parts[0].shape[0]

    def body(*refs):
        *ins, out, low = refs
        total = ins[0][...]
        for ref in ins[1:]:
            total = total + ref[...]
        out[...] = total
        low[...] = total.astype(BF16)

    return call(
        body, [shape(strip), shape(strip, dtype=BF16)], *parts, moved=2**20, after=[token]
    )


def retiled(blocks, links, count, token):
    rows, strip = blocks.shape[1], blocks.shape[3]
    tiles = strip // LANES

    def body(k_ref, out, sems):
        copies = []
        for i, link in enumerate(links()):
            for t in range(tiles):
                copy = pltpu.make_async_copy(
                    k_ref.at[link, :, :, pl.ds(t * LANES, LANES)], out.at[i, t], sems.at[i, t]
                )
                copy.start()
                copies.append(copy)
        for copy in copies:
            copy.wait()

    packed, token = call(
        body,
        [pltpu.VMEM((count, tiles, rows, 2, LANES), BF16)],
        blocks,
        moved=count * rows * 2 * strip * 4,
        scratch=[pltpu.SemaphoreType.DMA((count, tiles))],
        after=[token],
        any_args=1,
        any_outs=True,
    )
    return packed, token


def link_products(packed, pieces, acc, n, last, after=()):
    count, tiles, rows = packed.shape[:3]
    packed = packed.reshape(count, tiles, 2 * rows, LANES)
    packed = pltpu.with_memory_space_constraint(packed, pltpu.VMEM)
    strip = tiles * LANES
    block = min(512, 2 * rows)

    def body(*refs):
        k_ref, own_ref, other_ref = refs[:3]
        acc_ref = refs[3] if acc is not None else None
        outs = refs[3 + (acc is not None) : -3]
        weights, even_acc, odd_acc = refs[-3:]
        half = lax.axis_index("coef")
        weights[:, pl.ds(pl.multiple_of(half * LANES, LANES), LANES)] = own_ref[...]
        weights[:, pl.ds(pl.multiple_of((1 - half) * LANES, LANES), LANES)] = other_ref[...]
        for start in range(0, 2 * rows, block):
            here = slice(start, start + block)
            left = jnp.concatenate(
                [k_ref[i, t, here, :] for i in range(count) for t in range(tiles)], axis=1
            )
            right = jnp.concatenate([weights[...]] * count, axis=0)
            product = jnp.dot(left, right, preferred_element_type=F32)
            even_acc[here, :] = product[:, :LANES]
            odd_acc[here, :] = product[:, LANES:]
        me = lax.axis_index("rhs")
        size = rows // len(outs)
        for s in range(len(outs)):
            start = mate(me, s, n) * size if last else 0
            even = even_acc[pl.ds(2 * start, size, stride=2), :]
            odd = odd_acc[pl.ds(2 * start + 1, size, stride=2), :]
            total = even + odd
            if acc_ref is not None:
                total = total + acc_ref[pl.ds(start, size), :]
            outs[s][...] = total

    args = [packed, *pieces] + ([acc] if acc is not None else [])
    *result, token = call(
        body,
        [shape(rows // n)] * n if last else [shape(rows)],
        *args,
        flops=4 * count * rows * 2 * strip * LANES,
        moved=count * rows * 2 * strip * 2,
        scratch=[
            pltpu.VMEM((strip, 2 * LANES), BF16),
            pltpu.VMEM((2 * rows, LANES), F32),
            pltpu.VMEM((2 * rows, LANES), F32),
        ],
        after=after,
    )
    return (result if last else result[0]), token


def link_groups(links):
    reach = (links - 1) // 2
    panels = lax.axis_size("panel")
    groups = []
    if links == 2 * panels + 1 and panels & (panels - 1) == 0:
        for s in range(panels):

            def numbers(s=s):
                me = lax.axis_index("panel")
                start = lax.rem((me ^ s) - me + reach + panels, panels)
                return [start + panels * i for i in range(3 if s == 0 else 2)]

            bring = functools.partial(swapped, axis="panel", s=s, n=panels)
            groups.append((bring, numbers, 3 if s == 0 else 2))
        return groups
    offsets = {}
    for link in range(links):
        offsets.setdefault((link - reach) % panels, []).append(link)
    for o in sorted(offsets, key=lambda o: min(o, panels - o)):
        bring = functools.partial(shifted, axis="panel", by=o)
        groups.append((bring, functools.partial(list, offsets[o]), len(offsets[o])))
    return groups


def operate(packed, groups, low, direction, between):
    n = lax.axis_size("rhs")
    last = len(groups) - 1
    arrived = [low] + [bring(low) for bring, _, _ in groups[:0:-1]][::-1]
    directions = [direction] + [swapped(direction, "rhs", s, n) for s in range(1, n)]
    acc, after, tokens = None, (), []
    for place in range(last + 1):
        piece = arrived[place]
        if place:
            piece, _ = lax.optimization_barrier((piece, tokens[max(0, place - 2)]))
        pair = [piece, swapped(piece, "coef", 1, 2)]
        if place == 1:
            after = (*after, *directions[1:])
        acc, token = link_products(packed[place], pair, acc, n, place == last, after)
        after = ()
        if place == 0:
            after = (between(token),)
            tokens.append((token, *after))
        else:
            tokens.append((token,))
    return acc, directions


PACKED = LANES // 2 + SUB


def corner():
    row = lax.broadcasted_iota(jnp.int32, (LANES // 2, LANES), 0)
    lane = lax.broadcasted_iota(jnp.int32, (LANES // 2, LANES), 1)
    return row, lane, lane < LANES // 2


def packed_symmetric(matrix):
    half = LANES // 2
    row, lane, left = corner()
    top = matrix[:half]
    last = pltpu.roll(matrix[half:], half, 1)
    body = jnp.where(left & (lane > row), last, top)
    diagonal = jnp.sum(jnp.where(lane == row, last, 0.0), axis=0, keepdims=True)
    return jnp.concatenate([body, jnp.broadcast_to(diagonal, (SUB, LANES))], axis=0)


def unpacked_symmetric(rows):
    half = LANES // 2
    row, lane, left = corner()
    body, diagonal = rows[:half], rows[half : half + 1]
    top = jnp.where(left & (lane >= row), 0.0, body)
    last = jnp.where(left & (lane > row), body, 0.0)
    sides = jnp.concatenate([top, pltpu.roll(last, half, 1)], axis=0)
    top = jnp.where(lane == row, body, 0.0)
    last = jnp.where(lane == row, jnp.broadcast_to(diagonal, body.shape), 0.0)
    return sides + sides.T + jnp.concatenate([top, pltpu.roll(last, half, 1)], axis=0)


def symmetric(raw):
    return 0.5 * (raw + raw.T)


JOINT = PACKED + SUB + LANES


def linear_grams(parts, directions, before, beta, first, final):
    strip = parts[0].shape[0]
    n = len(parts)
    extra = [] if first or final else [*before, beta]
    rows = PACKED if final else JOINT // 2

    def body(*refs):
        images, ds = refs[:n], refs[n : 2 * n]
        rest = refs[2 * n : 2 * n + len(extra)]
        outs = refs[2 * n + len(extra) :]
        curve = cross = None
        for s in range(n):
            image, d = images[s][...], ds[s][...]
            term = mm(d, image, (0, 0))
            curve = term if s == 0 else curve + term
            if extra:
                r = d - mm(rest[s][...], rest[n][...])
                term = mm(r, image, (0, 0))
                cross = term if s == 0 else cross + term
        if final:
            outs[0][...] = packed_symmetric(symmetric(curve))
            return
        mine, mates, stacked = outs
        if first:
            r = ds[0][...]
            sym, whole = mm(r, r, (0, 0)), curve
        else:
            sym, whole = symmetric(curve), cross
        stacked[:PACKED] = packed_symmetric(sym)
        stacked[PACKED : PACKED + SUB] = jnp.zeros((SUB, LANES), F32)
        stacked[PACKED + SUB :] = whole
        half = lax.axis_index("coef")
        mine[...] = stacked[pl.ds(pl.multiple_of(half * rows, SUB), rows), :]
        mates[...] = stacked[pl.ds(pl.multiple_of((1 - half) * rows, SUB), rows), :]

    *pieces, _ = call(
        body,
        [shape(rows)] * (1 if final else 2),
        *parts,
        *directions,
        *extra,
        flops=24 * n * strip * LANES * LANES,
        moved=2**20,
        scratch=[] if final else [pltpu.VMEM((2 * rows, LANES), F32)],
    )
    return pieces


def square_gram(image_parts):
    strip = image_parts[0].shape[0]
    parts = len(image_parts)

    def body(*refs):
        ins, image_out, out = refs[:parts], refs[parts], refs[parts + 1]
        image = ins[0][...]
        for ref in ins[1:]:
            image = image + ref[...]
        image_out[...] = image
        out[...] = packed_symmetric(mm(image, image, (0, 0)))

    image, square, _ = call(
        body,
        [shape(strip), shape(PACKED)],
        *image_parts,
        flops=12 * strip * LANES * LANES,
        moved=2**20,
    )
    return image, square


def eliminated(*systems):
    n = systems[0][0].shape[0]
    strips = n // SUB
    place = lax.broadcasted_iota(jnp.int32, (SUB, LANES), 0)

    def cut(value):
        return [value[SUB * k : SUB * (k + 1)] for k in range(strips)]

    def lanes_of(value, lane):
        return jnp.broadcast_to(value[:, lane : lane + 1], (SUB, LANES))

    held = [(cut(matrix), cut(sides)) for matrix, sides in systems]

    def rows_of(value):
        return [jnp.broadcast_to(value[i : i + 1], (SUB, LANES)) for i in range(SUB)]

    def update(k, j, spread):
        for (a, b), (rows_a, rows_b) in zip(held, spread):
            row_a, row_b = a[k], b[k]
            for i in range(SUB):
                factor = lanes_of(a[k], SUB * j + i)
                row_a = row_a - factor * rows_a[i]
                row_b = row_b - factor * rows_b[i]
            a[k], b[k] = row_a, row_b

    for j in range(strips):
        if j:
            spread = [(rows_of(a[j - 1]), rows_of(b[j - 1])) for a, b in held]
            update(j, j - 1, spread)
        waiting = [k for k in range(strips) if j and k not in (j, j - 1)]
        now = [
            [a[j], b[j], *(lanes_of(a[j], SUB * j + i) for i in range(SUB))] for a, b in held
        ]
        for i in range(SUB):
            here = place == i
            for index, values in enumerate(now):
                column = values[2 + i]
                inverse = 1.0 / column[i : i + 1]

                def step(value):
                    row = value[i : i + 1] * inverse
                    return jnp.where(here, row, value - column * row)

                now[index] = [
                    step(value) if place_of < 2 or place_of > 2 + i else value
                    for place_of, value in enumerate(values)
                ]
            for k in waiting[2 * i : 2 * i + 2]:
                update(k, j - 1, spread)
        for (a, b), values in zip(held, now):
            a[j], b[j] = values[:2]
    spread = [(rows_of(a[-1]), rows_of(b[-1])) for a, b in held]
    for k in range(strips - 1):
        update(k, strips - 1, spread)
    return [jnp.concatenate(b, axis=0) for _, b in held]


def identity():
    return (
        lax.broadcasted_iota(jnp.int32, (LANES, LANES), 0)
        == lax.broadcasted_iota(jnp.int32, (LANES, LANES), 1)
    ).astype(F32)


def between_iterations(gram, solution, direction, alpha, token):
    strip = direction.shape[0]
    fields = [direction, alpha] + ([] if solution is None else [solution])

    def body(g, d, a, *refs):
        inverse, out = refs[-2:]
        inverse[...] = eliminated((g[...], identity()))[0]
        change = mm(d[...], a[...])
        out[...] = change if solution is None else refs[0][...] + change

    return call(
        body,
        [shape(LANES), shape(strip)],
        gram,
        *fields,
        flops=2**30,
        moved=2**20,
        after=[token],
    )


def advance(pieces, gram, residual, direction, solution, image, first, final):
    strip = residual.shape[0]
    n = len(pieces)
    rows = pieces[0].shape[0]
    fields = [residual, *image, *([] if first else [gram])]
    fields += [direction, solution] if final else []
    many = len(image)

    def body(*refs):
        ins, refs = refs[:n], refs[n:]
        rest, outs = refs[: len(fields)], refs[len(fields) :]
        if final:
            raw = ins[0]
        else:
            *outs, raw = outs
            half = lax.axis_index("coef")
            raw[pl.ds(pl.multiple_of(half * rows, SUB), rows), :] = ins[0][...]
            raw[pl.ds(pl.multiple_of((1 - half) * rows, SUB), rows), :] = ins[1][...]
        sym = unpacked_symmetric(raw[:PACKED, :])
        curvature = symmetric(raw[PACKED + SUB :, :]) if first else sym
        if first:
            g = sym
            alpha, inverse = eliminated((curvature, g), (g, identity()))
        else:
            g = rest[1 + many][...]
            (alpha,) = eliminated((curvature, g))
        image_value = rest[1][...]
        for ref in rest[2 : 1 + many]:
            image_value = image_value + ref[...]
        outs[0][...] = rest[0][...] - mm(image_value, alpha)
        if final:
            outs[1][...] = rest[-1][...] + mm(rest[-2][...], alpha)
            return
        shared = mm(raw[PACKED + SUB :, :], alpha)
        outs[1][...] = alpha
        outs[2][...] = g - (shared + shared.T)
        if first:
            outs[3][...] = inverse

    out = [shape(strip), shape(strip)] if final else [shape(strip)] + [shape(LANES)] * (2 + first)
    return call(
        body,
        out,
        *pieces,
        *fields,
        flops=2**30,
        moved=2**20,
        scratch=[] if final else [pltpu.VMEM((2 * rows, LANES), F32)],
    )[:-1]


def turn(square, alpha, partial, inverse, residual, direction):
    strip = residual.shape[0]

    def body(square, alpha, partial, inverse, r, d, new_d, low, beta_out, gram_out):
        a = alpha[...]
        following = partial[...] + mm(a, mm(unpacked_symmetric(square[...]), a), (0, 0))
        beta = mm(inverse[...], following)
        value = r[...] + mm(d[...], beta)
        low[...] = value.astype(BF16)
        new_d[...] = value
        beta_out[...] = beta
        gram_out[...] = following

    return call(
        body,
        [shape(strip), shape(strip, dtype=BF16), shape(LANES), shape(LANES)],
        square,
        alpha,
        partial,
        inverse,
        residual,
        direction,
        flops=2**28,
        moved=2**20,
    )[:-1]


def shards(couplings, observations, replicate_mask):
    links, rows = couplings.shape[1], couplings.shape[3]
    strip = couplings.shape[6]
    blocks = couplings.reshape(links, rows, couplings.shape[4], strip)
    blocks = pltpu.with_memory_space_constraint(blocks, pltpu.HBM)
    n = lax.axis_size("rhs")
    obs_matrix = observations.reshape(observations.shape[0], rows)
    parts, token = right_side_parts(obs_matrix, replicate_mask, n, strip)
    own = [parts[0]] + [swapped(parts[s], "rhs", s, n) for s in range(1, n)]
    groups = link_groups(links)
    packed = []
    for _, numbers, count in groups[:2]:
        value, token = retiled(blocks, numbers, count, token)
        packed.append(value)
    residual, low, token = sum_and_round(own, token)
    for _, numbers, count in groups[2:]:
        value, token = retiled(blocks, numbers, count, token)
        packed.append(value)
    retile_token = token
    direction = residual
    solution = gram = beta = before = alpha = inverse = None
    for step in range(ITERS):
        first, final = step == 0, step + 1 == ITERS
        state = [inverse, solution]

        def between(token):
            if first:
                return retile_token
            *state[:], token = between_iterations(gram, solution, before[0], alpha, token)
            return token

        parts, directions = operate(packed, groups, low, direction, between)
        inverse, solution = state
        image_parts = [parts[0]] + [swapped(parts[s], "rhs", s, n) for s in range(1, n)]
        linear = linear_grams(parts, directions, before, beta, first, final)
        if final:
            residual, solution = advance(
                reduce_whole(*linear), gram, residual, direction, solution, image_parts, first, final
            )
            break
        image, square = square_gram(image_parts)
        linear = reduce_halves(*linear, square)
        (square,) = reduce_whole(square)
        residual, alpha, partial, *rest = advance(
            linear, gram, residual, direction, solution, [image], first, final
        )
        if first:
            (inverse,) = rest
        before = directions
        direction, low, beta, gram = turn(
            square, alpha, partial, inverse, residual, direction
        )
    shape_out = (1, 1, strip, LANES)
    return (solution.reshape(shape_out), residual.reshape(shape_out))


def solution(mesh):
    placed = (
        P("panel", None, "coef", None, None, "rhs", None),
        P(("groups", "rhs"), "panel", "coef", None),
        P(("groups", "rhs"), None),
    )
    return jax.shard_map(
        shards,
        mesh=mesh,
        in_specs=placed,
        out_specs=(
            P(("groups", "panel"), "coef", "rhs", None),
            P(("groups", "panel"), "coef", "rhs", None),
        ),
        check_vma=False,
    )
```

```python
import functools

import jax
import jax.numpy as jnp
from jax import lax
from jax.experimental import pallas as pl
from jax.experimental.pallas import tpu as pltpu
from jax.sharding import PartitionSpec as P

ITERS = 3
LANES = 128
SUB = 8
VMEM_LIMIT = 14 * 2**20
F32 = jnp.float32
BF16 = jnp.bfloat16
VMEM = pl.BlockSpec(memory_space=pltpu.VMEM)
ANY = pl.BlockSpec(memory_space=pl.ANY)
HBM = pl.BlockSpec(memory_space=pltpu.HBM)


def mm(a, b, dims=(1, 0)):
    return lax.dot_general(
        a,
        b,
        (((dims[0],), (dims[1],)), ((), ())),
        precision=lax.Precision.HIGHEST,
        preferred_element_type=F32,
    )


def call(body, outs, *args, flops=0, moved=0, scratch=(), after=(), any_args=0, any_outs=False):
    inputs, outputs, waits = len(args), len(outs), len(after)

    def ordered(*refs):
        token = refs[inputs + waits + outputs]
        token[...] = jnp.zeros_like(token)
        body(
            *refs[:inputs],
            *refs[inputs + waits : inputs + waits + outputs],
            *refs[inputs + waits + outputs + 1 :],
        )

    return pl.pallas_call(
        ordered,
        out_shape=list(outs) + [shape(SUB)],
        in_specs=[HBM] * any_args + [VMEM] * (inputs - any_args) + [ANY] * waits,
        out_specs=[ANY if any_outs else VMEM] * outputs + [VMEM],
        scratch_shapes=list(scratch),
        cost_estimate=pl.CostEstimate(flops=flops, bytes_accessed=moved, transcendentals=0),
        compiler_params=pltpu.CompilerParams(vmem_limit_bytes=VMEM_LIMIT),
    )(*args, *after)


def shape(rows, cols=LANES, dtype=F32):
    return jax.ShapeDtypeStruct((rows, cols), dtype)


def permute(value, axis, pairs):
    return lax.ppermute(value, axis, pairs)


def shifted(value, axis, by):
    n = lax.axis_size(axis)
    return permute(value, axis, [((i + by) % n, i) for i in range(n)])


def mate(i, s, n):
    return i ^ s if n & (n - 1) == 0 else (s - i) % n


def swapped(value, axis, s, n):
    return permute(value, axis, [(mate(i, s, n), i) for i in range(n)])


def sum_near(value):
    axes = ("panel", "rhs")
    count = lax.axis_size(axes)
    one, two, three = (swapped(value, axes, s, count) for s in (1, 2, 3))
    return (value + one) + (two + three)


def from_far(value):
    axes = ("panel", "rhs")
    return swapped(value, axes, 4, lax.axis_size(axes))


def sum_far(value, meanwhile=None):
    other = from_far(value)
    if meanwhile is not None:
        other, _ = lax.optimization_barrier((other, meanwhile))
    return value + other


def by_stages():
    return lax.axis_size("panel") == 4 and lax.axis_size("rhs") == 2


def reduce_one(value):
    value = value + swapped(value, "coef", 1, 2)
    if not by_stages():
        value = lax.psum(value, ("panel", "rhs"))
        return value, value
    near = sum_near(value)
    return sum_far(near), near


def reduce_both(mine, mates, square):
    value = mine + swapped(mates, "coef", 1, 2)
    whole = square + swapped(square, "coef", 1, 2)
    if by_stages():
        rows = value.shape[0]
        value = sum_far(value, meanwhile=square)
        both = sum_near(jnp.concatenate([value, whole], axis=0))
        value, whole = both[:rows], both[rows:]
        terms = [whole, from_far(whole)]
    else:
        value, whole = lax.psum((value, whole), ("panel", "rhs"))
        terms = [whole]
    return [value, swapped(value, "coef", 1, 2)], terms


def right_side_parts(obs, mask, n, strip):
    def body(obs_hbm, mask_hbm, *refs):
        *outs, obs_ref, mask_ref, sems = refs
        copies = [
            pltpu.make_async_copy(mask_hbm, mask_ref, sems.at[0]),
            pltpu.make_async_copy(obs_hbm, obs_ref, sems.at[1]),
        ]
        for copy in copies:
            copy.start()
        for copy in copies:
            copy.wait()
        signs = (2 * mask_ref[...] - 1).astype(BF16)
        me = lax.axis_index("rhs")
        for s in range(n):
            place = pl.multiple_of(mate(me, s, n) * strip, strip)
            outs[s][...] = lax.dot_general(
                obs_ref[:, pl.ds(place, strip)],
                signs,
                (((0,), (0,)), ((), ())),
                preferred_element_type=F32,
            )

    *parts, token = call(
        body,
        [shape(strip)] * n,
        pltpu.with_memory_space_constraint(obs, pltpu.HBM),
        pltpu.with_memory_space_constraint(mask, pltpu.HBM),
        flops=2 * obs.size * LANES,
        moved=2 * obs.size,
        scratch=[
            pltpu.VMEM(obs.shape, BF16),
            pltpu.VMEM(mask.shape, mask.dtype),
            pltpu.SemaphoreType.DMA((2,)),
        ],
        any_args=2,
    )
    return parts, token


def sum_and_round(parts, token):
    strip = parts[0].shape[0]

    def body(*refs):
        *ins, out, low = refs
        total = ins[0][...]
        for ref in ins[1:]:
            total = total + ref[...]
        out[...] = total
        low[...] = total.astype(BF16)

    return call(
        body, [shape(strip), shape(strip, dtype=BF16)], *parts, moved=2**20, after=[token]
    )


def retiled(blocks, links, count, token):
    rows, strip = blocks.shape[1], blocks.shape[3]
    tiles = strip // LANES

    def body(k_ref, out, sems):
        copies = []
        for i, link in enumerate(links()):
            for t in range(tiles):
                copy = pltpu.make_async_copy(
                    k_ref.at[link, :, :, pl.ds(t * LANES, LANES)], out.at[i, t], sems.at[i, t]
                )
                copy.start()
                copies.append(copy)
        for copy in copies:
            copy.wait()

    packed, token = call(
        body,
        [pltpu.VMEM((count, tiles, rows, 2, LANES), BF16)],
        blocks,
        moved=count * rows * 2 * strip * 4,
        scratch=[pltpu.SemaphoreType.DMA((count, tiles))],
        after=[token],
        any_args=1,
        any_outs=True,
    )
    return packed, token


def link_products(packed, pieces, acc, n, last, after=()):
    count, tiles, rows = packed.shape[:3]
    packed = packed.reshape(count, tiles, 2 * rows, LANES)
    packed = pltpu.with_memory_space_constraint(packed, pltpu.VMEM)
    strip = tiles * LANES
    block = min(512, 2 * rows)

    def body(*refs):
        k_ref, own_ref, other_ref = refs[:3]
        acc_ref = refs[3] if acc is not None else None
        outs = refs[3 + (acc is not None) : -3]
        weights, even_acc, odd_acc = refs[-3:]
        half = lax.axis_index("coef")
        weights[:, pl.ds(pl.multiple_of(half * LANES, LANES), LANES)] = own_ref[...]
        weights[:, pl.ds(pl.multiple_of((1 - half) * LANES, LANES), LANES)] = other_ref[...]
        for start in range(0, 2 * rows, block):
            here = slice(start, start + block)
            left = jnp.concatenate(
                [k_ref[i, t, here, :] for i in range(count) for t in range(tiles)], axis=1
            )
            right = jnp.concatenate([weights[...]] * count, axis=0)
            product = jnp.dot(left, right, preferred_element_type=F32)
            even_acc[here, :] = product[:, :LANES]
            odd_acc[here, :] = product[:, LANES:]
        me = lax.axis_index("rhs")
        size = rows // len(outs)
        for s in range(len(outs)):
            start = mate(me, s, n) * size if last else 0
            even = even_acc[pl.ds(2 * start, size, stride=2), :]
            odd = odd_acc[pl.ds(2 * start + 1, size, stride=2), :]
            total = even + odd
            if acc_ref is not None:
                total = total + acc_ref[pl.ds(start, size), :]
            outs[s][...] = total

    args = [packed, *pieces] + ([acc] if acc is not None else [])
    *result, token = call(
        body,
        [shape(rows // n)] * n if last else [shape(rows)],
        *args,
        flops=4 * count * rows * 2 * strip * LANES,
        moved=count * rows * 2 * strip * 2,
        scratch=[
            pltpu.VMEM((strip, 2 * LANES), BF16),
            pltpu.VMEM((2 * rows, LANES), F32),
            pltpu.VMEM((2 * rows, LANES), F32),
        ],
        after=after,
    )
    return (result if last else result[0]), token


def link_groups(links):
    reach = (links - 1) // 2
    panels = lax.axis_size("panel")
    groups = []
    if links == 2 * panels + 1 and panels & (panels - 1) == 0:
        for s in range(panels):

            def numbers(s=s):
                me = lax.axis_index("panel")
                start = lax.rem((me ^ s) - me + reach + panels, panels)
                return [start + panels * i for i in range(3 if s == 0 else 2)]

            bring = functools.partial(swapped, axis="panel", s=s, n=panels)
            groups.append((bring, numbers, 3 if s == 0 else 2))
        return groups
    offsets = {}
    for link in range(links):
        offsets.setdefault((link - reach) % panels, []).append(link)
    for o in sorted(offsets, key=lambda o: min(o, panels - o)):
        bring = functools.partial(shifted, axis="panel", by=o)
        groups.append((bring, functools.partial(list, offsets[o]), len(offsets[o])))
    return groups


def operate(packed, groups, low, direction, between):
    n = lax.axis_size("rhs")
    last = len(groups) - 1
    arrived = [low] + [bring(low) for bring, _, _ in groups[:0:-1]][::-1]
    directions = [direction] + [swapped(direction, "rhs", s, n) for s in range(1, n)]
    acc, after, tokens = None, (), []
    for place in range(last + 1):
        piece = arrived[place]
        if place:
            piece, held = lax.optimization_barrier((piece, tokens[0 if place < last else -1]))
            after = (*after, *held)
        pair = [piece, swapped(piece, "coef", 1, 2)]
        if place == 1:
            after = (*after, *directions[1:])
        acc, token = link_products(packed[place], pair, acc, n, place == last, after)
        after = ()
        if place == 0:
            after = (between(token),)
            tokens.append((token, *after))
        else:
            tokens.append((token,))
    return acc, directions


PACKED = LANES // 2 + SUB


def corner():
    row = lax.broadcasted_iota(jnp.int32, (LANES // 2, LANES), 0)
    lane = lax.broadcasted_iota(jnp.int32, (LANES // 2, LANES), 1)
    return row, lane, lane < LANES // 2


def packed_symmetric(matrix):
    half = LANES // 2
    row, lane, left = corner()
    top = matrix[:half]
    last = pltpu.roll(matrix[half:], half, 1)
    body = jnp.where(left & (lane > row), last, top)
    diagonal = jnp.sum(jnp.where(lane == row, last, 0.0), axis=0, keepdims=True)
    return jnp.concatenate([body, jnp.broadcast_to(diagonal, (SUB, LANES))], axis=0)


def unpacked_symmetric(rows):
    half = LANES // 2
    row, lane, left = corner()
    body, diagonal = rows[:half], rows[half : half + 1]
    top = jnp.where(left & (lane >= row), 0.0, body)
    last = jnp.where(left & (lane > row), body, 0.0)
    sides = jnp.concatenate([top, pltpu.roll(last, half, 1)], axis=0)
    top = jnp.where(lane == row, body, 0.0)
    last = jnp.where(lane == row, jnp.broadcast_to(diagonal, body.shape), 0.0)
    return sides + sides.T + jnp.concatenate([top, pltpu.roll(last, half, 1)], axis=0)


def symmetric(raw):
    return 0.5 * (raw + raw.T)


JOINT = PACKED + SUB + LANES


def linear_grams(parts, directions, before, beta, first, final):
    strip = parts[0].shape[0]
    n = len(parts)
    extra = [] if first or final else [*before, beta]
    rows = PACKED if final else JOINT // 2

    def body(*refs):
        images, ds = refs[:n], refs[n : 2 * n]
        rest = refs[2 * n : 2 * n + len(extra)]
        outs = refs[2 * n + len(extra) :]
        curve = cross = None
        for s in range(n):
            image, d = images[s][...], ds[s][...]
            term = mm(d, image, (0, 0))
            curve = term if s == 0 else curve + term
            if extra:
                r = d - mm(rest[s][...], rest[n][...])
                term = mm(r, image, (0, 0))
                cross = term if s == 0 else cross + term
        if final:
            outs[0][...] = packed_symmetric(symmetric(curve))
            return
        mine, mates, stacked = outs
        if first:
            r = ds[0][...]
            sym, whole = mm(r, r, (0, 0)), curve
        else:
            sym, whole = symmetric(curve), cross
        stacked[:PACKED] = packed_symmetric(sym)
        stacked[PACKED : PACKED + SUB] = jnp.zeros((SUB, LANES), F32)
        stacked[PACKED + SUB :] = whole
        half = lax.axis_index("coef")
        mine[...] = stacked[pl.ds(pl.multiple_of(half * rows, SUB), rows), :]
        mates[...] = stacked[pl.ds(pl.multiple_of((1 - half) * rows, SUB), rows), :]

    *pieces, _ = call(
        body,
        [shape(rows)] * (1 if final else 2),
        *parts,
        *directions,
        *extra,
        flops=24 * n * strip * LANES * LANES,
        moved=2**20,
        scratch=[] if final else [pltpu.VMEM((2 * rows, LANES), F32)],
    )
    return pieces


def square_gram(image_parts):
    strip = image_parts[0].shape[0]
    parts = len(image_parts)

    def body(*refs):
        ins, image_out, out = refs[:parts], refs[parts], refs[parts + 1]
        image = ins[0][...]
        for ref in ins[1:]:
            image = image + ref[...]
        image_out[...] = image
        out[...] = packed_symmetric(mm(image, image, (0, 0)))

    image, square, _ = call(
        body,
        [shape(strip), shape(PACKED)],
        *image_parts,
        flops=12 * strip * LANES * LANES,
        moved=2**20,
    )
    return image, square


def inverted(matrices, lane):
    strips = matrices[0].shape[0] // SUB
    place = lax.broadcasted_iota(jnp.int32, (SUB, LANES), 0)
    held = [[value[SUB * k : SUB * (k + 1)] for k in range(strips)] for value in matrices]

    def lanes_of(value, at):
        return jnp.broadcast_to(value[:, at : at + 1], (SUB, LANES))

    def rows_of(value):
        return [jnp.broadcast_to(value[i : i + 1], (SUB, LANES)) for i in range(SUB)]

    def update(k, j, spread):
        for a, rows in zip(held, spread):
            row = a[k]
            for i in range(SUB):
                row = row - lanes_of(a[k], lane + SUB * j + i) * rows[i]
            a[k] = row

    for j in range(strips):
        if j:
            spread = [rows_of(a[j - 1]) for a in held]
            update(j, j - 1, spread)
        waiting = [k for k in range(strips) if j and k not in (j, j - 1)]
        now = [
            [a[j], *(lanes_of(a[j], lane + SUB * j + i) for i in range(SUB))] for a in held
        ]
        for i in range(SUB):
            here = place == i
            for index, values in enumerate(now):
                column = values[1 + i]
                inverse = 1.0 / column[i : i + 1]

                def step(value):
                    row = value[i : i + 1] * inverse
                    return jnp.where(here, row, value - column * row)

                now[index] = [
                    step(value) if at < 1 or at > 1 + i else value
                    for at, value in enumerate(values)
                ]
            for k in waiting[i : i + 1]:
                update(k, j - 1, spread)
        for a, values in zip(held, now):
            a[j] = values[0]
    spread = [rows_of(a[-1]) for a in held]
    for k in range(strips - 1):
        update(k, strips - 1, spread)
    return [jnp.concatenate(a, axis=0) for a in held]


def eliminated(*systems):
    half = LANES // 2
    row = lax.broadcasted_iota(jnp.int32, (half, LANES), 0)
    lane = lax.broadcasted_iota(jnp.int32, (half, LANES), 1)
    left = lane < half
    first = inverted(
        [
            jnp.where(left, matrix[:half], (lane - half == row).astype(F32))
            for matrix, _ in systems
        ],
        0,
    )
    tops, lasts = [], []
    for (matrix, sides), value in zip(systems, first):
        value = pltpu.roll(value, half, 1)[:, :half]
        top = mm(value, jnp.concatenate([matrix[:half], sides[:half]], axis=1))
        low = jnp.concatenate([matrix[half:], sides[half:]], axis=1)
        tops.append(top)
        lasts.append(low - mm(matrix[half:, :half], top))
    second = inverted(
        [jnp.where(left, (lane == row).astype(F32), last[:, :LANES]) for last in lasts], half
    )
    found = []
    for top, last, value in zip(tops, lasts, second):
        low = mm(value[:, :half], last[:, LANES:])
        high = top[:, LANES:] - mm(
            top[:, :LANES], jnp.concatenate([jnp.zeros_like(low), low], axis=0)
        )
        found.append(jnp.concatenate([high, low], axis=0))
    return found


def identity():
    return (
        lax.broadcasted_iota(jnp.int32, (LANES, LANES), 0)
        == lax.broadcasted_iota(jnp.int32, (LANES, LANES), 1)
    ).astype(F32)


def between_iterations(gram, solution, direction, alpha, token):
    strip = direction.shape[0]
    fields = [direction, alpha] + ([] if solution is None else [solution])

    def body(g, d, a, *refs):
        inverse, out = refs[-2:]
        inverse[...] = eliminated((g[...], identity()))[0]
        change = mm(d[...], a[...])
        out[...] = change if solution is None else refs[0][...] + change

    return call(
        body,
        [shape(LANES), shape(strip)],
        gram,
        *fields,
        flops=2**30,
        moved=2**20,
        after=[token],
    )


def last_alpha(small, gram):
    def body(small, g, out):
        out[...] = eliminated((unpacked_symmetric(small[...]), g[...]))[0]

    return call(body, [shape(LANES)], small, gram, flops=2**30, moved=2**20)[0]


def finish(alpha, residual, direction, solution, image):
    strip = residual.shape[0]

    def body(a, r, d, s, *refs):
        *images, out, new_r = refs
        image = images[0][...]
        for ref in images[1:]:
            image = image + ref[...]
        out[...] = s[...] + mm(d[...], a[...])
        new_r[...] = r[...] - mm(image, a[...])

    return call(
        body,
        [shape(strip), shape(strip)],
        alpha,
        residual,
        direction,
        solution,
        *image,
        flops=2**28,
        moved=2**20,
    )[:-1]


def advance(pieces, gram, residual, image):
    strip = residual.shape[0]
    rows = pieces[0].shape[0]
    first = gram is None
    fields = [*pieces, residual, image] + ([] if first else [gram])

    def body(*refs):
        mine, mates, r, image, *refs = refs
        *refs, raw = refs
        half = lax.axis_index("coef")
        raw[pl.ds(pl.multiple_of(half * rows, SUB), rows), :] = mine[...]
        raw[pl.ds(pl.multiple_of((1 - half) * rows, SUB), rows), :] = mates[...]
        sym, whole = unpacked_symmetric(raw[:PACKED, :]), raw[PACKED + SUB :, :]
        if first:
            new_r, alpha_out, partial, inverse_out = refs
            g = sym
            alpha, inverse_out[...] = eliminated((symmetric(whole), g), (g, identity()))
        else:
            g_ref, new_r, alpha_out, partial = refs
            g = g_ref[...]
            (alpha,) = eliminated((sym, g))
        new_r[...] = r[...] - mm(image[...], alpha)
        shared = mm(whole, alpha)
        alpha_out[...] = alpha
        partial[...] = g - (shared + shared.T)

    return call(
        body,
        [shape(strip)] + [shape(LANES)] * (2 + first),
        *fields,
        flops=2**30,
        moved=2**20,
        scratch=[pltpu.VMEM((2 * rows, LANES), F32)],
    )[:-1]


def turn(square, alpha, partial, inverse, residual, direction):
    strip = residual.shape[0]

    def body(alpha, partial, inverse, r, d, *refs):
        *terms, new_d, low, beta_out, gram_out = refs
        square = terms[0][...]
        for ref in terms[1:]:
            square = square + ref[...]
        a = alpha[...]
        following = partial[...] + mm(a, mm(unpacked_symmetric(square), a), (0, 0))
        beta = mm(inverse[...], following)
        value = r[...] + mm(d[...], beta)
        low[...] = value.astype(BF16)
        new_d[...] = value
        beta_out[...] = beta
        gram_out[...] = following

    return call(
        body,
        [shape(strip), shape(strip, dtype=BF16), shape(LANES), shape(LANES)],
        alpha,
        partial,
        inverse,
        residual,
        direction,
        *square,
        flops=2**28,
        moved=2**20,
    )[:-1]


def shards(couplings, observations, replicate_mask):
    links, rows = couplings.shape[1], couplings.shape[3]
    strip = couplings.shape[6]
    blocks = couplings.reshape(links, rows, couplings.shape[4], strip)
    blocks = pltpu.with_memory_space_constraint(blocks, pltpu.HBM)
    n = lax.axis_size("rhs")
    obs_matrix = observations.reshape(observations.shape[0], rows)
    parts, token = right_side_parts(obs_matrix, replicate_mask, n, strip)
    own = [parts[0]] + [swapped(parts[s], "rhs", s, n) for s in range(1, n)]
    groups = link_groups(links)
    packed = []
    for _, numbers, count in groups[:2]:
        value, token = retiled(blocks, numbers, count, token)
        packed.append(value)
    residual, low, token = sum_and_round(own, token)
    for _, numbers, count in groups[2:]:
        value, token = retiled(blocks, numbers, count, token)
        packed.append(value)
    retile_token = token
    direction = residual
    solution = gram = beta = before = alpha = inverse = None
    for step in range(ITERS):
        first, final = step == 0, step + 1 == ITERS
        state = [inverse, solution]

        def between(token):
            if first:
                return retile_token
            *state[:], token = between_iterations(gram, solution, before[0], alpha, token)
            return token

        parts, directions = operate(packed, groups, low, direction, between)
        inverse, solution = state
        linear = linear_grams(parts, directions, before, beta, first, final)
        if final:
            small, near = reduce_one(*linear)
            parts[1:], _ = lax.optimization_barrier((parts[1:], near))
        image_parts = [parts[0]] + [swapped(parts[s], "rhs", s, n) for s in range(1, n)]
        if final:
            alpha = last_alpha(small, gram)
            solution, residual = finish(alpha, residual, direction, solution, image_parts)
            break
        image, square = square_gram(image_parts)
        linear, square = reduce_both(*linear, square)
        residual, alpha, partial, *rest = advance(linear, gram, residual, image)
        if first:
            (inverse,) = rest
        square[1:], alpha = lax.optimization_barrier((square[1:], alpha))
        before = directions
        direction, low, beta, gram = turn(
            square, alpha, partial, inverse, residual, direction
        )
    shape_out = (1, 1, strip, LANES)
    return (solution.reshape(shape_out), residual.reshape(shape_out))


def solution(mesh):
    placed = (
        P("panel", None, "coef", None, None, "rhs", None),
        P(("groups", "rhs"), "panel", "coef", None),
        P(("groups", "rhs"), None),
    )
    return jax.shard_map(
        shards,
        mesh=mesh,
        in_specs=placed,
        out_specs=(
            P(("groups", "panel"), "coef", "rhs", None),
            P(("groups", "panel"), "coef", "rhs", None),
        ),
        check_vma=False,
    )
```

```python
import functools

import jax
import jax.numpy as jnp
from jax import lax
from jax.experimental import pallas as pl
from jax.experimental.pallas import tpu as pltpu
from jax.sharding import PartitionSpec as P

ITERS = 3
LANES = 128
SUB = 8
VMEM_LIMIT = 14 * 2**20
F32 = jnp.float32
BF16 = jnp.bfloat16
VMEM = pl.BlockSpec(memory_space=pltpu.VMEM)
ANY = pl.BlockSpec(memory_space=pl.ANY)
HBM = pl.BlockSpec(memory_space=pltpu.HBM)


def mm(a, b, dims=(1, 0)):
    return lax.dot_general(
        a,
        b,
        (((dims[0],), (dims[1],)), ((), ())),
        precision=lax.Precision.HIGHEST,
        preferred_element_type=F32,
    )


def call(body, outs, *args, scratch=(), after=(), any_args=0, any_outs=False):
    inputs, outputs, waits = len(args), len(outs), len(after)

    def ordered(*refs):
        token = refs[inputs + waits + outputs]
        token[...] = jnp.zeros_like(token)
        body(
            *refs[:inputs],
            *refs[inputs + waits : inputs + waits + outputs],
            *refs[inputs + waits + outputs + 1 :],
        )

    return pl.pallas_call(
        ordered,
        out_shape=list(outs) + [shape(SUB)],
        in_specs=[HBM] * any_args + [VMEM] * (inputs - any_args) + [ANY] * waits,
        out_specs=[ANY if any_outs else VMEM] * outputs + [VMEM],
        scratch_shapes=list(scratch),
        cost_estimate=pl.CostEstimate(flops=1, bytes_accessed=1, transcendentals=0),
        compiler_params=pltpu.CompilerParams(vmem_limit_bytes=VMEM_LIMIT),
    )(*args, *after)


def shape(rows, cols=LANES, dtype=F32):
    return jax.ShapeDtypeStruct((rows, cols), dtype)


def permute(value, axis, pairs):
    return lax.ppermute(value, axis, pairs)


def shifted(value, axis, by):
    n = lax.axis_size(axis)
    return permute(value, axis, [((i + by) % n, i) for i in range(n)])


def mate(i, s, n):
    return i ^ s if n & (n - 1) == 0 else (s - i) % n


def swapped(value, axis, s, n):
    return permute(value, axis, [(mate(i, s, n), i) for i in range(n)])


def sum_near(value):
    axes = ("panel", "rhs")
    count = lax.axis_size(axes)
    one, two, three = (swapped(value, axes, s, count) for s in (1, 2, 3))
    return (value + one) + (two + three)


def from_far(value):
    axes = ("panel", "rhs")
    return swapped(value, axes, 4, lax.axis_size(axes))


def sum_far(value, meanwhile=None):
    other = from_far(value)
    if meanwhile is not None:
        other, _ = lax.optimization_barrier((other, meanwhile))
    return value + other


def by_stages():
    return lax.axis_size("panel") == 4 and lax.axis_size("rhs") == 2


def reduce_one(value):
    value = value + swapped(value, "coef", 1, 2)
    if not by_stages():
        value = lax.psum(value, ("panel", "rhs"))
        return value, value
    near = sum_near(value)
    return sum_far(near), near


def reduce_both(mine, mates, square):
    value = mine + swapped(mates, "coef", 1, 2)
    whole = square + swapped(square, "coef", 1, 2)
    if by_stages():
        rows = value.shape[0]
        value = sum_far(value, meanwhile=square)
        both = sum_near(jnp.concatenate([value, whole], axis=0))
        value, whole = both[:rows], both[rows:]
        terms = [whole, from_far(whole)]
    else:
        value, whole = lax.psum((value, whole), ("panel", "rhs"))
        terms = [whole]
    return [value, swapped(value, "coef", 1, 2)], terms


def right_side_parts(obs, mask, n, strip):
    def body(obs_hbm, mask_hbm, *refs):
        *outs, obs_ref, mask_ref, sems = refs
        copies = [
            pltpu.make_async_copy(mask_hbm, mask_ref, sems.at[0]),
            pltpu.make_async_copy(obs_hbm, obs_ref, sems.at[1]),
        ]
        for copy in copies:
            copy.start()
        for copy in copies:
            copy.wait()
        signs = (2 * mask_ref[...] - 1).astype(BF16)
        me = lax.axis_index("rhs")
        for s in range(n):
            place = pl.multiple_of(mate(me, s, n) * strip, strip)
            outs[s][...] = lax.dot_general(
                obs_ref[:, pl.ds(place, strip)],
                signs,
                (((0,), (0,)), ((), ())),
                preferred_element_type=F32,
            )

    *parts, token = call(
        body,
        [shape(strip)] * n,
        pltpu.with_memory_space_constraint(obs, pltpu.HBM),
        pltpu.with_memory_space_constraint(mask, pltpu.HBM),
        scratch=[
            pltpu.VMEM(obs.shape, BF16),
            pltpu.VMEM(mask.shape, mask.dtype),
            pltpu.SemaphoreType.DMA((2,)),
        ],
        any_args=2,
    )
    return parts, token


def sum_and_round(parts, token):
    strip = parts[0].shape[0]

    def body(*refs):
        *ins, out, low = refs
        total = ins[0][...]
        for ref in ins[1:]:
            total = total + ref[...]
        out[...] = total
        low[...] = total.astype(BF16)

    return call(
        body, [shape(strip), shape(strip, dtype=BF16)], *parts, after=[token]
    )


def retiled(blocks, links, count, token):
    rows, strip = blocks.shape[1], blocks.shape[3]
    tiles = strip // LANES

    def body(k_ref, out, sems):
        copies = []
        for i, link in enumerate(links()):
            for t in range(tiles):
                copy = pltpu.make_async_copy(
                    k_ref.at[link, :, :, pl.ds(t * LANES, LANES)], out.at[i, t], sems.at[i, t]
                )
                copy.start()
                copies.append(copy)
        for copy in copies:
            copy.wait()

    packed, token = call(
        body,
        [pltpu.VMEM((count, tiles, rows, 2, LANES), BF16)],
        blocks,
        scratch=[pltpu.SemaphoreType.DMA((count, tiles))],
        after=[token],
        any_args=1,
        any_outs=True,
    )
    return packed, token


def link_products(packed, pieces, acc, n, last, after=()):
    count, tiles, rows = packed.shape[:3]
    packed = packed.reshape(count, tiles, 2 * rows, LANES)
    packed = pltpu.with_memory_space_constraint(packed, pltpu.VMEM)
    strip = tiles * LANES
    block = min(512, 2 * rows)

    def body(*refs):
        k_ref, own_ref, other_ref = refs[:3]
        acc_ref = refs[3] if acc is not None else None
        outs = refs[3 + (acc is not None) : -3]
        weights, even_acc, odd_acc = refs[-3:]
        half = lax.axis_index("coef")
        weights[:, pl.ds(pl.multiple_of(half * LANES, LANES), LANES)] = own_ref[...]
        weights[:, pl.ds(pl.multiple_of((1 - half) * LANES, LANES), LANES)] = other_ref[...]
        for start in range(0, 2 * rows, block):
            here = slice(start, start + block)
            left = jnp.concatenate(
                [k_ref[i, t, here, :] for i in range(count) for t in range(tiles)], axis=1
            )
            right = jnp.concatenate([weights[...]] * count, axis=0)
            product = jnp.dot(left, right, preferred_element_type=F32)
            even_acc[here, :] = product[:, :LANES]
            odd_acc[here, :] = product[:, LANES:]
        me = lax.axis_index("rhs")
        size = rows // len(outs)
        for s in range(len(outs)):
            start = mate(me, s, n) * size if last else 0
            even = even_acc[pl.ds(2 * start, size, stride=2), :]
            odd = odd_acc[pl.ds(2 * start + 1, size, stride=2), :]
            total = even + odd
            if acc_ref is not None:
                total = total + acc_ref[pl.ds(start, size), :]
            outs[s][...] = total

    args = [packed, *pieces] + ([acc] if acc is not None else [])
    *result, token = call(
        body,
        [shape(rows // n)] * n if last else [shape(rows)],
        *args,
        scratch=[
            pltpu.VMEM((strip, 2 * LANES), BF16),
            pltpu.VMEM((2 * rows, LANES), F32),
            pltpu.VMEM((2 * rows, LANES), F32),
        ],
        after=after,
    )
    return (result if last else result[0]), token


def link_groups(links):
    reach = (links - 1) // 2
    panels = lax.axis_size("panel")
    groups = []
    if links == 2 * panels + 1 and panels & (panels - 1) == 0:
        for s in range(panels):

            def numbers(s=s):
                me = lax.axis_index("panel")
                start = lax.rem((me ^ s) - me + reach + panels, panels)
                return [start + panels * i for i in range(3 if s == 0 else 2)]

            bring = functools.partial(swapped, axis="panel", s=s, n=panels)
            groups.append((bring, numbers, 3 if s == 0 else 2))
        return groups
    offsets = {}
    for link in range(links):
        offsets.setdefault((link - reach) % panels, []).append(link)
    for o in sorted(offsets, key=lambda o: min(o, panels - o)):
        bring = functools.partial(shifted, axis="panel", by=o)
        groups.append((bring, functools.partial(list, offsets[o]), len(offsets[o])))
    return groups


def operate(packed, groups, low, direction, between):
    n = lax.axis_size("rhs")
    last = len(groups) - 1
    arrived = [low] + [bring(low) for bring, _, _ in groups[:0:-1]][::-1]
    directions = [direction] + [swapped(direction, "rhs", s, n) for s in range(1, n)]
    acc, after, tokens = None, (), []
    for place in range(last + 1):
        piece = arrived[place]
        if place:
            piece, held = lax.optimization_barrier((piece, tokens[0 if place < last else -1]))
            after = (*after, *held)
        pair = [piece, swapped(piece, "coef", 1, 2)]
        if place == 1:
            after = (*after, *directions[1:])
        acc, token = link_products(packed[place], pair, acc, n, place == last, after)
        after = ()
        if place == 0:
            after = (between(token),)
            tokens.append((token, *after))
        else:
            tokens.append((token,))
    return acc, directions


PACKED = LANES // 2 + SUB


def corner():
    row = lax.broadcasted_iota(jnp.int32, (LANES // 2, LANES), 0)
    lane = lax.broadcasted_iota(jnp.int32, (LANES // 2, LANES), 1)
    return row, lane, lane < LANES // 2


def packed_symmetric(matrix):
    half = LANES // 2
    row, lane, left = corner()
    top = matrix[:half]
    last = pltpu.roll(matrix[half:], half, 1)
    body = jnp.where(left & (lane > row), last, top)
    diagonal = jnp.sum(jnp.where(lane == row, last, 0.0), axis=0, keepdims=True)
    return jnp.concatenate([body, jnp.broadcast_to(diagonal, (SUB, LANES))], axis=0)


def unpacked_symmetric(rows):
    half = LANES // 2
    row, lane, left = corner()
    body, diagonal = rows[:half], rows[half : half + 1]
    top = jnp.where(left & (lane >= row), 0.0, body)
    last = jnp.where(left & (lane > row), body, 0.0)
    sides = jnp.concatenate([top, pltpu.roll(last, half, 1)], axis=0)
    top = jnp.where(lane == row, body, 0.0)
    last = jnp.where(lane == row, jnp.broadcast_to(diagonal, body.shape), 0.0)
    return sides + sides.T + jnp.concatenate([top, pltpu.roll(last, half, 1)], axis=0)


def symmetric(raw):
    return 0.5 * (raw + raw.T)


JOINT = PACKED + SUB + LANES


def linear_grams(parts, directions, before, beta, first, final):
    strip = parts[0].shape[0]
    n = len(parts)
    extra = [] if first or final else [*before, beta]
    rows = PACKED if final else JOINT // 2

    def body(*refs):
        images, ds = refs[:n], refs[n : 2 * n]
        rest = refs[2 * n : 2 * n + len(extra)]
        outs = refs[2 * n + len(extra) :]
        curve = cross = None
        for s in range(n):
            image, d = images[s][...], ds[s][...]
            term = mm(d, image, (0, 0))
            curve = term if s == 0 else curve + term
            if extra:
                r = d - mm(rest[s][...], rest[n][...])
                term = mm(r, image, (0, 0))
                cross = term if s == 0 else cross + term
        if final:
            outs[0][...] = packed_symmetric(symmetric(curve))
            return
        mine, mates, stacked = outs
        if first:
            r = ds[0][...]
            sym, whole = mm(r, r, (0, 0)), curve
        else:
            sym, whole = symmetric(curve), cross
        stacked[:PACKED] = packed_symmetric(sym)
        stacked[PACKED : PACKED + SUB] = jnp.zeros((SUB, LANES), F32)
        stacked[PACKED + SUB :] = whole
        half = lax.axis_index("coef")
        mine[...] = stacked[pl.ds(pl.multiple_of(half * rows, SUB), rows), :]
        mates[...] = stacked[pl.ds(pl.multiple_of((1 - half) * rows, SUB), rows), :]

    *pieces, _ = call(
        body,
        [shape(rows)] * (1 if final else 2),
        *parts,
        *directions,
        *extra,
        scratch=[] if final else [pltpu.VMEM((2 * rows, LANES), F32)],
    )
    return pieces


def square_gram(image_parts):
    strip = image_parts[0].shape[0]
    parts = len(image_parts)

    def body(*refs):
        ins, image_out, out = refs[:parts], refs[parts], refs[parts + 1]
        image = ins[0][...]
        for ref in ins[1:]:
            image = image + ref[...]
        image_out[...] = image
        out[...] = packed_symmetric(mm(image, image, (0, 0)))

    image, square, _ = call(
        body,
        [shape(strip), shape(PACKED)],
        *image_parts,
    )
    return image, square


def inverted(matrices, lane):
    strips = matrices[0].shape[0] // SUB
    many = len(matrices)
    place = lax.broadcasted_iota(jnp.int32, (SUB, LANES), 0)

    def lanes_of(value, at):
        return jnp.broadcast_to(value[:, at : at + 1], (SUB, LANES))

    def rows_of(value):
        return [jnp.broadcast_to(value[i : i + 1], (SUB, LANES)) for i in range(SUB)]

    def updated(row, rows):
        factors = [lanes_of(row, i) for i in range(SUB)]
        for factor, other in zip(factors, rows):
            row = row - factor * other
        return row

    def step(_, carry):
        held = [list(carry[m * strips : (m + 1) * strips]) for m in range(many)]
        rows = [rows_of(value) for value in carry[many * strips :]]
        now = []
        for a, last in zip(held, rows):
            a[1] = updated(a[1], last)
            now.append([a[1], *(lanes_of(a[1], SUB + i) for i in range(SUB))])
        for i in range(SUB):
            here = place == i
            for index, values in enumerate(now):
                column = values[1 + i]
                inverse = 1.0 / column[i : i + 1]

                def pivot(value):
                    row = value[i : i + 1] * inverse
                    return jnp.where(here, row, value - column * row)

                now[index] = [
                    pivot(value) if at < 1 or at > 1 + i else value
                    for at, value in enumerate(values)
                ]
            if 2 + i < strips:
                for a, last in zip(held, rows):
                    a[2 + i] = updated(a[2 + i], last)
        turned = []
        for a, values in zip(held, now):
            a[1] = values[0]
            turned.append([pltpu.roll(row, LANES - SUB, 1) for row in a[1:] + a[:1]])
        return tuple([row for a in turned for row in a] + [a[0] for a in turned])

    start = []
    for value in matrices:
        value = pltpu.roll(value, (SUB - lane) % LANES, 1)
        a = [value[SUB * k : SUB * (k + 1)] for k in range(strips)]
        start += a[-1:] + a[:-1]
    start += [jnp.zeros((SUB, LANES), F32)] * many
    carry = lax.fori_loop(0, strips, step, tuple(start))
    found = []
    for m in range(many):
        a = list(carry[m * strips : (m + 1) * strips])
        rows = rows_of(carry[many * strips + m])
        a = [updated(row, rows) for row in a[1:]] + a[:1]
        found.append(pltpu.roll(jnp.concatenate(a, axis=0), LANES - SUB, 1))
    return found


def eliminated(*systems):
    half = LANES // 2
    row = lax.broadcasted_iota(jnp.int32, (half, LANES), 0)
    lane = lax.broadcasted_iota(jnp.int32, (half, LANES), 1)
    left = lane < half
    first = inverted(
        [
            jnp.where(left, matrix[:half], (lane - half == row).astype(F32))
            for matrix, _ in systems
        ],
        0,
    )
    tops, lasts = [], []
    for (matrix, sides), value in zip(systems, first):
        top = mm(value[:, :half], jnp.concatenate([matrix[:half], sides[:half]], axis=1))
        low = jnp.concatenate([matrix[half:], sides[half:]], axis=1)
        tops.append(top)
        lasts.append(low - mm(matrix[half:, :half], top))
    second = inverted(
        [jnp.where(left, (lane == row).astype(F32), last[:, :LANES]) for last in lasts], half
    )
    found = []
    for top, last, value in zip(tops, lasts, second):
        low = mm(value[:, :half], last[:, LANES:])
        high = top[:, LANES:] - mm(
            top[:, :LANES], jnp.concatenate([jnp.zeros_like(low), low], axis=0)
        )
        found.append(jnp.concatenate([high, low], axis=0))
    return found


def identity():
    return (
        lax.broadcasted_iota(jnp.int32, (LANES, LANES), 0)
        == lax.broadcasted_iota(jnp.int32, (LANES, LANES), 1)
    ).astype(F32)


def stepped(solution, direction, alpha, token):
    fields = [direction, alpha] + ([] if solution is None else [solution])

    def body(d, a, *refs):
        change = mm(d[...], a[...])
        refs[-1][...] = change if solution is None else refs[0][...] + change

    return call(body, [shape(direction.shape[0])], *fields, after=[token])


def last_alpha(small, gram):
    def body(small, g, out):
        out[...] = eliminated((unpacked_symmetric(small[...]), g[...]))[0]

    return call(body, [shape(LANES)], small, gram)[0]


def finish(alpha, residual, direction, solution, image):
    strip = residual.shape[0]

    def body(a, r, d, s, *refs):
        *images, out, new_r = refs
        image = images[0][...]
        for ref in images[1:]:
            image = image + ref[...]
        out[...] = s[...] + mm(d[...], a[...])
        new_r[...] = r[...] - mm(image, a[...])

    return call(
        body,
        [shape(strip), shape(strip)],
        alpha,
        residual,
        direction,
        solution,
        *image,
    )[:-1]


def advance(pieces, gram, residual, image):
    strip = residual.shape[0]
    rows = pieces[0].shape[0]
    first = gram is None
    fields = [*pieces, residual, image] + ([] if first else [gram])

    def body(*refs):
        mine, mates, r, image, *refs = refs
        *refs, raw = refs
        half = lax.axis_index("coef")
        raw[pl.ds(pl.multiple_of(half * rows, SUB), rows), :] = mine[...]
        raw[pl.ds(pl.multiple_of((1 - half) * rows, SUB), rows), :] = mates[...]
        sym, whole = unpacked_symmetric(raw[:PACKED, :]), raw[PACKED + SUB :, :]
        *refs, new_r, alpha_out, partial, inverse_out = refs
        g = sym if first else refs[0][...]
        curvature = symmetric(whole) if first else sym
        alpha, inverse_out[...] = eliminated((curvature, g), (g, identity()))
        new_r[...] = r[...] - mm(image[...], alpha)
        shared = mm(whole, alpha)
        alpha_out[...] = alpha
        partial[...] = g - (shared + shared.T)

    return call(
        body,
        [shape(strip)] + [shape(LANES)] * 3,
        *fields,
        scratch=[pltpu.VMEM((2 * rows, LANES), F32)],
    )[:-1]


def turn(square, alpha, partial, inverse, residual, direction):
    strip = residual.shape[0]

    def body(alpha, partial, inverse, r, d, *refs):
        *terms, new_d, low, beta_out, gram_out = refs
        square = terms[0][...]
        for ref in terms[1:]:
            square = square + ref[...]
        a = alpha[...]
        following = partial[...] + mm(a, mm(unpacked_symmetric(square), a), (0, 0))
        beta = mm(inverse[...], following)
        value = r[...] + mm(d[...], beta)
        low[...] = value.astype(BF16)
        new_d[...] = value
        beta_out[...] = beta
        gram_out[...] = following

    return call(
        body,
        [shape(strip), shape(strip, dtype=BF16), shape(LANES), shape(LANES)],
        alpha,
        partial,
        inverse,
        residual,
        direction,
        *square,
    )[:-1]


def shards(couplings, observations, replicate_mask):
    links, rows = couplings.shape[1], couplings.shape[3]
    strip = couplings.shape[6]
    blocks = couplings.reshape(links, rows, couplings.shape[4], strip)
    blocks = pltpu.with_memory_space_constraint(blocks, pltpu.HBM)
    n = lax.axis_size("rhs")
    obs_matrix = observations.reshape(observations.shape[0], rows)
    parts, token = right_side_parts(obs_matrix, replicate_mask, n, strip)
    own = [parts[0]] + [swapped(parts[s], "rhs", s, n) for s in range(1, n)]
    groups = link_groups(links)
    packed = []
    for _, numbers, count in groups[:2]:
        value, token = retiled(blocks, numbers, count, token)
        packed.append(value)
    residual, low, token = sum_and_round(own, token)
    for _, numbers, count in groups[2:]:
        value, token = retiled(blocks, numbers, count, token)
        packed.append(value)
    retile_token = token
    direction = residual
    solution = gram = beta = before = alpha = None
    for step in range(ITERS):
        first, final = step == 0, step + 1 == ITERS
        state = [solution]

        def between(token):
            if first:
                return retile_token
            state[0], token = stepped(solution, before[0], alpha, token)
            return token

        parts, directions = operate(packed, groups, low, direction, between)
        (solution,) = state
        linear = linear_grams(parts, directions, before, beta, first, final)
        if final:
            small, near = reduce_one(*linear)
            parts[1:], _ = lax.optimization_barrier((parts[1:], near))
        image_parts = [parts[0]] + [swapped(parts[s], "rhs", s, n) for s in range(1, n)]
        if final:
            alpha = last_alpha(small, gram)
            solution, residual = finish(alpha, residual, direction, solution, image_parts)
            break
        image, square = square_gram(image_parts)
        linear, square = reduce_both(*linear, square)
        residual, alpha, partial, inverse = advance(linear, gram, residual, image)
        square[1:], alpha = lax.optimization_barrier((square[1:], alpha))
        before = directions
        direction, low, beta, gram = turn(
            square, alpha, partial, inverse, residual, direction
        )
    shape_out = (1, 1, strip, LANES)
    return (solution.reshape(shape_out), residual.reshape(shape_out))


def solution(mesh):
    placed = (
        P("panel", None, "coef", None, None, "rhs", None),
        P(("groups", "rhs"), "panel", "coef", None),
        P(("groups", "rhs"), None),
    )
    return jax.shard_map(
        shards,
        mesh=mesh,
        in_specs=placed,
        out_specs=(
            P(("groups", "panel"), "coef", "rhs", None),
            P(("groups", "panel"), "coef", "rhs", None),
        ),
        check_vma=False,
    )
```

```python
import functools

import jax
import jax.numpy as jnp
from jax import lax
from jax.experimental import pallas as pl
from jax.experimental.pallas import tpu as pltpu
from jax.sharding import PartitionSpec as P

ITERS = 3
LANES = 128
SUB = 8
VMEM_LIMIT = 14 * 2**20
F32 = jnp.float32
BF16 = jnp.bfloat16
VMEM = pl.BlockSpec(memory_space=pltpu.VMEM)
ANY = pl.BlockSpec(memory_space=pl.ANY)
HBM = pl.BlockSpec(memory_space=pltpu.HBM)


def mm(a, b, dims=(1, 0)):
    return lax.dot_general(
        a,
        b,
        (((dims[0],), (dims[1],)), ((), ())),
        precision=lax.Precision.HIGHEST,
        preferred_element_type=F32,
    )


def call(body, outs, *args, scratch=(), after=(), any_args=0, any_outs=False):
    inputs, outputs, waits = len(args), len(outs), len(after)

    def ordered(*refs):
        token = refs[inputs + waits + outputs]
        token[...] = jnp.zeros_like(token)
        body(
            *refs[:inputs],
            *refs[inputs + waits : inputs + waits + outputs],
            *refs[inputs + waits + outputs + 1 :],
        )

    return pl.pallas_call(
        ordered,
        out_shape=list(outs) + [shape(SUB)],
        in_specs=[HBM] * any_args + [VMEM] * (inputs - any_args) + [ANY] * waits,
        out_specs=[ANY if any_outs else VMEM] * outputs + [VMEM],
        scratch_shapes=list(scratch),
        cost_estimate=pl.CostEstimate(flops=1, bytes_accessed=1, transcendentals=0),
        compiler_params=pltpu.CompilerParams(vmem_limit_bytes=VMEM_LIMIT),
    )(*args, *after)


def shape(rows, cols=LANES, dtype=F32):
    return jax.ShapeDtypeStruct((rows, cols), dtype)


def permute(value, axis, pairs):
    return lax.ppermute(value, axis, pairs)


def shifted(value, axis, by):
    n = lax.axis_size(axis)
    return permute(value, axis, [((i + by) % n, i) for i in range(n)])


def mate(i, s, n):
    return i ^ s if n & (n - 1) == 0 else (s - i) % n


def swapped(value, axis, s, n):
    return permute(value, axis, [(mate(i, s, n), i) for i in range(n)])


def sum_near(value):
    axes = ("panel", "rhs")
    count = lax.axis_size(axes)
    one, two, three = (swapped(value, axes, s, count) for s in (1, 2, 3))
    return (value + one) + (two + three)


def from_far(value):
    axes = ("panel", "rhs")
    return swapped(value, axes, 4, lax.axis_size(axes))


def sum_far(value, meanwhile=None):
    other = from_far(value)
    if meanwhile is not None:
        other, _ = lax.optimization_barrier((other, meanwhile))
    return value + other


def by_stages():
    return lax.axis_size("panel") == 4 and lax.axis_size("rhs") == 2


def reduce_one(value):
    value = value + swapped(value, "coef", 1, 2)
    if not by_stages():
        value = lax.psum(value, ("panel", "rhs"))
        return value, value
    near = sum_near(value)
    return sum_far(near), near


def reduce_both(mine, mates, square):
    value = mine + swapped(mates, "coef", 1, 2)
    whole = square + swapped(square, "coef", 1, 2)
    if by_stages():
        rows = value.shape[0]
        value = sum_far(value, meanwhile=square)
        both = sum_near(jnp.concatenate([value, whole], axis=0))
        value, whole = both[:rows], both[rows:]
        terms = [whole, from_far(whole)]
    else:
        value, whole = lax.psum((value, whole), ("panel", "rhs"))
        terms = [whole]
    return [value, swapped(value, "coef", 1, 2)], terms


def right_side_parts(obs, mask, n, strip):
    def body(obs_hbm, mask_hbm, *refs):
        *outs, obs_ref, mask_ref, sems = refs
        copies = [
            pltpu.make_async_copy(mask_hbm, mask_ref, sems.at[0]),
            pltpu.make_async_copy(obs_hbm, obs_ref, sems.at[1]),
        ]
        for copy in copies:
            copy.start()
        for copy in copies:
            copy.wait()
        signs = (2 * mask_ref[...] - 1).astype(BF16)
        me = lax.axis_index("rhs")
        for s in range(n):
            place = pl.multiple_of(mate(me, s, n) * strip, strip)
            outs[s][...] = lax.dot_general(
                obs_ref[:, pl.ds(place, strip)],
                signs,
                (((0,), (0,)), ((), ())),
                preferred_element_type=F32,
            )

    *parts, token = call(
        body,
        [shape(strip)] * n,
        pltpu.with_memory_space_constraint(obs, pltpu.HBM),
        pltpu.with_memory_space_constraint(mask, pltpu.HBM),
        scratch=[
            pltpu.VMEM(obs.shape, BF16),
            pltpu.VMEM(mask.shape, mask.dtype),
            pltpu.SemaphoreType.DMA((2,)),
        ],
        any_args=2,
    )
    return parts, token


def sum_and_round(parts, token):
    strip = parts[0].shape[0]

    def body(*refs):
        *ins, out, low = refs
        total = ins[0][...]
        for ref in ins[1:]:
            total = total + ref[...]
        out[...] = total
        low[...] = total.astype(BF16)

    return call(
        body, [shape(strip), shape(strip, dtype=BF16)], *parts, after=[token]
    )


def retiled(blocks, links, count, token):
    rows, strip = blocks.shape[1], blocks.shape[3]
    tiles = strip // LANES

    def body(k_ref, out, sems):
        copies = []
        for i, link in enumerate(links()):
            for t in range(tiles):
                copy = pltpu.make_async_copy(
                    k_ref.at[link, :, :, pl.ds(t * LANES, LANES)], out.at[i, t], sems.at[i, t]
                )
                copy.start()
                copies.append(copy)
        for copy in copies:
            copy.wait()

    packed, token = call(
        body,
        [pltpu.VMEM((count, tiles, rows, 2, LANES), BF16)],
        blocks,
        scratch=[pltpu.SemaphoreType.DMA((count, tiles))],
        after=[token],
        any_args=1,
        any_outs=True,
    )
    return packed, token


def link_products(packed, pieces, acc, n, last, after=()):
    tiles, rows = packed[0].shape[1:3]
    counts = [value.shape[0] for value in packed]
    many = len(packed)
    packed = [
        pltpu.with_memory_space_constraint(
            value.reshape(value.shape[0], tiles, 2 * rows, LANES), pltpu.VMEM
        )
        for value in packed
    ]
    strip = tiles * LANES
    block = min(512, 2 * rows)

    def body(*refs):
        k_refs, piece_refs = refs[:many], refs[many : 3 * many]
        acc_ref = refs[3 * many] if acc is not None else None
        outs = refs[3 * many + (acc is not None) : -3]
        weights, even_acc, odd_acc = refs[-3:]
        half = lax.axis_index("coef")
        own = pl.ds(pl.multiple_of(half * LANES, LANES), LANES)
        other = pl.ds(pl.multiple_of((1 - half) * LANES, LANES), LANES)
        at = 0
        for g in range(many):
            for _ in range(counts[g]):
                weights[at : at + strip, own] = piece_refs[2 * g][...]
                weights[at : at + strip, other] = piece_refs[2 * g + 1][...]
                at += strip
        for start in range(0, 2 * rows, block):
            here = slice(start, start + block)
            left = jnp.concatenate(
                [
                    k_refs[g][i, t, here, :]
                    for g in range(many)
                    for i in range(counts[g])
                    for t in range(tiles)
                ],
                axis=1,
            )
            product = jnp.dot(left, weights[...], preferred_element_type=F32)
            even_acc[here, :] = product[:, :LANES]
            odd_acc[here, :] = product[:, LANES:]
        me = lax.axis_index("rhs")
        size = rows // len(outs)
        for s in range(len(outs)):
            start = mate(me, s, n) * size if last else 0
            even = even_acc[pl.ds(2 * start, size, stride=2), :]
            odd = odd_acc[pl.ds(2 * start + 1, size, stride=2), :]
            total = even + odd
            if acc_ref is not None:
                total = total + acc_ref[pl.ds(start, size), :]
            outs[s][...] = total

    args = [*packed, *(value for pair in pieces for value in pair)]
    args += [acc] if acc is not None else []
    *result, token = call(
        body,
        [shape(rows // n)] * n if last else [shape(rows)],
        *args,
        scratch=[
            pltpu.VMEM((sum(counts) * strip, 2 * LANES), BF16),
            pltpu.VMEM((2 * rows, LANES), F32),
            pltpu.VMEM((2 * rows, LANES), F32),
        ],
        after=after,
    )
    return (result if last else result[0]), token


def link_groups(links):
    reach = (links - 1) // 2
    panels = lax.axis_size("panel")
    groups = []
    if links == 2 * panels + 1 and panels & (panels - 1) == 0:
        for s in range(panels):

            def numbers(s=s):
                me = lax.axis_index("panel")
                start = lax.rem((me ^ s) - me + reach + panels, panels)
                return [start + panels * i for i in range(3 if s == 0 else 2)]

            bring = functools.partial(swapped, axis="panel", s=s, n=panels)
            groups.append((bring, numbers, 3 if s == 0 else 2))
        return groups
    offsets = {}
    for link in range(links):
        offsets.setdefault((link - reach) % panels, []).append(link)
    for o in sorted(offsets, key=lambda o: min(o, panels - o)):
        bring = functools.partial(shifted, axis="panel", by=o)
        groups.append((bring, functools.partial(list, offsets[o]), len(offsets[o])))
    return groups


def operate(packed, groups, low, direction, between):
    n = lax.axis_size("rhs")
    last = len(groups) - 1
    arrived = [low] + [bring(low) for bring, _, _ in groups[:0:-1]][::-1]
    directions = [direction] + [swapped(direction, "rhs", s, n) for s in range(1, n)]
    pairs = [[low, swapped(low, "coef", 1, 2)]]
    acc, token = link_products(packed[:1], pairs, None, n, last == 0)
    after = (token, between(token))
    for piece in arrived[1:]:
        piece, _ = lax.optimization_barrier((piece, after))
        pairs.append([piece, swapped(piece, "coef", 1, 2)])
    after = (*after, *directions[1:])
    if last > 1:
        acc, _ = link_products(packed[1:last], pairs[1:last], acc, n, False, after)
    if last:
        acc, _ = link_products(packed[last:], pairs[last:], acc, n, True, after)
    return acc, directions


PACKED = LANES // 2 + SUB


def corner():
    row = lax.broadcasted_iota(jnp.int32, (LANES // 2, LANES), 0)
    lane = lax.broadcasted_iota(jnp.int32, (LANES // 2, LANES), 1)
    return row, lane, lane < LANES // 2


def packed_symmetric(matrix):
    half = LANES // 2
    row, lane, left = corner()
    top = matrix[:half]
    last = pltpu.roll(matrix[half:], half, 1)
    body = jnp.where(left & (lane > row), last, top)
    diagonal = jnp.sum(jnp.where(lane == row, last, 0.0), axis=0, keepdims=True)
    return jnp.concatenate([body, jnp.broadcast_to(diagonal, (SUB, LANES))], axis=0)


def unpacked_symmetric(rows):
    half = LANES // 2
    row, lane, left = corner()
    body, diagonal = rows[:half], rows[half : half + 1]
    top = jnp.where(left & (lane >= row), 0.0, body)
    last = jnp.where(left & (lane > row), body, 0.0)
    sides = jnp.concatenate([top, pltpu.roll(last, half, 1)], axis=0)
    top = jnp.where(lane == row, body, 0.0)
    last = jnp.where(lane == row, jnp.broadcast_to(diagonal, body.shape), 0.0)
    return sides + sides.T + jnp.concatenate([top, pltpu.roll(last, half, 1)], axis=0)


def symmetric(raw):
    return 0.5 * (raw + raw.T)


JOINT = PACKED + SUB + LANES


def linear_grams(parts, directions, before, beta, first, final):
    strip = parts[0].shape[0]
    n = len(parts)
    extra = [] if first or final else [*before, beta]
    rows = PACKED if final else JOINT // 2

    def body(*refs):
        images, ds = refs[:n], refs[n : 2 * n]
        rest = refs[2 * n : 2 * n + len(extra)]
        outs = refs[2 * n + len(extra) :]
        curve = cross = None
        for s in range(n):
            image, d = images[s][...], ds[s][...]
            term = mm(d, image, (0, 0))
            curve = term if s == 0 else curve + term
            if extra:
                r = d - mm(rest[s][...], rest[n][...])
                term = mm(r, image, (0, 0))
                cross = term if s == 0 else cross + term
        if final:
            outs[0][...] = packed_symmetric(symmetric(curve))
            return
        mine, mates, stacked = outs
        if first:
            r = ds[0][...]
            sym, whole = mm(r, r, (0, 0)), curve
        else:
            sym, whole = symmetric(curve), cross
        stacked[:PACKED] = packed_symmetric(sym)
        stacked[PACKED : PACKED + SUB] = jnp.zeros((SUB, LANES), F32)
        stacked[PACKED + SUB :] = whole
        half = lax.axis_index("coef")
        mine[...] = stacked[pl.ds(pl.multiple_of(half * rows, SUB), rows), :]
        mates[...] = stacked[pl.ds(pl.multiple_of((1 - half) * rows, SUB), rows), :]

    *pieces, _ = call(
        body,
        [shape(rows)] * (1 if final else 2),
        *parts,
        *directions,
        *extra,
        scratch=[] if final else [pltpu.VMEM((2 * rows, LANES), F32)],
    )
    return pieces


def square_gram(image_parts):
    strip = image_parts[0].shape[0]
    parts = len(image_parts)

    def body(*refs):
        ins, image_out, out = refs[:parts], refs[parts], refs[parts + 1]
        image = ins[0][...]
        for ref in ins[1:]:
            image = image + ref[...]
        image_out[...] = image
        out[...] = packed_symmetric(mm(image, image, (0, 0)))

    image, square, _ = call(
        body,
        [shape(strip), shape(PACKED)],
        *image_parts,
    )
    return image, square


def inverted(matrices, lane):
    strips = matrices[0].shape[0] // SUB
    place = lax.broadcasted_iota(jnp.int32, (SUB, LANES), 0)
    held = [[value[SUB * k : SUB * (k + 1)] for k in range(strips)] for value in matrices]

    def lanes_of(value, at):
        return jnp.broadcast_to(value[:, at : at + 1], (SUB, LANES))

    def rows_of(value):
        return [jnp.broadcast_to(value[i : i + 1], (SUB, LANES)) for i in range(SUB)]

    def update(k, j, spread):
        for a, rows in zip(held, spread):
            row = a[k]
            for i in range(SUB):
                row = row - lanes_of(a[k], lane + SUB * j + i) * rows[i]
            a[k] = row

    for j in range(strips):
        if j:
            spread = [rows_of(a[j - 1]) for a in held]
            update(j, j - 1, spread)
        waiting = [k for k in range(strips) if j and k not in (j, j - 1)]
        now = [
            [a[j], *(lanes_of(a[j], lane + SUB * j + i) for i in range(SUB))] for a in held
        ]
        for i in range(SUB):
            here = place == i
            for index, values in enumerate(now):
                column = values[1 + i]
                inverse = 1.0 / column[i : i + 1]

                def step(value):
                    row = value[i : i + 1] * inverse
                    return jnp.where(here, row, value - column * row)

                now[index] = [
                    step(value) if at < 1 or at > 1 + i else value
                    for at, value in enumerate(values)
                ]
            for k in waiting[i : i + 1]:
                update(k, j - 1, spread)
        for a, values in zip(held, now):
            a[j] = values[0]
    spread = [rows_of(a[-1]) for a in held]
    for k in range(strips - 1):
        update(k, strips - 1, spread)
    return [jnp.concatenate(a, axis=0) for a in held]


def eliminated(*systems):
    half = LANES // 2
    row = lax.broadcasted_iota(jnp.int32, (half, LANES), 0)
    lane = lax.broadcasted_iota(jnp.int32, (half, LANES), 1)
    left = lane < half
    first = inverted(
        [
            jnp.where(left, matrix[:half], (lane - half == row).astype(F32))
            for matrix, _ in systems
        ],
        0,
    )
    tops, lasts = [], []
    for (matrix, sides), value in zip(systems, first):
        value = pltpu.roll(value, half, 1)[:, :half]
        top = mm(value, jnp.concatenate([matrix[:half], sides[:half]], axis=1))
        low = jnp.concatenate([matrix[half:], sides[half:]], axis=1)
        tops.append(top)
        lasts.append(low - mm(matrix[half:, :half], top))
    second = inverted(
        [jnp.where(left, (lane == row).astype(F32), last[:, :LANES]) for last in lasts], half
    )
    found = []
    for top, last, value in zip(tops, lasts, second):
        low = mm(value[:, :half], last[:, LANES:])
        high = top[:, LANES:] - mm(
            top[:, :LANES], jnp.concatenate([jnp.zeros_like(low), low], axis=0)
        )
        found.append(jnp.concatenate([high, low], axis=0))
    return found


def eliminated_alone(matrix, sides):
    n = matrix.shape[0]
    strips = n // SUB
    place = lax.broadcasted_iota(jnp.int32, (SUB, LANES), 0)

    def cut(value):
        return [value[SUB * k : SUB * (k + 1)] for k in range(strips)]

    def lanes_of(value, lane):
        return jnp.broadcast_to(value[:, lane : lane + 1], (SUB, LANES))

    held = [(cut(matrix), cut(sides))]

    def rows_of(value):
        return [jnp.broadcast_to(value[i : i + 1], (SUB, LANES)) for i in range(SUB)]

    def update(k, j, spread):
        for (a, b), (rows_a, rows_b) in zip(held, spread):
            row_a, row_b = a[k], b[k]
            for i in range(SUB):
                factor = lanes_of(a[k], SUB * j + i)
                row_a = row_a - factor * rows_a[i]
                row_b = row_b - factor * rows_b[i]
            a[k], b[k] = row_a, row_b

    for j in range(strips):
        if j:
            spread = [(rows_of(a[j - 1]), rows_of(b[j - 1])) for a, b in held]
            update(j, j - 1, spread)
        waiting = [k for k in range(strips) if j and k not in (j, j - 1)]
        now = [
            [a[j], b[j], *(lanes_of(a[j], SUB * j + i) for i in range(SUB))] for a, b in held
        ]
        for i in range(SUB):
            here = place == i
            for index, values in enumerate(now):
                column = values[2 + i]
                inverse = 1.0 / column[i : i + 1]

                def step(value):
                    row = value[i : i + 1] * inverse
                    return jnp.where(here, row, value - column * row)

                now[index] = [
                    step(value) if place_of < 2 or place_of > 2 + i else value
                    for place_of, value in enumerate(values)
                ]
            for k in waiting[2 * i : 2 * i + 2]:
                update(k, j - 1, spread)
        for (a, b), values in zip(held, now):
            a[j], b[j] = values[:2]
    spread = [(rows_of(a[-1]), rows_of(b[-1])) for a, b in held]
    for k in range(strips - 1):
        update(k, strips - 1, spread)
    return jnp.concatenate(held[0][1], axis=0)


def identity():
    return (
        lax.broadcasted_iota(jnp.int32, (LANES, LANES), 0)
        == lax.broadcasted_iota(jnp.int32, (LANES, LANES), 1)
    ).astype(F32)


def stepped(solution, direction, alpha, token):
    fields = [direction, alpha] + ([] if solution is None else [solution])

    def body(d, a, *refs):
        change = mm(d[...], a[...])
        refs[-1][...] = change if solution is None else refs[0][...] + change

    return call(body, [shape(direction.shape[0])], *fields, after=[token])


def finish(small, gram, residual, direction, solution, image):
    strip = residual.shape[0]

    def body(small, g, r, d, s, *refs):
        *images, out, new_r = refs
        alpha = eliminated_alone(unpacked_symmetric(small[...]), g[...])
        image = images[0][...]
        for ref in images[1:]:
            image = image + ref[...]
        out[...] = s[...] + mm(d[...], alpha)
        new_r[...] = r[...] - mm(image, alpha)

    return call(
        body,
        [shape(strip), shape(strip)],
        small,
        gram,
        residual,
        direction,
        solution,
        *image,
    )[:-1]


def advance(pieces, gram, residual, image):
    strip = residual.shape[0]
    rows = pieces[0].shape[0]
    first = gram is None
    fields = [*pieces, residual, image] + ([] if first else [gram])

    def body(*refs):
        mine, mates, r, image, *refs = refs
        *refs, raw = refs
        half = lax.axis_index("coef")
        raw[pl.ds(pl.multiple_of(half * rows, SUB), rows), :] = mine[...]
        raw[pl.ds(pl.multiple_of((1 - half) * rows, SUB), rows), :] = mates[...]
        sym, whole = unpacked_symmetric(raw[:PACKED, :]), raw[PACKED + SUB :, :]
        *refs, new_r, alpha_out, partial, inverse_out = refs
        g = sym if first else refs[0][...]
        curvature = symmetric(whole) if first else sym
        alpha, inverse_out[...] = eliminated((curvature, g), (g, identity()))
        new_r[...] = r[...] - mm(image[...], alpha)
        shared = mm(whole, alpha)
        alpha_out[...] = alpha
        partial[...] = g - (shared + shared.T)

    return call(
        body,
        [shape(strip)] + [shape(LANES)] * 3,
        *fields,
        scratch=[pltpu.VMEM((2 * rows, LANES), F32)],
    )[:-1]


def turn(square, alpha, partial, inverse, residual, direction):
    strip = residual.shape[0]

    def body(alpha, partial, inverse, r, d, *refs):
        *terms, new_d, low, beta_out, gram_out = refs
        square = terms[0][...]
        for ref in terms[1:]:
            square = square + ref[...]
        a = alpha[...]
        following = partial[...] + mm(a, mm(unpacked_symmetric(square), a), (0, 0))
        beta = mm(inverse[...], following)
        value = r[...] + mm(d[...], beta)
        low[...] = value.astype(BF16)
        new_d[...] = value
        beta_out[...] = beta
        gram_out[...] = following

    return call(
        body,
        [shape(strip), shape(strip, dtype=BF16), shape(LANES), shape(LANES)],
        alpha,
        partial,
        inverse,
        residual,
        direction,
        *square,
    )[:-1]


def shards(couplings, observations, replicate_mask):
    links, rows = couplings.shape[1], couplings.shape[3]
    strip = couplings.shape[6]
    blocks = couplings.reshape(links, rows, couplings.shape[4], strip)
    blocks = pltpu.with_memory_space_constraint(blocks, pltpu.HBM)
    n = lax.axis_size("rhs")
    obs_matrix = observations.reshape(observations.shape[0], rows)
    parts, token = right_side_parts(obs_matrix, replicate_mask, n, strip)
    own = [parts[0]] + [swapped(parts[s], "rhs", s, n) for s in range(1, n)]
    groups = link_groups(links)
    packed = []
    for _, numbers, count in groups[:2]:
        value, token = retiled(blocks, numbers, count, token)
        packed.append(value)
    residual, low, token = sum_and_round(own, token)
    for _, numbers, count in groups[2:]:
        value, token = retiled(blocks, numbers, count, token)
        packed.append(value)
    retile_token = token
    direction = residual
    solution = gram = beta = before = alpha = None
    for step in range(ITERS):
        first, final = step == 0, step + 1 == ITERS
        state = [solution]

        def between(token):
            if first:
                return retile_token
            state[0], token = stepped(solution, before[0], alpha, token)
            return token

        parts, directions = operate(packed, groups, low, direction, between)
        (solution,) = state
        linear = linear_grams(parts, directions, before, beta, first, final)
        if final:
            small, near = reduce_one(*linear)
            parts[1:], _ = lax.optimization_barrier((parts[1:], near))
        image_parts = [parts[0]] + [swapped(parts[s], "rhs", s, n) for s in range(1, n)]
        if final:
            solution, residual = finish(
                small, gram, residual, direction, solution, image_parts
            )
            break
        image, square = square_gram(image_parts)
        linear, square = reduce_both(*linear, square)
        residual, alpha, partial, inverse = advance(linear, gram, residual, image)
        square[1:], alpha = lax.optimization_barrier((square[1:], alpha))
        before = directions
        direction, low, beta, gram = turn(
            square, alpha, partial, inverse, residual, direction
        )
    shape_out = (1, 1, strip, LANES)
    return (solution.reshape(shape_out), residual.reshape(shape_out))


def solution(mesh):
    placed = (
        P("panel", None, "coef", None, None, "rhs", None),
        P(("groups", "rhs"), "panel", "coef", None),
        P(("groups", "rhs"), None),
    )
    return jax.shard_map(
        shards,
        mesh=mesh,
        in_specs=placed,
        out_specs=(
            P(("groups", "panel"), "coef", "rhs", None),
            P(("groups", "panel"), "coef", "rhs", None),
        ),
        check_vma=False,
    )
```

```python
import functools

import jax
import jax.numpy as jnp
from jax import lax
from jax.experimental import pallas as pl
from jax.experimental.pallas import tpu as pltpu
from jax.sharding import PartitionSpec as P

ITERS = 3
LANES = 128
SUB = 8
VMEM_LIMIT = 14 * 2**20
F32 = jnp.float32
BF16 = jnp.bfloat16
VMEM = pl.BlockSpec(memory_space=pltpu.VMEM)
ANY = pl.BlockSpec(memory_space=pl.ANY)
HBM = pl.BlockSpec(memory_space=pltpu.HBM)


def mm(a, b, dims=(1, 0)):
    return lax.dot_general(
        a,
        b,
        (((dims[0],), (dims[1],)), ((), ())),
        precision=lax.Precision.HIGHEST,
        preferred_element_type=F32,
    )


def call(body, outs, *args, scratch=(), after=(), any_args=0, any_outs=False):
    inputs, outputs, waits = len(args), len(outs), len(after)

    def ordered(*refs):
        token = refs[inputs + waits + outputs]
        token[...] = jnp.zeros_like(token)
        body(
            *refs[:inputs],
            *refs[inputs + waits : inputs + waits + outputs],
            *refs[inputs + waits + outputs + 1 :],
        )

    return pl.pallas_call(
        ordered,
        out_shape=list(outs) + [shape(SUB)],
        in_specs=[HBM] * any_args + [VMEM] * (inputs - any_args) + [ANY] * waits,
        out_specs=[ANY if any_outs else VMEM] * outputs + [VMEM],
        scratch_shapes=list(scratch),
        cost_estimate=pl.CostEstimate(flops=1, bytes_accessed=1, transcendentals=0),
        compiler_params=pltpu.CompilerParams(vmem_limit_bytes=VMEM_LIMIT),
    )(*args, *after)


def shape(rows, cols=LANES, dtype=F32):
    return jax.ShapeDtypeStruct((rows, cols), dtype)


def permute(value, axis, pairs):
    return lax.ppermute(value, axis, pairs)


def shifted(value, axis, by):
    n = lax.axis_size(axis)
    return permute(value, axis, [((i + by) % n, i) for i in range(n)])


def mate(i, s, n):
    return i ^ s if n & (n - 1) == 0 else (s - i) % n


def swapped(value, axis, s, n):
    return permute(value, axis, [(mate(i, s, n), i) for i in range(n)])


def sum_near(value):
    axes = ("panel", "rhs")
    count = lax.axis_size(axes)
    one, two, three = (swapped(value, axes, s, count) for s in (1, 2, 3))
    return (value + one) + (two + three)


def from_far(value):
    axes = ("panel", "rhs")
    return swapped(value, axes, 4, lax.axis_size(axes))


def sum_far(value, meanwhile=None):
    other = from_far(value)
    if meanwhile is not None:
        other, _ = lax.optimization_barrier((other, meanwhile))
    return value + other


def by_stages():
    return lax.axis_size("panel") == 4 and lax.axis_size("rhs") == 2


def reduce_one(value):
    value = value + swapped(value, "coef", 1, 2)
    if not by_stages():
        return lax.psum(value, ("panel", "rhs"))
    return sum_far(sum_near(value))


def reduce_both(mine, mates, square):
    value = mine + swapped(mates, "coef", 1, 2)
    whole = square + swapped(square, "coef", 1, 2)
    if by_stages():
        rows = value.shape[0]
        value = sum_far(value, meanwhile=square)
        both = sum_near(jnp.concatenate([value, whole], axis=0))
        value, whole = both[:rows], both[rows:]
        terms = [whole, from_far(whole)]
    else:
        value, whole = lax.psum((value, whole), ("panel", "rhs"))
        terms = [whole]
    return [value, swapped(value, "coef", 1, 2)], terms


def right_side_parts(obs, mask, n, strip):
    def body(obs_hbm, mask_hbm, *refs):
        *outs, obs_ref, mask_ref, sems = refs
        copies = [
            pltpu.make_async_copy(mask_hbm, mask_ref, sems.at[0]),
            pltpu.make_async_copy(obs_hbm, obs_ref, sems.at[1]),
        ]
        for copy in copies:
            copy.start()
        for copy in copies:
            copy.wait()
        signs = (2 * mask_ref[...] - 1).astype(BF16)
        me = lax.axis_index("rhs")
        for s in range(n):
            place = pl.multiple_of(mate(me, s, n) * strip, strip)
            outs[s][...] = lax.dot_general(
                obs_ref[:, pl.ds(place, strip)],
                signs,
                (((0,), (0,)), ((), ())),
                preferred_element_type=F32,
            )

    *parts, token = call(
        body,
        [shape(strip)] * n,
        pltpu.with_memory_space_constraint(obs, pltpu.HBM),
        pltpu.with_memory_space_constraint(mask, pltpu.HBM),
        scratch=[
            pltpu.VMEM(obs.shape, BF16),
            pltpu.VMEM(mask.shape, mask.dtype),
            pltpu.SemaphoreType.DMA((2,)),
        ],
        any_args=2,
    )
    return parts, token


def sum_and_round(parts, token):
    strip = parts[0].shape[0]

    def body(*refs):
        *ins, out, low = refs
        total = ins[0][...]
        for ref in ins[1:]:
            total = total + ref[...]
        out[...] = total
        low[...] = total.astype(BF16)

    return call(
        body, [shape(strip), shape(strip, dtype=BF16)], *parts, after=[token]
    )


def retiled(blocks, links, count, token):
    rows, strip = blocks.shape[1], blocks.shape[3]
    tiles = strip // LANES

    def body(k_ref, out, sems):
        copies = []
        for i, link in enumerate(links()):
            for t in range(tiles):
                copy = pltpu.make_async_copy(
                    k_ref.at[link, :, :, pl.ds(t * LANES, LANES)], out.at[i, t], sems.at[i, t]
                )
                copy.start()
                copies.append(copy)
        for copy in copies:
            copy.wait()

    packed, token = call(
        body,
        [pltpu.VMEM((count, tiles, rows, 2, LANES), BF16)],
        blocks,
        scratch=[pltpu.SemaphoreType.DMA((count, tiles))],
        after=[token],
        any_args=1,
        any_outs=True,
    )
    return packed, token


def link_products(packed, pieces, acc, n, slots, after=()):
    tiles, rows = packed[0].shape[1:3]
    counts = [value.shape[0] for value in packed]
    many = len(packed)
    packed = [
        pltpu.with_memory_space_constraint(
            value.reshape(value.shape[0], tiles, 2 * rows, LANES), pltpu.VMEM
        )
        for value in packed
    ]
    strip = tiles * LANES
    size = rows if slots is None else rows // n
    block = min(512, 2 * size)

    def body(*refs):
        k_refs, piece_refs = refs[:many], refs[many : 3 * many]
        acc_ref = refs[3 * many] if acc is not None else None
        outs = refs[3 * many + (acc is not None) : -3]
        weights, even_acc, odd_acc = refs[-3:]
        half = lax.axis_index("coef")
        own = pl.ds(pl.multiple_of(half * LANES, LANES), LANES)
        other = pl.ds(pl.multiple_of((1 - half) * LANES, LANES), LANES)
        at = 0
        for g in range(many):
            for _ in range(counts[g]):
                weights[at : at + strip, own] = piece_refs[2 * g][...]
                weights[at : at + strip, other] = piece_refs[2 * g + 1][...]
                at += strip
        me = lax.axis_index("rhs")
        for out, s in zip(outs, [None] if slots is None else slots):
            first = 0 if s is None else pl.multiple_of(mate(me, s, n) * size, size)
            for start in range(0, 2 * size, block):
                here = slice(start, start + block)
                left = jnp.concatenate(
                    [
                        k_refs[g][i, t, pl.ds(2 * first + start, block), :]
                        for g in range(many)
                        for i in range(counts[g])
                        for t in range(tiles)
                    ],
                    axis=1,
                )
                product = jnp.dot(left, weights[...], preferred_element_type=F32)
                even_acc[here, :] = product[:, :LANES]
                odd_acc[here, :] = product[:, LANES:]
            even = even_acc[pl.ds(0, size, stride=2), :]
            odd = odd_acc[pl.ds(1, size, stride=2), :]
            total = even + odd
            if acc_ref is not None:
                total = total + acc_ref[pl.ds(first, size), :]
            out[...] = total

    args = [*packed, *(value for pair in pieces for value in pair)]
    args += [acc] if acc is not None else []
    *result, token = call(
        body,
        [shape(size)] * (1 if slots is None else len(slots)),
        *args,
        scratch=[
            pltpu.VMEM((sum(counts) * strip, 2 * LANES), BF16),
            pltpu.VMEM((2 * size, LANES), F32),
            pltpu.VMEM((2 * size, LANES), F32),
        ],
        after=after,
    )
    return result, token


def link_groups(links):
    reach = (links - 1) // 2
    panels = lax.axis_size("panel")
    groups = []
    if links == 2 * panels + 1 and panels & (panels - 1) == 0:
        for s in range(panels):

            def numbers(s=s):
                me = lax.axis_index("panel")
                start = lax.rem((me ^ s) - me + reach + panels, panels)
                return [start + panels * i for i in range(3 if s == 0 else 2)]

            bring = functools.partial(swapped, axis="panel", s=s, n=panels)
            groups.append((bring, numbers, 3 if s == 0 else 2))
        return groups
    offsets = {}
    for link in range(links):
        offsets.setdefault((link - reach) % panels, []).append(link)
    for o in sorted(offsets, key=lambda o: min(o, panels - o)):
        bring = functools.partial(shifted, axis="panel", by=o)
        groups.append((bring, functools.partial(list, offsets[o]), len(offsets[o])))
    return groups


def operate(packed, groups, low, direction, between):
    n = lax.axis_size("rhs")
    arrived = [low] + [bring(low) for bring, _, _ in groups[:0:-1]][::-1]
    directions = [direction] + [swapped(direction, "rhs", s, n) for s in range(1, n)]
    pairs = [[low, swapped(low, "coef", 1, 2)]]
    (acc,), token = link_products(packed[:1], pairs, None, n, None)
    after = (token, between(token))
    for place, piece in enumerate(arrived[1:]):
        piece, _ = lax.optimization_barrier((piece, after))
        if place > 1:
            piece, pairs[place - 1][1] = lax.optimization_barrier((piece, pairs[place - 1][1]))
        pairs.append([piece, swapped(piece, "coef", 1, 2)])
    after = (*after, *directions[1:])
    mates, token = link_products(packed[1:], pairs[1:], acc, n, range(1, n), after)
    own, _ = link_products(packed[1:], pairs[1:], acc, n, [0], (token,))
    return own + mates, directions


PACKED = LANES // 2 + SUB


def corner():
    row = lax.broadcasted_iota(jnp.int32, (LANES // 2, LANES), 0)
    lane = lax.broadcasted_iota(jnp.int32, (LANES // 2, LANES), 1)
    return row, lane, lane < LANES // 2


def packed_symmetric(matrix):
    half = LANES // 2
    row, lane, left = corner()
    top = matrix[:half]
    last = pltpu.roll(matrix[half:], half, 1)
    body = jnp.where(left & (lane > row), last, top)
    diagonal = jnp.sum(jnp.where(lane == row, last, 0.0), axis=0, keepdims=True)
    return jnp.concatenate([body, jnp.broadcast_to(diagonal, (SUB, LANES))], axis=0)


def unpacked_symmetric(rows):
    half = LANES // 2
    row, lane, left = corner()
    body, diagonal = rows[:half], rows[half : half + 1]
    top = jnp.where(left & (lane >= row), 0.0, body)
    last = jnp.where(left & (lane > row), body, 0.0)
    sides = jnp.concatenate([top, pltpu.roll(last, half, 1)], axis=0)
    top = jnp.where(lane == row, body, 0.0)
    last = jnp.where(lane == row, jnp.broadcast_to(diagonal, body.shape), 0.0)
    return sides + sides.T + jnp.concatenate([top, pltpu.roll(last, half, 1)], axis=0)


def symmetric(raw):
    return 0.5 * (raw + raw.T)


JOINT = PACKED + SUB + LANES


def linear_grams(parts, directions, residual, turns, first, final):
    strip = parts[0].shape[0]
    n = len(parts)
    extra = [] if first or final else [residual, *turns]
    rows = PACKED if final else JOINT // 2

    def body(*refs):
        images, ds = refs[:n], refs[n : 2 * n]
        rest = refs[2 * n : 2 * n + len(extra)]
        outs = refs[2 * n + len(extra) :]
        curve = cross = None
        for s in range(n):
            image, d = images[s][...], ds[s][...]
            term = mm(d, image, (0, 0))
            curve = term if s == 0 else curve + term
            if extra:
                r = rest[0][...] if s == 0 else d - rest[s][...]
                term = mm(r, image, (0, 0))
                cross = term if s == 0 else cross + term
        if final:
            outs[0][...] = packed_symmetric(symmetric(curve))
            return
        mine, mates, stacked = outs
        if first:
            r = ds[0][...]
            sym, whole = mm(r, r, (0, 0)), curve
        else:
            sym, whole = symmetric(curve), cross
        stacked[:PACKED] = packed_symmetric(sym)
        stacked[PACKED : PACKED + SUB] = jnp.zeros((SUB, LANES), F32)
        stacked[PACKED + SUB :] = whole
        half = lax.axis_index("coef")
        mine[...] = stacked[pl.ds(pl.multiple_of(half * rows, SUB), rows), :]
        mates[...] = stacked[pl.ds(pl.multiple_of((1 - half) * rows, SUB), rows), :]

    *pieces, _ = call(
        body,
        [shape(rows)] * (1 if final else 2),
        *parts,
        *directions,
        *extra,
        scratch=[] if final else [pltpu.VMEM((2 * rows, LANES), F32)],
    )
    return pieces


def square_gram(image_parts):
    strip = image_parts[0].shape[0]
    parts = len(image_parts)

    def body(*refs):
        ins, image_out, out = refs[:parts], refs[parts], refs[parts + 1]
        image = ins[0][...]
        for ref in ins[1:]:
            image = image + ref[...]
        image_out[...] = image
        out[...] = packed_symmetric(mm(image, image, (0, 0)))

    image, square, _ = call(
        body,
        [shape(strip), shape(PACKED)],
        *image_parts,
    )
    return image, square


def reciprocal(value):
    near = pl.reciprocal(value, approx=True)
    for _ in range(2):
        near = near * (2.0 - value * near)
    return near


def next_pivot(column, following, i, inverse):
    product = column[i + 1 : i + 2] * following[i : i + 1]
    return following[i + 1 : i + 2] - product * inverse


def inverted(matrices, lane):
    strips = matrices[0].shape[0] // SUB
    place = lax.broadcasted_iota(jnp.int32, (SUB, LANES), 0)
    held = [[value[SUB * k : SUB * (k + 1)] for k in range(strips)] for value in matrices]

    def lanes_of(value, at):
        return jnp.broadcast_to(value[:, at : at + 1], (SUB, LANES))

    def rows_of(value):
        return [jnp.broadcast_to(value[i : i + 1], (SUB, LANES)) for i in range(SUB)]

    def update(k, j, spread):
        for a, rows in zip(held, spread):
            row = a[k]
            for i in range(SUB):
                row = row - lanes_of(a[k], lane + SUB * j + i) * rows[i]
            a[k] = row

    for j in range(strips):
        if j:
            spread = [rows_of(a[j - 1]) for a in held]
            update(j, j - 1, spread)
        waiting = [k for k in range(strips) if j and k not in (j, j - 1)]
        now = [
            [a[j], *(lanes_of(a[j], lane + SUB * j + i) for i in range(SUB))] for a in held
        ]
        pivots = [values[1][:1] for values in now]
        for i in range(SUB):
            here = place == i
            for index, values in enumerate(now):
                column = values[1 + i]
                inverse = reciprocal(pivots[index])
                if i + 1 < SUB:
                    pivots[index] = next_pivot(column, values[2 + i], i, inverse)

                def step(value):
                    row = value[i : i + 1] * inverse
                    return jnp.where(here, row, value - column * row)

                now[index] = [
                    step(value) if at < 1 or at > 1 + i else value
                    for at, value in enumerate(values)
                ]
            for k in waiting[i : i + 1]:
                update(k, j - 1, spread)
        for a, values in zip(held, now):
            a[j] = values[0]
    spread = [rows_of(a[-1]) for a in held]
    for k in range(strips - 1):
        update(k, strips - 1, spread)
    return [jnp.concatenate(a, axis=0) for a in held]


def eliminated(*systems):
    half = LANES // 2
    row = lax.broadcasted_iota(jnp.int32, (half, LANES), 0)
    lane = lax.broadcasted_iota(jnp.int32, (half, LANES), 1)
    left = lane < half
    first = inverted(
        [
            jnp.where(left, matrix[:half], (lane - half == row).astype(F32))
            for matrix, _ in systems
        ],
        0,
    )
    tops, lasts = [], []
    for (matrix, sides), value in zip(systems, first):
        value = pltpu.roll(value, half, 1)[:, :half]
        top = mm(value, jnp.concatenate([matrix[:half], sides[:half]], axis=1))
        low = jnp.concatenate([matrix[half:], sides[half:]], axis=1)
        tops.append(top)
        lasts.append(low - mm(matrix[half:, :half], top))
    second = inverted(
        [jnp.where(left, (lane == row).astype(F32), last[:, :LANES]) for last in lasts], half
    )
    found = []
    for top, last, value in zip(tops, lasts, second):
        low = mm(value[:, :half], last[:, LANES:])
        high = top[:, LANES:] - mm(
            top[:, :LANES], jnp.concatenate([jnp.zeros_like(low), low], axis=0)
        )
        found.append(jnp.concatenate([high, low], axis=0))
    return found


def eliminated_alone(matrix, sides):
    n = matrix.shape[0]
    strips = n // SUB
    place = lax.broadcasted_iota(jnp.int32, (SUB, LANES), 0)

    def cut(value):
        return [value[SUB * k : SUB * (k + 1)] for k in range(strips)]

    def lanes_of(value, lane):
        return jnp.broadcast_to(value[:, lane : lane + 1], (SUB, LANES))

    held = [(cut(matrix), cut(sides))]

    def rows_of(value):
        return [jnp.broadcast_to(value[i : i + 1], (SUB, LANES)) for i in range(SUB)]

    def update(k, j, spread):
        for (a, b), (rows_a, rows_b) in zip(held, spread):
            row_a, row_b = a[k], b[k]
            for i in range(SUB):
                factor = lanes_of(a[k], SUB * j + i)
                row_a = row_a - factor * rows_a[i]
                row_b = row_b - factor * rows_b[i]
            a[k], b[k] = row_a, row_b

    for j in range(strips):
        if j:
            spread = [(rows_of(a[j - 1]), rows_of(b[j - 1])) for a, b in held]
            update(j, j - 1, spread)
        waiting = [k for k in range(strips) if j and k not in (j, j - 1)]
        now = [
            [a[j], b[j], *(lanes_of(a[j], SUB * j + i) for i in range(SUB))] for a, b in held
        ]
        pivots = [values[2][:1] for values in now]
        for i in range(SUB):
            here = place == i
            for index, values in enumerate(now):
                column = values[2 + i]
                inverse = reciprocal(pivots[index])
                if i + 1 < SUB:
                    pivots[index] = next_pivot(column, values[3 + i], i, inverse)

                def step(value):
                    row = value[i : i + 1] * inverse
                    return jnp.where(here, row, value - column * row)

                now[index] = [
                    step(value) if place_of < 2 or place_of > 2 + i else value
                    for place_of, value in enumerate(values)
                ]
            for k in waiting[2 * i : 2 * i + 2]:
                update(k, j - 1, spread)
        for (a, b), values in zip(held, now):
            a[j], b[j] = values[:2]
    spread = [(rows_of(a[-1]), rows_of(b[-1])) for a, b in held]
    for k in range(strips - 1):
        update(k, strips - 1, spread)
    return jnp.concatenate(held[0][1], axis=0)


def identity():
    return (
        lax.broadcasted_iota(jnp.int32, (LANES, LANES), 0)
        == lax.broadcasted_iota(jnp.int32, (LANES, LANES), 1)
    ).astype(F32)


def stepped(solution, before, alpha, beta, token):
    fields = [*before, alpha, beta] + ([] if solution is None else [solution])
    n = len(before)

    def body(*refs):
        ds, a, b, refs = refs[:n], refs[n], refs[n + 1], refs[n + 2 :]
        change = mm(ds[0][...], a[...])
        refs[-n][...] = change if solution is None else refs[0][...] + change
        for s in range(1, n):
            refs[s - n][...] = mm(ds[s][...], b[...])

    solution, *turns, token = call(
        body, [shape(before[0].shape[0])] * n, *fields, after=[token]
    )
    return solution, turns, token


def finish(small, gram, residual, direction, solution, image):
    strip = residual.shape[0]

    def body(small, g, r, d, s, *refs):
        *images, out, new_r = refs
        alpha = eliminated_alone(unpacked_symmetric(small[...]), g[...])
        image = images[0][...]
        for ref in images[1:]:
            image = image + ref[...]
        out[...] = s[...] + mm(d[...], alpha)
        new_r[...] = r[...] - mm(image, alpha)

    return call(
        body,
        [shape(strip), shape(strip)],
        small,
        gram,
        residual,
        direction,
        solution,
        *image,
    )[:-1]


def advance(pieces, gram, residual, image):
    strip = residual.shape[0]
    rows = pieces[0].shape[0]
    first = gram is None
    fields = [*pieces, residual, image] + ([] if first else [gram])

    def body(*refs):
        mine, mates, r, image, *refs = refs
        *refs, raw = refs
        half = lax.axis_index("coef")
        raw[pl.ds(pl.multiple_of(half * rows, SUB), rows), :] = mine[...]
        raw[pl.ds(pl.multiple_of((1 - half) * rows, SUB), rows), :] = mates[...]
        sym, whole = unpacked_symmetric(raw[:PACKED, :]), raw[PACKED + SUB :, :]
        *refs, new_r, alpha_out, partial, inverse_out = refs
        g = sym if first else refs[0][...]
        curvature = symmetric(whole) if first else sym
        alpha, inverse_out[...] = eliminated((curvature, g), (g, identity()))
        new_r[...] = r[...] - mm(image[...], alpha)
        shared = mm(whole, alpha)
        alpha_out[...] = alpha
        partial[...] = g - (shared + shared.T)

    return call(
        body,
        [shape(strip)] + [shape(LANES)] * 3,
        *fields,
        scratch=[pltpu.VMEM((2 * rows, LANES), F32)],
    )[:-1]


def turn(square, alpha, partial, inverse, residual, direction):
    strip = residual.shape[0]

    def body(alpha, partial, inverse, r, d, *refs):
        *terms, new_d, low, beta_out, gram_out = refs
        square = terms[0][...]
        for ref in terms[1:]:
            square = square + ref[...]
        a = alpha[...]
        following = partial[...] + mm(a, mm(unpacked_symmetric(square), a), (0, 0))
        beta = mm(inverse[...], following)
        value = r[...] + mm(d[...], beta)
        low[...] = value.astype(BF16)
        new_d[...] = value
        beta_out[...] = beta
        gram_out[...] = following

    return call(
        body,
        [shape(strip), shape(strip, dtype=BF16), shape(LANES), shape(LANES)],
        alpha,
        partial,
        inverse,
        residual,
        direction,
        *square,
    )[:-1]


def shards(couplings, observations, replicate_mask):
    links, rows = couplings.shape[1], couplings.shape[3]
    strip = couplings.shape[6]
    blocks = couplings.reshape(links, rows, couplings.shape[4], strip)
    blocks = pltpu.with_memory_space_constraint(blocks, pltpu.HBM)
    n = lax.axis_size("rhs")
    obs_matrix = observations.reshape(observations.shape[0], rows)
    parts, token = right_side_parts(obs_matrix, replicate_mask, n, strip)
    own = [parts[0]] + [swapped(parts[s], "rhs", s, n) for s in range(1, n)]
    groups = link_groups(links)
    packed = []
    for _, numbers, count in groups[:2]:
        value, token = retiled(blocks, numbers, count, token)
        packed.append(value)
    residual, low, token = sum_and_round(own, token)
    for _, numbers, count in groups[2:]:
        value, token = retiled(blocks, numbers, count, token)
        packed.append(value)
    retile_token = token
    direction = residual
    solution = gram = beta = before = alpha = None
    for step in range(ITERS):
        first, final = step == 0, step + 1 == ITERS
        state = [solution, None]

        def between(token):
            if first:
                return retile_token
            *state[:], token = stepped(solution, before, alpha, beta, token)
            return token

        parts, directions = operate(packed, groups, low, direction, between)
        solution, turns = state
        image_parts = [parts[0]] + [swapped(parts[s], "rhs", s, n) for s in range(1, n)]
        linear = linear_grams(parts, directions, residual, turns, first, final)
        if final:
            small = reduce_one(*linear)
            solution, residual = finish(
                small, gram, residual, direction, solution, image_parts
            )
            break
        image, square = square_gram(image_parts)
        linear, square = reduce_both(*linear, square)
        residual, alpha, partial, inverse = advance(linear, gram, residual, image)
        square[1:], alpha = lax.optimization_barrier((square[1:], alpha))
        before = directions
        direction, low, beta, gram = turn(
            square, alpha, partial, inverse, residual, direction
        )
    shape_out = (1, 1, strip, LANES)
    return (solution.reshape(shape_out), residual.reshape(shape_out))


def solution(mesh):
    placed = (
        P("panel", None, "coef", None, None, "rhs", None),
        P(("groups", "rhs"), "panel", "coef", None),
        P(("groups", "rhs"), None),
    )
    return jax.shard_map(
        shards,
        mesh=mesh,
        in_specs=placed,
        out_specs=(
            P(("groups", "panel"), "coef", "rhs", None),
            P(("groups", "panel"), "coef", "rhs", None),
        ),
        check_vma=False,
    )
```

```python
import functools

import jax
import jax.numpy as jnp
from jax import lax
from jax.experimental import pallas as pl
from jax.experimental.pallas import tpu as pltpu
from jax.sharding import PartitionSpec as P

ITERS = 3
LANES = 128
SUB = 8
VMEM_LIMIT = 14 * 2**20
F32 = jnp.float32
BF16 = jnp.bfloat16
VMEM = pl.BlockSpec(memory_space=pltpu.VMEM)
ANY = pl.BlockSpec(memory_space=pl.ANY)
HBM = pl.BlockSpec(memory_space=pltpu.HBM)


def mm(a, b, dims=(1, 0)):
    return lax.dot_general(
        a,
        b,
        (((dims[0],), (dims[1],)), ((), ())),
        precision=lax.Precision.HIGHEST,
        preferred_element_type=F32,
    )


def call(body, outs, *args, scratch=(), after=(), any_args=0, any_outs=False):
    inputs, outputs, waits = len(args), len(outs), len(after)

    def ordered(*refs):
        token = refs[inputs + waits + outputs]
        token[...] = jnp.zeros_like(token)
        body(
            *refs[:inputs],
            *refs[inputs + waits : inputs + waits + outputs],
            *refs[inputs + waits + outputs + 1 :],
        )

    return pl.pallas_call(
        ordered,
        out_shape=list(outs) + [shape(SUB)],
        in_specs=[HBM] * any_args + [VMEM] * (inputs - any_args) + [ANY] * waits,
        out_specs=[ANY if any_outs else VMEM] * outputs + [VMEM],
        scratch_shapes=list(scratch),
        cost_estimate=pl.CostEstimate(flops=1, bytes_accessed=1, transcendentals=0),
        compiler_params=pltpu.CompilerParams(vmem_limit_bytes=VMEM_LIMIT),
    )(*args, *after)


def shape(rows, cols=LANES, dtype=F32):
    return jax.ShapeDtypeStruct((rows, cols), dtype)


def permute(value, axis, pairs):
    return lax.ppermute(value, axis, pairs)


def shifted(value, axis, by):
    n = lax.axis_size(axis)
    return permute(value, axis, [((i + by) % n, i) for i in range(n)])


def mate(i, s, n):
    return i ^ s if n & (n - 1) == 0 else (s - i) % n


def swapped(value, axis, s, n):
    return permute(value, axis, [(mate(i, s, n), i) for i in range(n)])


def sum_near(value):
    axes = ("panel", "rhs")
    count = lax.axis_size(axes)
    one, two, three = (swapped(value, axes, s, count) for s in (1, 2, 3))
    return (value + one) + (two + three)


def from_far(value):
    axes = ("panel", "rhs")
    return swapped(value, axes, 4, lax.axis_size(axes))


def sum_far(value, meanwhile=None):
    other = from_far(value)
    if meanwhile is not None:
        other, _ = lax.optimization_barrier((other, meanwhile))
    return value + other


def by_stages():
    return lax.axis_size("panel") == 4 and lax.axis_size("rhs") == 2


def reduce_one(value):
    value = value + swapped(value, "coef", 1, 2)
    if not by_stages():
        return lax.psum(value, ("panel", "rhs"))
    return sum_far(sum_near(value))


def reduce_both(mine, mates, square):
    value = mine + swapped(mates, "coef", 1, 2)
    whole = square + swapped(square, "coef", 1, 2)
    if by_stages():
        rows = value.shape[0]
        value = sum_far(value, meanwhile=square)
        both = sum_near(jnp.concatenate([value, whole], axis=0))
        value, whole = both[:rows], both[rows:]
        terms = [whole, from_far(whole)]
    else:
        value, whole = lax.psum((value, whole), ("panel", "rhs"))
        terms = [whole]
    return [value, swapped(value, "coef", 1, 2)], terms


def right_side_parts(obs, mask, n, strip):
    def body(obs_hbm, mask_hbm, *refs):
        *outs, obs_ref, mask_ref, sems = refs
        copies = [
            pltpu.make_async_copy(mask_hbm, mask_ref, sems.at[0]),
            pltpu.make_async_copy(obs_hbm, obs_ref, sems.at[1]),
        ]
        for copy in copies:
            copy.start()
        for copy in copies:
            copy.wait()
        signs = (2 * mask_ref[...] - 1).astype(BF16)
        me = lax.axis_index("rhs")
        for s in range(n):
            place = pl.multiple_of(mate(me, s, n) * strip, strip)
            outs[s][...] = lax.dot_general(
                obs_ref[:, pl.ds(place, strip)],
                signs,
                (((0,), (0,)), ((), ())),
                preferred_element_type=F32,
            )

    *parts, token = call(
        body,
        [shape(strip)] * n,
        pltpu.with_memory_space_constraint(obs, pltpu.HBM),
        pltpu.with_memory_space_constraint(mask, pltpu.HBM),
        scratch=[
            pltpu.VMEM(obs.shape, BF16),
            pltpu.VMEM(mask.shape, mask.dtype),
            pltpu.SemaphoreType.DMA((2,)),
        ],
        any_args=2,
    )
    return parts, token


def sum_and_round(parts, token):
    strip = parts[0].shape[0]

    def body(*refs):
        *ins, out, low = refs
        total = ins[0][...]
        for ref in ins[1:]:
            total = total + ref[...]
        out[...] = total
        low[...] = total.astype(BF16)

    return call(
        body, [shape(strip), shape(strip, dtype=BF16)], *parts, after=[token]
    )


def retiled(blocks, links, count, token):
    rows, strip = blocks.shape[1], blocks.shape[3]
    tiles = strip // LANES

    def body(k_ref, out, sems):
        copies = []
        for i, link in enumerate(links()):
            for t in range(tiles):
                copy = pltpu.make_async_copy(
                    k_ref.at[link, :, :, pl.ds(t * LANES, LANES)], out.at[i, t], sems.at[i, t]
                )
                copy.start()
                copies.append(copy)
        for copy in copies:
            copy.wait()

    packed, token = call(
        body,
        [pltpu.VMEM((count, tiles, rows, 2, LANES), BF16)],
        blocks,
        scratch=[pltpu.SemaphoreType.DMA((count, tiles))],
        after=[token],
        any_args=1,
        any_outs=True,
    )
    return packed, token


def link_products(packed, pieces, acc, n, slots, after=()):
    tiles, rows = packed[0].shape[1:3]
    counts = [value.shape[0] for value in packed]
    many = len(packed)
    packed = [
        pltpu.with_memory_space_constraint(
            value.reshape(value.shape[0], tiles, 2 * rows, LANES), pltpu.VMEM
        )
        for value in packed
    ]
    strip = tiles * LANES
    size = rows if slots is None else rows // n
    block = min(512, 2 * size)

    def body(*refs):
        k_refs, piece_refs = refs[:many], refs[many : 3 * many]
        acc_ref = refs[3 * many] if acc is not None else None
        outs = refs[3 * many + (acc is not None) : -3]
        weights, even_acc, odd_acc = refs[-3:]
        half = lax.axis_index("coef")
        own = pl.ds(pl.multiple_of(half * LANES, LANES), LANES)
        other = pl.ds(pl.multiple_of((1 - half) * LANES, LANES), LANES)
        for g in range(many):
            weights[g, :, own] = piece_refs[2 * g][...]
            weights[g, :, other] = piece_refs[2 * g + 1][...]
        me = lax.axis_index("rhs")
        for out, s in zip(outs, [None] if slots is None else slots):
            first = 0 if s is None else pl.multiple_of(mate(me, s, n) * size, size)
            for start in range(0, 2 * size, block):
                here = slice(start, start + block)
                product = None
                for g in range(many):
                    for i in range(counts[g]):
                        left = jnp.concatenate(
                            [
                                k_refs[g][i, t, pl.ds(2 * first + start, block), :]
                                for t in range(tiles)
                            ],
                            axis=1,
                        )
                        term = jnp.dot(left, weights[g], preferred_element_type=F32)
                        product = term if product is None else product + term
                even_acc[here, :] = product[:, :LANES]
                odd_acc[here, :] = product[:, LANES:]
            even = even_acc[pl.ds(0, size, stride=2), :]
            odd = odd_acc[pl.ds(1, size, stride=2), :]
            total = even + odd
            if acc_ref is not None:
                total = total + acc_ref[pl.ds(first, size), :]
            out[...] = total

    args = [*packed, *(value for pair in pieces for value in pair)]
    args += [acc] if acc is not None else []
    *result, token = call(
        body,
        [shape(size)] * (1 if slots is None else len(slots)),
        *args,
        scratch=[
            pltpu.VMEM((many, strip, 2 * LANES), BF16),
            pltpu.VMEM((2 * size, LANES), F32),
            pltpu.VMEM((2 * size, LANES), F32),
        ],
        after=after,
    )
    return result, token


def link_groups(links):
    reach = (links - 1) // 2
    panels = lax.axis_size("panel")
    groups = []
    if links == 2 * panels + 1 and panels & (panels - 1) == 0:
        for s in range(panels):

            def numbers(s=s):
                me = lax.axis_index("panel")
                start = lax.rem((me ^ s) - me + reach + panels, panels)
                return [start + panels * i for i in range(3 if s == 0 else 2)]

            bring = functools.partial(swapped, axis="panel", s=s, n=panels)
            groups.append((bring, numbers, 3 if s == 0 else 2))
        return groups
    offsets = {}
    for link in range(links):
        offsets.setdefault((link - reach) % panels, []).append(link)
    for o in sorted(offsets, key=lambda o: min(o, panels - o)):
        bring = functools.partial(shifted, axis="panel", by=o)
        groups.append((bring, functools.partial(list, offsets[o]), len(offsets[o])))
    return groups


def operate(packed, groups, low, direction, between, final):
    n = lax.axis_size("rhs")
    arrived = [low] + [bring(low) for bring, _, _ in groups[:0:-1]][::-1]
    directions = [direction] + [swapped(direction, "rhs", s, n) for s in range(1, n)]
    pairs = [[low, swapped(low, "coef", 1, 2)]]
    (acc,), token = link_products(packed[:1], pairs, None, n, None)
    after = (token, between(token))
    for piece in arrived[1:]:
        piece, _ = lax.optimization_barrier((piece, after))
        pairs.append([piece, swapped(piece, "coef", 1, 2)])
    after = (*after, *directions[1:])
    if len(groups) > 2:
        (acc,), _ = link_products(packed[1:-1], pairs[1:-1], acc, n, None, after)
    if final:
        parts, _ = link_products(packed[-1:], pairs[-1:], acc, n, range(n), after)
        return parts, directions
    mates, token = link_products(packed[-1:], pairs[-1:], acc, n, range(1, n), after)
    own, _ = link_products(packed[-1:], pairs[-1:], acc, n, [0], (token,))
    return own + mates, directions


PACKED = LANES // 2 + SUB


def corner():
    row = lax.broadcasted_iota(jnp.int32, (LANES // 2, LANES), 0)
    lane = lax.broadcasted_iota(jnp.int32, (LANES // 2, LANES), 1)
    return row, lane, lane < LANES // 2


def packed_symmetric(matrix):
    half = LANES // 2
    row, lane, left = corner()
    top = matrix[:half]
    last = pltpu.roll(matrix[half:], half, 1)
    body = jnp.where(left & (lane > row), last, top)
    diagonal = jnp.sum(jnp.where(lane == row, last, 0.0), axis=0, keepdims=True)
    return jnp.concatenate([body, jnp.broadcast_to(diagonal, (SUB, LANES))], axis=0)


def unpacked_symmetric(rows):
    half = LANES // 2
    row, lane, left = corner()
    body, diagonal = rows[:half], rows[half : half + 1]
    top = jnp.where(left & (lane >= row), 0.0, body)
    last = jnp.where(left & (lane > row), body, 0.0)
    sides = jnp.concatenate([top, pltpu.roll(last, half, 1)], axis=0)
    top = jnp.where(lane == row, body, 0.0)
    last = jnp.where(lane == row, jnp.broadcast_to(diagonal, body.shape), 0.0)
    return sides + sides.T + jnp.concatenate([top, pltpu.roll(last, half, 1)], axis=0)


def symmetric(raw):
    return 0.5 * (raw + raw.T)


JOINT = PACKED + SUB + LANES


def linear_grams(parts, directions, residual, turns, first, final):
    strip = parts[0].shape[0]
    n = len(parts)
    extra = [] if first or final else [residual, *turns]
    rows = PACKED if final else JOINT // 2

    def body(*refs):
        images, ds = refs[:n], refs[n : 2 * n]
        rest = refs[2 * n : 2 * n + len(extra)]
        outs = refs[2 * n + len(extra) :]
        curve = cross = None
        for s in range(n):
            image, d = images[s][...], ds[s][...]
            term = mm(d, image, (0, 0))
            curve = term if s == 0 else curve + term
            if extra:
                r = rest[0][...] if s == 0 else d - rest[s][...]
                term = mm(r, image, (0, 0))
                cross = term if s == 0 else cross + term
        if final:
            outs[0][...] = packed_symmetric(symmetric(curve))
            return
        mine, mates, stacked = outs
        if first:
            r = ds[0][...]
            sym, whole = mm(r, r, (0, 0)), curve
        else:
            sym, whole = symmetric(curve), cross
        stacked[:PACKED] = packed_symmetric(sym)
        stacked[PACKED : PACKED + SUB] = jnp.zeros((SUB, LANES), F32)
        stacked[PACKED + SUB :] = whole
        half = lax.axis_index("coef")
        mine[...] = stacked[pl.ds(pl.multiple_of(half * rows, SUB), rows), :]
        mates[...] = stacked[pl.ds(pl.multiple_of((1 - half) * rows, SUB), rows), :]

    *pieces, _ = call(
        body,
        [shape(rows)] * (1 if final else 2),
        *parts,
        *directions,
        *extra,
        scratch=[] if final else [pltpu.VMEM((2 * rows, LANES), F32)],
    )
    return pieces


def square_gram(image_parts):
    strip = image_parts[0].shape[0]
    parts = len(image_parts)

    def body(*refs):
        ins, image_out, out = refs[:parts], refs[parts], refs[parts + 1]
        image = ins[0][...]
        for ref in ins[1:]:
            image = image + ref[...]
        image_out[...] = image
        out[...] = packed_symmetric(mm(image, image, (0, 0)))

    image, square, _ = call(
        body,
        [shape(strip), shape(PACKED)],
        *image_parts,
    )
    return image, square


def reciprocal(value):
    near = pl.reciprocal(value, approx=True)
    for _ in range(2):
        near = near * (2.0 - value * near)
    return near


def next_pivot(column, following, i, inverse):
    product = column[i + 1 : i + 2] * following[i : i + 1]
    return following[i + 1 : i + 2] - product * inverse


def inverted(matrices, lane):
    strips = matrices[0].shape[0] // SUB
    place = lax.broadcasted_iota(jnp.int32, (SUB, LANES), 0)
    held = [[value[SUB * k : SUB * (k + 1)] for k in range(strips)] for value in matrices]

    def lanes_of(value, at):
        return jnp.broadcast_to(value[:, at : at + 1], (SUB, LANES))

    def rows_of(value):
        return [jnp.broadcast_to(value[i : i + 1], (SUB, LANES)) for i in range(SUB)]

    def update(k, j, spread):
        for a, rows in zip(held, spread):
            row = a[k]
            for i in range(SUB):
                row = row - lanes_of(a[k], lane + SUB * j + i) * rows[i]
            a[k] = row

    for j in range(strips):
        if j:
            spread = [rows_of(a[j - 1]) for a in held]
            update(j, j - 1, spread)
        waiting = [k for k in range(strips) if j and k not in (j, j - 1)]
        now = [
            [a[j], *(lanes_of(a[j], lane + SUB * j + i) for i in range(SUB))] for a in held
        ]
        for i in range(SUB):
            here = place == i
            for index, values in enumerate(now):
                column = values[1 + i]
                inverse = 1.0 / column[i : i + 1]

                def step(value):
                    row = value[i : i + 1] * inverse
                    return jnp.where(here, row, value - column * row)

                now[index] = [
                    step(value) if at < 1 or at > 1 + i else value
                    for at, value in enumerate(values)
                ]
            for k in waiting[i : i + 1]:
                update(k, j - 1, spread)
        for a, values in zip(held, now):
            a[j] = values[0]
    spread = [rows_of(a[-1]) for a in held]
    for k in range(strips - 1):
        update(k, strips - 1, spread)
    return [jnp.concatenate(a, axis=0) for a in held]


def eliminated(*systems):
    half = LANES // 2
    row = lax.broadcasted_iota(jnp.int32, (half, LANES), 0)
    lane = lax.broadcasted_iota(jnp.int32, (half, LANES), 1)
    left = lane < half
    first = inverted(
        [
            jnp.where(left, matrix[:half], (lane - half == row).astype(F32))
            for matrix, _ in systems
        ],
        0,
    )
    tops, lasts = [], []
    for (matrix, sides), value in zip(systems, first):
        value = pltpu.roll(value, half, 1)[:, :half]
        top = mm(value, jnp.concatenate([matrix[:half], sides[:half]], axis=1))
        low = jnp.concatenate([matrix[half:], sides[half:]], axis=1)
        tops.append(top)
        lasts.append(low - mm(matrix[half:, :half], top))
    second = inverted(
        [jnp.where(left, (lane == row).astype(F32), last[:, :LANES]) for last in lasts], half
    )
    found = []
    for top, last, value in zip(tops, lasts, second):
        low = mm(value[:, :half], last[:, LANES:])
        high = top[:, LANES:] - mm(
            top[:, :LANES], jnp.concatenate([jnp.zeros_like(low), low], axis=0)
        )
        found.append(jnp.concatenate([high, low], axis=0))
    return found


def eliminated_alone(matrix, sides):
    n = matrix.shape[0]
    strips = n // SUB
    place = lax.broadcasted_iota(jnp.int32, (SUB, LANES), 0)

    def cut(value):
        return [value[SUB * k : SUB * (k + 1)] for k in range(strips)]

    def lanes_of(value, lane):
        return jnp.broadcast_to(value[:, lane : lane + 1], (SUB, LANES))

    held = [(cut(matrix), cut(sides))]

    def rows_of(value):
        return [jnp.broadcast_to(value[i : i + 1], (SUB, LANES)) for i in range(SUB)]

    def update(k, j, spread):
        for (a, b), (rows_a, rows_b) in zip(held, spread):
            row_a, row_b = a[k], b[k]
            for i in range(SUB):
                factor = lanes_of(a[k], SUB * j + i)
                row_a = row_a - factor * rows_a[i]
                row_b = row_b - factor * rows_b[i]
            a[k], b[k] = row_a, row_b

    for j in range(strips):
        if j:
            spread = [(rows_of(a[j - 1]), rows_of(b[j - 1])) for a, b in held]
            update(j, j - 1, spread)
        waiting = [k for k in range(strips) if j and k not in (j, j - 1)]
        now = [
            [a[j], b[j], *(lanes_of(a[j], SUB * j + i) for i in range(SUB))] for a, b in held
        ]
        pivots = [values[2][:1] for values in now]
        for i in range(SUB):
            here = place == i
            for index, values in enumerate(now):
                column = values[2 + i]
                inverse = reciprocal(pivots[index])
                if i + 1 < SUB:
                    pivots[index] = next_pivot(column, values[3 + i], i, inverse)

                def step(value):
                    row = value[i : i + 1] * inverse
                    return jnp.where(here, row, value - column * row)

                now[index] = [
                    step(value) if place_of < 2 or place_of > 2 + i else value
                    for place_of, value in enumerate(values)
                ]
            for k in waiting[2 * i : 2 * i + 2]:
                update(k, j - 1, spread)
        for (a, b), values in zip(held, now):
            a[j], b[j] = values[:2]
    spread = [(rows_of(a[-1]), rows_of(b[-1])) for a, b in held]
    for k in range(strips - 1):
        update(k, strips - 1, spread)
    return jnp.concatenate(held[0][1], axis=0)


def identity():
    return (
        lax.broadcasted_iota(jnp.int32, (LANES, LANES), 0)
        == lax.broadcasted_iota(jnp.int32, (LANES, LANES), 1)
    ).astype(F32)


def stepped(solution, before, alpha, beta, token):
    fields = [*before, alpha, beta] + ([] if solution is None else [solution])
    n = len(before)

    def body(*refs):
        ds, a, b, refs = refs[:n], refs[n], refs[n + 1], refs[n + 2 :]
        change = mm(ds[0][...], a[...])
        refs[-n][...] = change if solution is None else refs[0][...] + change
        for s in range(1, n):
            refs[s - n][...] = mm(ds[s][...], b[...])

    solution, *turns, token = call(
        body, [shape(before[0].shape[0])] * n, *fields, after=[token]
    )
    return solution, turns, token


def finish(small, gram, residual, direction, solution, image):
    strip = residual.shape[0]

    def body(small, g, r, d, s, *refs):
        *images, out, new_r = refs
        alpha = eliminated_alone(unpacked_symmetric(small[...]), g[...])
        image = images[0][...]
        for ref in images[1:]:
            image = image + ref[...]
        out[...] = s[...] + mm(d[...], alpha)
        new_r[...] = r[...] - mm(image, alpha)

    return call(
        body,
        [shape(strip), shape(strip)],
        small,
        gram,
        residual,
        direction,
        solution,
        *image,
    )[:-1]


def advance(pieces, gram, residual, image):
    strip = residual.shape[0]
    rows = pieces[0].shape[0]
    first = gram is None
    fields = [*pieces, residual, image] + ([] if first else [gram])

    def body(*refs):
        mine, mates, r, image, *refs = refs
        *refs, raw = refs
        half = lax.axis_index("coef")
        raw[pl.ds(pl.multiple_of(half * rows, SUB), rows), :] = mine[...]
        raw[pl.ds(pl.multiple_of((1 - half) * rows, SUB), rows), :] = mates[...]
        sym, whole = unpacked_symmetric(raw[:PACKED, :]), raw[PACKED + SUB :, :]
        *refs, new_r, alpha_out, partial, inverse_out = refs
        g = sym if first else refs[0][...]
        curvature = symmetric(whole) if first else sym
        alpha, inverse_out[...] = eliminated((curvature, g), (g, identity()))
        new_r[...] = r[...] - mm(image[...], alpha)
        shared = mm(whole, alpha)
        alpha_out[...] = alpha
        partial[...] = g - (shared + shared.T)

    return call(
        body,
        [shape(strip)] + [shape(LANES)] * 3,
        *fields,
        scratch=[pltpu.VMEM((2 * rows, LANES), F32)],
    )[:-1]


def turn(square, alpha, partial, inverse, residual, direction):
    strip = residual.shape[0]

    def body(alpha, partial, inverse, r, d, *refs):
        *terms, new_d, low, beta_out, gram_out = refs
        square = terms[0][...]
        for ref in terms[1:]:
            square = square + ref[...]
        a = alpha[...]
        following = partial[...] + mm(a, mm(unpacked_symmetric(square), a), (0, 0))
        beta = mm(inverse[...], following)
        value = r[...] + mm(d[...], beta)
        low[...] = value.astype(BF16)
        new_d[...] = value
        beta_out[...] = beta
        gram_out[...] = following

    return call(
        body,
        [shape(strip), shape(strip, dtype=BF16), shape(LANES), shape(LANES)],
        alpha,
        partial,
        inverse,
        residual,
        direction,
        *square,
    )[:-1]


def shards(couplings, observations, replicate_mask):
    links, rows = couplings.shape[1], couplings.shape[3]
    strip = couplings.shape[6]
    blocks = couplings.reshape(links, rows, couplings.shape[4], strip)
    blocks = pltpu.with_memory_space_constraint(blocks, pltpu.HBM)
    n = lax.axis_size("rhs")
    obs_matrix = observations.reshape(observations.shape[0], rows)
    parts, token = right_side_parts(obs_matrix, replicate_mask, n, strip)
    own = [parts[0]] + [swapped(parts[s], "rhs", s, n) for s in range(1, n)]
    groups = link_groups(links)
    packed = []
    for _, numbers, count in groups[:2]:
        value, token = retiled(blocks, numbers, count, token)
        packed.append(value)
    residual, low, token = sum_and_round(own, token)
    for _, numbers, count in groups[2:]:
        value, token = retiled(blocks, numbers, count, token)
        packed.append(value)
    retile_token = token
    direction = residual
    solution = gram = beta = before = alpha = None
    for step in range(ITERS):
        first, final = step == 0, step + 1 == ITERS
        state = [solution, None]

        def between(token):
            if first:
                return retile_token
            *state[:], token = stepped(solution, before, alpha, beta, token)
            return token

        parts, directions = operate(packed, groups, low, direction, between, final)
        solution, turns = state
        image_parts = [parts[0]] + [swapped(parts[s], "rhs", s, n) for s in range(1, n)]
        linear = linear_grams(parts, directions, residual, turns, first, final)
        if final:
            small = reduce_one(*linear)
            solution, residual = finish(
                small, gram, residual, direction, solution, image_parts
            )
            break
        image, square = square_gram(image_parts)
        linear, square = reduce_both(*linear, square)
        residual, alpha, partial, inverse = advance(linear, gram, residual, image)
        square[1:], alpha = lax.optimization_barrier((square[1:], alpha))
        before = directions
        direction, low, beta, gram = turn(
            square, alpha, partial, inverse, residual, direction
        )
    shape_out = (1, 1, strip, LANES)
    return (solution.reshape(shape_out), residual.reshape(shape_out))


def solution(mesh):
    placed = (
        P("panel", None, "coef", None, None, "rhs", None),
        P(("groups", "rhs"), "panel", "coef", None),
        P(("groups", "rhs"), None),
    )
    return jax.shard_map(
        shards,
        mesh=mesh,
        in_specs=placed,
        out_specs=(
            P(("groups", "panel"), "coef", "rhs", None),
            P(("groups", "panel"), "coef", "rhs", None),
        ),
        check_vma=False,
    )
```

```python
import functools

import jax
import jax.numpy as jnp
from jax import lax
from jax.experimental import pallas as pl
from jax.experimental.pallas import tpu as pltpu
from jax.sharding import PartitionSpec as P

ITERS = 3
LANES = 128
SUB = 8
VMEM_LIMIT = 14 * 2**20
F32 = jnp.float32
BF16 = jnp.bfloat16
VMEM = pl.BlockSpec(memory_space=pltpu.VMEM)
ANY = pl.BlockSpec(memory_space=pl.ANY)
HBM = pl.BlockSpec(memory_space=pltpu.HBM)


def mm(a, b, dims=(1, 0)):
    return lax.dot_general(
        a,
        b,
        (((dims[0],), (dims[1],)), ((), ())),
        precision=lax.Precision.HIGHEST,
        preferred_element_type=F32,
    )


def call(body, outs, *args, scratch=(), after=(), any_args=0, any_outs=False):
    inputs, outputs, waits = len(args), len(outs), len(after)

    def ordered(*refs):
        token = refs[inputs + waits + outputs]
        token[...] = jnp.zeros_like(token)
        body(
            *refs[:inputs],
            *refs[inputs + waits : inputs + waits + outputs],
            *refs[inputs + waits + outputs + 1 :],
        )

    return pl.pallas_call(
        ordered,
        out_shape=list(outs) + [shape(SUB)],
        in_specs=[HBM] * any_args + [VMEM] * (inputs - any_args) + [ANY] * waits,
        out_specs=[ANY if any_outs else VMEM] * outputs + [VMEM],
        scratch_shapes=list(scratch),
        cost_estimate=pl.CostEstimate(flops=1, bytes_accessed=1, transcendentals=0),
        compiler_params=pltpu.CompilerParams(vmem_limit_bytes=VMEM_LIMIT),
    )(*args, *after)


def shape(rows, cols=LANES, dtype=F32):
    return jax.ShapeDtypeStruct((rows, cols), dtype)


def permute(value, axis, pairs):
    return lax.ppermute(value, axis, pairs)


def shifted(value, axis, by):
    n = lax.axis_size(axis)
    return permute(value, axis, [((i + by) % n, i) for i in range(n)])


def mate(i, s, n):
    return i ^ s if n & (n - 1) == 0 else (s - i) % n


def swapped(value, axis, s, n):
    return permute(value, axis, [(mate(i, s, n), i) for i in range(n)])


def sum_near(value):
    axes = ("panel", "rhs")
    count = lax.axis_size(axes)
    one, two, three = (swapped(value, axes, s, count) for s in (1, 2, 3))
    return (value + one) + (two + three)


def from_far(value):
    axes = ("panel", "rhs")
    return swapped(value, axes, 4, lax.axis_size(axes))


def sum_far(value, meanwhile=None):
    other = from_far(value)
    if meanwhile is not None:
        other, _ = lax.optimization_barrier((other, meanwhile))
    return value + other


def by_stages():
    return lax.axis_size("panel") == 4 and lax.axis_size("rhs") == 2


def reduce_one(value):
    value = value + swapped(value, "coef", 1, 2)
    if not by_stages():
        return lax.psum(value, ("panel", "rhs"))
    return sum_far(sum_near(value))


def reduce_both(mine, mates, square):
    value = mine + swapped(mates, "coef", 1, 2)
    whole = square + swapped(square, "coef", 1, 2)
    if by_stages():
        rows = value.shape[0]
        value = sum_far(value, meanwhile=square)
        both = sum_near(jnp.concatenate([value, whole], axis=0))
        value, whole = both[:rows], both[rows:]
        terms = [whole, from_far(whole)]
    else:
        value, whole = lax.psum((value, whole), ("panel", "rhs"))
        terms = [whole]
    return [value, swapped(value, "coef", 1, 2)], terms


def right_side_parts(obs, mask, n, strip):
    def body(obs_hbm, mask_hbm, *refs):
        *outs, obs_ref, mask_ref, sems = refs
        copies = [
            pltpu.make_async_copy(mask_hbm, mask_ref, sems.at[0]),
            pltpu.make_async_copy(obs_hbm, obs_ref, sems.at[1]),
        ]
        for copy in copies:
            copy.start()
        for copy in copies:
            copy.wait()
        signs = (2 * mask_ref[...] - 1).astype(BF16)
        me = lax.axis_index("rhs")
        for s in range(n):
            place = pl.multiple_of(mate(me, s, n) * strip, strip)
            outs[s][...] = lax.dot_general(
                obs_ref[:, pl.ds(place, strip)],
                signs,
                (((0,), (0,)), ((), ())),
                preferred_element_type=F32,
            )

    *parts, token = call(
        body,
        [shape(strip)] * n,
        pltpu.with_memory_space_constraint(obs, pltpu.HBM),
        pltpu.with_memory_space_constraint(mask, pltpu.HBM),
        scratch=[
            pltpu.VMEM(obs.shape, BF16),
            pltpu.VMEM(mask.shape, mask.dtype),
            pltpu.SemaphoreType.DMA((2,)),
        ],
        any_args=2,
    )
    return parts, token


def sum_and_round(parts, token):
    strip = parts[0].shape[0]

    def body(*refs):
        *ins, out, low = refs
        total = ins[0][...]
        for ref in ins[1:]:
            total = total + ref[...]
        out[...] = total
        low[...] = total.astype(BF16)

    return call(
        body, [shape(strip), shape(strip, dtype=BF16)], *parts, after=[token]
    )


def retiled(blocks, links, count, token):
    rows, strip = blocks.shape[1], blocks.shape[3]
    tiles = strip // LANES

    def body(k_ref, out, sems):
        copies = []
        for i, link in enumerate(links()):
            for t in range(tiles):
                copy = pltpu.make_async_copy(
                    k_ref.at[link, :, :, pl.ds(t * LANES, LANES)], out.at[i, t], sems.at[i, t]
                )
                copy.start()
                copies.append(copy)
        for copy in copies:
            copy.wait()

    packed, token = call(
        body,
        [pltpu.VMEM((count, tiles, rows, 2, LANES), BF16)],
        blocks,
        scratch=[pltpu.SemaphoreType.DMA((count, tiles))],
        after=[token],
        any_args=1,
        any_outs=True,
    )
    return packed, token


def link_products(packed, pieces, acc, n, slots, after=()):
    tiles, rows = packed[0].shape[1:3]
    counts = [value.shape[0] for value in packed]
    many = len(packed)
    packed = [
        pltpu.with_memory_space_constraint(
            value.reshape(value.shape[0], tiles, 2 * rows, LANES), pltpu.VMEM
        )
        for value in packed
    ]
    strip = tiles * LANES
    size = rows if slots is None else rows // n
    block = min(512, 2 * size)

    def body(*refs):
        k_refs, piece_refs = refs[:many], refs[many : 3 * many]
        acc_ref = refs[3 * many] if acc is not None else None
        outs = refs[3 * many + (acc is not None) : -3]
        weights, even_acc, odd_acc = refs[-3:]
        half = lax.axis_index("coef")
        own = pl.ds(pl.multiple_of(half * LANES, LANES), LANES)
        other = pl.ds(pl.multiple_of((1 - half) * LANES, LANES), LANES)
        for g in range(many):
            weights[g, :, own] = piece_refs[2 * g][...]
            weights[g, :, other] = piece_refs[2 * g + 1][...]
        me = lax.axis_index("rhs")
        for out, s in zip(outs, [None] if slots is None else slots):
            first = 0 if s is None else pl.multiple_of(mate(me, s, n) * size, size)
            for start in range(0, 2 * size, block):
                here = slice(start, start + block)
                product = None
                for g in range(many):
                    for i in range(counts[g]):
                        left = jnp.concatenate(
                            [
                                k_refs[g][i, t, pl.ds(2 * first + start, block), :]
                                for t in range(tiles)
                            ],
                            axis=1,
                        )
                        term = jnp.dot(left, weights[g], preferred_element_type=F32)
                        product = term if product is None else product + term
                even_acc[here, :] = product[:, :LANES]
                odd_acc[here, :] = product[:, LANES:]
            even = even_acc[pl.ds(0, size, stride=2), :]
            odd = odd_acc[pl.ds(1, size, stride=2), :]
            total = even + odd
            if acc_ref is not None:
                total = total + acc_ref[pl.ds(first, size), :]
            out[...] = total

    args = [*packed, *(value for pair in pieces for value in pair)]
    args += [acc] if acc is not None else []
    *result, token = call(
        body,
        [shape(size)] * (1 if slots is None else len(slots)),
        *args,
        scratch=[
            pltpu.VMEM((many, strip, 2 * LANES), BF16),
            pltpu.VMEM((2 * size, LANES), F32),
            pltpu.VMEM((2 * size, LANES), F32),
        ],
        after=after,
    )
    return result, token


def link_groups(links):
    reach = (links - 1) // 2
    panels = lax.axis_size("panel")
    groups = []
    if links == 2 * panels + 1 and panels & (panels - 1) == 0:
        for s in sorted(range(panels), key=lambda s: (s > 0, s % 2)):

            def numbers(s=s):
                me = lax.axis_index("panel")
                start = lax.rem((me ^ s) - me + reach + panels, panels)
                return [start + panels * i for i in range(3 if s == 0 else 2)]

            bring = functools.partial(swapped, axis="panel", s=s, n=panels)
            groups.append((bring, numbers, 3 if s == 0 else 2))
        return groups
    offsets = {}
    for link in range(links):
        offsets.setdefault((link - reach) % panels, []).append(link)
    for o in sorted(offsets, key=lambda o: min(o, panels - o)):
        bring = functools.partial(shifted, axis="panel", by=o)
        groups.append((bring, functools.partial(list, offsets[o]), len(offsets[o])))
    return groups


def operate(packed, groups, low, direction, between, final):
    n = lax.axis_size("rhs")
    arrived = [low] + [bring(low) for bring, _, _ in groups[:0:-1]][::-1]
    directions = [direction] + [swapped(direction, "rhs", s, n) for s in range(1, n)]
    pairs = [[low, swapped(low, "coef", 1, 2)]]
    (acc,), token = link_products(packed[:1], pairs, None, n, None)
    after = (token, between(token))
    for piece in arrived[1:]:
        piece, _ = lax.optimization_barrier((piece, after))
        pairs.append([piece, swapped(piece, "coef", 1, 2)])
    after = (*after, *directions[1:])
    if len(groups) > 2:
        (acc,), _ = link_products(packed[1:-1], pairs[1:-1], acc, n, None, after)
    if final:
        parts, _ = link_products(packed[-1:], pairs[-1:], acc, n, range(n), after)
        return parts, directions
    mates, token = link_products(packed[-1:], pairs[-1:], acc, n, range(1, n), after)
    own, _ = link_products(packed[-1:], pairs[-1:], acc, n, [0], (token,))
    return own + mates, directions


PACKED = LANES // 2 + SUB


def corner():
    row = lax.broadcasted_iota(jnp.int32, (LANES // 2, LANES), 0)
    lane = lax.broadcasted_iota(jnp.int32, (LANES // 2, LANES), 1)
    return row, lane, lane < LANES // 2


def packed_symmetric(matrix):
    half = LANES // 2
    row, lane, left = corner()
    top = matrix[:half]
    last = pltpu.roll(matrix[half:], half, 1)
    body = jnp.where(left & (lane > row), last, top)
    diagonal = jnp.sum(jnp.where(lane == row, last, 0.0), axis=0, keepdims=True)
    return jnp.concatenate([body, jnp.broadcast_to(diagonal, (SUB, LANES))], axis=0)


def unpacked_symmetric(rows):
    half = LANES // 2
    row, lane, left = corner()
    body, diagonal = rows[:half], rows[half : half + 1]
    top = jnp.where(left & (lane >= row), 0.0, body)
    last = jnp.where(left & (lane > row), body, 0.0)
    sides = jnp.concatenate([top, pltpu.roll(last, half, 1)], axis=0)
    top = jnp.where(lane == row, body, 0.0)
    last = jnp.where(lane == row, jnp.broadcast_to(diagonal, body.shape), 0.0)
    return sides + sides.T + jnp.concatenate([top, pltpu.roll(last, half, 1)], axis=0)


def symmetric(raw):
    return 0.5 * (raw + raw.T)


JOINT = PACKED + SUB + LANES


def linear_grams(parts, directions, residual, turns, first, final):
    strip = parts[0].shape[0]
    n = len(parts)
    extra = [] if first or final else [residual, *turns]
    rows = PACKED if final else JOINT // 2

    def body(*refs):
        images, ds = refs[:n], refs[n : 2 * n]
        rest = refs[2 * n : 2 * n + len(extra)]
        outs = refs[2 * n + len(extra) :]
        found = None
        for s in range(n):
            image, right = images[s][...], ds[s][...]
            if extra:
                r = rest[0][...] if s == 0 else right - rest[s][...]
                right = jnp.concatenate([right, r], axis=1)
            term = mm(image, right, (0, 0))
            found = term if s == 0 else found + term
        if final:
            outs[0][...] = packed_symmetric(symmetric(found))
            return
        mine, mates, stacked = outs
        if first:
            r = ds[0][...]
            sym, whole = mm(r, r, (0, 0)), found
        else:
            sym, whole = symmetric(found[:, :LANES]), found[:, LANES:]
        stacked[:PACKED] = packed_symmetric(sym)
        stacked[PACKED : PACKED + SUB] = jnp.zeros((SUB, LANES), F32)
        stacked[PACKED + SUB :] = whole
        half = lax.axis_index("coef")
        mine[...] = stacked[pl.ds(pl.multiple_of(half * rows, SUB), rows), :]
        mates[...] = stacked[pl.ds(pl.multiple_of((1 - half) * rows, SUB), rows), :]

    *pieces, _ = call(
        body,
        [shape(rows)] * (1 if final else 2),
        *parts,
        *directions,
        *extra,
        scratch=[] if final else [pltpu.VMEM((2 * rows, LANES), F32)],
    )
    return pieces


def square_gram(image_parts):
    strip = image_parts[0].shape[0]
    parts = len(image_parts)

    def body(*refs):
        ins, image_out, out = refs[:parts], refs[parts], refs[parts + 1]
        image = ins[0][...]
        for ref in ins[1:]:
            image = image + ref[...]
        image_out[...] = image
        out[...] = packed_symmetric(mm(image, image, (0, 0)))

    image, square, _ = call(
        body,
        [shape(strip), shape(PACKED)],
        *image_parts,
    )
    return image, square


def reciprocal(value):
    near = pl.reciprocal(value, approx=True)
    for _ in range(2):
        near = near * (2.0 - value * near)
    return near


def next_pivot(column, following, i, inverse):
    product = column[i + 1 : i + 2] * following[i : i + 1]
    return following[i + 1 : i + 2] - product * inverse


def inverted(matrices, lane):
    strips = matrices[0].shape[0] // SUB
    place = lax.broadcasted_iota(jnp.int32, (SUB, LANES), 0)
    held = [[value[SUB * k : SUB * (k + 1)] for k in range(strips)] for value in matrices]

    def lanes_of(value, at):
        return jnp.broadcast_to(value[:, at : at + 1], (SUB, LANES))

    def rows_of(value):
        return [jnp.broadcast_to(value[i : i + 1], (SUB, LANES)) for i in range(SUB)]

    def update(k, j, spread):
        for a, rows in zip(held, spread):
            row = a[k]
            for i in range(SUB):
                row = row - lanes_of(a[k], lane + SUB * j + i) * rows[i]
            a[k] = row

    for j in range(strips):
        if j:
            spread = [rows_of(a[j - 1]) for a in held]
            update(j, j - 1, spread)
        waiting = [k for k in range(strips) if j and k not in (j, j - 1)]
        now = [
            [a[j], *(lanes_of(a[j], lane + SUB * j + i) for i in range(SUB))] for a in held
        ]
        for i in range(SUB):
            here = place == i
            for index, values in enumerate(now):
                column = values[1 + i]
                inverse = 1.0 / column[i : i + 1]

                def step(value):
                    row = value[i : i + 1] * inverse
                    return jnp.where(here, row, value - column * row)

                now[index] = [
                    step(value) if at < 1 or at > 1 + i else value
                    for at, value in enumerate(values)
                ]
            for k in waiting[i : i + 1]:
                update(k, j - 1, spread)
        for a, values in zip(held, now):
            a[j] = values[0]
    spread = [rows_of(a[-1]) for a in held]
    for k in range(strips - 1):
        update(k, strips - 1, spread)
    return [jnp.concatenate(a, axis=0) for a in held]


def eliminated(*systems):
    half = LANES // 2
    row = lax.broadcasted_iota(jnp.int32, (half, LANES), 0)
    lane = lax.broadcasted_iota(jnp.int32, (half, LANES), 1)
    left = lane < half
    first = inverted(
        [
            jnp.where(left, matrix[:half], (lane - half == row).astype(F32))
            for matrix, _ in systems
        ],
        0,
    )
    tops, lasts = [], []
    for (matrix, sides), value in zip(systems, first):
        value = pltpu.roll(value, half, 1)[:, :half]
        top = mm(value, jnp.concatenate([matrix[:half], sides[:half]], axis=1))
        low = jnp.concatenate([matrix[half:], sides[half:]], axis=1)
        tops.append(top)
        lasts.append(low - mm(matrix[half:, :half], top))
    second = inverted(
        [jnp.where(left, (lane == row).astype(F32), last[:, :LANES]) for last in lasts], half
    )
    found = []
    for top, last, value in zip(tops, lasts, second):
        low = mm(value[:, :half], last[:, LANES:])
        high = top[:, LANES:] - mm(
            top[:, :LANES], jnp.concatenate([jnp.zeros_like(low), low], axis=0)
        )
        found.append(jnp.concatenate([high, low], axis=0))
    return found


def eliminated_alone(matrix, sides):
    n = matrix.shape[0]
    strips = n // SUB
    place = lax.broadcasted_iota(jnp.int32, (SUB, LANES), 0)

    def cut(value):
        return [value[SUB * k : SUB * (k + 1)] for k in range(strips)]

    def lanes_of(value, lane):
        return jnp.broadcast_to(value[:, lane : lane + 1], (SUB, LANES))

    held = [(cut(matrix), cut(sides))]

    def rows_of(value):
        return [jnp.broadcast_to(value[i : i + 1], (SUB, LANES)) for i in range(SUB)]

    def update(k, j, spread):
        for (a, b), (rows_a, rows_b) in zip(held, spread):
            row_a, row_b = a[k], b[k]
            for i in range(SUB):
                factor = lanes_of(a[k], SUB * j + i)
                row_a = row_a - factor * rows_a[i]
                row_b = row_b - factor * rows_b[i]
            a[k], b[k] = row_a, row_b

    for j in range(strips):
        if j:
            spread = [(rows_of(a[j - 1]), rows_of(b[j - 1])) for a, b in held]
            update(j, j - 1, spread)
        waiting = [k for k in range(strips) if j and k not in (j, j - 1)]
        now = [
            [a[j], b[j], *(lanes_of(a[j], SUB * j + i) for i in range(SUB))] for a, b in held
        ]
        pivots = [values[2][:1] for values in now]
        for i in range(SUB):
            here = place == i
            for index, values in enumerate(now):
                column = values[2 + i]
                inverse = reciprocal(pivots[index])
                if i + 1 < SUB:
                    pivots[index] = next_pivot(column, values[3 + i], i, inverse)

                def step(value):
                    row = value[i : i + 1] * inverse
                    return jnp.where(here, row, value - column * row)

                now[index] = [
                    step(value) if place_of < 2 or place_of > 2 + i else value
                    for place_of, value in enumerate(values)
                ]
            for k in waiting[2 * i : 2 * i + 2]:
                update(k, j - 1, spread)
        for (a, b), values in zip(held, now):
            a[j], b[j] = values[:2]
    spread = [(rows_of(a[-1]), rows_of(b[-1])) for a, b in held]
    for k in range(strips - 1):
        update(k, strips - 1, spread)
    return jnp.concatenate(held[0][1], axis=0)


def identity():
    return (
        lax.broadcasted_iota(jnp.int32, (LANES, LANES), 0)
        == lax.broadcasted_iota(jnp.int32, (LANES, LANES), 1)
    ).astype(F32)


def stepped(solution, before, alpha, beta, token):
    fields = [*before, alpha, beta] + ([] if solution is None else [solution])
    n = len(before)

    def body(*refs):
        ds, a, b, refs = refs[:n], refs[n], refs[n + 1], refs[n + 2 :]
        change = mm(ds[0][...], a[...])
        refs[-n][...] = change if solution is None else refs[0][...] + change
        for s in range(1, n):
            refs[s - n][...] = mm(ds[s][...], b[...])

    solution, *turns, token = call(
        body, [shape(before[0].shape[0])] * n, *fields, after=[token]
    )
    return solution, turns, token


def finish(small, gram, residual, direction, solution, image):
    strip = residual.shape[0]

    def body(small, g, r, d, s, *refs):
        *images, out, new_r = refs
        alpha = eliminated_alone(unpacked_symmetric(small[...]), g[...])
        image = images[0][...]
        for ref in images[1:]:
            image = image + ref[...]
        out[...] = s[...] + mm(d[...], alpha)
        new_r[...] = r[...] - mm(image, alpha)

    return call(
        body,
        [shape(strip), shape(strip)],
        small,
        gram,
        residual,
        direction,
        solution,
        *image,
    )[:-1]


def advance(pieces, gram, residual, image):
    strip = residual.shape[0]
    rows = pieces[0].shape[0]
    first = gram is None
    fields = [*pieces, residual, image] + ([] if first else [gram])

    def body(*refs):
        mine, mates, r, image, *refs = refs
        *refs, raw = refs
        half = lax.axis_index("coef")
        raw[pl.ds(pl.multiple_of(half * rows, SUB), rows), :] = mine[...]
        raw[pl.ds(pl.multiple_of((1 - half) * rows, SUB), rows), :] = mates[...]
        sym, whole = unpacked_symmetric(raw[:PACKED, :]), raw[PACKED + SUB :, :]
        *refs, new_r, alpha_out, partial, inverse_out = refs
        g = sym if first else refs[0][...]
        curvature = symmetric(whole) if first else sym
        alpha, inverse_out[...] = eliminated((curvature, g), (g, identity()))
        new_r[...] = r[...] - mm(image[...], alpha)
        shared = mm(whole, alpha, (0, 0))
        alpha_out[...] = alpha
        partial[...] = g - (shared + shared.T)

    return call(
        body,
        [shape(strip)] + [shape(LANES)] * 3,
        *fields,
        scratch=[pltpu.VMEM((2 * rows, LANES), F32)],
    )[:-1]


def turn(square, alpha, partial, inverse, residual, direction):
    strip = residual.shape[0]

    def body(alpha, partial, inverse, r, d, *refs):
        *terms, new_d, low, beta_out, gram_out = refs
        square = terms[0][...]
        for ref in terms[1:]:
            square = square + ref[...]
        a = alpha[...]
        following = partial[...] + mm(a, mm(unpacked_symmetric(square), a), (0, 0))
        beta = mm(inverse[...], following)
        value = r[...] + mm(d[...], beta)
        low[...] = value.astype(BF16)
        new_d[...] = value
        beta_out[...] = beta
        gram_out[...] = following

    return call(
        body,
        [shape(strip), shape(strip, dtype=BF16), shape(LANES), shape(LANES)],
        alpha,
        partial,
        inverse,
        residual,
        direction,
        *square,
    )[:-1]


def shards(couplings, observations, replicate_mask):
    links, rows = couplings.shape[1], couplings.shape[3]
    strip = couplings.shape[6]
    blocks = couplings.reshape(links, rows, couplings.shape[4], strip)
    blocks = pltpu.with_memory_space_constraint(blocks, pltpu.HBM)
    n = lax.axis_size("rhs")
    obs_matrix = observations.reshape(observations.shape[0], rows)
    parts, token = right_side_parts(obs_matrix, replicate_mask, n, strip)
    own = [parts[0]] + [swapped(parts[s], "rhs", s, n) for s in range(1, n)]
    groups = link_groups(links)
    packed = []
    for _, numbers, count in groups[:2]:
        value, token = retiled(blocks, numbers, count, token)
        packed.append(value)
    residual, low, token = sum_and_round(own, token)
    for _, numbers, count in groups[2:]:
        value, token = retiled(blocks, numbers, count, token)
        packed.append(value)
    retile_token = token
    direction = residual
    solution = gram = beta = before = alpha = None
    for step in range(ITERS):
        first, final = step == 0, step + 1 == ITERS
        state = [solution, None]

        def between(token):
            if first:
                return retile_token
            *state[:], token = stepped(solution, before, alpha, beta, token)
            return token

        parts, directions = operate(packed, groups, low, direction, between, final)
        solution, turns = state
        image_parts = [parts[0]] + [swapped(parts[s], "rhs", s, n) for s in range(1, n)]
        linear = linear_grams(parts, directions, residual, turns, first, final)
        if final:
            small = reduce_one(*linear)
            solution, residual = finish(
                small, gram, residual, direction, solution, image_parts
            )
            break
        image, square = square_gram(image_parts)
        linear, square = reduce_both(*linear, square)
        residual, alpha, partial, inverse = advance(linear, gram, residual, image)
        square[1:], alpha = lax.optimization_barrier((square[1:], alpha))
        before = directions
        direction, low, beta, gram = turn(
            square, alpha, partial, inverse, residual, direction
        )
    shape_out = (1, 1, strip, LANES)
    return (solution.reshape(shape_out), residual.reshape(shape_out))


def solution(mesh):
    placed = (
        P("panel", None, "coef", None, None, "rhs", None),
        P(("groups", "rhs"), "panel", "coef", None),
        P(("groups", "rhs"), None),
    )
    return jax.shard_map(
        shards,
        mesh=mesh,
        in_specs=placed,
        out_specs=(
            P(("groups", "panel"), "coef", "rhs", None),
            P(("groups", "panel"), "coef", "rhs", None),
        ),
        check_vma=False,
    )
```

```python
import functools

import jax
import jax.numpy as jnp
from jax import lax
from jax.experimental import pallas as pl
from jax.experimental.pallas import tpu as pltpu
from jax.sharding import PartitionSpec as P

ITERS = 3
LANES = 128
SUB = 8
VMEM_LIMIT = 14 * 2**20
F32 = jnp.float32
BF16 = jnp.bfloat16
VMEM = pl.BlockSpec(memory_space=pltpu.VMEM)
ANY = pl.BlockSpec(memory_space=pl.ANY)
HBM = pl.BlockSpec(memory_space=pltpu.HBM)


def mm(a, b, dims=(1, 0)):
    return lax.dot_general(
        a,
        b,
        (((dims[0],), (dims[1],)), ((), ())),
        precision=lax.Precision.HIGHEST,
        preferred_element_type=F32,
    )


def call(body, outs, *args, scratch=(), after=(), any_args=0, any_outs=False):
    inputs, outputs, waits = len(args), len(outs), len(after)

    def ordered(*refs):
        token = refs[inputs + waits + outputs]
        token[...] = jnp.zeros_like(token)
        body(
            *refs[:inputs],
            *refs[inputs + waits : inputs + waits + outputs],
            *refs[inputs + waits + outputs + 1 :],
        )

    return pl.pallas_call(
        ordered,
        out_shape=list(outs) + [shape(SUB)],
        in_specs=[HBM] * any_args + [VMEM] * (inputs - any_args) + [ANY] * waits,
        out_specs=[ANY if any_outs else VMEM] * outputs + [VMEM],
        scratch_shapes=list(scratch),
        cost_estimate=pl.CostEstimate(flops=1, bytes_accessed=1, transcendentals=0),
        compiler_params=pltpu.CompilerParams(vmem_limit_bytes=VMEM_LIMIT),
    )(*args, *after)


def shape(rows, cols=LANES, dtype=F32):
    return jax.ShapeDtypeStruct((rows, cols), dtype)


def permute(value, axis, pairs):
    return lax.ppermute(value, axis, pairs)


def shifted(value, axis, by):
    n = lax.axis_size(axis)
    return permute(value, axis, [((i + by) % n, i) for i in range(n)])


def mate(i, s, n):
    return i ^ s if n & (n - 1) == 0 else (s - i) % n


def swapped(value, axis, s, n):
    return permute(value, axis, [(mate(i, s, n), i) for i in range(n)])


def sum_near(value):
    axes = ("panel", "rhs")
    count = lax.axis_size(axes)
    one, two, three = (swapped(value, axes, s, count) for s in (1, 2, 3))
    return (value + one) + (two + three)


def from_far(value):
    axes = ("panel", "rhs")
    return swapped(value, axes, 4, lax.axis_size(axes))


def sum_far(value, meanwhile=None):
    other = from_far(value)
    if meanwhile is not None:
        other, _ = lax.optimization_barrier((other, meanwhile))
    return value + other


def by_stages():
    return lax.axis_size("panel") == 4 and lax.axis_size("rhs") == 2


def reduce_one(value):
    value = value + swapped(value, "coef", 1, 2)
    if not by_stages():
        return lax.psum(value, ("panel", "rhs"))
    return sum_far(sum_near(value))


def reduce_both(mine, mates, square):
    value = mine + swapped(mates, "coef", 1, 2)
    whole = square + swapped(square, "coef", 1, 2)
    if by_stages():
        rows = value.shape[0]
        value = sum_far(value, meanwhile=square)
        both = sum_near(jnp.concatenate([value, whole], axis=0))
        value, whole = both[:rows], both[rows:]
        terms = [whole, from_far(whole)]
    else:
        value, whole = lax.psum((value, whole), ("panel", "rhs"))
        terms = [whole]
    return [value, swapped(value, "coef", 1, 2)], terms


def right_side_parts(obs, mask, n, strip):
    def body(obs_hbm, mask_hbm, *refs):
        *outs, obs_ref, mask_ref, sems = refs
        copies = [
            pltpu.make_async_copy(mask_hbm, mask_ref, sems.at[0]),
            pltpu.make_async_copy(obs_hbm, obs_ref, sems.at[1]),
        ]
        for copy in copies:
            copy.start()
        for copy in copies:
            copy.wait()
        signs = (2 * mask_ref[...] - 1).astype(BF16)
        me = lax.axis_index("rhs")
        for s in range(n):
            place = pl.multiple_of(mate(me, s, n) * strip, strip)
            outs[s][...] = lax.dot_general(
                obs_ref[:, pl.ds(place, strip)],
                signs,
                (((0,), (0,)), ((), ())),
                preferred_element_type=F32,
            )

    *parts, token = call(
        body,
        [shape(strip)] * n,
        pltpu.with_memory_space_constraint(obs, pltpu.HBM),
        pltpu.with_memory_space_constraint(mask, pltpu.HBM),
        scratch=[
            pltpu.VMEM(obs.shape, BF16),
            pltpu.VMEM(mask.shape, mask.dtype),
            pltpu.SemaphoreType.DMA((2,)),
        ],
        any_args=2,
    )
    return parts, token


def sum_and_round(parts, token):
    strip = parts[0].shape[0]

    def body(*refs):
        *ins, out, low = refs
        total = ins[0][...]
        for ref in ins[1:]:
            total = total + ref[...]
        out[...] = total
        low[...] = total.astype(BF16)

    return call(
        body, [shape(strip), shape(strip, dtype=BF16)], *parts, after=[token]
    )


def retiled(blocks, links, count, token):
    rows, strip = blocks.shape[1], blocks.shape[3]
    tiles = strip // LANES

    def body(k_ref, out, sems):
        copies = []
        for i, link in enumerate(links()):
            for t in range(tiles):
                copy = pltpu.make_async_copy(
                    k_ref.at[link, :, :, pl.ds(t * LANES, LANES)], out.at[i, t], sems.at[i, t]
                )
                copy.start()
                copies.append(copy)
        for copy in copies:
            copy.wait()

    packed, token = call(
        body,
        [pltpu.VMEM((count, tiles, rows, 2, LANES), BF16)],
        blocks,
        scratch=[pltpu.SemaphoreType.DMA((count, tiles))],
        after=[token],
        any_args=1,
        any_outs=True,
    )
    return packed, token


def link_products(packed, pieces, acc, n, slots, after=()):
    tiles, rows = packed[0].shape[1:3]
    counts = [value.shape[0] for value in packed]
    many = len(packed)
    packed = [
        pltpu.with_memory_space_constraint(
            value.reshape(value.shape[0], tiles, 2 * rows, LANES), pltpu.VMEM
        )
        for value in packed
    ]
    strip = tiles * LANES
    size = rows if slots is None else rows // n
    block = min(512, 2 * size)

    def body(*refs):
        k_refs, piece_refs = refs[:many], refs[many : 3 * many]
        acc_ref = refs[3 * many] if acc is not None else None
        outs = refs[3 * many + (acc is not None) : -3]
        weights, even_acc, odd_acc = refs[-3:]
        half = lax.axis_index("coef")
        own = pl.ds(pl.multiple_of(half * LANES, LANES), LANES)
        other = pl.ds(pl.multiple_of((1 - half) * LANES, LANES), LANES)
        for g in range(many):
            weights[g, :, own] = piece_refs[2 * g][...]
            weights[g, :, other] = piece_refs[2 * g + 1][...]
        me = lax.axis_index("rhs")
        for out, s in zip(outs, [None] if slots is None else slots):
            first = 0 if s is None else pl.multiple_of(mate(me, s, n) * size, size)
            for start in range(0, 2 * size, block):
                here = slice(start, start + block)
                product = None
                for g in range(many):
                    for i in range(counts[g]):
                        left = jnp.concatenate(
                            [
                                k_refs[g][i, t, pl.ds(2 * first + start, block), :]
                                for t in range(tiles)
                            ],
                            axis=1,
                        )
                        term = jnp.dot(left, weights[g], preferred_element_type=F32)
                        product = term if product is None else product + term
                even_acc[here, :] = product[:, :LANES]
                odd_acc[here, :] = product[:, LANES:]
            even = even_acc[pl.ds(0, size, stride=2), :]
            odd = odd_acc[pl.ds(1, size, stride=2), :]
            total = even + odd
            if acc_ref is not None:
                total = total + acc_ref[pl.ds(first, size), :]
            out[...] = total

    args = [*packed, *(value for pair in pieces for value in pair)]
    args += [acc] if acc is not None else []
    *result, token = call(
        body,
        [shape(size)] * (1 if slots is None else len(slots)),
        *args,
        scratch=[
            pltpu.VMEM((many, strip, 2 * LANES), BF16),
            pltpu.VMEM((2 * size, LANES), F32),
            pltpu.VMEM((2 * size, LANES), F32),
        ],
        after=after,
    )
    return result, token


def link_groups(links):
    reach = (links - 1) // 2
    panels = lax.axis_size("panel")
    groups = []
    if links == 2 * panels + 1 and panels & (panels - 1) == 0:
        for s in range(panels):

            def numbers(s=s):
                me = lax.axis_index("panel")
                start = lax.rem((me ^ s) - me + reach + panels, panels)
                return [start + panels * i for i in range(3 if s == 0 else 2)]

            bring = functools.partial(swapped, axis="panel", s=s, n=panels)
            groups.append((bring, numbers, 3 if s == 0 else 2))
        return groups
    offsets = {}
    for link in range(links):
        offsets.setdefault((link - reach) % panels, []).append(link)
    for o in sorted(offsets, key=lambda o: min(o, panels - o)):
        bring = functools.partial(shifted, axis="panel", by=o)
        groups.append((bring, functools.partial(list, offsets[o]), len(offsets[o])))
    return groups


def operate(packed, groups, low, direction, between, final):
    n = lax.axis_size("rhs")
    arrived = [low] + [bring(low) for bring, _, _ in groups[1:]]
    if len(groups) == lax.axis_size("panel") == 4:
        inner = permute(low, "panel", [(1, 2), (2, 1)])
        arrived[3] = inner + permute(arrived[2], "panel", [(2, 3), (1, 0)])
    directions = [direction] + [swapped(direction, "rhs", s, n) for s in range(1, n)]
    pairs = [[low, swapped(low, "coef", 1, 2)]]
    (acc,), token = link_products(packed[:1], pairs, None, n, None)
    after = (token, between(token))
    for piece in arrived[1:]:
        piece, _ = lax.optimization_barrier((piece, after))
        pairs.append([piece, swapped(piece, "coef", 1, 2)])
    after = (*after, *directions[1:])
    if len(groups) > 2:
        (acc,), _ = link_products(packed[1:-1], pairs[1:-1], acc, n, None, after)
    if final:
        parts, _ = link_products(packed[-1:], pairs[-1:], acc, n, range(n), after)
        return parts, directions
    mates, token = link_products(packed[-1:], pairs[-1:], acc, n, range(1, n), after)
    own, _ = link_products(packed[-1:], pairs[-1:], acc, n, [0], (token,))
    return own + mates, directions


PACKED = LANES // 2 + SUB


def corner():
    row = lax.broadcasted_iota(jnp.int32, (LANES // 2, LANES), 0)
    lane = lax.broadcasted_iota(jnp.int32, (LANES // 2, LANES), 1)
    return row, lane, lane < LANES // 2


def packed_symmetric(matrix):
    half = LANES // 2
    row, lane, left = corner()
    top = matrix[:half]
    last = pltpu.roll(matrix[half:], half, 1)
    body = jnp.where(left & (lane > row), last, top)
    diagonal = jnp.sum(jnp.where(lane == row, last, 0.0), axis=0, keepdims=True)
    return jnp.concatenate([body, jnp.broadcast_to(diagonal, (SUB, LANES))], axis=0)


def unpacked_symmetric(rows):
    half = LANES // 2
    row, lane, left = corner()
    body, diagonal = rows[:half], rows[half : half + 1]
    top = jnp.where(left & (lane >= row), 0.0, body)
    last = jnp.where(left & (lane > row), body, 0.0)
    sides = jnp.concatenate([top, pltpu.roll(last, half, 1)], axis=0)
    top = jnp.where(lane == row, body, 0.0)
    last = jnp.where(lane == row, jnp.broadcast_to(diagonal, body.shape), 0.0)
    return sides + sides.T + jnp.concatenate([top, pltpu.roll(last, half, 1)], axis=0)


def symmetric(raw):
    return 0.5 * (raw + raw.T)


JOINT = PACKED + SUB + LANES


def linear_grams(parts, directions, residual, turns, first, final):
    strip = parts[0].shape[0]
    n = len(parts)
    extra = [] if first or final else [residual, *turns]
    rows = PACKED if final else JOINT // 2

    def body(*refs):
        images, ds = refs[:n], refs[n : 2 * n]
        rest = refs[2 * n : 2 * n + len(extra)]
        outs = refs[2 * n + len(extra) :]
        found = None
        for s in range(n):
            image, right = images[s][...], ds[s][...]
            if extra:
                r = rest[0][...] if s == 0 else right - rest[s][...]
                right = jnp.concatenate([right, r], axis=1)
            term = mm(image, right, (0, 0))
            found = term if s == 0 else found + term
        if final:
            outs[0][...] = packed_symmetric(symmetric(found))
            return
        mine, mates, stacked = outs
        if first:
            r = ds[0][...]
            sym, whole = mm(r, r, (0, 0)), found
        else:
            sym, whole = symmetric(found[:, :LANES]), found[:, LANES:]
        stacked[:PACKED] = packed_symmetric(sym)
        stacked[PACKED : PACKED + SUB] = jnp.zeros((SUB, LANES), F32)
        stacked[PACKED + SUB :] = whole
        half = lax.axis_index("coef")
        mine[...] = stacked[pl.ds(pl.multiple_of(half * rows, SUB), rows), :]
        mates[...] = stacked[pl.ds(pl.multiple_of((1 - half) * rows, SUB), rows), :]

    *pieces, _ = call(
        body,
        [shape(rows)] * (1 if final else 2),
        *parts,
        *directions,
        *extra,
        scratch=[] if final else [pltpu.VMEM((2 * rows, LANES), F32)],
    )
    return pieces


def square_gram(image_parts):
    strip = image_parts[0].shape[0]
    parts = len(image_parts)

    def body(*refs):
        ins, image_out, out = refs[:parts], refs[parts], refs[parts + 1]
        image = ins[0][...]
        for ref in ins[1:]:
            image = image + ref[...]
        image_out[...] = image
        out[...] = packed_symmetric(mm(image, image, (0, 0)))

    image, square, _ = call(
        body,
        [shape(strip), shape(PACKED)],
        *image_parts,
    )
    return image, square


def reciprocal(value):
    near = pl.reciprocal(value, approx=True)
    for _ in range(2):
        near = near * (2.0 - value * near)
    return near


def next_pivot(column, following, i, inverse):
    product = column[i + 1 : i + 2] * following[i : i + 1]
    return following[i + 1 : i + 2] - product * inverse


def inverted(matrices, lane):
    strips = matrices[0].shape[0] // SUB
    place = lax.broadcasted_iota(jnp.int32, (SUB, LANES), 0)
    held = [[value[SUB * k : SUB * (k + 1)] for k in range(strips)] for value in matrices]

    def lanes_of(value, at):
        return jnp.broadcast_to(value[:, at : at + 1], (SUB, LANES))

    def rows_of(value):
        return [jnp.broadcast_to(value[i : i + 1], (SUB, LANES)) for i in range(SUB)]

    def update(k, j, spread):
        for a, rows in zip(held, spread):
            row = a[k]
            for i in range(SUB):
                row = row - lanes_of(a[k], lane + SUB * j + i) * rows[i]
            a[k] = row

    for j in range(strips):
        if j:
            spread = [rows_of(a[j - 1]) for a in held]
            update(j, j - 1, spread)
        waiting = [k for k in range(strips) if j and k not in (j, j - 1)]
        now = [
            [a[j], *(lanes_of(a[j], lane + SUB * j + i) for i in range(SUB))] for a in held
        ]
        for i in range(SUB):
            here = place == i
            for index, values in enumerate(now):
                column = values[1 + i]
                inverse = 1.0 / column[i : i + 1]

                def step(value):
                    row = value[i : i + 1] * inverse
                    return jnp.where(here, row, value - column * row)

                now[index] = [
                    step(value) if at < 1 or at > 1 + i else value
                    for at, value in enumerate(values)
                ]
            for k in waiting[i : i + 1]:
                update(k, j - 1, spread)
        for a, values in zip(held, now):
            a[j] = values[0]
    spread = [rows_of(a[-1]) for a in held]
    for k in range(strips - 1):
        update(k, strips - 1, spread)
    return [jnp.concatenate(a, axis=0) for a in held]


def eliminated(*systems):
    half = LANES // 2
    row = lax.broadcasted_iota(jnp.int32, (half, LANES), 0)
    lane = lax.broadcasted_iota(jnp.int32, (half, LANES), 1)
    left = lane < half
    first = inverted(
        [
            jnp.where(left, matrix[:half], (lane - half == row).astype(F32))
            for matrix, _ in systems
        ],
        0,
    )
    tops, lasts = [], []
    for (matrix, sides), value in zip(systems, first):
        value = pltpu.roll(value, half, 1)[:, :half]
        top = mm(value, jnp.concatenate([matrix[:half], sides[:half]], axis=1))
        low = jnp.concatenate([matrix[half:], sides[half:]], axis=1)
        tops.append(top)
        lasts.append(low - mm(matrix[half:, :half], top))
    second = inverted(
        [jnp.where(left, (lane == row).astype(F32), last[:, :LANES]) for last in lasts], half
    )
    found = []
    for top, last, value in zip(tops, lasts, second):
        low = mm(value[:, :half], last[:, LANES:])
        high = top[:, LANES:] - mm(
            top[:, :LANES], jnp.concatenate([jnp.zeros_like(low), low], axis=0)
        )
        found.append(jnp.concatenate([high, low], axis=0))
    return found


def eliminated_alone(matrix, sides):
    n = matrix.shape[0]
    strips = n // SUB
    place = lax.broadcasted_iota(jnp.int32, (SUB, LANES), 0)

    def cut(value):
        return [value[SUB * k : SUB * (k + 1)] for k in range(strips)]

    def lanes_of(value, lane):
        return jnp.broadcast_to(value[:, lane : lane + 1], (SUB, LANES))

    held = [(cut(matrix), cut(sides))]

    def rows_of(value):
        return [jnp.broadcast_to(value[i : i + 1], (SUB, LANES)) for i in range(SUB)]

    def update(k, j, spread):
        for (a, b), (rows_a, rows_b) in zip(held, spread):
            row_a, row_b = a[k], b[k]
            for i in range(SUB):
                factor = lanes_of(a[k], SUB * j + i)
                row_a = row_a - factor * rows_a[i]
                row_b = row_b - factor * rows_b[i]
            a[k], b[k] = row_a, row_b

    for j in range(strips):
        if j:
            spread = [(rows_of(a[j - 1]), rows_of(b[j - 1])) for a, b in held]
            update(j, j - 1, spread)
        waiting = [k for k in range(strips) if j and k not in (j, j - 1)]
        now = [
            [a[j], b[j], *(lanes_of(a[j], SUB * j + i) for i in range(SUB))] for a, b in held
        ]
        pivots = [values[2][:1] for values in now]
        for i in range(SUB):
            here = place == i
            for index, values in enumerate(now):
                column = values[2 + i]
                inverse = reciprocal(pivots[index])
                if i + 1 < SUB:
                    pivots[index] = next_pivot(column, values[3 + i], i, inverse)

                def step(value):
                    row = value[i : i + 1] * inverse
                    return jnp.where(here, row, value - column * row)

                now[index] = [
                    step(value) if place_of < 2 or place_of > 2 + i else value
                    for place_of, value in enumerate(values)
                ]
            for k in waiting[2 * i : 2 * i + 2]:
                update(k, j - 1, spread)
        for (a, b), values in zip(held, now):
            a[j], b[j] = values[:2]
    spread = [(rows_of(a[-1]), rows_of(b[-1])) for a, b in held]
    for k in range(strips - 1):
        update(k, strips - 1, spread)
    return jnp.concatenate(held[0][1], axis=0)


def identity():
    return (
        lax.broadcasted_iota(jnp.int32, (LANES, LANES), 0)
        == lax.broadcasted_iota(jnp.int32, (LANES, LANES), 1)
    ).astype(F32)


def stepped(solution, before, alpha, beta, token):
    fields = [*before, alpha, beta] + ([] if solution is None else [solution])
    n = len(before)

    def body(*refs):
        ds, a, b, refs = refs[:n], refs[n], refs[n + 1], refs[n + 2 :]
        change = mm(ds[0][...], a[...])
        refs[-n][...] = change if solution is None else refs[0][...] + change
        for s in range(1, n):
            refs[s - n][...] = mm(ds[s][...], b[...])

    solution, *turns, token = call(
        body, [shape(before[0].shape[0])] * n, *fields, after=[token]
    )
    return solution, turns, token


def finish(small, gram, residual, direction, solution, image):
    strip = residual.shape[0]

    def body(small, g, r, d, s, *refs):
        *images, out, new_r = refs
        alpha = eliminated_alone(unpacked_symmetric(small[...]), g[...])
        image = images[0][...]
        for ref in images[1:]:
            image = image + ref[...]
        out[...] = s[...] + mm(d[...], alpha)
        new_r[...] = r[...] - mm(image, alpha)

    return call(
        body,
        [shape(strip), shape(strip)],
        small,
        gram,
        residual,
        direction,
        solution,
        *image,
    )[:-1]


def advance(pieces, gram, residual, image):
    strip = residual.shape[0]
    rows = pieces[0].shape[0]
    first = gram is None
    fields = [*pieces, residual, image] + ([] if first else [gram])

    def body(*refs):
        mine, mates, r, image, *refs = refs
        *refs, raw = refs
        half = lax.axis_index("coef")
        raw[pl.ds(pl.multiple_of(half * rows, SUB), rows), :] = mine[...]
        raw[pl.ds(pl.multiple_of((1 - half) * rows, SUB), rows), :] = mates[...]
        sym, whole = unpacked_symmetric(raw[:PACKED, :]), raw[PACKED + SUB :, :]
        *refs, new_r, alpha_out, partial, inverse_out = refs
        g = sym if first else refs[0][...]
        curvature = symmetric(whole) if first else sym
        alpha, inverse_out[...] = eliminated((curvature, g), (g, identity()))
        new_r[...] = r[...] - mm(image[...], alpha)
        shared = mm(whole, alpha, (0, 0))
        alpha_out[...] = alpha
        partial[...] = g - (shared + shared.T)

    return call(
        body,
        [shape(strip)] + [shape(LANES)] * 3,
        *fields,
        scratch=[pltpu.VMEM((2 * rows, LANES), F32)],
    )[:-1]


def turn(square, alpha, partial, inverse, residual, direction):
    strip = residual.shape[0]

    def body(alpha, partial, inverse, r, d, *refs):
        *terms, new_d, low, beta_out, gram_out = refs
        square = terms[0][...]
        for ref in terms[1:]:
            square = square + ref[...]
        a = alpha[...]
        following = partial[...] + mm(a, mm(unpacked_symmetric(square), a), (0, 0))
        beta = mm(inverse[...], following)
        value = r[...] + mm(d[...], beta)
        low[...] = value.astype(BF16)
        new_d[...] = value
        beta_out[...] = beta
        gram_out[...] = following

    return call(
        body,
        [shape(strip), shape(strip, dtype=BF16), shape(LANES), shape(LANES)],
        alpha,
        partial,
        inverse,
        residual,
        direction,
        *square,
    )[:-1]


def shards(couplings, observations, replicate_mask):
    links, rows = couplings.shape[1], couplings.shape[3]
    strip = couplings.shape[6]
    blocks = couplings.reshape(links, rows, couplings.shape[4], strip)
    blocks = pltpu.with_memory_space_constraint(blocks, pltpu.HBM)
    n = lax.axis_size("rhs")
    obs_matrix = observations.reshape(observations.shape[0], rows)
    parts, token = right_side_parts(obs_matrix, replicate_mask, n, strip)
    own = [parts[0]] + [swapped(parts[s], "rhs", s, n) for s in range(1, n)]
    groups = link_groups(links)
    packed = []
    for _, numbers, count in groups[:2]:
        value, token = retiled(blocks, numbers, count, token)
        packed.append(value)
    residual, low, token = sum_and_round(own, token)
    for _, numbers, count in groups[2:]:
        value, token = retiled(blocks, numbers, count, token)
        packed.append(value)
    retile_token = token
    direction = residual
    solution = gram = beta = before = alpha = None
    for step in range(ITERS):
        first, final = step == 0, step + 1 == ITERS
        state = [solution, None]

        def between(token):
            if first:
                return retile_token
            *state[:], token = stepped(solution, before, alpha, beta, token)
            return token

        parts, directions = operate(packed, groups, low, direction, between, final)
        solution, turns = state
        image_parts = [parts[0]] + [swapped(parts[s], "rhs", s, n) for s in range(1, n)]
        linear = linear_grams(parts, directions, residual, turns, first, final)
        if final:
            small = reduce_one(*linear)
            solution, residual = finish(
                small, gram, residual, direction, solution, image_parts
            )
            break
        image, square = square_gram(image_parts)
        linear, square = reduce_both(*linear, square)
        residual, alpha, partial, inverse = advance(linear, gram, residual, image)
        square[1:], alpha = lax.optimization_barrier((square[1:], alpha))
        before = directions
        direction, low, beta, gram = turn(
            square, alpha, partial, inverse, residual, direction
        )
    shape_out = (1, 1, strip, LANES)
    return (solution.reshape(shape_out), residual.reshape(shape_out))


def solution(mesh):
    placed = (
        P("panel", None, "coef", None, None, "rhs", None),
        P(("groups", "rhs"), "panel", "coef", None),
        P(("groups", "rhs"), None),
    )
    return jax.shard_map(
        shards,
        mesh=mesh,
        in_specs=placed,
        out_specs=(
            P(("groups", "panel"), "coef", "rhs", None),
            P(("groups", "panel"), "coef", "rhs", None),
        ),
        check_vma=False,
    )
```

```python
import functools

import jax
import jax.numpy as jnp
from jax import lax
from jax.experimental import pallas as pl
from jax.experimental.pallas import tpu as pltpu
from jax.sharding import PartitionSpec as P

ITERS = 3
LANES = 128
SUB = 8
VMEM_LIMIT = 14 * 2**20
F32 = jnp.float32
BF16 = jnp.bfloat16
VMEM = pl.BlockSpec(memory_space=pltpu.VMEM)
ANY = pl.BlockSpec(memory_space=pl.ANY)
HBM = pl.BlockSpec(memory_space=pltpu.HBM)


def mm(a, b, dims=(1, 0)):
    return lax.dot_general(
        a,
        b,
        (((dims[0],), (dims[1],)), ((), ())),
        precision=lax.Precision.HIGHEST,
        preferred_element_type=F32,
    )


def call(body, outs, *args, scratch=(), after=(), any_args=0, any_outs=False):
    inputs, outputs, waits = len(args), len(outs), len(after)

    def ordered(*refs):
        token = refs[inputs + waits + outputs]
        token[...] = jnp.zeros_like(token)
        body(
            *refs[:inputs],
            *refs[inputs + waits : inputs + waits + outputs],
            *refs[inputs + waits + outputs + 1 :],
        )

    return pl.pallas_call(
        ordered,
        out_shape=list(outs) + [shape(SUB)],
        in_specs=[HBM] * any_args + [VMEM] * (inputs - any_args) + [ANY] * waits,
        out_specs=[ANY if any_outs else VMEM] * outputs + [VMEM],
        scratch_shapes=list(scratch),
        cost_estimate=pl.CostEstimate(flops=1, bytes_accessed=1, transcendentals=0),
        compiler_params=pltpu.CompilerParams(vmem_limit_bytes=VMEM_LIMIT),
    )(*args, *after)


def shape(rows, cols=LANES, dtype=F32):
    return jax.ShapeDtypeStruct((rows, cols), dtype)


def permute(value, axis, pairs):
    return lax.ppermute(value, axis, pairs)


def shifted(value, axis, by):
    n = lax.axis_size(axis)
    return permute(value, axis, [((i + by) % n, i) for i in range(n)])


def mate(i, s, n):
    return i ^ s if n & (n - 1) == 0 else (s - i) % n


def swapped(value, axis, s, n):
    return permute(value, axis, [(mate(i, s, n), i) for i in range(n)])


def sum_near(value):
    axes = ("panel", "rhs")
    count = lax.axis_size(axes)
    three, two, one = (swapped(value, axes, s, count) for s in (3, 2, 1))
    return (value + one) + (two + three)


def from_far(value):
    axes = ("panel", "rhs")
    return swapped(value, axes, 4, lax.axis_size(axes))


def sum_far(value, meanwhile=None):
    other = from_far(value)
    if meanwhile is not None:
        other, _ = lax.optimization_barrier((other, meanwhile))
    return value + other


def by_stages():
    return lax.axis_size("panel") == 4 and lax.axis_size("rhs") == 2


def reduce_one(value):
    value = value + swapped(value, "coef", 1, 2)
    if not by_stages():
        return lax.psum(value, ("panel", "rhs"))
    return sum_far(sum_near(value))


def reduce_both(mine, mates, square):
    value = mine + swapped(mates, "coef", 1, 2)
    whole = square + swapped(square, "coef", 1, 2)
    if by_stages():
        rows = value.shape[0]
        value = sum_far(value, meanwhile=square)
        both = sum_near(jnp.concatenate([value, whole], axis=0))
        value, whole = both[:rows], both[rows:]
        terms = [whole, from_far(whole)]
    else:
        value, whole = lax.psum((value, whole), ("panel", "rhs"))
        terms = [whole]
    return [value, swapped(value, "coef", 1, 2)], terms


def right_side_parts(obs, mask, n, strip):
    def body(obs_hbm, mask_hbm, *refs):
        *outs, obs_ref, mask_ref, sems = refs
        copies = [
            pltpu.make_async_copy(mask_hbm, mask_ref, sems.at[0]),
            pltpu.make_async_copy(obs_hbm, obs_ref, sems.at[1]),
        ]
        for copy in copies:
            copy.start()
        for copy in copies:
            copy.wait()
        signs = (2 * mask_ref[...] - 1).astype(BF16)
        me = lax.axis_index("rhs")
        for s in range(n):
            place = pl.multiple_of(mate(me, s, n) * strip, strip)
            outs[s][...] = lax.dot_general(
                obs_ref[:, pl.ds(place, strip)],
                signs,
                (((0,), (0,)), ((), ())),
                preferred_element_type=F32,
            )

    *parts, token = call(
        body,
        [shape(strip)] * n,
        pltpu.with_memory_space_constraint(obs, pltpu.HBM),
        pltpu.with_memory_space_constraint(mask, pltpu.HBM),
        scratch=[
            pltpu.VMEM(obs.shape, BF16),
            pltpu.VMEM(mask.shape, mask.dtype),
            pltpu.SemaphoreType.DMA((2,)),
        ],
        any_args=2,
    )
    return parts, token


def sum_and_round(parts, token):
    strip = parts[0].shape[0]

    def body(*refs):
        *ins, out, low = refs
        total = ins[0][...]
        for ref in ins[1:]:
            total = total + ref[...]
        out[...] = total
        low[...] = total.astype(BF16)

    return call(
        body, [shape(strip), shape(strip, dtype=BF16)], *parts, after=[token]
    )


def retiled(blocks, links, count, token):
    rows, strip = blocks.shape[1], blocks.shape[3]
    tiles = strip // LANES

    def body(k_ref, out, sems):
        copies = []
        for i, link in enumerate(links()):
            for t in range(tiles):
                copy = pltpu.make_async_copy(
                    k_ref.at[link, :, :, pl.ds(t * LANES, LANES)], out.at[i, t], sems.at[i, t]
                )
                copy.start()
                copies.append(copy)
        for copy in copies:
            copy.wait()

    packed, token = call(
        body,
        [pltpu.VMEM((count, tiles, rows, 2, LANES), BF16)],
        blocks,
        scratch=[pltpu.SemaphoreType.DMA((count, tiles))],
        after=[token],
        any_args=1,
        any_outs=True,
    )
    return packed, token


def link_products(packed, pieces, acc, n, slots, after=()):
    tiles, rows = packed[0].shape[1:3]
    counts = [value.shape[0] for value in packed]
    many = len(packed)
    packed = [
        pltpu.with_memory_space_constraint(
            value.reshape(value.shape[0], tiles, 2 * rows, LANES), pltpu.VMEM
        )
        for value in packed
    ]
    strip = tiles * LANES
    size = rows if slots is None else rows // n
    block = min(512, 2 * size)

    def body(*refs):
        k_refs, piece_refs = refs[:many], refs[many : 3 * many]
        acc_ref = refs[3 * many] if acc is not None else None
        outs = refs[3 * many + (acc is not None) : -3]
        weights, even_acc, odd_acc = refs[-3:]
        half = lax.axis_index("coef")
        own = pl.ds(pl.multiple_of(half * LANES, LANES), LANES)
        other = pl.ds(pl.multiple_of((1 - half) * LANES, LANES), LANES)
        for g in range(many):
            weights[g, :, own] = piece_refs[2 * g][...]
            weights[g, :, other] = piece_refs[2 * g + 1][...]
        me = lax.axis_index("rhs")
        for out, s in zip(outs, [None] if slots is None else slots):
            first = 0 if s is None else pl.multiple_of(mate(me, s, n) * size, size)
            for start in range(0, 2 * size, block):
                here = slice(start, start + block)
                product = None
                for g in range(many):
                    for i in range(counts[g]):
                        left = jnp.concatenate(
                            [
                                k_refs[g][i, t, pl.ds(2 * first + start, block), :]
                                for t in range(tiles)
                            ],
                            axis=1,
                        )
                        term = jnp.dot(left, weights[g], preferred_element_type=F32)
                        product = term if product is None else product + term
                even_acc[here, :] = product[:, :LANES]
                odd_acc[here, :] = product[:, LANES:]
            even = even_acc[pl.ds(0, size, stride=2), :]
            odd = odd_acc[pl.ds(1, size, stride=2), :]
            total = even + odd
            if acc_ref is not None:
                total = total + acc_ref[pl.ds(first, size), :]
            out[...] = total

    args = [*packed, *(value for pair in pieces for value in pair)]
    args += [acc] if acc is not None else []
    *result, token = call(
        body,
        [shape(size)] * (1 if slots is None else len(slots)),
        *args,
        scratch=[
            pltpu.VMEM((many, strip, 2 * LANES), BF16),
            pltpu.VMEM((2 * size, LANES), F32),
            pltpu.VMEM((2 * size, LANES), F32),
        ],
        after=after,
    )
    return result, token


def link_groups(links):
    reach = (links - 1) // 2
    panels = lax.axis_size("panel")
    groups = []
    if links == 2 * panels + 1 and panels & (panels - 1) == 0:
        for s in range(panels):

            def numbers(s=s):
                me = lax.axis_index("panel")
                start = lax.rem((me ^ s) - me + reach + panels, panels)
                return [start + panels * i for i in range(3 if s == 0 else 2)]

            bring = functools.partial(swapped, axis="panel", s=s, n=panels)
            groups.append((bring, numbers, 3 if s == 0 else 2))
        return groups
    offsets = {}
    for link in range(links):
        offsets.setdefault((link - reach) % panels, []).append(link)
    for o in sorted(offsets, key=lambda o: min(o, panels - o)):
        bring = functools.partial(shifted, axis="panel", by=o)
        groups.append((bring, functools.partial(list, offsets[o]), len(offsets[o])))
    return groups


def operate(packed, groups, low, direction, between, final):
    n = lax.axis_size("rhs")
    arrived = [low] + [bring(low) for bring, _, _ in groups[1:]]
    directions = [direction] + [swapped(direction, "rhs", s, n) for s in range(1, n)]
    pairs = [[low, swapped(low, "coef", 1, 2)]]
    (acc,), token = link_products(packed[:1], pairs, None, n, None)
    after = (token, between(token))
    for piece in arrived[1:]:
        piece, _ = lax.optimization_barrier((piece, after))
        pairs.append([piece, swapped(piece, "coef", 1, 2)])
    after = (*after, *directions[1:])
    if len(groups) > 2:
        (acc,), _ = link_products(packed[1:-1], pairs[1:-1], acc, n, None, after)
    if final:
        parts, _ = link_products(packed[-1:], pairs[-1:], acc, n, range(n), after)
        return parts, directions
    mates, token = link_products(packed[-1:], pairs[-1:], acc, n, range(1, n), after)
    own, _ = link_products(packed[-1:], pairs[-1:], acc, n, [0], (token,))
    return own + mates, directions


PACKED = LANES // 2 + SUB


def corner():
    row = lax.broadcasted_iota(jnp.int32, (LANES // 2, LANES), 0)
    lane = lax.broadcasted_iota(jnp.int32, (LANES // 2, LANES), 1)
    return row, lane, lane < LANES // 2


def packed_symmetric(matrix):
    half = LANES // 2
    row, lane, left = corner()
    top = matrix[:half]
    last = pltpu.roll(matrix[half:], half, 1)
    body = jnp.where(left & (lane > row), last, top)
    diagonal = jnp.sum(jnp.where(lane == row, last, 0.0), axis=0, keepdims=True)
    return jnp.concatenate([body, jnp.broadcast_to(diagonal, (SUB, LANES))], axis=0)


def unpacked_symmetric(rows):
    half = LANES // 2
    row, lane, left = corner()
    body, diagonal = rows[:half], rows[half : half + 1]
    top = jnp.where(left & (lane >= row), 0.0, body)
    last = jnp.where(left & (lane > row), body, 0.0)
    sides = jnp.concatenate([top, pltpu.roll(last, half, 1)], axis=0)
    top = jnp.where(lane == row, body, 0.0)
    last = jnp.where(lane == row, jnp.broadcast_to(diagonal, body.shape), 0.0)
    return sides + sides.T + jnp.concatenate([top, pltpu.roll(last, half, 1)], axis=0)


def symmetric(raw):
    return 0.5 * (raw + raw.T)


JOINT = PACKED + SUB + LANES


def linear_grams(parts, directions, residual, turns, gram, final):
    strip = parts[0].shape[0]
    n = len(parts)
    first = gram is not None
    extra = [gram] if first else [] if final else [residual, *turns]
    rows = PACKED if final else JOINT // 2

    def body(*refs):
        images, ds = refs[:n], refs[n : 2 * n]
        rest = refs[2 * n : 2 * n + len(extra)]
        outs = refs[2 * n + len(extra) :]
        found = None
        for s in range(n):
            image, right = images[s][...], ds[s][...]
            if extra and not first:
                r = rest[0][...] if s == 0 else right - rest[s][...]
                right = jnp.concatenate([right, r], axis=1)
            term = mm(image, right, (0, 0))
            found = term if s == 0 else found + term
        if final:
            outs[0][...] = packed_symmetric(symmetric(found))
            return
        mine, mates, stacked = outs
        if first:
            stacked[:PACKED], whole = rest[0][...], found
        else:
            stacked[:PACKED] = packed_symmetric(symmetric(found[:, :LANES]))
            whole = found[:, LANES:]
        stacked[PACKED : PACKED + SUB] = jnp.zeros((SUB, LANES), F32)
        stacked[PACKED + SUB :] = whole
        half = lax.axis_index("coef")
        mine[...] = stacked[pl.ds(pl.multiple_of(half * rows, SUB), rows), :]
        mates[...] = stacked[pl.ds(pl.multiple_of((1 - half) * rows, SUB), rows), :]

    *pieces, _ = call(
        body,
        [shape(rows)] * (1 if final else 2),
        *parts,
        *directions,
        *extra,
        scratch=[] if final else [pltpu.VMEM((2 * rows, LANES), F32)],
    )
    return pieces


def gram_of(field, *tokens):
    def body(field, out):
        value = field[...]
        out[...] = packed_symmetric(mm(value, value, (0, 0)))

    return call(body, [shape(PACKED)], field, after=tokens)


def square_gram(image_parts):
    strip = image_parts[0].shape[0]
    parts = len(image_parts)

    def body(*refs):
        ins, image_out, out = refs[:parts], refs[parts], refs[parts + 1]
        image = ins[0][...]
        for ref in ins[1:]:
            image = image + ref[...]
        image_out[...] = image
        out[...] = packed_symmetric(mm(image, image, (0, 0)))

    image, square, _ = call(
        body,
        [shape(strip), shape(PACKED)],
        *image_parts,
    )
    return image, square


def reciprocal(value):
    near = pl.reciprocal(value, approx=True)
    for _ in range(2):
        near = near * (2.0 - value * near)
    return near


def next_pivot(column, following, i, inverse):
    product = column[i + 1 : i + 2] * following[i : i + 1]
    return following[i + 1 : i + 2] - product * inverse


def inverted(matrices, lane):
    strips = matrices[0].shape[0] // SUB
    place = lax.broadcasted_iota(jnp.int32, (SUB, LANES), 0)
    held = [[value[SUB * k : SUB * (k + 1)] for k in range(strips)] for value in matrices]

    def lanes_of(value, at):
        return jnp.broadcast_to(value[:, at : at + 1], (SUB, LANES))

    def rows_of(value):
        return [jnp.broadcast_to(value[i : i + 1], (SUB, LANES)) for i in range(SUB)]

    def update(k, j, spread):
        for a, rows in zip(held, spread):
            row = a[k]
            for i in range(SUB):
                row = row - lanes_of(a[k], lane + SUB * j + i) * rows[i]
            a[k] = row

    for j in range(strips):
        if j:
            spread = [rows_of(a[j - 1]) for a in held]
            update(j, j - 1, spread)
        waiting = [k for k in range(strips) if j and k not in (j, j - 1)]
        now = [
            [a[j], *(lanes_of(a[j], lane + SUB * j + i) for i in range(SUB))] for a in held
        ]
        for i in range(SUB):
            here = place == i
            for index, values in enumerate(now):
                column = values[1 + i]
                inverse = 1.0 / column[i : i + 1]

                def step(value):
                    row = value[i : i + 1] * inverse
                    return jnp.where(here, row, value - column * row)

                now[index] = [
                    step(value) if at < 1 or at > 1 + i else value
                    for at, value in enumerate(values)
                ]
            for k in waiting[i : i + 1]:
                update(k, j - 1, spread)
        for a, values in zip(held, now):
            a[j] = values[0]
    spread = [rows_of(a[-1]) for a in held]
    for k in range(strips - 1):
        update(k, strips - 1, spread)
    return [jnp.concatenate(a, axis=0) for a in held]


def eliminated(*systems):
    half = LANES // 2
    row = lax.broadcasted_iota(jnp.int32, (half, LANES), 0)
    lane = lax.broadcasted_iota(jnp.int32, (half, LANES), 1)
    left = lane < half
    first = inverted(
        [
            jnp.where(left, matrix[:half], (lane - half == row).astype(F32))
            for matrix, _ in systems
        ],
        0,
    )
    tops, lasts = [], []
    for (matrix, sides), value in zip(systems, first):
        value = pltpu.roll(value, half, 1)[:, :half]
        top = mm(value, jnp.concatenate([matrix[:half], sides[:half]], axis=1))
        low = jnp.concatenate([matrix[half:], sides[half:]], axis=1)
        tops.append(top)
        lasts.append(low - mm(matrix[half:, :half], top))
    second = inverted(
        [jnp.where(left, (lane == row).astype(F32), last[:, :LANES]) for last in lasts], half
    )
    found = []
    for top, last, value in zip(tops, lasts, second):
        low = mm(value[:, :half], last[:, LANES:])
        high = top[:, LANES:] - mm(
            top[:, :LANES], jnp.concatenate([jnp.zeros_like(low), low], axis=0)
        )
        found.append(jnp.concatenate([high, low], axis=0))
    return found


def eliminated_alone(matrix, sides):
    n = matrix.shape[0]
    strips = n // SUB
    place = lax.broadcasted_iota(jnp.int32, (SUB, LANES), 0)

    def cut(value):
        return [value[SUB * k : SUB * (k + 1)] for k in range(strips)]

    def lanes_of(value, lane):
        return jnp.broadcast_to(value[:, lane : lane + 1], (SUB, LANES))

    held = [(cut(matrix), cut(sides))]

    def rows_of(value):
        return [jnp.broadcast_to(value[i : i + 1], (SUB, LANES)) for i in range(SUB)]

    def update(k, j, spread):
        for (a, b), (rows_a, rows_b) in zip(held, spread):
            row_a, row_b = a[k], b[k]
            for i in range(SUB):
                factor = lanes_of(a[k], SUB * j + i)
                row_a = row_a - factor * rows_a[i]
                row_b = row_b - factor * rows_b[i]
            a[k], b[k] = row_a, row_b

    for j in range(strips):
        if j:
            spread = [(rows_of(a[j - 1]), rows_of(b[j - 1])) for a, b in held]
            update(j, j - 1, spread)
        waiting = [k for k in range(strips) if j and k not in (j, j - 1)]
        now = [
            [a[j], b[j], *(lanes_of(a[j], SUB * j + i) for i in range(SUB))] for a, b in held
        ]
        pivots = [values[2][:1] for values in now]
        for i in range(SUB):
            here = place == i
            for index, values in enumerate(now):
                column = values[2 + i]
                inverse = reciprocal(pivots[index])
                if i + 1 < SUB:
                    pivots[index] = next_pivot(column, values[3 + i], i, inverse)

                def step(value):
                    row = value[i : i + 1] * inverse
                    return jnp.where(here, row, value - column * row)

                now[index] = [
                    step(value) if place_of < 2 or place_of > 2 + i else value
                    for place_of, value in enumerate(values)
                ]
            for k in waiting[2 * i : 2 * i + 2]:
                update(k, j - 1, spread)
        for (a, b), values in zip(held, now):
            a[j], b[j] = values[:2]
    spread = [(rows_of(a[-1]), rows_of(b[-1])) for a, b in held]
    for k in range(strips - 1):
        update(k, strips - 1, spread)
    return jnp.concatenate(held[0][1], axis=0)


def identity():
    return (
        lax.broadcasted_iota(jnp.int32, (LANES, LANES), 0)
        == lax.broadcasted_iota(jnp.int32, (LANES, LANES), 1)
    ).astype(F32)


def stepped(solution, before, alpha, beta, token):
    fields = [*before, alpha, beta] + ([] if solution is None else [solution])
    n = len(before)

    def body(*refs):
        ds, a, b, refs = refs[:n], refs[n], refs[n + 1], refs[n + 2 :]
        change = mm(ds[0][...], a[...])
        refs[-n][...] = change if solution is None else refs[0][...] + change
        for s in range(1, n):
            refs[s - n][...] = mm(ds[s][...], b[...])

    solution, *turns, token = call(
        body, [shape(before[0].shape[0])] * n, *fields, after=[token]
    )
    return solution, turns, token


def finish(small, gram, residual, direction, solution, image):
    strip = residual.shape[0]

    def body(small, g, r, d, s, *refs):
        *images, out, new_r = refs
        alpha = eliminated_alone(unpacked_symmetric(small[...]), g[...])
        image = images[0][...]
        for ref in images[1:]:
            image = image + ref[...]
        out[...] = s[...] + mm(d[...], alpha)
        new_r[...] = r[...] - mm(image, alpha)

    return call(
        body,
        [shape(strip), shape(strip)],
        small,
        gram,
        residual,
        direction,
        solution,
        *image,
    )[:-1]


def step_sizes(pieces, gram):
    rows = pieces[0].shape[0]
    first = gram is None
    fields = [*pieces] + ([] if first else [gram])

    def body(mine, mates, *refs):
        *refs, alpha_out, whole_out, inverse_out, gram_out, raw = refs
        half = lax.axis_index("coef")
        raw[pl.ds(pl.multiple_of(half * rows, SUB), rows), :] = mine[...]
        raw[pl.ds(pl.multiple_of((1 - half) * rows, SUB), rows), :] = mates[...]
        sym, whole = unpacked_symmetric(raw[:PACKED, :]), raw[PACKED + SUB :, :]
        g = sym if first else refs[0][...]
        curvature = symmetric(whole) if first else sym
        alpha_out[...], inverse_out[...] = eliminated((curvature, g), (g, identity()))
        whole_out[...] = whole
        gram_out[...] = g

    return call(
        body,
        [shape(LANES)] * 4,
        *fields,
        scratch=[pltpu.VMEM((2 * rows, LANES), F32)],
    )[:-1]


def turn(square, alpha, whole, inverse, gram, residual, direction, image):
    strip = residual.shape[0]

    def body(alpha, whole, inverse, gram, r, d, image, *refs):
        *terms, r_out, new_d, low, beta_out, gram_out = refs
        square = terms[0][...]
        for ref in terms[1:]:
            square = square + ref[...]
        a = alpha[...]
        shared = mm(whole[...], a, (0, 0))
        quadratic = mm(a, mm(unpacked_symmetric(square), a), (0, 0))
        following = gram[...] - (shared + shared.T) + quadratic
        beta = mm(inverse[...], following)
        new_r = r[...] - mm(image[...], a)
        value = new_r + mm(d[...], beta)
        r_out[...] = new_r
        low[...] = value.astype(BF16)
        new_d[...] = value
        beta_out[...] = beta
        gram_out[...] = following

    return call(
        body,
        [shape(strip), shape(strip), shape(strip, dtype=BF16), shape(LANES), shape(LANES)],
        alpha,
        whole,
        inverse,
        gram,
        residual,
        direction,
        image,
        *square,
    )[:-1]


def shards(couplings, observations, replicate_mask):
    links, rows = couplings.shape[1], couplings.shape[3]
    strip = couplings.shape[6]
    blocks = couplings.reshape(links, rows, couplings.shape[4], strip)
    blocks = pltpu.with_memory_space_constraint(blocks, pltpu.HBM)
    n = lax.axis_size("rhs")
    obs_matrix = observations.reshape(observations.shape[0], rows)
    parts, token = right_side_parts(obs_matrix, replicate_mask, n, strip)
    own = [parts[0]] + [swapped(parts[s], "rhs", s, n) for s in range(1, n)]
    groups = link_groups(links)
    packed = []
    for _, numbers, count in groups[:2]:
        value, token = retiled(blocks, numbers, count, token)
        packed.append(value)
    residual, low, token = sum_and_round(own, token)
    for _, numbers, count in groups[2:]:
        value, token = retiled(blocks, numbers, count, token)
        packed.append(value)
    retile_token = token
    direction = residual
    solution = gram = beta = before = alpha = None
    for step in range(ITERS):
        first, final = step == 0, step + 1 == ITERS
        state = [solution, None, None]

        def between(token):
            if first:
                state[2], token = gram_of(residual, token, retile_token)
                return token
            *state[:2], token = stepped(solution, before, alpha, beta, token)
            return token

        parts, directions = operate(packed, groups, low, direction, between, final)
        solution, turns, own_gram = state
        image_parts = [parts[0]] + [swapped(parts[s], "rhs", s, n) for s in range(1, n)]
        linear = linear_grams(parts, directions, residual, turns, own_gram, final)
        if final:
            small = reduce_one(*linear)
            solution, residual = finish(
                small, gram, residual, direction, solution, image_parts
            )
            break
        image, square = square_gram(image_parts)
        linear, square = reduce_both(*linear, square)
        alpha, whole, inverse, gram = step_sizes(linear, gram)
        square[1:], alpha = lax.optimization_barrier((square[1:], alpha))
        before = directions
        residual, direction, low, beta, gram = turn(
            square, alpha, whole, inverse, gram, residual, direction, image
        )
    shape_out = (1, 1, strip, LANES)
    return (solution.reshape(shape_out), residual.reshape(shape_out))


def solution(mesh):
    placed = (
        P("panel", None, "coef", None, None, "rhs", None),
        P(("groups", "rhs"), "panel", "coef", None),
        P(("groups", "rhs"), None),
    )
    return jax.shard_map(
        shards,
        mesh=mesh,
        in_specs=placed,
        out_specs=(
            P(("groups", "panel"), "coef", "rhs", None),
            P(("groups", "panel"), "coef", "rhs", None),
        ),
        check_vma=False,
    )
```

```python
import functools

import jax
import jax.numpy as jnp
from jax import lax
from jax.experimental import pallas as pl
from jax.experimental.pallas import tpu as pltpu
from jax.sharding import PartitionSpec as P

ITERS = 3
LANES = 128
SUB = 8
VMEM_LIMIT = 14 * 2**20
F32 = jnp.float32
BF16 = jnp.bfloat16
VMEM = pl.BlockSpec(memory_space=pltpu.VMEM)
ANY = pl.BlockSpec(memory_space=pl.ANY)
HBM = pl.BlockSpec(memory_space=pltpu.HBM)


def mm(a, b, dims=(1, 0)):
    return lax.dot_general(
        a,
        b,
        (((dims[0],), (dims[1],)), ((), ())),
        precision=lax.Precision.HIGHEST,
        preferred_element_type=F32,
    )


def halves(value):
    high = value.astype(BF16)
    return high, (value - high.astype(F32)).astype(BF16)


def mm_field(a, b, dims=(1, 0)):
    def part(left, right):
        return lax.dot_general(
            left, right, (((dims[0],), (dims[1],)), ((), ())), preferred_element_type=F32
        )

    (a, a_low), (b, b_low) = halves(a), halves(b)
    return part(a, b) + (part(a, b_low) + part(a_low, b))


def square_of(field):
    high, low = halves(field)
    both = lax.dot_general(
        high,
        jnp.concatenate([high, low], axis=1),
        (((0,), (0,)), ((), ())),
        preferred_element_type=F32,
    )
    cross = both[:, LANES:]
    return both[:, :LANES] + (cross + cross.T)


def call(body, outs, *args, scratch=(), after=(), any_args=0, any_outs=False):
    inputs, outputs, waits = len(args), len(outs), len(after)

    def ordered(*refs):
        token = refs[inputs + waits + outputs]
        token[...] = jnp.zeros_like(token)
        body(
            *refs[:inputs],
            *refs[inputs + waits : inputs + waits + outputs],
            *refs[inputs + waits + outputs + 1 :],
        )

    return pl.pallas_call(
        ordered,
        out_shape=list(outs) + [shape(SUB)],
        in_specs=[HBM] * any_args + [VMEM] * (inputs - any_args) + [ANY] * waits,
        out_specs=[ANY if any_outs else VMEM] * outputs + [VMEM],
        scratch_shapes=list(scratch),
        cost_estimate=pl.CostEstimate(flops=1, bytes_accessed=1, transcendentals=0),
        compiler_params=pltpu.CompilerParams(vmem_limit_bytes=VMEM_LIMIT),
    )(*args, *after)


def shape(rows, cols=LANES, dtype=F32):
    return jax.ShapeDtypeStruct((rows, cols), dtype)


def permute(value, axis, pairs):
    return lax.ppermute(value, axis, pairs)


def shifted(value, axis, by):
    n = lax.axis_size(axis)
    return permute(value, axis, [((i + by) % n, i) for i in range(n)])


def mate(i, s, n):
    return i ^ s if n & (n - 1) == 0 else (s - i) % n


def swapped(value, axis, s, n):
    return permute(value, axis, [(mate(i, s, n), i) for i in range(n)])


def sum_near(value):
    axes = ("panel", "rhs")
    count = lax.axis_size(axes)
    three, two, one = (swapped(value, axes, s, count) for s in (3, 2, 1))
    return (value + one) + (two + three)


def from_far(value):
    axes = ("panel", "rhs")
    return swapped(value, axes, 4, lax.axis_size(axes))


def sum_far(value, meanwhile=None):
    other = from_far(value)
    if meanwhile is not None:
        other, _ = lax.optimization_barrier((other, meanwhile))
    return value + other


def by_stages():
    return lax.axis_size("panel") == 4 and lax.axis_size("rhs") == 2


def reduce_one(value):
    value = value + swapped(value, "coef", 1, 2)
    if not by_stages():
        return lax.psum(value, ("panel", "rhs"))
    return sum_far(sum_near(value))


def reduce_both(mine, mates, square):
    value = mine + swapped(mates, "coef", 1, 2)
    whole = square + swapped(square, "coef", 1, 2)
    if by_stages():
        rows = value.shape[0]
        value = sum_far(value, meanwhile=square)
        both = sum_near(jnp.concatenate([value, whole], axis=0))
        value, whole = both[:rows], both[rows:]
        terms = [whole, from_far(whole)]
    else:
        value, whole = lax.psum((value, whole), ("panel", "rhs"))
        terms = [whole]
    return [value, swapped(value, "coef", 1, 2)], terms


def right_side_parts(obs, mask, n, strip):
    def body(obs_hbm, mask_hbm, *refs):
        *outs, obs_ref, mask_ref, sems = refs
        copies = [
            pltpu.make_async_copy(mask_hbm, mask_ref, sems.at[0]),
            pltpu.make_async_copy(obs_hbm, obs_ref, sems.at[1]),
        ]
        for copy in copies:
            copy.start()
        for copy in copies:
            copy.wait()
        signs = (2 * mask_ref[...] - 1).astype(BF16)
        me = lax.axis_index("rhs")
        for s in range(n):
            place = pl.multiple_of(mate(me, s, n) * strip, strip)
            outs[s][...] = lax.dot_general(
                obs_ref[:, pl.ds(place, strip)],
                signs,
                (((0,), (0,)), ((), ())),
                preferred_element_type=F32,
            )

    *parts, token = call(
        body,
        [shape(strip)] * n,
        pltpu.with_memory_space_constraint(obs, pltpu.HBM),
        pltpu.with_memory_space_constraint(mask, pltpu.HBM),
        scratch=[
            pltpu.VMEM(obs.shape, BF16),
            pltpu.VMEM(mask.shape, mask.dtype),
            pltpu.SemaphoreType.DMA((2,)),
        ],
        any_args=2,
    )
    return parts, token


def sum_and_round(parts, token):
    strip = parts[0].shape[0]

    def body(*refs):
        *ins, out, low = refs
        total = ins[0][...]
        for ref in ins[1:]:
            total = total + ref[...]
        out[...] = total
        low[...] = total.astype(BF16)

    return call(
        body, [shape(strip), shape(strip, dtype=BF16)], *parts, after=[token]
    )


def retiled(blocks, links, count, token):
    rows, strip = blocks.shape[1], blocks.shape[3]
    tiles = strip // LANES

    def body(k_ref, out, sems):
        copies = []
        for i, link in enumerate(links()):
            for t in range(tiles):
                copy = pltpu.make_async_copy(
                    k_ref.at[link, :, :, pl.ds(t * LANES, LANES)], out.at[i, t], sems.at[i, t]
                )
                copy.start()
                copies.append(copy)
        for copy in copies:
            copy.wait()

    packed, token = call(
        body,
        [pltpu.VMEM((count, tiles, rows, 2, LANES), BF16)],
        blocks,
        scratch=[pltpu.SemaphoreType.DMA((count, tiles))],
        after=[token],
        any_args=1,
        any_outs=True,
    )
    return packed, token


def link_products(packed, pieces, acc, n, slots, after=()):
    tiles, rows = packed[0].shape[1:3]
    counts = [value.shape[0] for value in packed]
    many = len(packed)
    packed = [
        pltpu.with_memory_space_constraint(
            value.reshape(value.shape[0], tiles, 2 * rows, LANES), pltpu.VMEM
        )
        for value in packed
    ]
    strip = tiles * LANES
    size = rows if slots is None else rows // n
    block = min(512, 2 * size)

    def body(*refs):
        k_refs, piece_refs = refs[:many], refs[many : 3 * many]
        acc_refs = refs[3 * many : 3 * many + len(acc)]
        outs = refs[3 * many + len(acc) : -3]
        weights, even_acc, odd_acc = refs[-3:]
        half = lax.axis_index("coef")
        own = pl.ds(pl.multiple_of(half * LANES, LANES), LANES)
        other = pl.ds(pl.multiple_of((1 - half) * LANES, LANES), LANES)
        for g in range(many):
            weights[g, :, own] = piece_refs[2 * g][...]
            weights[g, :, other] = piece_refs[2 * g + 1][...]
        me = lax.axis_index("rhs")
        for place, (out, s) in enumerate(zip(outs, [None] if slots is None else slots)):
            first = 0 if s is None else pl.multiple_of(mate(me, s, n) * size, size)
            for start in range(0, 2 * size, block):
                here = slice(start, start + block)
                product = None
                for g in range(many):
                    for i in range(counts[g]):
                        left = jnp.concatenate(
                            [
                                k_refs[g][i, t, pl.ds(2 * first + start, block), :]
                                for t in range(tiles)
                            ],
                            axis=1,
                        )
                        term = jnp.dot(left, weights[g], preferred_element_type=F32)
                        product = term if product is None else product + term
                even_acc[here, :] = product[:, :LANES]
                odd_acc[here, :] = product[:, LANES:]
            even = even_acc[pl.ds(0, size, stride=2), :]
            odd = odd_acc[pl.ds(1, size, stride=2), :]
            total = even + odd
            if acc and acc[0].shape[0] == rows:
                total = total + acc_refs[0][pl.ds(first, size), :]
            elif acc:
                total = total + acc_refs[place][...]
            out[...] = total

    args = [*packed, *(value for pair in pieces for value in pair)]
    args += acc
    *result, token = call(
        body,
        [shape(size)] * (1 if slots is None else len(slots)),
        *args,
        scratch=[
            pltpu.VMEM((many, strip, 2 * LANES), BF16),
            pltpu.VMEM((2 * size, LANES), F32),
            pltpu.VMEM((2 * size, LANES), F32),
        ],
        after=after,
    )
    return result, token


def link_groups(links):
    reach = (links - 1) // 2
    panels = lax.axis_size("panel")
    groups = []
    if links == 2 * panels + 1 and panels & (panels - 1) == 0:
        for s in sorted(range(panels), key=lambda s: (s > 0, s % 2)):

            def numbers(s=s):
                me = lax.axis_index("panel")
                start = lax.rem((me ^ s) - me + reach + panels, panels)
                return [start + panels * i for i in range(3 if s == 0 else 2)]

            bring = functools.partial(swapped, axis="panel", s=s, n=panels)
            groups.append((bring, numbers, 3 if s == 0 else 2))
        return groups
    offsets = {}
    for link in range(links):
        offsets.setdefault((link - reach) % panels, []).append(link)
    for o in sorted(offsets, key=lambda o: min(o, panels - o)):
        bring = functools.partial(shifted, axis="panel", by=o)
        groups.append((bring, functools.partial(list, offsets[o]), len(offsets[o])))
    return groups


def operate(packed, groups, low, direction, between, final):
    n = lax.axis_size("rhs")
    arrived = [low] + [bring(low) for bring, _, _ in groups[1:]]
    directions = [direction] + [swapped(direction, "rhs", s, n) for s in range(1, n)]
    pairs = [[low, swapped(low, "coef", 1, 2)]]
    acc, token = link_products(packed[:1], pairs, [], n, None)
    after = (token, between(token))
    for piece in arrived[1:]:
        piece, _ = lax.optimization_barrier((piece, after))
        pairs.append([piece, swapped(piece, "coef", 1, 2)])
    after = (*after, *directions[1:])
    if final:
        acc, _ = link_products(packed[1:-1], pairs[1:-1], acc, n, None, after)
        parts, _ = link_products(packed[-1:], pairs[-1:], acc, n, range(n), after)
        return parts, directions
    mates, _ = link_products(packed[1:-1], pairs[1:-1], acc, n, range(1, n), after)
    mates, token = link_products(packed[-1:], pairs[-1:], mates, n, range(1, n), after)
    own, _ = link_products(packed[1:], pairs[1:], acc, n, [0], (token,))
    return own + mates, directions


PACKED = LANES // 2 + SUB


def corner():
    row = lax.broadcasted_iota(jnp.int32, (LANES // 2, LANES), 0)
    lane = lax.broadcasted_iota(jnp.int32, (LANES // 2, LANES), 1)
    return row, lane, lane < LANES // 2


def packed_symmetric(matrix):
    half = LANES // 2
    row, lane, left = corner()
    top = matrix[:half]
    last = pltpu.roll(matrix[half:], half, 1)
    body = jnp.where(left & (lane > row), last, top)
    diagonal = jnp.sum(jnp.where(lane == row, last, 0.0), axis=0, keepdims=True)
    return jnp.concatenate([body, jnp.broadcast_to(diagonal, (SUB, LANES))], axis=0)


def unpacked_symmetric(rows):
    half = LANES // 2
    row, lane, left = corner()
    body, diagonal = rows[:half], rows[half : half + 1]
    top = jnp.where(left & (lane >= row), 0.0, body)
    last = jnp.where(left & (lane > row), body, 0.0)
    sides = jnp.concatenate([top, pltpu.roll(last, half, 1)], axis=0)
    top = jnp.where(lane == row, body, 0.0)
    last = jnp.where(lane == row, jnp.broadcast_to(diagonal, body.shape), 0.0)
    return sides + sides.T + jnp.concatenate([top, pltpu.roll(last, half, 1)], axis=0)


def symmetric(raw):
    return 0.5 * (raw + raw.T)


JOINT = PACKED + SUB + LANES


def linear_grams(parts, directions, residual, turns, gram, final):
    strip = parts[0].shape[0]
    n = len(parts)
    first = gram is not None
    extra = [gram] if first else [] if final else [residual, *turns]
    rows = PACKED if final else JOINT // 2

    def body(*refs):
        images, ds = refs[:n], refs[n : 2 * n]
        rest = refs[2 * n : 2 * n + len(extra)]
        outs = refs[2 * n + len(extra) :]
        found = None
        for s in range(n):
            image, right = images[s][...], ds[s][...]
            if extra and not first:
                r = rest[0][...] if s == 0 else right - rest[s][...]
                right = jnp.concatenate([right, r], axis=1)
            term = mm_field(image, right, (0, 0))
            found = term if s == 0 else found + term
        if final:
            outs[0][...] = packed_symmetric(symmetric(found))
            return
        mine, mates, stacked = outs
        if first:
            stacked[:PACKED], whole = rest[0][...], found
        else:
            stacked[:PACKED] = packed_symmetric(symmetric(found[:, :LANES]))
            whole = found[:, LANES:]
        stacked[PACKED : PACKED + SUB] = jnp.zeros((SUB, LANES), F32)
        stacked[PACKED + SUB :] = whole
        half = lax.axis_index("coef")
        mine[...] = stacked[pl.ds(pl.multiple_of(half * rows, SUB), rows), :]
        mates[...] = stacked[pl.ds(pl.multiple_of((1 - half) * rows, SUB), rows), :]

    *pieces, _ = call(
        body,
        [shape(rows)] * (1 if final else 2),
        *parts,
        *directions,
        *extra,
        scratch=[] if final else [pltpu.VMEM((2 * rows, LANES), F32)],
    )
    return pieces


def gram_of(field, *tokens):
    def body(field, out):
        value = field[...]
        out[...] = packed_symmetric(square_of(value))

    return call(body, [shape(PACKED)], field, after=tokens)


def square_gram(image_parts):
    strip = image_parts[0].shape[0]
    parts = len(image_parts)

    def body(*refs):
        ins, image_out, out = refs[:parts], refs[parts], refs[parts + 1]
        image = ins[0][...]
        for ref in ins[1:]:
            image = image + ref[...]
        image_out[...] = image
        out[...] = packed_symmetric(square_of(image))

    image, square, _ = call(
        body,
        [shape(strip), shape(PACKED)],
        *image_parts,
    )
    return image, square


def reciprocal(value):
    near = pl.reciprocal(value, approx=True)
    for _ in range(2):
        near = near * (2.0 - value * near)
    return near


def next_pivot(column, following, i, inverse):
    product = column[i + 1 : i + 2] * following[i : i + 1]
    return following[i + 1 : i + 2] - product * inverse


def inverted(matrices, lane):
    strips = matrices[0].shape[0] // SUB
    place = lax.broadcasted_iota(jnp.int32, (SUB, LANES), 0)
    held = [[value[SUB * k : SUB * (k + 1)] for k in range(strips)] for value in matrices]

    def lanes_of(value, at):
        return jnp.broadcast_to(value[:, at : at + 1], (SUB, LANES))

    def rows_of(value):
        return [jnp.broadcast_to(value[i : i + 1], (SUB, LANES)) for i in range(SUB)]

    def update(k, j, spread):
        for a, rows in zip(held, spread):
            row = a[k]
            for i in range(SUB):
                row = row - lanes_of(a[k], lane + SUB * j + i) * rows[i]
            a[k] = row

    for j in range(strips):
        if j:
            spread = [rows_of(a[j - 1]) for a in held]
            update(j, j - 1, spread)
        waiting = [k for k in range(strips) if j and k not in (j, j - 1)]
        now = [
            [a[j], *(lanes_of(a[j], lane + SUB * j + i) for i in range(SUB))] for a in held
        ]
        for i in range(SUB):
            here = place == i
            for index, values in enumerate(now):
                column = values[1 + i]
                inverse = 1.0 / column[i : i + 1]

                def step(value):
                    row = value[i : i + 1] * inverse
                    return jnp.where(here, row, value - column * row)

                now[index] = [
                    step(value) if at < 1 or at > 1 + i else value
                    for at, value in enumerate(values)
                ]
            for k in waiting[i : i + 1]:
                update(k, j - 1, spread)
        for a, values in zip(held, now):
            a[j] = values[0]
    spread = [rows_of(a[-1]) for a in held]
    for k in range(strips - 1):
        update(k, strips - 1, spread)
    return [jnp.concatenate(a, axis=0) for a in held]


def eliminated(*systems):
    half = LANES // 2
    row = lax.broadcasted_iota(jnp.int32, (half, LANES), 0)
    lane = lax.broadcasted_iota(jnp.int32, (half, LANES), 1)
    left = lane < half
    first = inverted(
        [
            jnp.where(left, matrix[:half], (lane - half == row).astype(F32))
            for matrix, _ in systems
        ],
        0,
    )
    tops, lasts = [], []
    for (matrix, sides), value in zip(systems, first):
        value = pltpu.roll(value, half, 1)[:, :half]
        top = mm(value, jnp.concatenate([matrix[:half], sides[:half]], axis=1))
        low = jnp.concatenate([matrix[half:], sides[half:]], axis=1)
        tops.append(top)
        lasts.append(low - mm(matrix[half:, :half], top))
    second = inverted(
        [jnp.where(left, (lane == row).astype(F32), last[:, :LANES]) for last in lasts], half
    )
    found = []
    for top, last, value in zip(tops, lasts, second):
        low = mm(value[:, :half], last[:, LANES:])
        high = top[:, LANES:] - mm(
            top[:, :LANES], jnp.concatenate([jnp.zeros_like(low), low], axis=0)
        )
        found.append(jnp.concatenate([high, low], axis=0))
    return found


def eliminated_alone(matrix, sides):
    n = matrix.shape[0]
    strips = n // SUB
    place = lax.broadcasted_iota(jnp.int32, (SUB, LANES), 0)

    def cut(value):
        return [value[SUB * k : SUB * (k + 1)] for k in range(strips)]

    def lanes_of(value, lane):
        return jnp.broadcast_to(value[:, lane : lane + 1], (SUB, LANES))

    held = [(cut(matrix), cut(sides))]

    def rows_of(value):
        return [jnp.broadcast_to(value[i : i + 1], (SUB, LANES)) for i in range(SUB)]

    def update(k, j, spread):
        for (a, b), (rows_a, rows_b) in zip(held, spread):
            row_a, row_b = a[k], b[k]
            for i in range(SUB):
                factor = lanes_of(a[k], SUB * j + i)
                row_a = row_a - factor * rows_a[i]
                row_b = row_b - factor * rows_b[i]
            a[k], b[k] = row_a, row_b

    for j in range(strips):
        if j:
            spread = [(rows_of(a[j - 1]), rows_of(b[j - 1])) for a, b in held]
            update(j, j - 1, spread)
        waiting = [k for k in range(strips) if j and k not in (j, j - 1)]
        now = [
            [a[j], b[j], *(lanes_of(a[j], SUB * j + i) for i in range(SUB))] for a, b in held
        ]
        pivots = [values[2][:1] for values in now]
        for i in range(SUB):
            here = place == i
            for index, values in enumerate(now):
                column = values[2 + i]
                inverse = reciprocal(pivots[index])
                if i + 1 < SUB:
                    pivots[index] = next_pivot(column, values[3 + i], i, inverse)

                def step(value):
                    row = value[i : i + 1] * inverse
                    return jnp.where(here, row, value - column * row)

                now[index] = [
                    step(value) if place_of < 2 or place_of > 2 + i else value
                    for place_of, value in enumerate(values)
                ]
            for k in waiting[2 * i : 2 * i + 2]:
                update(k, j - 1, spread)
        for (a, b), values in zip(held, now):
            a[j], b[j] = values[:2]
    spread = [(rows_of(a[-1]), rows_of(b[-1])) for a, b in held]
    for k in range(strips - 1):
        update(k, strips - 1, spread)
    return jnp.concatenate(held[0][1], axis=0)


def identity():
    return (
        lax.broadcasted_iota(jnp.int32, (LANES, LANES), 0)
        == lax.broadcasted_iota(jnp.int32, (LANES, LANES), 1)
    ).astype(F32)


def stepped(solution, before, alpha, beta, token):
    fields = [*before, alpha, beta] + ([] if solution is None else [solution])
    n = len(before)

    def body(*refs):
        ds, a, b, refs = refs[:n], refs[n], refs[n + 1], refs[n + 2 :]
        change = mm_field(ds[0][...], a[...])
        refs[-n][...] = change if solution is None else refs[0][...] + change
        for s in range(1, n):
            refs[s - n][...] = mm_field(ds[s][...], b[...])

    solution, *turns, token = call(
        body, [shape(before[0].shape[0])] * n, *fields, after=[token]
    )
    return solution, turns, token


def finish(small, gram, residual, direction, solution, image):
    strip = residual.shape[0]

    def body(small, g, r, d, s, *refs):
        *images, out, new_r = refs
        alpha = eliminated_alone(unpacked_symmetric(small[...]), g[...])
        image = images[0][...]
        for ref in images[1:]:
            image = image + ref[...]
        out[...] = s[...] + mm_field(d[...], alpha)
        new_r[...] = r[...] - mm_field(image, alpha)

    return call(
        body,
        [shape(strip), shape(strip)],
        small,
        gram,
        residual,
        direction,
        solution,
        *image,
    )[:-1]


def step_sizes(pieces, gram):
    rows = pieces[0].shape[0]
    first = gram is None
    fields = [*pieces] + ([] if first else [gram])

    def body(mine, mates, *refs):
        *refs, alpha_out, whole_out, inverse_out, gram_out, raw = refs
        half = lax.axis_index("coef")
        raw[pl.ds(pl.multiple_of(half * rows, SUB), rows), :] = mine[...]
        raw[pl.ds(pl.multiple_of((1 - half) * rows, SUB), rows), :] = mates[...]
        sym, whole = unpacked_symmetric(raw[:PACKED, :]), raw[PACKED + SUB :, :]
        g = sym if first else refs[0][...]
        curvature = symmetric(whole) if first else sym
        alpha_out[...], inverse_out[...] = eliminated((curvature, g), (g, identity()))
        whole_out[...] = whole
        gram_out[...] = g

    return call(
        body,
        [shape(LANES)] * 4,
        *fields,
        scratch=[pltpu.VMEM((2 * rows, LANES), F32)],
    )[:-1]


def turn(square, alpha, whole, inverse, gram, residual, direction, image):
    strip = residual.shape[0]

    def body(alpha, whole, inverse, gram, r, d, image, *refs):
        *terms, r_out, new_d, low, beta_out, gram_out = refs
        square = terms[0][...]
        for ref in terms[1:]:
            square = square + ref[...]
        a = alpha[...]
        shared = mm(whole[...], a, (0, 0))
        quadratic = mm(a, mm(unpacked_symmetric(square), a), (0, 0))
        following = gram[...] - (shared + shared.T) + quadratic
        beta = mm(inverse[...], following)
        new_r = r[...] - mm_field(image[...], a)
        value = new_r + mm_field(d[...], beta)
        r_out[...] = new_r
        low[...] = value.astype(BF16)
        new_d[...] = value
        beta_out[...] = beta
        gram_out[...] = following

    return call(
        body,
        [shape(strip), shape(strip), shape(strip, dtype=BF16), shape(LANES), shape(LANES)],
        alpha,
        whole,
        inverse,
        gram,
        residual,
        direction,
        image,
        *square,
    )[:-1]


def shards(couplings, observations, replicate_mask):
    links, rows = couplings.shape[1], couplings.shape[3]
    strip = couplings.shape[6]
    blocks = couplings.reshape(links, rows, couplings.shape[4], strip)
    blocks = pltpu.with_memory_space_constraint(blocks, pltpu.HBM)
    n = lax.axis_size("rhs")
    obs_matrix = observations.reshape(observations.shape[0], rows)
    parts, token = right_side_parts(obs_matrix, replicate_mask, n, strip)
    own = [parts[0]] + [swapped(parts[s], "rhs", s, n) for s in range(1, n)]
    groups = link_groups(links)
    packed = []
    for _, numbers, count in groups[:2]:
        value, token = retiled(blocks, numbers, count, token)
        packed.append(value)
    residual, low, token = sum_and_round(own, token)
    for _, numbers, count in groups[2:]:
        value, token = retiled(blocks, numbers, count, token)
        packed.append(value)
    retile_token = token
    direction = residual
    solution = gram = beta = before = alpha = None
    for step in range(ITERS):
        first, final = step == 0, step + 1 == ITERS
        state = [solution, None, None]

        def between(token):
            if first:
                state[2], token = gram_of(residual, token, retile_token)
                return token
            *state[:2], token = stepped(solution, before, alpha, beta, token)
            return token

        parts, directions = operate(packed, groups, low, direction, between, final)
        solution, turns, own_gram = state
        image_parts = [parts[0]] + [swapped(parts[s], "rhs", s, n) for s in range(1, n)]
        linear = linear_grams(parts, directions, residual, turns, own_gram, final)
        if final:
            small = reduce_one(*linear)
            solution, residual = finish(
                small, gram, residual, direction, solution, image_parts
            )
            break
        image, square = square_gram(image_parts)
        linear, square = reduce_both(*linear, square)
        alpha, whole, inverse, gram = step_sizes(linear, gram)
        square[1:], alpha = lax.optimization_barrier((square[1:], alpha))
        before = directions
        residual, direction, low, beta, gram = turn(
            square, alpha, whole, inverse, gram, residual, direction, image
        )
    shape_out = (1, 1, strip, LANES)
    return (solution.reshape(shape_out), residual.reshape(shape_out))


def solution(mesh):
    placed = (
        P("panel", None, "coef", None, None, "rhs", None),
        P(("groups", "rhs"), "panel", "coef", None),
        P(("groups", "rhs"), None),
    )
    return jax.shard_map(
        shards,
        mesh=mesh,
        in_specs=placed,
        out_specs=(
            P(("groups", "panel"), "coef", "rhs", None),
            P(("groups", "panel"), "coef", "rhs", None),
        ),
        check_vma=False,
    )
```

```python
import functools

import jax
import jax.numpy as jnp
from jax import lax
from jax.experimental import pallas as pl
from jax.experimental.pallas import tpu as pltpu
from jax.sharding import PartitionSpec as P

ITERS = 3
PARTS = 2
LANES = 128
SUB = 8
VMEM_LIMIT = 14 * 2**20
F32 = jnp.float32
BF16 = jnp.bfloat16
VMEM = pl.BlockSpec(memory_space=pltpu.VMEM)
ANY = pl.BlockSpec(memory_space=pl.ANY)
HBM = pl.BlockSpec(memory_space=pltpu.HBM)


def mm(a, b, dims=(1, 0)):
    return lax.dot_general(
        a,
        b,
        (((dims[0],), (dims[1],)), ((), ())),
        precision=lax.Precision.HIGHEST,
        preferred_element_type=F32,
    )


def call(body, outs, *args, scratch=(), after=(), any_args=0, any_outs=False):
    inputs, outputs, waits = len(args), len(outs), len(after)

    def ordered(*refs):
        token = refs[inputs + waits + outputs]
        token[...] = jnp.zeros_like(token)
        body(
            *refs[:inputs],
            *refs[inputs + waits : inputs + waits + outputs],
            *refs[inputs + waits + outputs + 1 :],
        )

    return pl.pallas_call(
        ordered,
        out_shape=list(outs) + [shape(SUB)],
        in_specs=[HBM] * any_args + [VMEM] * (inputs - any_args) + [ANY] * waits,
        out_specs=[ANY if any_outs else VMEM] * outputs + [VMEM],
        scratch_shapes=list(scratch),
        cost_estimate=pl.CostEstimate(flops=1, bytes_accessed=1, transcendentals=0),
        compiler_params=pltpu.CompilerParams(vmem_limit_bytes=VMEM_LIMIT),
    )(*args, *after)


def shape(rows, cols=LANES, dtype=F32):
    return jax.ShapeDtypeStruct((rows, cols), dtype)


def permute(value, axis, pairs):
    return lax.ppermute(value, axis, pairs)


def shifted(value, axis, by):
    n = lax.axis_size(axis)
    return permute(value, axis, [((i + by) % n, i) for i in range(n)])


def mate(i, s, n):
    return i ^ s if n & (n - 1) == 0 else (s - i) % n


def swapped(value, axis, s, n):
    return permute(value, axis, [(mate(i, s, n), i) for i in range(n)])


def sum_near(value):
    axes = ("panel", "rhs")
    count = lax.axis_size(axes)
    three, two, one = (swapped(value, axes, s, count) for s in (3, 2, 1))
    return (value + one) + (two + three)


def from_far(value):
    axes = ("panel", "rhs")
    return swapped(value, axes, 4, lax.axis_size(axes))


def sum_far(value, meanwhile=None):
    other = from_far(value)
    if meanwhile is not None:
        other, _ = lax.optimization_barrier((other, meanwhile))
    return value + other


def by_stages():
    return lax.axis_size("panel") == 4 and lax.axis_size("rhs") == 2


def reduce_one(value):
    value = value + swapped(value, "coef", 1, 2)
    if not by_stages():
        return lax.psum(value, ("panel", "rhs"))
    return sum_far(sum_near(value))


def reduce_both(mine, mates, square):
    value = mine + swapped(mates, "coef", 1, 2)
    whole = square + swapped(square, "coef", 1, 2)
    if by_stages():
        rows = value.shape[0]
        value = sum_far(value, meanwhile=square)
        both = sum_near(jnp.concatenate([value, whole], axis=0))
        value, whole = both[:rows], both[rows:]
        terms = [whole, from_far(whole)]
    else:
        value, whole = lax.psum((value, whole), ("panel", "rhs"))
        terms = [whole]
    return [value, swapped(value, "coef", 1, 2)], terms


def right_side_parts(obs, mask, n, strip):
    def body(obs_hbm, mask_hbm, *refs):
        *outs, obs_ref, mask_ref, sems = refs
        copies = [
            pltpu.make_async_copy(mask_hbm, mask_ref, sems.at[0]),
            pltpu.make_async_copy(obs_hbm, obs_ref, sems.at[1]),
        ]
        for copy in copies:
            copy.start()
        for copy in copies:
            copy.wait()
        signs = (2 * mask_ref[...] - 1).astype(BF16)
        me = lax.axis_index("rhs")
        for s in range(n):
            place = pl.multiple_of(mate(me, s, n) * strip, strip)
            outs[s][...] = lax.dot_general(
                obs_ref[:, pl.ds(place, strip)],
                signs,
                (((0,), (0,)), ((), ())),
                preferred_element_type=F32,
            )

    *parts, token = call(
        body,
        [shape(strip)] * n,
        pltpu.with_memory_space_constraint(obs, pltpu.HBM),
        pltpu.with_memory_space_constraint(mask, pltpu.HBM),
        scratch=[
            pltpu.VMEM(obs.shape, BF16),
            pltpu.VMEM(mask.shape, mask.dtype),
            pltpu.SemaphoreType.DMA((2,)),
        ],
        any_args=2,
    )
    return parts, token


def sum_and_round(parts, token):
    strip = parts[0].shape[0]

    def body(*refs):
        *ins, out, low = refs
        total = ins[0][...]
        for ref in ins[1:]:
            total = total + ref[...]
        out[...] = total
        low[...] = total.astype(BF16)

    return call(
        body, [shape(strip), shape(strip, dtype=BF16)], *parts, after=[token]
    )


def retiled(blocks, links, count, token):
    rows, strip = blocks.shape[1], blocks.shape[3]
    tiles = strip // LANES

    def body(k_ref, out, sems):
        copies = []
        for i, link in enumerate(links()):
            for t in range(tiles):
                copy = pltpu.make_async_copy(
                    k_ref.at[link, :, :, pl.ds(t * LANES, LANES)], out.at[i, t], sems.at[i, t]
                )
                copy.start()
                copies.append(copy)
        for copy in copies:
            copy.wait()

    packed, token = call(
        body,
        [pltpu.VMEM((count, tiles, rows, 2, LANES), BF16)],
        blocks,
        scratch=[pltpu.SemaphoreType.DMA((count, tiles))],
        after=[token],
        any_args=1,
        any_outs=True,
    )
    return packed, token


def link_products(packed, pieces, acc, n, slots, after=()):
    tiles, rows = packed[0].shape[1:3]
    counts = [value.shape[0] for value in packed]
    many = len(packed)
    packed = [
        pltpu.with_memory_space_constraint(
            value.reshape(value.shape[0], tiles, 2 * rows, LANES), pltpu.VMEM
        )
        for value in packed
    ]
    strip = tiles * LANES
    size = rows if slots is None else rows // n
    block = min(512, 2 * size)

    def body(*refs):
        k_refs, refs = refs[:many], refs[many:]
        piece_refs = []
        for pair in pieces:
            piece_refs.append(refs[: len(pair)])
            refs = refs[len(pair) :]
        acc_ref = refs[0] if acc is not None else None
        outs = refs[acc is not None : -3]
        weights, even_acc, odd_acc = refs[-3:]
        half = lax.axis_index("coef")
        own = pl.ds(pl.multiple_of(half * LANES, LANES), LANES)
        other = pl.ds(pl.multiple_of((1 - half) * LANES, LANES), LANES)
        for g, (mine, *theirs) in enumerate(piece_refs):
            weights[g, :, own] = mine[...]
            size_of = strip // len(theirs)
            for i, part in enumerate(theirs):
                weights[g, i * size_of : (i + 1) * size_of, other] = part[...]
        me = lax.axis_index("rhs")
        for out, s in zip(outs, [None] if slots is None else slots):
            first = 0 if s is None else pl.multiple_of(mate(me, s, n) * size, size)
            for start in range(0, 2 * size, block):
                here = slice(start, start + block)
                product = None
                for g in range(many):
                    for i in range(counts[g]):
                        left = jnp.concatenate(
                            [
                                k_refs[g][i, t, pl.ds(2 * first + start, block), :]
                                for t in range(tiles)
                            ],
                            axis=1,
                        )
                        term = jnp.dot(left, weights[g], preferred_element_type=F32)
                        product = term if product is None else product + term
                even_acc[here, :] = product[:, :LANES]
                odd_acc[here, :] = product[:, LANES:]
            even = even_acc[pl.ds(0, size, stride=2), :]
            odd = odd_acc[pl.ds(1, size, stride=2), :]
            total = even + odd
            if acc_ref is not None:
                total = total + acc_ref[pl.ds(first, size), :]
            out[...] = total

    args = [*packed, *(value for pair in pieces for value in pair)]
    args += [acc] if acc is not None else []
    *result, token = call(
        body,
        [shape(size)] * (1 if slots is None else len(slots)),
        *args,
        scratch=[
            pltpu.VMEM((many, strip, 2 * LANES), BF16),
            pltpu.VMEM((2 * size, LANES), F32),
            pltpu.VMEM((2 * size, LANES), F32),
        ],
        after=after,
    )
    return result, token


def link_groups(links):
    reach = (links - 1) // 2
    panels = lax.axis_size("panel")
    groups = []
    if links == 2 * panels + 1 and panels & (panels - 1) == 0:
        for s in sorted(range(panels), key=lambda s: (s > 0, s % 2)):

            def numbers(s=s):
                me = lax.axis_index("panel")
                start = lax.rem((me ^ s) - me + reach + panels, panels)
                return [start + panels * i for i in range(3 if s == 0 else 2)]

            bring = functools.partial(swapped, axis="panel", s=s, n=panels)
            groups.append((bring, numbers, 3 if s == 0 else 2))
        return groups
    offsets = {}
    for link in range(links):
        offsets.setdefault((link - reach) % panels, []).append(link)
    for o in sorted(offsets, key=lambda o: min(o, panels - o)):
        bring = functools.partial(shifted, axis="panel", by=o)
        groups.append((bring, functools.partial(list, offsets[o]), len(offsets[o])))
    return groups


def operate(packed, groups, low, direction, between, final):
    n = lax.axis_size("rhs")
    arrived = [low] + [bring(low) for bring, _, _ in groups[1:]]
    directions = [direction] + [swapped(direction, "rhs", s, n) for s in range(1, n)]
    pairs = [[low, swapped(low, "coef", 1, 2)]]
    (acc,), token = link_products(packed[:1], pairs, None, n, None)
    after = (token, between(token))
    held = (*after, *directions[1:])
    for piece in arrived[1:-1]:
        piece, _ = lax.optimization_barrier((piece, after))
        rows = piece.shape[0] // PARTS
        cut = [piece[i * rows : (i + 1) * rows] for i in range(PARTS)]
        pairs.append([piece, *(swapped(part, "coef", 1, 2) for part in cut)])
    if len(groups) > 2:
        (acc,), token = link_products(packed[1:-1], pairs[1:], acc, n, None, held)
        held = (token,)
    piece, held = lax.optimization_barrier((arrived[-1], held))
    pairs.append([piece, swapped(piece, "coef", 1, 2)])
    if final:
        parts, _ = link_products(packed[-1:], pairs[-1:], acc, n, range(n), held)
        return parts, directions
    mates, token = link_products(packed[-1:], pairs[-1:], acc, n, range(1, n), held)
    own, _ = link_products(packed[-1:], pairs[-1:], acc, n, [0], (token,))
    return own + mates, directions


PACKED = LANES // 2 + SUB


def corner():
    row = lax.broadcasted_iota(jnp.int32, (LANES // 2, LANES), 0)
    lane = lax.broadcasted_iota(jnp.int32, (LANES // 2, LANES), 1)
    return row, lane, lane < LANES // 2


def packed_symmetric(matrix):
    half = LANES // 2
    row, lane, left = corner()
    top = matrix[:half]
    last = pltpu.roll(matrix[half:], half, 1)
    body = jnp.where(left & (lane > row), last, top)
    diagonal = jnp.sum(jnp.where(lane == row, last, 0.0), axis=0, keepdims=True)
    return jnp.concatenate([body, jnp.broadcast_to(diagonal, (SUB, LANES))], axis=0)


def unpacked_symmetric(rows):
    half = LANES // 2
    row, lane, left = corner()
    body, diagonal = rows[:half], rows[half : half + 1]
    top = jnp.where(left & (lane >= row), 0.0, body)
    last = jnp.where(left & (lane > row), body, 0.0)
    sides = jnp.concatenate([top, pltpu.roll(last, half, 1)], axis=0)
    top = jnp.where(lane == row, body, 0.0)
    last = jnp.where(lane == row, jnp.broadcast_to(diagonal, body.shape), 0.0)
    return sides + sides.T + jnp.concatenate([top, pltpu.roll(last, half, 1)], axis=0)


def symmetric(raw):
    return 0.5 * (raw + raw.T)


JOINT = PACKED + SUB + LANES


def linear_grams(parts, directions, residual, turns, gram, final):
    strip = parts[0].shape[0]
    n = len(parts)
    first = gram is not None
    extra = [gram] if first else [] if final else [residual, *turns]
    rows = PACKED if final else JOINT // 2

    def body(*refs):
        images, ds = refs[:n], refs[n : 2 * n]
        rest = refs[2 * n : 2 * n + len(extra)]
        outs = refs[2 * n + len(extra) :]
        found = None
        for s in range(n):
            image, right = images[s][...], ds[s][...]
            if extra and not first:
                r = rest[0][...] if s == 0 else right - rest[s][...]
                right = jnp.concatenate([right, r], axis=1)
            term = mm(image, right, (0, 0))
            found = term if s == 0 else found + term
        if final:
            outs[0][...] = packed_symmetric(symmetric(found))
            return
        mine, mates, stacked = outs
        if first:
            stacked[:PACKED], whole = rest[0][...], found
        else:
            stacked[:PACKED] = packed_symmetric(symmetric(found[:, :LANES]))
            whole = found[:, LANES:]
        stacked[PACKED : PACKED + SUB] = jnp.zeros((SUB, LANES), F32)
        stacked[PACKED + SUB :] = whole
        half = lax.axis_index("coef")
        mine[...] = stacked[pl.ds(pl.multiple_of(half * rows, SUB), rows), :]
        mates[...] = stacked[pl.ds(pl.multiple_of((1 - half) * rows, SUB), rows), :]

    *pieces, _ = call(
        body,
        [shape(rows)] * (1 if final else 2),
        *parts,
        *directions,
        *extra,
        scratch=[] if final else [pltpu.VMEM((2 * rows, LANES), F32)],
    )
    return pieces


def gram_of(field, *tokens):
    def body(field, out):
        value = field[...]
        out[...] = packed_symmetric(mm(value, value, (0, 0)))

    return call(body, [shape(PACKED)], field, after=tokens)


def square_gram(image_parts):
    strip = image_parts[0].shape[0]
    parts = len(image_parts)

    def body(*refs):
        ins, image_out, out = refs[:parts], refs[parts], refs[parts + 1]
        image = ins[0][...]
        for ref in ins[1:]:
            image = image + ref[...]
        image_out[...] = image
        out[...] = packed_symmetric(mm(image, image, (0, 0)))

    image, square, _ = call(
        body,
        [shape(strip), shape(PACKED)],
        *image_parts,
    )
    return image, square


def reciprocal(value):
    near = pl.reciprocal(value, approx=True)
    for _ in range(2):
        near = near * (2.0 - value * near)
    return near


def next_pivot(column, following, i, inverse):
    product = column[i + 1 : i + 2] * following[i : i + 1]
    return following[i + 1 : i + 2] - product * inverse


def inverted(matrices, lane):
    strips = matrices[0].shape[0] // SUB
    place = lax.broadcasted_iota(jnp.int32, (SUB, LANES), 0)
    held = [[value[SUB * k : SUB * (k + 1)] for k in range(strips)] for value in matrices]

    def lanes_of(value, at):
        return jnp.broadcast_to(value[:, at : at + 1], (SUB, LANES))

    def rows_of(value):
        return [jnp.broadcast_to(value[i : i + 1], (SUB, LANES)) for i in range(SUB)]

    def update(k, j, spread):
        for a, rows in zip(held, spread):
            row = a[k]
            for i in range(SUB):
                row = row - lanes_of(a[k], lane + SUB * j + i) * rows[i]
            a[k] = row

    for j in range(strips):
        if j:
            spread = [rows_of(a[j - 1]) for a in held]
            update(j, j - 1, spread)
        waiting = [k for k in range(strips) if j and k not in (j, j - 1)]
        now = [
            [a[j], *(lanes_of(a[j], lane + SUB * j + i) for i in range(SUB))] for a in held
        ]
        for i in range(SUB):
            here = place == i
            for index, values in enumerate(now):
                column = values[1 + i]
                inverse = 1.0 / column[i : i + 1]

                def step(value):
                    row = value[i : i + 1] * inverse
                    return jnp.where(here, row, value - column * row)

                now[index] = [
                    step(value) if at < 1 or at > 1 + i else value
                    for at, value in enumerate(values)
                ]
            for k in waiting[i : i + 1]:
                update(k, j - 1, spread)
        for a, values in zip(held, now):
            a[j] = values[0]
    spread = [rows_of(a[-1]) for a in held]
    for k in range(strips - 1):
        update(k, strips - 1, spread)
    return [jnp.concatenate(a, axis=0) for a in held]


def eliminated(*systems):
    half = LANES // 2
    row = lax.broadcasted_iota(jnp.int32, (half, LANES), 0)
    lane = lax.broadcasted_iota(jnp.int32, (half, LANES), 1)
    left = lane < half
    first = inverted(
        [
            jnp.where(left, matrix[:half], (lane - half == row).astype(F32))
            for matrix, _ in systems
        ],
        0,
    )
    tops, lasts = [], []
    for (matrix, sides), value in zip(systems, first):
        value = pltpu.roll(value, half, 1)[:, :half]
        top = mm(value, jnp.concatenate([matrix[:half], sides[:half]], axis=1))
        low = jnp.concatenate([matrix[half:], sides[half:]], axis=1)
        tops.append(top)
        lasts.append(low - mm(matrix[half:, :half], top))
    second = inverted(
        [jnp.where(left, (lane == row).astype(F32), last[:, :LANES]) for last in lasts], half
    )
    found = []
    for top, last, value in zip(tops, lasts, second):
        low = mm(value[:, :half], last[:, LANES:])
        high = top[:, LANES:] - mm(
            top[:, :LANES], jnp.concatenate([jnp.zeros_like(low), low], axis=0)
        )
        found.append(jnp.concatenate([high, low], axis=0))
    return found


def eliminated_alone(matrix, sides):
    n = matrix.shape[0]
    strips = n // SUB
    place = lax.broadcasted_iota(jnp.int32, (SUB, LANES), 0)

    def cut(value):
        return [value[SUB * k : SUB * (k + 1)] for k in range(strips)]

    def lanes_of(value, lane):
        return jnp.broadcast_to(value[:, lane : lane + 1], (SUB, LANES))

    held = [(cut(matrix), cut(sides))]

    def rows_of(value):
        return [jnp.broadcast_to(value[i : i + 1], (SUB, LANES)) for i in range(SUB)]

    def update(k, j, spread):
        for (a, b), (rows_a, rows_b) in zip(held, spread):
            row_a, row_b = a[k], b[k]
            for i in range(SUB):
                factor = lanes_of(a[k], SUB * j + i)
                row_a = row_a - factor * rows_a[i]
                row_b = row_b - factor * rows_b[i]
            a[k], b[k] = row_a, row_b

    for j in range(strips):
        if j:
            spread = [(rows_of(a[j - 1]), rows_of(b[j - 1])) for a, b in held]
            update(j, j - 1, spread)
        waiting = [k for k in range(strips) if j and k not in (j, j - 1)]
        now = [
            [a[j], b[j], *(lanes_of(a[j], SUB * j + i) for i in range(SUB))] for a, b in held
        ]
        pivots = [values[2][:1] for values in now]
        for i in range(SUB):
            here = place == i
            for index, values in enumerate(now):
                column = values[2 + i]
                inverse = reciprocal(pivots[index])
                if i + 1 < SUB:
                    pivots[index] = next_pivot(column, values[3 + i], i, inverse)

                def step(value):
                    row = value[i : i + 1] * inverse
                    return jnp.where(here, row, value - column * row)

                now[index] = [
                    step(value) if place_of < 2 or place_of > 2 + i else value
                    for place_of, value in enumerate(values)
                ]
            for k in waiting[2 * i : 2 * i + 2]:
                update(k, j - 1, spread)
        for (a, b), values in zip(held, now):
            a[j], b[j] = values[:2]
    spread = [(rows_of(a[-1]), rows_of(b[-1])) for a, b in held]
    for k in range(strips - 1):
        update(k, strips - 1, spread)
    return jnp.concatenate(held[0][1], axis=0)


def identity():
    return (
        lax.broadcasted_iota(jnp.int32, (LANES, LANES), 0)
        == lax.broadcasted_iota(jnp.int32, (LANES, LANES), 1)
    ).astype(F32)


def stepped(solution, before, alpha, beta, token):
    fields = [*before, alpha, beta] + ([] if solution is None else [solution])
    n = len(before)

    def body(*refs):
        ds, a, b, refs = refs[:n], refs[n], refs[n + 1], refs[n + 2 :]
        change = mm(ds[0][...], a[...])
        refs[-n][...] = change if solution is None else refs[0][...] + change
        for s in range(1, n):
            refs[s - n][...] = mm(ds[s][...], b[...])

    solution, *turns, token = call(
        body, [shape(before[0].shape[0])] * n, *fields, after=[token]
    )
    return solution, turns, token


def finish(small, gram, residual, direction, solution, image):
    strip = residual.shape[0]

    def body(small, g, r, d, s, *refs):
        *images, out, new_r = refs
        alpha = eliminated_alone(unpacked_symmetric(small[...]), g[...])
        image = images[0][...]
        for ref in images[1:]:
            image = image + ref[...]
        out[...] = s[...] + mm(d[...], alpha)
        new_r[...] = r[...] - mm(image, alpha)

    return call(
        body,
        [shape(strip), shape(strip)],
        small,
        gram,
        residual,
        direction,
        solution,
        *image,
    )[:-1]


def step_sizes(pieces, gram):
    rows = pieces[0].shape[0]
    first = gram is None
    fields = [*pieces] + ([] if first else [gram])

    def body(mine, mates, *refs):
        *refs, alpha_out, whole_out, inverse_out, gram_out, raw = refs
        half = lax.axis_index("coef")
        raw[pl.ds(pl.multiple_of(half * rows, SUB), rows), :] = mine[...]
        raw[pl.ds(pl.multiple_of((1 - half) * rows, SUB), rows), :] = mates[...]
        sym, whole = unpacked_symmetric(raw[:PACKED, :]), raw[PACKED + SUB :, :]
        g = sym if first else refs[0][...]
        curvature = symmetric(whole) if first else sym
        alpha_out[...], inverse_out[...] = eliminated((curvature, g), (g, identity()))
        whole_out[...] = whole
        gram_out[...] = g

    return call(
        body,
        [shape(LANES)] * 4,
        *fields,
        scratch=[pltpu.VMEM((2 * rows, LANES), F32)],
    )[:-1]


def turn(square, alpha, whole, inverse, gram, residual, direction, image):
    strip = residual.shape[0]

    def body(alpha, whole, inverse, gram, r, d, image, *refs):
        *terms, r_out, new_d, low, beta_out, gram_out = refs
        square = terms[0][...]
        for ref in terms[1:]:
            square = square + ref[...]
        a = alpha[...]
        shared = mm(whole[...], a, (0, 0))
        quadratic = mm(a, mm(unpacked_symmetric(square), a), (0, 0))
        following = gram[...] - (shared + shared.T) + quadratic
        beta = mm(inverse[...], following)
        new_r = r[...] - mm(image[...], a)
        value = new_r + mm(d[...], beta)
        r_out[...] = new_r
        low[...] = value.astype(BF16)
        new_d[...] = value
        beta_out[...] = beta
        gram_out[...] = following

    return call(
        body,
        [shape(strip), shape(strip), shape(strip, dtype=BF16), shape(LANES), shape(LANES)],
        alpha,
        whole,
        inverse,
        gram,
        residual,
        direction,
        image,
        *square,
    )[:-1]


def shards(couplings, observations, replicate_mask):
    links, rows = couplings.shape[1], couplings.shape[3]
    strip = couplings.shape[6]
    blocks = couplings.reshape(links, rows, couplings.shape[4], strip)
    blocks = pltpu.with_memory_space_constraint(blocks, pltpu.HBM)
    n = lax.axis_size("rhs")
    obs_matrix = observations.reshape(observations.shape[0], rows)
    parts, token = right_side_parts(obs_matrix, replicate_mask, n, strip)
    own = [parts[0]] + [swapped(parts[s], "rhs", s, n) for s in range(1, n)]
    groups = link_groups(links)
    packed = []
    for _, numbers, count in groups[:2]:
        value, token = retiled(blocks, numbers, count, token)
        packed.append(value)
    residual, low, token = sum_and_round(own, token)
    for _, numbers, count in groups[2:]:
        value, token = retiled(blocks, numbers, count, token)
        packed.append(value)
    retile_token = token
    direction = residual
    solution = gram = beta = before = alpha = None
    for step in range(ITERS):
        first, final = step == 0, step + 1 == ITERS
        state = [solution, None, None]

        def between(token):
            if first:
                state[2], token = gram_of(residual, token, retile_token)
                return token
            *state[:2], token = stepped(solution, before, alpha, beta, token)
            return token

        parts, directions = operate(packed, groups, low, direction, between, final)
        solution, turns, own_gram = state
        image_parts = [parts[0]] + [swapped(parts[s], "rhs", s, n) for s in range(1, n)]
        linear = linear_grams(parts, directions, residual, turns, own_gram, final)
        if final:
            small = reduce_one(*linear)
            solution, residual = finish(
                small, gram, residual, direction, solution, image_parts
            )
            break
        image, square = square_gram(image_parts)
        linear, square = reduce_both(*linear, square)
        alpha, whole, inverse, gram = step_sizes(linear, gram)
        square[1:], alpha = lax.optimization_barrier((square[1:], alpha))
        before = directions
        residual, direction, low, beta, gram = turn(
            square, alpha, whole, inverse, gram, residual, direction, image
        )
    shape_out = (1, 1, strip, LANES)
    return (solution.reshape(shape_out), residual.reshape(shape_out))


def solution(mesh):
    placed = (
        P("panel", None, "coef", None, None, "rhs", None),
        P(("groups", "rhs"), "panel", "coef", None),
        P(("groups", "rhs"), None),
    )
    return jax.shard_map(
        shards,
        mesh=mesh,
        in_specs=placed,
        out_specs=(
            P(("groups", "panel"), "coef", "rhs", None),
            P(("groups", "panel"), "coef", "rhs", None),
        ),
        check_vma=False,
    )
```

```python
import functools

import jax
import jax.numpy as jnp
from jax import lax
from jax.experimental import pallas as pl
from jax.experimental.pallas import tpu as pltpu
from jax.sharding import PartitionSpec as P

ITERS = 3
PARTS = 2
LANES = 128
SUB = 8
VMEM_LIMIT = 14 * 2**20
F32 = jnp.float32
BF16 = jnp.bfloat16
VMEM = pl.BlockSpec(memory_space=pltpu.VMEM)
ANY = pl.BlockSpec(memory_space=pl.ANY)
HBM = pl.BlockSpec(memory_space=pltpu.HBM)


def mm(a, b, dims=(1, 0)):
    return lax.dot_general(
        a,
        b,
        (((dims[0],), (dims[1],)), ((), ())),
        precision=lax.Precision.HIGHEST,
        preferred_element_type=F32,
    )


def call(body, outs, *args, scratch=(), after=(), any_args=0, any_outs=False):
    inputs, outputs, waits = len(args), len(outs), len(after)

    def ordered(*refs):
        token = refs[inputs + waits + outputs]
        token[...] = jnp.zeros_like(token)
        body(
            *refs[:inputs],
            *refs[inputs + waits : inputs + waits + outputs],
            *refs[inputs + waits + outputs + 1 :],
        )

    return pl.pallas_call(
        ordered,
        out_shape=list(outs) + [shape(SUB)],
        in_specs=[HBM] * any_args + [VMEM] * (inputs - any_args) + [ANY] * waits,
        out_specs=[ANY if any_outs else VMEM] * outputs + [VMEM],
        scratch_shapes=list(scratch),
        cost_estimate=pl.CostEstimate(flops=1, bytes_accessed=1, transcendentals=0),
        compiler_params=pltpu.CompilerParams(vmem_limit_bytes=VMEM_LIMIT),
    )(*args, *after)


def shape(rows, cols=LANES, dtype=F32):
    return jax.ShapeDtypeStruct((rows, cols), dtype)


def permute(value, axis, pairs):
    return lax.ppermute(value, axis, pairs)


def shifted(value, axis, by):
    n = lax.axis_size(axis)
    return permute(value, axis, [((i + by) % n, i) for i in range(n)])


def mate(i, s, n):
    return i ^ s if n & (n - 1) == 0 else (s - i) % n


def swapped(value, axis, s, n):
    return permute(value, axis, [(mate(i, s, n), i) for i in range(n)])


def sum_near(value):
    axes = ("panel", "rhs")
    count = lax.axis_size(axes)
    three, two, one = (swapped(value, axes, s, count) for s in (3, 2, 1))
    return (value + one) + (two + three)


def from_far(value):
    axes = ("panel", "rhs")
    return swapped(value, axes, 4, lax.axis_size(axes))


def sum_far(value, meanwhile=None):
    other = from_far(value)
    if meanwhile is not None:
        other, _ = lax.optimization_barrier((other, meanwhile))
    return value + other


def by_stages():
    return lax.axis_size("panel") == 4 and lax.axis_size("rhs") == 2


def reduce_one(value):
    value = value + swapped(value, "coef", 1, 2)
    if not by_stages():
        return lax.psum(value, ("panel", "rhs"))
    return sum_far(sum_near(value))


def reduce_both(mine, mates, square):
    value = mine + swapped(mates, "coef", 1, 2)
    whole = square + swapped(square, "coef", 1, 2)
    if by_stages():
        rows = value.shape[0]
        value = sum_far(value, meanwhile=square)
        both = sum_near(jnp.concatenate([value, whole], axis=0))
        value, whole = both[:rows], both[rows:]
        terms = [whole, from_far(whole)]
    else:
        value, whole = lax.psum((value, whole), ("panel", "rhs"))
        terms = [whole]
    return [value, swapped(value, "coef", 1, 2)], terms


def right_side_parts(obs, mask, n, strip):
    def body(obs_hbm, mask_hbm, *refs):
        *outs, obs_ref, mask_ref, sems = refs
        copies = [
            pltpu.make_async_copy(mask_hbm, mask_ref, sems.at[0]),
            pltpu.make_async_copy(obs_hbm, obs_ref, sems.at[1]),
        ]
        for copy in copies:
            copy.start()
        for copy in copies:
            copy.wait()
        signs = (2 * mask_ref[...] - 1).astype(BF16)
        me = lax.axis_index("rhs")
        for s in range(n):
            place = pl.multiple_of(mate(me, s, n) * strip, strip)
            outs[s][...] = lax.dot_general(
                obs_ref[:, pl.ds(place, strip)],
                signs,
                (((0,), (0,)), ((), ())),
                preferred_element_type=F32,
            )

    *parts, token = call(
        body,
        [shape(strip)] * n,
        pltpu.with_memory_space_constraint(obs, pltpu.HBM),
        pltpu.with_memory_space_constraint(mask, pltpu.HBM),
        scratch=[
            pltpu.VMEM(obs.shape, BF16),
            pltpu.VMEM(mask.shape, mask.dtype),
            pltpu.SemaphoreType.DMA((2,)),
        ],
        any_args=2,
    )
    return parts, token


def sum_and_round(parts, token):
    strip = parts[0].shape[0]

    def body(*refs):
        *ins, out, low = refs
        total = ins[0][...]
        for ref in ins[1:]:
            total = total + ref[...]
        out[...] = total
        low[...] = total.astype(BF16)

    return call(
        body, [shape(strip), shape(strip, dtype=BF16)], *parts, after=[token]
    )


def retiled(blocks, links, count, token):
    rows, strip = blocks.shape[1], blocks.shape[3]
    tiles = strip // LANES

    def body(k_ref, out, sems):
        copies = []
        for i, link in enumerate(links()):
            for t in range(tiles):
                copy = pltpu.make_async_copy(
                    k_ref.at[link, :, :, pl.ds(t * LANES, LANES)], out.at[i, t], sems.at[i, t]
                )
                copy.start()
                copies.append(copy)
        for copy in copies:
            copy.wait()

    packed, token = call(
        body,
        [pltpu.VMEM((count, tiles, rows, 2, LANES), BF16)],
        blocks,
        scratch=[pltpu.SemaphoreType.DMA((count, tiles))],
        after=[token],
        any_args=1,
        any_outs=True,
    )
    return packed, token


def link_products(packed, pieces, acc, n, slots, after=()):
    tiles, rows = packed[0].shape[1:3]
    counts = [value.shape[0] for value in packed]
    many = len(packed)
    packed = [
        pltpu.with_memory_space_constraint(
            value.reshape(value.shape[0], tiles, 2 * rows, LANES), pltpu.VMEM
        )
        for value in packed
    ]
    strip = tiles * LANES
    size = rows if slots is None else rows // n
    block = min(512, 2 * size)

    def body(*refs):
        k_refs, refs = refs[:many], refs[many:]
        piece_refs = []
        for pair in pieces:
            piece_refs.append(refs[: len(pair)])
            refs = refs[len(pair) :]
        acc_ref = refs[0] if acc is not None else None
        outs = refs[acc is not None : -3]
        weights, even_acc, odd_acc = refs[-3:]
        half = lax.axis_index("coef")
        own = pl.ds(pl.multiple_of(half * LANES, LANES), LANES)
        other = pl.ds(pl.multiple_of((1 - half) * LANES, LANES), LANES)
        for g, (mine, *theirs) in enumerate(piece_refs):
            weights[g, :, own] = mine[...]
            size_of = strip // len(theirs)
            for i, part in enumerate(theirs):
                weights[g, i * size_of : (i + 1) * size_of, other] = part[...]
        me = lax.axis_index("rhs")
        for out, s in zip(outs, [None] if slots is None else slots):
            first = 0 if s is None else pl.multiple_of(mate(me, s, n) * size, size)
            for start in range(0, 2 * size, block):
                here = slice(start, start + block)
                product = None
                for g in range(many):
                    for i in range(counts[g]):
                        left = jnp.concatenate(
                            [
                                k_refs[g][i, t, pl.ds(2 * first + start, block), :]
                                for t in range(tiles)
                            ],
                            axis=1,
                        )
                        term = jnp.dot(left, weights[g], preferred_element_type=F32)
                        product = term if product is None else product + term
                even_acc[here, :] = product[:, :LANES]
                odd_acc[here, :] = product[:, LANES:]
            even = even_acc[pl.ds(0, size, stride=2), :]
            odd = odd_acc[pl.ds(1, size, stride=2), :]
            total = even + odd
            if acc_ref is not None:
                total = total + acc_ref[pl.ds(first, size), :]
            out[...] = total

    args = [*packed, *(value for pair in pieces for value in pair)]
    args += [acc] if acc is not None else []
    *result, token = call(
        body,
        [shape(size)] * (1 if slots is None else len(slots)),
        *args,
        scratch=[
            pltpu.VMEM((many, strip, 2 * LANES), BF16),
            pltpu.VMEM((2 * size, LANES), F32),
            pltpu.VMEM((2 * size, LANES), F32),
        ],
        after=after,
    )
    return result, token


def link_groups(links):
    reach = (links - 1) // 2
    panels = lax.axis_size("panel")
    groups = []
    if links == 2 * panels + 1 and panels & (panels - 1) == 0:
        for s in range(panels):

            def numbers(s=s):
                me = lax.axis_index("panel")
                start = lax.rem((me ^ s) - me + reach + panels, panels)
                return [start + panels * i for i in range(3 if s == 0 else 2)]

            bring = functools.partial(swapped, axis="panel", s=s, n=panels)
            groups.append((bring, numbers, 3 if s == 0 else 2))
        return groups
    offsets = {}
    for link in range(links):
        offsets.setdefault((link - reach) % panels, []).append(link)
    for o in sorted(offsets, key=lambda o: min(o, panels - o)):
        bring = functools.partial(shifted, axis="panel", by=o)
        groups.append((bring, functools.partial(list, offsets[o]), len(offsets[o])))
    return groups


def operate(packed, groups, low, direction, between, final):
    n = lax.axis_size("rhs")
    arrived = [low] + [bring(low) for bring, _, _ in groups[1:]]
    directions = [direction] + [swapped(direction, "rhs", s, n) for s in range(1, n)]
    pairs = [[low, swapped(low, "coef", 1, 2)]]
    (acc,), token = link_products(packed[:1], pairs, None, n, None)
    after = (token, between(token))
    held = (*after, *directions[1:])
    for piece in arrived[1:-1]:
        piece, _ = lax.optimization_barrier((piece, after))
        rows = piece.shape[0] // PARTS
        cut = [piece[i * rows : (i + 1) * rows] for i in range(PARTS)]
        pairs.append([piece, *(swapped(part, "coef", 1, 2) for part in cut)])
    if len(groups) > 2:
        (acc,), token = link_products(packed[1:-1], pairs[1:], acc, n, None, held)
        held = (token,)
    piece, held = lax.optimization_barrier((arrived[-1], held))
    pairs.append([piece, swapped(piece, "coef", 1, 2)])
    if final:
        parts, _ = link_products(packed[-1:], pairs[-1:], acc, n, range(n), held)
        return parts, directions
    mates, token = link_products(packed[-1:], pairs[-1:], acc, n, range(1, n), held)
    own, _ = link_products(packed[-1:], pairs[-1:], acc, n, [0], (token,))
    return own + mates, directions


PACKED = LANES // 2 + SUB


def corner():
    row = lax.broadcasted_iota(jnp.int32, (LANES // 2, LANES), 0)
    lane = lax.broadcasted_iota(jnp.int32, (LANES // 2, LANES), 1)
    return row, lane, lane < LANES // 2


def packed_symmetric(matrix):
    half = LANES // 2
    row, lane, left = corner()
    top = matrix[:half]
    last = pltpu.roll(matrix[half:], half, 1)
    body = jnp.where(left & (lane > row), last, top)
    diagonal = jnp.sum(jnp.where(lane == row, last, 0.0), axis=0, keepdims=True)
    return jnp.concatenate([body, jnp.broadcast_to(diagonal, (SUB, LANES))], axis=0)


def unpacked_symmetric(rows):
    half = LANES // 2
    row, lane, left = corner()
    body, diagonal = rows[:half], rows[half : half + 1]
    top = jnp.where(left & (lane >= row), 0.0, body)
    last = jnp.where(left & (lane > row), body, 0.0)
    sides = jnp.concatenate([top, pltpu.roll(last, half, 1)], axis=0)
    top = jnp.where(lane == row, body, 0.0)
    last = jnp.where(lane == row, jnp.broadcast_to(diagonal, body.shape), 0.0)
    return sides + sides.T + jnp.concatenate([top, pltpu.roll(last, half, 1)], axis=0)


def symmetric(raw):
    return 0.5 * (raw + raw.T)


JOINT = PACKED + SUB + LANES


def linear_grams(parts, directions, residual, turns, gram, final):
    strip = parts[0].shape[0]
    n = len(parts)
    first = gram is not None
    extra = [gram] if first else [] if final else [residual, *turns]
    rows = PACKED if final else JOINT // 2

    def body(*refs):
        images, ds = refs[:n], refs[n : 2 * n]
        rest = refs[2 * n : 2 * n + len(extra)]
        outs = refs[2 * n + len(extra) :]
        found = None
        for s in range(n):
            image, right = images[s][...], ds[s][...]
            if extra and not first:
                r = rest[0][...] if s == 0 else right - rest[s][...]
                right = jnp.concatenate([right, r], axis=1)
            term = mm(image, right, (0, 0))
            found = term if s == 0 else found + term
        if final:
            outs[0][...] = packed_symmetric(symmetric(found))
            return
        mine, mates, stacked = outs
        if first:
            stacked[:PACKED], whole = rest[0][...], found
        else:
            stacked[:PACKED] = packed_symmetric(symmetric(found[:, :LANES]))
            whole = found[:, LANES:]
        stacked[PACKED : PACKED + SUB] = jnp.zeros((SUB, LANES), F32)
        stacked[PACKED + SUB :] = whole
        half = lax.axis_index("coef")
        mine[...] = stacked[pl.ds(pl.multiple_of(half * rows, SUB), rows), :]
        mates[...] = stacked[pl.ds(pl.multiple_of((1 - half) * rows, SUB), rows), :]

    *pieces, _ = call(
        body,
        [shape(rows)] * (1 if final else 2),
        *parts,
        *directions,
        *extra,
        scratch=[] if final else [pltpu.VMEM((2 * rows, LANES), F32)],
    )
    return pieces


def gram_of(field, *tokens):
    def body(field, out):
        value = field[...]
        out[...] = packed_symmetric(mm(value, value, (0, 0)))

    return call(body, [shape(PACKED)], field, after=tokens)


def square_gram(image_parts):
    strip = image_parts[0].shape[0]
    parts = len(image_parts)

    def body(*refs):
        ins, image_out, out = refs[:parts], refs[parts], refs[parts + 1]
        image = ins[0][...]
        for ref in ins[1:]:
            image = image + ref[...]
        image_out[...] = image
        out[...] = packed_symmetric(mm(image, image, (0, 0)))

    image, square, _ = call(
        body,
        [shape(strip), shape(PACKED)],
        *image_parts,
    )
    return image, square


def reciprocal(value):
    near = pl.reciprocal(value, approx=True)
    for _ in range(2):
        near = near * (2.0 - value * near)
    return near


def next_pivot(column, following, i, inverse):
    product = column[i + 1 : i + 2] * following[i : i + 1]
    return following[i + 1 : i + 2] - product * inverse


def inverted(matrices, lane):
    strips = matrices[0].shape[0] // SUB
    place = lax.broadcasted_iota(jnp.int32, (SUB, LANES), 0)
    held = [[value[SUB * k : SUB * (k + 1)] for k in range(strips)] for value in matrices]

    def lanes_of(value, at):
        return jnp.broadcast_to(value[:, at : at + 1], (SUB, LANES))

    def rows_of(value):
        return [jnp.broadcast_to(value[i : i + 1], (SUB, LANES)) for i in range(SUB)]

    def update(k, j, spread):
        for a, rows in zip(held, spread):
            row = a[k]
            for i in range(SUB):
                row = row - lanes_of(a[k], lane + SUB * j + i) * rows[i]
            a[k] = row

    for j in range(strips):
        if j:
            spread = [rows_of(a[j - 1]) for a in held]
            update(j, j - 1, spread)
        waiting = [k for k in range(strips) if j and k not in (j, j - 1)]
        now = [
            [a[j], *(lanes_of(a[j], lane + SUB * j + i) for i in range(SUB))] for a in held
        ]
        for i in range(SUB):
            here = place == i
            for index, values in enumerate(now):
                column = values[1 + i]
                inverse = 1.0 / column[i : i + 1]

                def step(value):
                    row = value[i : i + 1] * inverse
                    return jnp.where(here, row, value - column * row)

                now[index] = [
                    step(value) if at < 1 or at > 1 + i else value
                    for at, value in enumerate(values)
                ]
            for k in waiting[i : i + 1]:
                update(k, j - 1, spread)
        for a, values in zip(held, now):
            a[j] = values[0]
    spread = [rows_of(a[-1]) for a in held]
    for k in range(strips - 1):
        update(k, strips - 1, spread)
    return [jnp.concatenate(a, axis=0) for a in held]


def eliminated(*systems):
    half = LANES // 2
    row = lax.broadcasted_iota(jnp.int32, (half, LANES), 0)
    lane = lax.broadcasted_iota(jnp.int32, (half, LANES), 1)
    left = lane < half
    first = inverted(
        [
            jnp.where(left, matrix[:half], (lane - half == row).astype(F32))
            for matrix, _ in systems
        ],
        0,
    )
    tops, lasts = [], []
    for (matrix, sides), value in zip(systems, first):
        value = pltpu.roll(value, half, 1)[:, :half]
        top = mm(value, jnp.concatenate([matrix[:half], sides[:half]], axis=1))
        low = jnp.concatenate([matrix[half:], sides[half:]], axis=1)
        tops.append(top)
        lasts.append(low - mm(matrix[half:, :half], top))
    second = inverted(
        [jnp.where(left, (lane == row).astype(F32), last[:, :LANES]) for last in lasts], half
    )
    found = []
    for top, last, value in zip(tops, lasts, second):
        low = mm(value[:, :half], last[:, LANES:])
        high = top[:, LANES:] - mm(
            top[:, :LANES], jnp.concatenate([jnp.zeros_like(low), low], axis=0)
        )
        found.append(jnp.concatenate([high, low], axis=0))
    return found


def eliminated_alone(matrix, sides):
    n = matrix.shape[0]
    strips = n // SUB
    place = lax.broadcasted_iota(jnp.int32, (SUB, LANES), 0)

    def cut(value):
        return [value[SUB * k : SUB * (k + 1)] for k in range(strips)]

    def lanes_of(value, lane):
        return jnp.broadcast_to(value[:, lane : lane + 1], (SUB, LANES))

    held = [(cut(matrix), cut(sides))]

    def rows_of(value):
        return [jnp.broadcast_to(value[i : i + 1], (SUB, LANES)) for i in range(SUB)]

    def update(k, j, spread):
        for (a, b), (rows_a, rows_b) in zip(held, spread):
            row_a, row_b = a[k], b[k]
            for i in range(SUB):
                factor = lanes_of(a[k], SUB * j + i)
                row_a = row_a - factor * rows_a[i]
                row_b = row_b - factor * rows_b[i]
            a[k], b[k] = row_a, row_b

    for j in range(strips):
        if j:
            spread = [(rows_of(a[j - 1]), rows_of(b[j - 1])) for a, b in held]
            update(j, j - 1, spread)
        waiting = [k for k in range(strips) if j and k not in (j, j - 1)]
        now = [
            [a[j], b[j], *(lanes_of(a[j], SUB * j + i) for i in range(SUB))] for a, b in held
        ]
        pivots = [values[2][:1] for values in now]
        for i in range(SUB):
            here = place == i
            for index, values in enumerate(now):
                column = values[2 + i]
                inverse = reciprocal(pivots[index])
                if i + 1 < SUB:
                    pivots[index] = next_pivot(column, values[3 + i], i, inverse)

                def step(value):
                    row = value[i : i + 1] * inverse
                    return jnp.where(here, row, value - column * row)

                now[index] = [
                    step(value) if place_of < 2 or place_of > 2 + i else value
                    for place_of, value in enumerate(values)
                ]
            for k in waiting[2 * i : 2 * i + 2]:
                update(k, j - 1, spread)
        for (a, b), values in zip(held, now):
            a[j], b[j] = values[:2]
    spread = [(rows_of(a[-1]), rows_of(b[-1])) for a, b in held]
    for k in range(strips - 1):
        update(k, strips - 1, spread)
    return jnp.concatenate(held[0][1], axis=0)


def identity():
    return (
        lax.broadcasted_iota(jnp.int32, (LANES, LANES), 0)
        == lax.broadcasted_iota(jnp.int32, (LANES, LANES), 1)
    ).astype(F32)


def stepped(solution, before, alpha, beta, token):
    fields = [*before, alpha, beta] + ([] if solution is None else [solution])
    n = len(before)

    def body(*refs):
        ds, a, b, refs = refs[:n], refs[n], refs[n + 1], refs[n + 2 :]
        change = mm(ds[0][...], a[...])
        refs[-n][...] = change if solution is None else refs[0][...] + change
        for s in range(1, n):
            refs[s - n][...] = mm(ds[s][...], b[...])

    solution, *turns, token = call(
        body, [shape(before[0].shape[0])] * n, *fields, after=[token]
    )
    return solution, turns, token


def finish(small, gram, residual, direction, solution, image):
    strip = residual.shape[0]

    def body(small, g, r, d, s, *refs):
        *images, out, new_r = refs
        alpha = eliminated_alone(unpacked_symmetric(small[...]), g[...])
        image = images[0][...]
        for ref in images[1:]:
            image = image + ref[...]
        out[...] = s[...] + mm(d[...], alpha)
        new_r[...] = r[...] - mm(image, alpha)

    return call(
        body,
        [shape(strip), shape(strip)],
        small,
        gram,
        residual,
        direction,
        solution,
        *image,
    )[:-1]


def step_sizes(pieces, gram):
    rows = pieces[0].shape[0]
    first = gram is None
    fields = [*pieces] + ([] if first else [gram])

    def body(mine, mates, *refs):
        *refs, alpha_out, whole_out, inverse_out, gram_out, raw = refs
        half = lax.axis_index("coef")
        raw[pl.ds(pl.multiple_of(half * rows, SUB), rows), :] = mine[...]
        raw[pl.ds(pl.multiple_of((1 - half) * rows, SUB), rows), :] = mates[...]
        sym, whole = unpacked_symmetric(raw[:PACKED, :]), raw[PACKED + SUB :, :]
        g = sym if first else refs[0][...]
        curvature = symmetric(whole) if first else sym
        alpha_out[...], inverse_out[...] = eliminated((curvature, g), (g, identity()))
        whole_out[...] = whole
        gram_out[...] = g

    return call(
        body,
        [shape(LANES)] * 4,
        *fields,
        scratch=[pltpu.VMEM((2 * rows, LANES), F32)],
    )[:-1]


def turn(square, alpha, whole, inverse, gram, residual, direction, image):
    strip = residual.shape[0]

    def body(alpha, whole, inverse, gram, r, d, image, *refs):
        *terms, r_out, new_d, low, beta_out, gram_out = refs
        square = terms[0][...]
        for ref in terms[1:]:
            square = square + ref[...]
        a = alpha[...]
        shared = mm(whole[...], a, (0, 0))
        quadratic = mm(a, mm(unpacked_symmetric(square), a), (0, 0))
        following = gram[...] - (shared + shared.T) + quadratic
        beta = mm(inverse[...], following)
        new_r = r[...] - mm(image[...], a)
        value = new_r + mm(d[...], beta)
        r_out[...] = new_r
        low[...] = value.astype(BF16)
        new_d[...] = value
        beta_out[...] = beta
        gram_out[...] = following

    return call(
        body,
        [shape(strip), shape(strip), shape(strip, dtype=BF16), shape(LANES), shape(LANES)],
        alpha,
        whole,
        inverse,
        gram,
        residual,
        direction,
        image,
        *square,
    )[:-1]


def shards(couplings, observations, replicate_mask):
    links, rows = couplings.shape[1], couplings.shape[3]
    strip = couplings.shape[6]
    blocks = couplings.reshape(links, rows, couplings.shape[4], strip)
    blocks = pltpu.with_memory_space_constraint(blocks, pltpu.HBM)
    n = lax.axis_size("rhs")
    obs_matrix = observations.reshape(observations.shape[0], rows)
    parts, token = right_side_parts(obs_matrix, replicate_mask, n, strip)
    own = [parts[0]] + [swapped(parts[s], "rhs", s, n) for s in range(1, n)]
    groups = link_groups(links)
    packed = []
    for _, numbers, count in groups[:2]:
        value, token = retiled(blocks, numbers, count, token)
        packed.append(value)
    residual, low, token = sum_and_round(own, token)
    for _, numbers, count in groups[2:]:
        value, token = retiled(blocks, numbers, count, token)
        packed.append(value)
    retile_token = token
    direction = residual
    solution = gram = beta = before = alpha = None
    for step in range(ITERS):
        first, final = step == 0, step + 1 == ITERS
        state = [solution, None, None]

        def between(token):
            if first:
                state[2], token = gram_of(residual, token, retile_token)
                return token
            *state[:2], token = stepped(solution, before, alpha, beta, token)
            return token

        parts, directions = operate(packed, groups, low, direction, between, final)
        solution, turns, own_gram = state
        image_parts = [parts[0]] + [swapped(parts[s], "rhs", s, n) for s in range(1, n)]
        linear = linear_grams(parts, directions, residual, turns, own_gram, final)
        if final:
            small = reduce_one(*linear)
            solution, residual = finish(
                small, gram, residual, direction, solution, image_parts
            )
            break
        image, square = square_gram(image_parts)
        linear, square = reduce_both(*linear, square)
        alpha, whole, inverse, gram = step_sizes(linear, gram)
        square[1:], alpha = lax.optimization_barrier((square[1:], alpha))
        before = directions
        residual, direction, low, beta, gram = turn(
            square, alpha, whole, inverse, gram, residual, direction, image
        )
    shape_out = (1, 1, strip, LANES)
    return (solution.reshape(shape_out), residual.reshape(shape_out))


def solution(mesh):
    placed = (
        P("panel", None, "coef", None, None, "rhs", None),
        P(("groups", "rhs"), "panel", "coef", None),
        P(("groups", "rhs"), None),
    )
    return jax.shard_map(
        shards,
        mesh=mesh,
        in_specs=placed,
        out_specs=(
            P(("groups", "panel"), "coef", "rhs", None),
            P(("groups", "panel"), "coef", "rhs", None),
        ),
        check_vma=False,
    )
```

```python
import functools

import jax
import jax.numpy as jnp
from jax import lax
from jax.experimental import pallas as pl
from jax.experimental.pallas import tpu as pltpu
from jax.sharding import PartitionSpec as P

ITERS = 3
PARTS = 2
LANES = 128
SUB = 8
VMEM_LIMIT = 14 * 2**20
F32 = jnp.float32
BF16 = jnp.bfloat16
VMEM = pl.BlockSpec(memory_space=pltpu.VMEM)
ANY = pl.BlockSpec(memory_space=pl.ANY)
HBM = pl.BlockSpec(memory_space=pltpu.HBM)


def mm(a, b, dims=(1, 0)):
    return lax.dot_general(
        a,
        b,
        (((dims[0],), (dims[1],)), ((), ())),
        precision=lax.Precision.HIGHEST,
        preferred_element_type=F32,
    )


def call(body, outs, *args, scratch=(), after=(), any_args=0, any_outs=False):
    inputs, outputs, waits = len(args), len(outs), len(after)

    def ordered(*refs):
        token = refs[inputs + waits + outputs]
        token[...] = jnp.zeros_like(token)
        body(
            *refs[:inputs],
            *refs[inputs + waits : inputs + waits + outputs],
            *refs[inputs + waits + outputs + 1 :],
        )

    return pl.pallas_call(
        ordered,
        out_shape=list(outs) + [shape(SUB)],
        in_specs=[HBM] * any_args + [VMEM] * (inputs - any_args) + [ANY] * waits,
        out_specs=[ANY if any_outs else VMEM] * outputs + [VMEM],
        scratch_shapes=list(scratch),
        cost_estimate=pl.CostEstimate(flops=1, bytes_accessed=1, transcendentals=0),
        compiler_params=pltpu.CompilerParams(vmem_limit_bytes=VMEM_LIMIT),
    )(*args, *after)


def shape(rows, cols=LANES, dtype=F32):
    return jax.ShapeDtypeStruct((rows, cols), dtype)


def permute(value, axis, pairs):
    return lax.ppermute(value, axis, pairs)


def shifted(value, axis, by):
    n = lax.axis_size(axis)
    return permute(value, axis, [((i + by) % n, i) for i in range(n)])


def mate(i, s, n):
    return i ^ s if n & (n - 1) == 0 else (s - i) % n


def swapped(value, axis, s, n):
    return permute(value, axis, [(mate(i, s, n), i) for i in range(n)])


def sum_near(value):
    axes = ("panel", "rhs")
    count = lax.axis_size(axes)
    three, two, one = (swapped(value, axes, s, count) for s in (3, 2, 1))
    return (value + one) + (two + three)


def from_far(value):
    axes = ("panel", "rhs")
    return swapped(value, axes, 4, lax.axis_size(axes))


def sum_far(value, meanwhile=None):
    other = from_far(value)
    if meanwhile is not None:
        other, _ = lax.optimization_barrier((other, meanwhile))
    return value + other


def by_stages():
    return lax.axis_size("panel") == 4 and lax.axis_size("rhs") == 2


def reduce_one(value):
    value = value + swapped(value, "coef", 1, 2)
    if not by_stages():
        return lax.psum(value, ("panel", "rhs"))
    return sum_far(sum_near(value))


def reduce_both(mine, mates, square):
    value = mine + swapped(mates, "coef", 1, 2)
    whole = square + swapped(square, "coef", 1, 2)
    if by_stages():
        rows = value.shape[0]
        value = sum_far(value, meanwhile=square)
        both = sum_near(jnp.concatenate([value, whole], axis=0))
        value, whole = both[:rows], both[rows:]
        terms = [whole, from_far(whole)]
    else:
        value, whole = lax.psum((value, whole), ("panel", "rhs"))
        terms = [whole]
    return [value, swapped(value, "coef", 1, 2)], terms


def right_side_parts(obs, mask, n, strip):
    def body(obs_hbm, mask_hbm, *refs):
        *outs, obs_ref, mask_ref, sems = refs
        copies = [
            pltpu.make_async_copy(mask_hbm, mask_ref, sems.at[0]),
            pltpu.make_async_copy(obs_hbm, obs_ref, sems.at[1]),
        ]
        for copy in copies:
            copy.start()
        for copy in copies:
            copy.wait()
        signs = (2 * mask_ref[...] - 1).astype(BF16)
        me = lax.axis_index("rhs")
        for s in range(n):
            place = pl.multiple_of(mate(me, s, n) * strip, strip)
            outs[s][...] = lax.dot_general(
                obs_ref[:, pl.ds(place, strip)],
                signs,
                (((0,), (0,)), ((), ())),
                preferred_element_type=F32,
            )

    *parts, token = call(
        body,
        [shape(strip)] * n,
        pltpu.with_memory_space_constraint(obs, pltpu.HBM),
        pltpu.with_memory_space_constraint(mask, pltpu.HBM),
        scratch=[
            pltpu.VMEM(obs.shape, BF16),
            pltpu.VMEM(mask.shape, mask.dtype),
            pltpu.SemaphoreType.DMA((2,)),
        ],
        any_args=2,
    )
    return parts, token


def sum_and_round(parts, token):
    strip = parts[0].shape[0]

    def body(*refs):
        *ins, out, low = refs
        total = ins[0][...]
        for ref in ins[1:]:
            total = total + ref[...]
        out[...] = total
        low[...] = total.astype(BF16)

    return call(
        body, [shape(strip), shape(strip, dtype=BF16)], *parts, after=[token]
    )


def retiled(blocks, links, count, token):
    rows, strip = blocks.shape[1], blocks.shape[3]
    tiles = strip // LANES

    def body(k_ref, out, sems):
        copies = []
        for i, link in enumerate(links()):
            for t in range(tiles):
                copy = pltpu.make_async_copy(
                    k_ref.at[link, :, :, pl.ds(t * LANES, LANES)], out.at[i, t], sems.at[i, t]
                )
                copy.start()
                copies.append(copy)
        for copy in copies:
            copy.wait()

    packed, token = call(
        body,
        [pltpu.VMEM((count, tiles, rows, 2, LANES), BF16)],
        blocks,
        scratch=[pltpu.SemaphoreType.DMA((count, tiles))],
        after=[token],
        any_args=1,
        any_outs=True,
    )
    return packed, token


def link_products(packed, pieces, acc, n, slots, after=()):
    tiles, rows = packed[0].shape[1:3]
    counts = [value.shape[0] for value in packed]
    many = len(packed)
    packed = [
        pltpu.with_memory_space_constraint(
            value.reshape(value.shape[0], tiles, 2 * rows, LANES), pltpu.VMEM
        )
        for value in packed
    ]
    strip = tiles * LANES
    size = rows if slots is None else rows // n
    block = min(512, 2 * size)

    def body(*refs):
        k_refs, refs = refs[:many], refs[many:]
        piece_refs = []
        for pair in pieces:
            piece_refs.append(refs[: len(pair)])
            refs = refs[len(pair) :]
        acc_ref = refs[0] if acc is not None else None
        outs = refs[acc is not None : -3]
        weights, even_acc, odd_acc = refs[-3:]
        half = lax.axis_index("coef")
        own = pl.ds(pl.multiple_of(half * LANES, LANES), LANES)
        other = pl.ds(pl.multiple_of((1 - half) * LANES, LANES), LANES)
        for g, (mine, *theirs) in enumerate(piece_refs):
            weights[g, :, own] = mine[...]
            size_of = strip // len(theirs)
            for i, part in enumerate(theirs):
                weights[g, i * size_of : (i + 1) * size_of, other] = part[...]
        me = lax.axis_index("rhs")
        for out, s in zip(outs, [None] if slots is None else slots):
            first = 0 if s is None else pl.multiple_of(mate(me, s, n) * size, size)
            for start in range(0, 2 * size, block):
                here = slice(start, start + block)
                product = None
                for g in range(many):
                    for i in range(counts[g]):
                        left = jnp.concatenate(
                            [
                                k_refs[g][i, t, pl.ds(2 * first + start, block), :]
                                for t in range(tiles)
                            ],
                            axis=1,
                        )
                        term = jnp.dot(left, weights[g], preferred_element_type=F32)
                        product = term if product is None else product + term
                even_acc[here, :] = product[:, :LANES]
                odd_acc[here, :] = product[:, LANES:]
            even = even_acc[pl.ds(0, size, stride=2), :]
            odd = odd_acc[pl.ds(1, size, stride=2), :]
            total = even + odd
            if acc_ref is not None:
                total = total + acc_ref[pl.ds(first, size), :]
            out[...] = total

    args = [*packed, *(value for pair in pieces for value in pair)]
    args += [acc] if acc is not None else []
    *result, token = call(
        body,
        [shape(size)] * (1 if slots is None else len(slots)),
        *args,
        scratch=[
            pltpu.VMEM((many, strip, 2 * LANES), BF16),
            pltpu.VMEM((2 * size, LANES), F32),
            pltpu.VMEM((2 * size, LANES), F32),
        ],
        after=after,
    )
    return result, token


def link_groups(links):
    reach = (links - 1) // 2
    panels = lax.axis_size("panel")
    groups = []
    if links == 2 * panels + 1 and panels & (panels - 1) == 0:
        for s in range(panels):

            def numbers(s=s):
                me = lax.axis_index("panel")
                start = lax.rem((me ^ s) - me + reach + panels, panels)
                return [start + panels * i for i in range(3 if s == 0 else 2)]

            bring = functools.partial(swapped, axis="panel", s=s, n=panels)
            groups.append((bring, numbers, 3 if s == 0 else 2))
        return groups
    offsets = {}
    for link in range(links):
        offsets.setdefault((link - reach) % panels, []).append(link)
    for o in sorted(offsets, key=lambda o: min(o, panels - o)):
        bring = functools.partial(shifted, axis="panel", by=o)
        groups.append((bring, functools.partial(list, offsets[o]), len(offsets[o])))
    return groups


def operate(packed, groups, low, direction, between, final):
    n = lax.axis_size("rhs")
    arrived = [low] + [bring(low) for bring, _, _ in groups[1:]]
    directions = [direction] + [swapped(direction, "rhs", s, n) for s in range(1, n)]
    pairs = [[low, swapped(low, "coef", 1, 2)]]
    (acc,), token = link_products(packed[:1], pairs, None, n, None)
    after = (token, between(token))
    held = (*after, *directions[1:])
    for place, piece in enumerate(arrived[1:], start=1):
        if final and place == len(groups) - 1:
            (acc,), token = link_products(packed[1:-1], pairs[1:], acc, n, None, held)
            piece, held = lax.optimization_barrier((piece, (token,)))
        else:
            piece, _ = lax.optimization_barrier((piece, after))
        rows = piece.shape[0] // PARTS
        cut = [piece]
        if final and place < len(groups) - 1:
            cut = [piece[i * rows : (i + 1) * rows] for i in range(PARTS)]
        pairs.append([piece, *(swapped(part, "coef", 1, 2) for part in cut)])
    if final:
        parts, _ = link_products(packed[-1:], pairs[-1:], acc, n, range(n), held)
        return parts, directions
    if len(groups) > 2:
        (acc,), _ = link_products(packed[1:-1], pairs[1:-1], acc, n, None, held)
    mates, token = link_products(packed[-1:], pairs[-1:], acc, n, range(1, n), held)
    own, _ = link_products(packed[-1:], pairs[-1:], acc, n, [0], (token,))
    return own + mates, directions


PACKED = LANES // 2 + SUB


def corner():
    row = lax.broadcasted_iota(jnp.int32, (LANES // 2, LANES), 0)
    lane = lax.broadcasted_iota(jnp.int32, (LANES // 2, LANES), 1)
    return row, lane, lane < LANES // 2


def packed_symmetric(matrix):
    half = LANES // 2
    row, lane, left = corner()
    top = matrix[:half]
    last = pltpu.roll(matrix[half:], half, 1)
    body = jnp.where(left & (lane > row), last, top)
    diagonal = jnp.sum(jnp.where(lane == row, last, 0.0), axis=0, keepdims=True)
    return jnp.concatenate([body, jnp.broadcast_to(diagonal, (SUB, LANES))], axis=0)


def unpacked_symmetric(rows):
    half = LANES // 2
    row, lane, left = corner()
    body, diagonal = rows[:half], rows[half : half + 1]
    top = jnp.where(left & (lane >= row), 0.0, body)
    last = jnp.where(left & (lane > row), body, 0.0)
    sides = jnp.concatenate([top, pltpu.roll(last, half, 1)], axis=0)
    top = jnp.where(lane == row, body, 0.0)
    last = jnp.where(lane == row, jnp.broadcast_to(diagonal, body.shape), 0.0)
    return sides + sides.T + jnp.concatenate([top, pltpu.roll(last, half, 1)], axis=0)


def symmetric(raw):
    return 0.5 * (raw + raw.T)


JOINT = PACKED + SUB + LANES


def linear_grams(parts, directions, residual, turns, gram, final):
    strip = parts[0].shape[0]
    n = len(parts)
    first = gram is not None
    extra = [gram] if first else [] if final else [residual, *turns]
    rows = PACKED if final else JOINT // 2

    def body(*refs):
        images, ds = refs[:n], refs[n : 2 * n]
        rest = refs[2 * n : 2 * n + len(extra)]
        outs = refs[2 * n + len(extra) :]
        found = None
        for s in range(n):
            image, right = images[s][...], ds[s][...]
            if extra and not first:
                r = rest[0][...] if s == 0 else right - rest[s][...]
                right = jnp.concatenate([right, r], axis=1)
            term = mm(image, right, (0, 0))
            found = term if s == 0 else found + term
        if final:
            outs[0][...] = packed_symmetric(symmetric(found))
            return
        mine, mates, stacked = outs
        if first:
            stacked[:PACKED], whole = rest[0][...], found
        else:
            stacked[:PACKED] = packed_symmetric(symmetric(found[:, :LANES]))
            whole = found[:, LANES:]
        stacked[PACKED : PACKED + SUB] = jnp.zeros((SUB, LANES), F32)
        stacked[PACKED + SUB :] = whole
        half = lax.axis_index("coef")
        mine[...] = stacked[pl.ds(pl.multiple_of(half * rows, SUB), rows), :]
        mates[...] = stacked[pl.ds(pl.multiple_of((1 - half) * rows, SUB), rows), :]

    *pieces, _ = call(
        body,
        [shape(rows)] * (1 if final else 2),
        *parts,
        *directions,
        *extra,
        scratch=[] if final else [pltpu.VMEM((2 * rows, LANES), F32)],
    )
    return pieces


def gram_of(field, *tokens):
    def body(field, out):
        value = field[...]
        out[...] = packed_symmetric(mm(value, value, (0, 0)))

    return call(body, [shape(PACKED)], field, after=tokens)


def square_gram(image_parts):
    strip = image_parts[0].shape[0]
    parts = len(image_parts)

    def body(*refs):
        ins, image_out, out = refs[:parts], refs[parts], refs[parts + 1]
        image = ins[0][...]
        for ref in ins[1:]:
            image = image + ref[...]
        image_out[...] = image
        out[...] = packed_symmetric(mm(image, image, (0, 0)))

    image, square, _ = call(
        body,
        [shape(strip), shape(PACKED)],
        *image_parts,
    )
    return image, square


def reciprocal(value):
    near = pl.reciprocal(value, approx=True)
    for _ in range(2):
        near = near * (2.0 - value * near)
    return near


def next_pivot(column, following, i, inverse):
    product = column[i + 1 : i + 2] * following[i : i + 1]
    return following[i + 1 : i + 2] - product * inverse


def inverted(matrices, lane):
    strips = matrices[0].shape[0] // SUB
    place = lax.broadcasted_iota(jnp.int32, (SUB, LANES), 0)
    held = [[value[SUB * k : SUB * (k + 1)] for k in range(strips)] for value in matrices]

    def lanes_of(value, at):
        return jnp.broadcast_to(value[:, at : at + 1], (SUB, LANES))

    def rows_of(value):
        return [jnp.broadcast_to(value[i : i + 1], (SUB, LANES)) for i in range(SUB)]

    def update(k, j, spread):
        for a, rows in zip(held, spread):
            row = a[k]
            for i in range(SUB):
                row = row - lanes_of(a[k], lane + SUB * j + i) * rows[i]
            a[k] = row

    for j in range(strips):
        if j:
            spread = [rows_of(a[j - 1]) for a in held]
            update(j, j - 1, spread)
        waiting = [k for k in range(strips) if j and k not in (j, j - 1)]
        now = [
            [a[j], *(lanes_of(a[j], lane + SUB * j + i) for i in range(SUB))] for a in held
        ]
        for i in range(SUB):
            here = place == i
            for index, values in enumerate(now):
                column = values[1 + i]
                inverse = 1.0 / column[i : i + 1]

                def step(value):
                    row = value[i : i + 1] * inverse
                    return jnp.where(here, row, value - column * row)

                now[index] = [
                    step(value) if at < 1 or at > 1 + i else value
                    for at, value in enumerate(values)
                ]
            for k in waiting[i : i + 1]:
                update(k, j - 1, spread)
        for a, values in zip(held, now):
            a[j] = values[0]
    spread = [rows_of(a[-1]) for a in held]
    for k in range(strips - 1):
        update(k, strips - 1, spread)
    return [jnp.concatenate(a, axis=0) for a in held]


def eliminated(*systems):
    half = LANES // 2
    row = lax.broadcasted_iota(jnp.int32, (half, LANES), 0)
    lane = lax.broadcasted_iota(jnp.int32, (half, LANES), 1)
    left = lane < half
    first = inverted(
        [
            jnp.where(left, matrix[:half], (lane - half == row).astype(F32))
            for matrix, _ in systems
        ],
        0,
    )
    tops, lasts = [], []
    for (matrix, sides), value in zip(systems, first):
        value = pltpu.roll(value, half, 1)[:, :half]
        top = mm(value, jnp.concatenate([matrix[:half], sides[:half]], axis=1))
        low = jnp.concatenate([matrix[half:], sides[half:]], axis=1)
        tops.append(top)
        lasts.append(low - mm(matrix[half:, :half], top))
    second = inverted(
        [jnp.where(left, (lane == row).astype(F32), last[:, :LANES]) for last in lasts], half
    )
    found = []
    for top, last, value in zip(tops, lasts, second):
        low = mm(value[:, :half], last[:, LANES:])
        high = top[:, LANES:] - mm(
            top[:, :LANES], jnp.concatenate([jnp.zeros_like(low), low], axis=0)
        )
        found.append(jnp.concatenate([high, low], axis=0))
    return found


def eliminated_alone(matrix, sides):
    n = matrix.shape[0]
    strips = n // SUB
    place = lax.broadcasted_iota(jnp.int32, (SUB, LANES), 0)

    def cut(value):
        return [value[SUB * k : SUB * (k + 1)] for k in range(strips)]

    def lanes_of(value, lane):
        return jnp.broadcast_to(value[:, lane : lane + 1], (SUB, LANES))

    held = [(cut(matrix), cut(sides))]

    def rows_of(value):
        return [jnp.broadcast_to(value[i : i + 1], (SUB, LANES)) for i in range(SUB)]

    def update(k, j, spread):
        for (a, b), (rows_a, rows_b) in zip(held, spread):
            row_a, row_b = a[k], b[k]
            for i in range(SUB):
                factor = lanes_of(a[k], SUB * j + i)
                row_a = row_a - factor * rows_a[i]
                row_b = row_b - factor * rows_b[i]
            a[k], b[k] = row_a, row_b

    for j in range(strips):
        if j:
            spread = [(rows_of(a[j - 1]), rows_of(b[j - 1])) for a, b in held]
            update(j, j - 1, spread)
        waiting = [k for k in range(strips) if j and k not in (j, j - 1)]
        now = [
            [a[j], b[j], *(lanes_of(a[j], SUB * j + i) for i in range(SUB))] for a, b in held
        ]
        pivots = [values[2][:1] for values in now]
        for i in range(SUB):
            here = place == i
            for index, values in enumerate(now):
                column = values[2 + i]
                inverse = reciprocal(pivots[index])
                if i + 1 < SUB:
                    pivots[index] = next_pivot(column, values[3 + i], i, inverse)

                def step(value):
                    row = value[i : i + 1] * inverse
                    return jnp.where(here, row, value - column * row)

                now[index] = [
                    step(value) if place_of < 2 or place_of > 2 + i else value
                    for place_of, value in enumerate(values)
                ]
            for k in waiting[2 * i : 2 * i + 2]:
                update(k, j - 1, spread)
        for (a, b), values in zip(held, now):
            a[j], b[j] = values[:2]
    spread = [(rows_of(a[-1]), rows_of(b[-1])) for a, b in held]
    for k in range(strips - 1):
        update(k, strips - 1, spread)
    return jnp.concatenate(held[0][1], axis=0)


def identity():
    return (
        lax.broadcasted_iota(jnp.int32, (LANES, LANES), 0)
        == lax.broadcasted_iota(jnp.int32, (LANES, LANES), 1)
    ).astype(F32)


def stepped(solution, before, alpha, beta, token):
    fields = [*before, alpha, beta] + ([] if solution is None else [solution])
    n = len(before)

    def body(*refs):
        ds, a, b, refs = refs[:n], refs[n], refs[n + 1], refs[n + 2 :]
        change = mm(ds[0][...], a[...])
        refs[-n][...] = change if solution is None else refs[0][...] + change
        for s in range(1, n):
            refs[s - n][...] = mm(ds[s][...], b[...])

    solution, *turns, token = call(
        body, [shape(before[0].shape[0])] * n, *fields, after=[token]
    )
    return solution, turns, token


def finish(small, gram, residual, direction, solution, image):
    strip = residual.shape[0]

    def body(small, g, r, d, s, *refs):
        *images, out, new_r = refs
        alpha = eliminated_alone(unpacked_symmetric(small[...]), g[...])
        image = images[0][...]
        for ref in images[1:]:
            image = image + ref[...]
        out[...] = s[...] + mm(d[...], alpha)
        new_r[...] = r[...] - mm(image, alpha)

    return call(
        body,
        [shape(strip), shape(strip)],
        small,
        gram,
        residual,
        direction,
        solution,
        *image,
    )[:-1]


def step_sizes(pieces, gram):
    rows = pieces[0].shape[0]
    first = gram is None
    fields = [*pieces] + ([] if first else [gram])

    def body(mine, mates, *refs):
        *refs, alpha_out, whole_out, inverse_out, gram_out, raw = refs
        half = lax.axis_index("coef")
        raw[pl.ds(pl.multiple_of(half * rows, SUB), rows), :] = mine[...]
        raw[pl.ds(pl.multiple_of((1 - half) * rows, SUB), rows), :] = mates[...]
        sym, whole = unpacked_symmetric(raw[:PACKED, :]), raw[PACKED + SUB :, :]
        g = sym if first else refs[0][...]
        curvature = symmetric(whole) if first else sym
        alpha_out[...], inverse_out[...] = eliminated((curvature, g), (g, identity()))
        whole_out[...] = whole
        gram_out[...] = g

    return call(
        body,
        [shape(LANES)] * 4,
        *fields,
        scratch=[pltpu.VMEM((2 * rows, LANES), F32)],
    )[:-1]


def turn(square, alpha, whole, inverse, gram, residual, direction, image):
    strip = residual.shape[0]

    def body(alpha, whole, inverse, gram, r, d, image, *refs):
        *terms, r_out, new_d, low, beta_out, gram_out = refs
        square = terms[0][...]
        for ref in terms[1:]:
            square = square + ref[...]
        a = alpha[...]
        shared = mm(whole[...], a, (0, 0))
        quadratic = mm(a, mm(unpacked_symmetric(square), a), (0, 0))
        following = gram[...] - (shared + shared.T) + quadratic
        beta = mm(inverse[...], following)
        new_r = r[...] - mm(image[...], a)
        value = new_r + mm(d[...], beta)
        r_out[...] = new_r
        low[...] = value.astype(BF16)
        new_d[...] = value
        beta_out[...] = beta
        gram_out[...] = following

    return call(
        body,
        [shape(strip), shape(strip), shape(strip, dtype=BF16), shape(LANES), shape(LANES)],
        alpha,
        whole,
        inverse,
        gram,
        residual,
        direction,
        image,
        *square,
    )[:-1]


def shards(couplings, observations, replicate_mask):
    links, rows = couplings.shape[1], couplings.shape[3]
    strip = couplings.shape[6]
    blocks = couplings.reshape(links, rows, couplings.shape[4], strip)
    blocks = pltpu.with_memory_space_constraint(blocks, pltpu.HBM)
    n = lax.axis_size("rhs")
    obs_matrix = observations.reshape(observations.shape[0], rows)
    parts, token = right_side_parts(obs_matrix, replicate_mask, n, strip)
    own = [parts[0]] + [swapped(parts[s], "rhs", s, n) for s in range(1, n)]
    groups = link_groups(links)
    packed = []
    for _, numbers, count in groups[:2]:
        value, token = retiled(blocks, numbers, count, token)
        packed.append(value)
    residual, low, token = sum_and_round(own, token)
    for _, numbers, count in groups[2:]:
        value, token = retiled(blocks, numbers, count, token)
        packed.append(value)
    retile_token = token
    direction = residual
    solution = gram = beta = before = alpha = None
    for step in range(ITERS):
        first, final = step == 0, step + 1 == ITERS
        state = [solution, None, None]

        def between(token):
            if first:
                state[2], token = gram_of(residual, token, retile_token)
                return token
            *state[:2], token = stepped(solution, before, alpha, beta, token)
            return token

        parts, directions = operate(packed, groups, low, direction, between, final)
        solution, turns, own_gram = state
        image_parts = [parts[0]] + [swapped(parts[s], "rhs", s, n) for s in range(1, n)]
        linear = linear_grams(parts, directions, residual, turns, own_gram, final)
        if final:
            small = reduce_one(*linear)
            solution, residual = finish(
                small, gram, residual, direction, solution, image_parts
            )
            break
        image, square = square_gram(image_parts)
        linear, square = reduce_both(*linear, square)
        alpha, whole, inverse, gram = step_sizes(linear, gram)
        square[1:], alpha = lax.optimization_barrier((square[1:], alpha))
        before = directions
        residual, direction, low, beta, gram = turn(
            square, alpha, whole, inverse, gram, residual, direction, image
        )
    shape_out = (1, 1, strip, LANES)
    return (solution.reshape(shape_out), residual.reshape(shape_out))


def solution(mesh):
    placed = (
        P("panel", None, "coef", None, None, "rhs", None),
        P(("groups", "rhs"), "panel", "coef", None),
        P(("groups", "rhs"), None),
    )
    return jax.shard_map(
        shards,
        mesh=mesh,
        in_specs=placed,
        out_specs=(
            P(("groups", "panel"), "coef", "rhs", None),
            P(("groups", "panel"), "coef", "rhs", None),
        ),
        check_vma=False,
    )
```

```python
import functools

import jax
import jax.numpy as jnp
from jax import lax
from jax.experimental import pallas as pl
from jax.experimental.pallas import tpu as pltpu
from jax.sharding import PartitionSpec as P

ITERS = 3
PARTS = 2
LANES = 128
SUB = 8
VMEM_LIMIT = 14 * 2**20
F32 = jnp.float32
BF16 = jnp.bfloat16
VMEM = pl.BlockSpec(memory_space=pltpu.VMEM)
ANY = pl.BlockSpec(memory_space=pl.ANY)
HBM = pl.BlockSpec(memory_space=pltpu.HBM)


def mm(a, b, dims=(1, 0)):
    return lax.dot_general(
        a,
        b,
        (((dims[0],), (dims[1],)), ((), ())),
        precision=lax.Precision.HIGHEST,
        preferred_element_type=F32,
    )


def halves(value):
    high = value.astype(BF16)
    return high, (value - high.astype(F32)).astype(BF16)


def mm_field(a, b):
    (a, a_low), (b, b_low) = halves(a), halves(b)

    def part(left, right):
        return jnp.dot(left, right, preferred_element_type=F32)

    return part(a, b) + (part(a, b_low) + part(a_low, b))


def call(body, outs, *args, scratch=(), after=(), any_args=0, any_outs=False):
    inputs, outputs, waits = len(args), len(outs), len(after)

    def ordered(*refs):
        token = refs[inputs + waits + outputs]
        token[...] = jnp.zeros_like(token)
        body(
            *refs[:inputs],
            *refs[inputs + waits : inputs + waits + outputs],
            *refs[inputs + waits + outputs + 1 :],
        )

    return pl.pallas_call(
        ordered,
        out_shape=list(outs) + [shape(SUB)],
        in_specs=[HBM] * any_args + [VMEM] * (inputs - any_args) + [ANY] * waits,
        out_specs=[ANY if any_outs else VMEM] * outputs + [VMEM],
        scratch_shapes=list(scratch),
        cost_estimate=pl.CostEstimate(flops=1, bytes_accessed=1, transcendentals=0),
        compiler_params=pltpu.CompilerParams(vmem_limit_bytes=VMEM_LIMIT),
    )(*args, *after)


def shape(rows, cols=LANES, dtype=F32):
    return jax.ShapeDtypeStruct((rows, cols), dtype)


def permute(value, axis, pairs):
    return lax.ppermute(value, axis, pairs)


def shifted(value, axis, by):
    n = lax.axis_size(axis)
    return permute(value, axis, [((i + by) % n, i) for i in range(n)])


def mate(i, s, n):
    return i ^ s if n & (n - 1) == 0 else (s - i) % n


def swapped(value, axis, s, n):
    return permute(value, axis, [(mate(i, s, n), i) for i in range(n)])


def sum_near(value):
    axes = ("panel", "rhs")
    count = lax.axis_size(axes)
    three, two, one = (swapped(value, axes, s, count) for s in (3, 2, 1))
    return (value + one) + (two + three)


def from_far(value):
    axes = ("panel", "rhs")
    return swapped(value, axes, 4, lax.axis_size(axes))


def sum_far(value, meanwhile=None):
    other = from_far(value)
    if meanwhile is not None:
        other, _ = lax.optimization_barrier((other, meanwhile))
    return value + other


def by_stages():
    return lax.axis_size("panel") == 4 and lax.axis_size("rhs") == 2


def reduce_one(value):
    value = value + swapped(value, "coef", 1, 2)
    if not by_stages():
        return lax.psum(value, ("panel", "rhs"))
    return sum_far(sum_near(value))


def reduce_both(mine, mates, square):
    value = mine + swapped(mates, "coef", 1, 2)
    whole = square + swapped(square, "coef", 1, 2)
    if by_stages():
        rows = value.shape[0]
        value = sum_far(value, meanwhile=square)
        both = sum_near(jnp.concatenate([value, whole], axis=0))
        value, whole = both[:rows], both[rows:]
        terms = [whole, from_far(whole)]
    else:
        value, whole = lax.psum((value, whole), ("panel", "rhs"))
        terms = [whole]
    return [value, swapped(value, "coef", 1, 2)], terms


def right_side_parts(obs, mask, n, strip):
    def body(obs_hbm, mask_hbm, *refs):
        *outs, obs_ref, mask_ref, sems = refs
        copies = [
            pltpu.make_async_copy(mask_hbm, mask_ref, sems.at[0]),
            pltpu.make_async_copy(obs_hbm, obs_ref, sems.at[1]),
        ]
        for copy in copies:
            copy.start()
        for copy in copies:
            copy.wait()
        signs = (2 * mask_ref[...] - 1).astype(BF16)
        me = lax.axis_index("rhs")
        for s in range(n):
            place = pl.multiple_of(mate(me, s, n) * strip, strip)
            outs[s][...] = lax.dot_general(
                obs_ref[:, pl.ds(place, strip)],
                signs,
                (((0,), (0,)), ((), ())),
                preferred_element_type=F32,
            )

    *parts, token = call(
        body,
        [shape(strip)] * n,
        pltpu.with_memory_space_constraint(obs, pltpu.HBM),
        pltpu.with_memory_space_constraint(mask, pltpu.HBM),
        scratch=[
            pltpu.VMEM(obs.shape, BF16),
            pltpu.VMEM(mask.shape, mask.dtype),
            pltpu.SemaphoreType.DMA((2,)),
        ],
        any_args=2,
    )
    return parts, token


def sum_and_round(parts, token):
    strip = parts[0].shape[0]

    def body(*refs):
        *ins, out, low = refs
        total = ins[0][...]
        for ref in ins[1:]:
            total = total + ref[...]
        out[...] = total
        low[...] = total.astype(BF16)

    return call(
        body, [shape(strip), shape(strip, dtype=BF16)], *parts, after=[token]
    )


def retiled(blocks, links, count, token):
    rows, strip = blocks.shape[1], blocks.shape[3]
    tiles = strip // LANES

    def body(k_ref, out, sems):
        copies = []
        for i, link in enumerate(links()):
            for t in range(tiles):
                copy = pltpu.make_async_copy(
                    k_ref.at[link, :, :, pl.ds(t * LANES, LANES)], out.at[i, t], sems.at[i, t]
                )
                copy.start()
                copies.append(copy)
        for copy in copies:
            copy.wait()

    packed, token = call(
        body,
        [pltpu.VMEM((count, tiles, rows, 2, LANES), BF16)],
        blocks,
        scratch=[pltpu.SemaphoreType.DMA((count, tiles))],
        after=[token],
        any_args=1,
        any_outs=True,
    )
    return packed, token


def link_products(packed, pieces, acc, n, slots, after=()):
    tiles, rows = packed[0].shape[1:3]
    counts = [value.shape[0] for value in packed]
    many = len(packed)
    packed = [
        pltpu.with_memory_space_constraint(
            value.reshape(value.shape[0], tiles, 2 * rows, LANES), pltpu.VMEM
        )
        for value in packed
    ]
    strip = tiles * LANES
    size = rows if slots is None else rows // n
    block = min(512, 2 * size)

    def body(*refs):
        k_refs, refs = refs[:many], refs[many:]
        piece_refs = []
        for pair in pieces:
            piece_refs.append(refs[: len(pair)])
            refs = refs[len(pair) :]
        acc_ref = refs[0] if acc is not None else None
        outs = refs[acc is not None : -3]
        weights, even_acc, odd_acc = refs[-3:]
        half = lax.axis_index("coef")
        own = pl.ds(pl.multiple_of(half * LANES, LANES), LANES)
        other = pl.ds(pl.multiple_of((1 - half) * LANES, LANES), LANES)
        for g, (mine, *theirs) in enumerate(piece_refs):
            weights[g, :, own] = mine[...]
            size_of = strip // len(theirs)
            for i, part in enumerate(theirs):
                weights[g, i * size_of : (i + 1) * size_of, other] = part[...]
        me = lax.axis_index("rhs")
        for out, s in zip(outs, [None] if slots is None else slots):
            first = 0 if s is None else pl.multiple_of(mate(me, s, n) * size, size)
            for start in range(0, 2 * size, block):
                here = slice(start, start + block)
                product = None
                for g in range(many):
                    for i in range(counts[g]):
                        left = jnp.concatenate(
                            [
                                k_refs[g][i, t, pl.ds(2 * first + start, block), :]
                                for t in range(tiles)
                            ],
                            axis=1,
                        )
                        term = jnp.dot(left, weights[g], preferred_element_type=F32)
                        product = term if product is None else product + term
                even_acc[here, :] = product[:, :LANES]
                odd_acc[here, :] = product[:, LANES:]
            even = even_acc[pl.ds(0, size, stride=2), :]
            odd = odd_acc[pl.ds(1, size, stride=2), :]
            total = even + odd
            if acc_ref is not None:
                total = total + acc_ref[pl.ds(first, size), :]
            out[...] = total

    args = [*packed, *(value for pair in pieces for value in pair)]
    args += [acc] if acc is not None else []
    *result, token = call(
        body,
        [shape(size)] * (1 if slots is None else len(slots)),
        *args,
        scratch=[
            pltpu.VMEM((many, strip, 2 * LANES), BF16),
            pltpu.VMEM((2 * size, LANES), F32),
            pltpu.VMEM((2 * size, LANES), F32),
        ],
        after=after,
    )
    return result, token


def link_groups(links):
    reach = (links - 1) // 2
    panels = lax.axis_size("panel")
    groups = []
    if links == 2 * panels + 1 and panels & (panels - 1) == 0:
        for s in range(panels):

            def numbers(s=s):
                me = lax.axis_index("panel")
                start = lax.rem((me ^ s) - me + reach + panels, panels)
                return [start + panels * i for i in range(3 if s == 0 else 2)]

            bring = functools.partial(swapped, axis="panel", s=s, n=panels)
            groups.append((bring, numbers, 3 if s == 0 else 2))
        return groups
    offsets = {}
    for link in range(links):
        offsets.setdefault((link - reach) % panels, []).append(link)
    for o in sorted(offsets, key=lambda o: min(o, panels - o)):
        bring = functools.partial(shifted, axis="panel", by=o)
        groups.append((bring, functools.partial(list, offsets[o]), len(offsets[o])))
    return groups


def operate(packed, groups, low, direction, between, final):
    n = lax.axis_size("rhs")
    arrived = [low] + [bring(low) for bring, _, _ in groups[1:]]
    directions = [direction] + [swapped(direction, "rhs", s, n) for s in range(1, n)]
    pairs = [[low, swapped(low, "coef", 1, 2)]]
    (acc,), token = link_products(packed[:1], pairs, None, n, None)
    after = (token, between(token))
    held = (*after, *directions[1:])
    for place, piece in enumerate(arrived[1:], start=1):
        if final and place == len(groups) - 1:
            (acc,), token = link_products(packed[1:-1], pairs[1:], acc, n, None, held)
            piece, held = lax.optimization_barrier((piece, (token,)))
        else:
            piece, _ = lax.optimization_barrier((piece, after))
        rows = piece.shape[0] // PARTS
        cut = [piece]
        if final and place < len(groups) - 1:
            cut = [piece[i * rows : (i + 1) * rows] for i in range(PARTS)]
        pairs.append([piece, *(swapped(part, "coef", 1, 2) for part in cut)])
    if final:
        parts, _ = link_products(packed[-1:], pairs[-1:], acc, n, range(n), held)
        return parts, directions
    if len(groups) > 2:
        (acc,), _ = link_products(packed[1:-1], pairs[1:-1], acc, n, None, held)
    mates, token = link_products(packed[-1:], pairs[-1:], acc, n, range(1, n), held)
    own, _ = link_products(packed[-1:], pairs[-1:], acc, n, [0], (token,))
    return own + mates, directions


PACKED = LANES // 2 + SUB


def corner():
    row = lax.broadcasted_iota(jnp.int32, (LANES // 2, LANES), 0)
    lane = lax.broadcasted_iota(jnp.int32, (LANES // 2, LANES), 1)
    return row, lane, lane < LANES // 2


def packed_symmetric(matrix):
    half = LANES // 2
    row, lane, left = corner()
    top = matrix[:half]
    last = pltpu.roll(matrix[half:], half, 1)
    body = jnp.where(left & (lane > row), last, top)
    diagonal = jnp.sum(jnp.where(lane == row, last, 0.0), axis=0, keepdims=True)
    return jnp.concatenate([body, jnp.broadcast_to(diagonal, (SUB, LANES))], axis=0)


def unpacked_symmetric(rows):
    half = LANES // 2
    row, lane, left = corner()
    body, diagonal = rows[:half], rows[half : half + 1]
    top = jnp.where(left & (lane >= row), 0.0, body)
    last = jnp.where(left & (lane > row), body, 0.0)
    sides = jnp.concatenate([top, pltpu.roll(last, half, 1)], axis=0)
    top = jnp.where(lane == row, body, 0.0)
    last = jnp.where(lane == row, jnp.broadcast_to(diagonal, body.shape), 0.0)
    return sides + sides.T + jnp.concatenate([top, pltpu.roll(last, half, 1)], axis=0)


def symmetric(raw):
    return 0.5 * (raw + raw.T)


JOINT = PACKED + SUB + LANES


def linear_grams(parts, directions, residual, turns, gram, final):
    strip = parts[0].shape[0]
    n = len(parts)
    first = gram is not None
    extra = [gram] if first else [] if final else [residual, *turns]
    rows = PACKED if final else JOINT // 2

    def body(*refs):
        images, ds = refs[:n], refs[n : 2 * n]
        rest = refs[2 * n : 2 * n + len(extra)]
        outs = refs[2 * n + len(extra) :]
        found = None
        for s in range(n):
            image, right = images[s][...], ds[s][...]
            if extra and not first:
                r = rest[0][...] if s == 0 else right - rest[s][...]
                right = jnp.concatenate([right, r], axis=1)
            term = mm(image, right, (0, 0))
            found = term if s == 0 else found + term
        if final:
            outs[0][...] = packed_symmetric(symmetric(found))
            return
        mine, mates, stacked = outs
        if first:
            stacked[:PACKED], whole = rest[0][...], found
        else:
            stacked[:PACKED] = packed_symmetric(symmetric(found[:, :LANES]))
            whole = found[:, LANES:]
        stacked[PACKED : PACKED + SUB] = jnp.zeros((SUB, LANES), F32)
        stacked[PACKED + SUB :] = whole
        half = lax.axis_index("coef")
        mine[...] = stacked[pl.ds(pl.multiple_of(half * rows, SUB), rows), :]
        mates[...] = stacked[pl.ds(pl.multiple_of((1 - half) * rows, SUB), rows), :]

    *pieces, _ = call(
        body,
        [shape(rows)] * (1 if final else 2),
        *parts,
        *directions,
        *extra,
        scratch=[] if final else [pltpu.VMEM((2 * rows, LANES), F32)],
    )
    return pieces


def gram_of(field, *tokens):
    def body(field, out):
        value = field[...]
        out[...] = packed_symmetric(mm(value, value, (0, 0)))

    return call(body, [shape(PACKED)], field, after=tokens)


def square_gram(image_parts):
    strip = image_parts[0].shape[0]
    parts = len(image_parts)

    def body(*refs):
        ins, image_out, out = refs[:parts], refs[parts], refs[parts + 1]
        image = ins[0][...]
        for ref in ins[1:]:
            image = image + ref[...]
        image_out[...] = image
        out[...] = packed_symmetric(mm(image, image, (0, 0)))

    image, square, _ = call(
        body,
        [shape(strip), shape(PACKED)],
        *image_parts,
    )
    return image, square


def reciprocal(value):
    near = pl.reciprocal(value, approx=True)
    for _ in range(2):
        near = near * (2.0 - value * near)
    return near


def next_pivot(column, following, i, inverse):
    product = column[i + 1 : i + 2] * following[i : i + 1]
    return following[i + 1 : i + 2] - product * inverse


def inverted(matrices, lane):
    strips = matrices[0].shape[0] // SUB
    place = lax.broadcasted_iota(jnp.int32, (SUB, LANES), 0)
    held = [[value[SUB * k : SUB * (k + 1)] for k in range(strips)] for value in matrices]

    def lanes_of(value, at):
        return jnp.broadcast_to(value[:, at : at + 1], (SUB, LANES))

    def rows_of(value):
        return [jnp.broadcast_to(value[i : i + 1], (SUB, LANES)) for i in range(SUB)]

    def update(k, j, spread):
        for a, rows in zip(held, spread):
            row = a[k]
            for i in range(SUB):
                row = row - lanes_of(a[k], lane + SUB * j + i) * rows[i]
            a[k] = row

    for j in range(strips):
        if j:
            spread = [rows_of(a[j - 1]) for a in held]
            update(j, j - 1, spread)
        waiting = [k for k in range(strips) if j and k not in (j, j - 1)]
        now = [
            [a[j], *(lanes_of(a[j], lane + SUB * j + i) for i in range(SUB))] for a in held
        ]
        for i in range(SUB):
            here = place == i
            for index, values in enumerate(now):
                column = values[1 + i]
                inverse = 1.0 / column[i : i + 1]

                def step(value):
                    row = value[i : i + 1] * inverse
                    return jnp.where(here, row, value - column * row)

                now[index] = [
                    step(value) if at < 1 or at > 1 + i else value
                    for at, value in enumerate(values)
                ]
            for k in waiting[i : i + 1]:
                update(k, j - 1, spread)
        for a, values in zip(held, now):
            a[j] = values[0]
    spread = [rows_of(a[-1]) for a in held]
    for k in range(strips - 1):
        update(k, strips - 1, spread)
    return [jnp.concatenate(a, axis=0) for a in held]


def eliminated(*systems):
    half = LANES // 2
    row = lax.broadcasted_iota(jnp.int32, (half, LANES), 0)
    lane = lax.broadcasted_iota(jnp.int32, (half, LANES), 1)
    left = lane < half
    first = inverted(
        [
            jnp.where(left, matrix[:half], (lane - half == row).astype(F32))
            for matrix, _ in systems
        ],
        0,
    )
    tops, lasts = [], []
    for (matrix, sides), value in zip(systems, first):
        value = pltpu.roll(value, half, 1)[:, :half]
        top = mm(value, jnp.concatenate([matrix[:half], sides[:half]], axis=1))
        low = jnp.concatenate([matrix[half:], sides[half:]], axis=1)
        tops.append(top)
        lasts.append(low - mm(matrix[half:, :half], top))
    second = inverted(
        [jnp.where(left, (lane == row).astype(F32), last[:, :LANES]) for last in lasts], half
    )
    found = []
    for top, last, value in zip(tops, lasts, second):
        low = mm(value[:, :half], last[:, LANES:])
        high = top[:, LANES:] - mm(
            top[:, :LANES], jnp.concatenate([jnp.zeros_like(low), low], axis=0)
        )
        found.append(jnp.concatenate([high, low], axis=0))
    return found


def eliminated_alone(matrix, sides):
    n = matrix.shape[0]
    strips = n // SUB
    place = lax.broadcasted_iota(jnp.int32, (SUB, LANES), 0)

    def cut(value):
        return [value[SUB * k : SUB * (k + 1)] for k in range(strips)]

    def lanes_of(value, lane):
        return jnp.broadcast_to(value[:, lane : lane + 1], (SUB, LANES))

    held = [(cut(matrix), cut(sides))]

    def rows_of(value):
        return [jnp.broadcast_to(value[i : i + 1], (SUB, LANES)) for i in range(SUB)]

    def update(k, j, spread):
        for (a, b), (rows_a, rows_b) in zip(held, spread):
            row_a, row_b = a[k], b[k]
            for i in range(SUB):
                factor = lanes_of(a[k], SUB * j + i)
                row_a = row_a - factor * rows_a[i]
                row_b = row_b - factor * rows_b[i]
            a[k], b[k] = row_a, row_b

    for j in range(strips):
        if j:
            spread = [(rows_of(a[j - 1]), rows_of(b[j - 1])) for a, b in held]
            update(j, j - 1, spread)
        waiting = [k for k in range(strips) if j and k not in (j, j - 1)]
        now = [
            [a[j], b[j], *(lanes_of(a[j], SUB * j + i) for i in range(SUB))] for a, b in held
        ]
        pivots = [values[2][:1] for values in now]
        for i in range(SUB):
            here = place == i
            for index, values in enumerate(now):
                column = values[2 + i]
                inverse = reciprocal(pivots[index])
                if i + 1 < SUB:
                    pivots[index] = next_pivot(column, values[3 + i], i, inverse)

                def step(value):
                    row = value[i : i + 1] * inverse
                    return jnp.where(here, row, value - column * row)

                now[index] = [
                    step(value) if place_of < 2 or place_of > 2 + i else value
                    for place_of, value in enumerate(values)
                ]
            for k in waiting[2 * i : 2 * i + 2]:
                update(k, j - 1, spread)
        for (a, b), values in zip(held, now):
            a[j], b[j] = values[:2]
    spread = [(rows_of(a[-1]), rows_of(b[-1])) for a, b in held]
    for k in range(strips - 1):
        update(k, strips - 1, spread)
    return jnp.concatenate(held[0][1], axis=0)


def identity():
    return (
        lax.broadcasted_iota(jnp.int32, (LANES, LANES), 0)
        == lax.broadcasted_iota(jnp.int32, (LANES, LANES), 1)
    ).astype(F32)


def stepped(solution, before, alpha, beta, token):
    fields = [*before, alpha, beta] + ([] if solution is None else [solution])
    n = len(before)

    def body(*refs):
        ds, a, b, refs = refs[:n], refs[n], refs[n + 1], refs[n + 2 :]
        change = mm(ds[0][...], a[...])
        refs[-n][...] = change if solution is None else refs[0][...] + change
        for s in range(1, n):
            refs[s - n][...] = mm(ds[s][...], b[...])

    solution, *turns, token = call(
        body, [shape(before[0].shape[0])] * n, *fields, after=[token]
    )
    return solution, turns, token


def finish(small, gram, residual, direction, solution, image):
    strip = residual.shape[0]

    def body(small, g, r, d, s, *refs):
        *images, out, new_r = refs
        alpha = eliminated_alone(unpacked_symmetric(small[...]), g[...])
        image = images[0][...]
        for ref in images[1:]:
            image = image + ref[...]
        out[...] = s[...] + mm_field(d[...], alpha)
        new_r[...] = r[...] - mm_field(image, alpha)

    return call(
        body,
        [shape(strip), shape(strip)],
        small,
        gram,
        residual,
        direction,
        solution,
        *image,
    )[:-1]


def step_sizes(pieces, gram):
    rows = pieces[0].shape[0]
    first = gram is None
    fields = [*pieces] + ([] if first else [gram])

    def body(mine, mates, *refs):
        *refs, alpha_out, whole_out, inverse_out, gram_out, raw = refs
        half = lax.axis_index("coef")
        raw[pl.ds(pl.multiple_of(half * rows, SUB), rows), :] = mine[...]
        raw[pl.ds(pl.multiple_of((1 - half) * rows, SUB), rows), :] = mates[...]
        sym, whole = unpacked_symmetric(raw[:PACKED, :]), raw[PACKED + SUB :, :]
        g = sym if first else refs[0][...]
        curvature = symmetric(whole) if first else sym
        alpha_out[...], inverse_out[...] = eliminated((curvature, g), (g, identity()))
        whole_out[...] = whole
        gram_out[...] = g

    return call(
        body,
        [shape(LANES)] * 4,
        *fields,
        scratch=[pltpu.VMEM((2 * rows, LANES), F32)],
    )[:-1]


def turn(square, alpha, whole, inverse, gram, residual, direction, image):
    strip = residual.shape[0]

    def body(alpha, whole, inverse, gram, r, d, image, *refs):
        *terms, r_out, new_d, low, beta_out, gram_out = refs
        square = terms[0][...]
        for ref in terms[1:]:
            square = square + ref[...]
        a = alpha[...]
        shared = mm(whole[...], a, (0, 0))
        quadratic = mm(a, mm(unpacked_symmetric(square), a), (0, 0))
        following = gram[...] - (shared + shared.T) + quadratic
        beta = mm(inverse[...], following)
        new_r = r[...] - mm_field(image[...], a)
        value = new_r + mm_field(d[...], beta)
        r_out[...] = new_r
        low[...] = value.astype(BF16)
        new_d[...] = value
        beta_out[...] = beta
        gram_out[...] = following

    return call(
        body,
        [shape(strip), shape(strip), shape(strip, dtype=BF16), shape(LANES), shape(LANES)],
        alpha,
        whole,
        inverse,
        gram,
        residual,
        direction,
        image,
        *square,
    )[:-1]


def shards(couplings, observations, replicate_mask):
    links, rows = couplings.shape[1], couplings.shape[3]
    strip = couplings.shape[6]
    blocks = couplings.reshape(links, rows, couplings.shape[4], strip)
    blocks = pltpu.with_memory_space_constraint(blocks, pltpu.HBM)
    n = lax.axis_size("rhs")
    obs_matrix = observations.reshape(observations.shape[0], rows)
    parts, token = right_side_parts(obs_matrix, replicate_mask, n, strip)
    own = [parts[0]] + [swapped(parts[s], "rhs", s, n) for s in range(1, n)]
    groups = link_groups(links)
    packed = []
    for _, numbers, count in groups[:2]:
        value, token = retiled(blocks, numbers, count, token)
        packed.append(value)
    residual, low, token = sum_and_round(own, token)
    for _, numbers, count in groups[2:]:
        value, token = retiled(blocks, numbers, count, token)
        packed.append(value)
    retile_token = token
    direction = residual
    solution = gram = beta = before = alpha = None
    for step in range(ITERS):
        first, final = step == 0, step + 1 == ITERS
        state = [solution, None, None]

        def between(token):
            if first:
                state[2], token = gram_of(residual, token, retile_token)
                return token
            *state[:2], token = stepped(solution, before, alpha, beta, token)
            return token

        parts, directions = operate(packed, groups, low, direction, between, final)
        solution, turns, own_gram = state
        image_parts = [parts[0]] + [swapped(parts[s], "rhs", s, n) for s in range(1, n)]
        linear = linear_grams(parts, directions, residual, turns, own_gram, final)
        if final:
            small = reduce_one(*linear)
            solution, residual = finish(
                small, gram, residual, direction, solution, image_parts
            )
            break
        image, square = square_gram(image_parts)
        linear, square = reduce_both(*linear, square)
        alpha, whole, inverse, gram = step_sizes(linear, gram)
        square[1:], alpha = lax.optimization_barrier((square[1:], alpha))
        before = directions
        residual, direction, low, beta, gram = turn(
            square, alpha, whole, inverse, gram, residual, direction, image
        )
    shape_out = (1, 1, strip, LANES)
    return (solution.reshape(shape_out), residual.reshape(shape_out))


def solution(mesh):
    placed = (
        P("panel", None, "coef", None, None, "rhs", None),
        P(("groups", "rhs"), "panel", "coef", None),
        P(("groups", "rhs"), None),
    )
    return jax.shard_map(
        shards,
        mesh=mesh,
        in_specs=placed,
        out_specs=(
            P(("groups", "panel"), "coef", "rhs", None),
            P(("groups", "panel"), "coef", "rhs", None),
        ),
        check_vma=False,
    )
```
